32 devices in a mesh: batch: 4 (over x, core), seq: 8 (over z, y).
Axes of the slice: x: 2, y: 2, z: 4, core: 2. Of those that a mesh axis runs over, the one named last changes fastest.
Arguments:
- tokens: bfloat16 [16, 1024, 768], P('batch', 'seq'), may hold values from -6 to 6
- ln1_gain: float32 [768], replicated, may hold values from 0.5 to 1.5
- ln1_bias: float32 [768], replicated, may hold values from -1.8 to 1.8
- qkv_weight: bfloat16 [768, 896], replicated, may hold values from -0.3125 to 0.3125
- qkv_bias: float32 [896], replicated, may hold values from -1.8 to 1.8
- out_weight: bfloat16 [768, 768], replicated, may hold values from -0.875 to 0.875
- ln2_gain: float32 [768], replicated, may hold values from 0.5 to 1.5
- ln2_bias: float32 [768], replicated, may hold values from -1.8 to 1.8
- fc1_weight: bfloat16 [768, 3072], replicated, may hold values from -0.21875 to 0.21875
- fc1_bias: float32 [3072], replicated, may hold values from -1.8 to 1.8
- fc2_weight: bfloat16 [3072, 768], replicated, may hold values from -0.109375 to 0.109375
- out_bias: float32 [768], replicated, may hold values from -1.8 to 1.8
- output_grad: bfloat16 [16, 1024, 768], P('batch', 'seq'), may hold values from -6 to 6
- key_value_grad: bfloat16 [16, 1024, 128], P('batch', 'seq'), may hold values from -6 to 6
Outputs:
- output: bfloat16 [16, 1024, 768], P('batch', 'seq')
- key_value: bfloat16 [16, 1024, 128], P('batch', 'seq')
- tokens_grad: bfloat16 [16, 1024, 768], P('batch', 'seq')
- ln1_gain_grad: float32 [768], replicated
- ln1_bias_grad: float32 [768], replicated
- qkv_weight_grad: float32 [768, 896], P('seq')
- qkv_bias_grad: float32 [896], replicated
- out_weight_grad: float32 [768, 768], P('seq')
- ln2_gain_grad: float32 [768], replicated
- ln2_bias_grad: float32 [768], replicated
- fc1_weight_grad: float32 [768, 3072], P('seq')
- fc1_bias_grad: float32 [3072], replicated
- fc2_weight_grad: float32 [3072, 768], P('seq')
- out_bias_grad: float32 [768], replicated
The draws below stay inside these ranges and needn't reach their ends.
All inputs are finite; a program needn't handle non-finite values.
Results may differ from the reference program's by a relative error of at most 0.015.
Values may be sent and summed in bfloat16 or wider, within the bound.
No kernel may reach another device: no remote copies, remote signals or barrier semaphores. Data moves between devices by JAX's collectives and lax.ppermute only.
A program may use at most 128 MiB of HBM per device.

```python
import math
import jax
import jax.numpy as jnp
from jax import lax

D = 768
HEADS = 12
HEAD_DIM = 64
FF = 3072
ROT = 16
LENGTH = 1024
SEQS = 16


def levels(key, extent, split, least, top_value):
    gain = 1.0
    for dim, shards_of in split:
        steps = jax.random.uniform(jax.random.fold_in(jax.random.fold_in(key, 6), dim), (shards_of,), jnp.float32, least / len(split), top_value / len(split))
        gain = gain * jnp.repeat(jnp.exp(steps), extent[dim] // shards_of).reshape((-1,) + (1,) * (len(extent) - 1 - dim))
    return gain


def bell_draw(own_key, extent, deviation, reach, shards=(), kind=jnp.bfloat16):
    drawn = deviation * jax.random.normal(own_key, extent, jnp.float32)
    if shards:
        drawn = drawn * levels(own_key, extent, shards, -0.22, 0.18)
    return jnp.clip(drawn, -reach, reach).astype(kind)


def setup_inputs(seed: int = 0) -> dict:
    key_list = jax.random.split(jax.random.key(seed), 15)
    return {
        "tokens": bell_draw(key_list[0], (SEQS, LENGTH, D), 1.0, 6.0, ((0, 4), (1, 8))),
        "ln1_gain": jnp.clip(1.0 + 0.1 * jax.random.normal(key_list[1], (D,), jnp.float32), 0.5, 1.5),
        "ln1_bias": bell_draw(key_list[2], (D,), 0.3, 1.8, (), jnp.float32),
        "qkv_weight": bell_draw(key_list[3], (D, D + 2 * HEAD_DIM), (D // 2) ** -0.5, 0.3125),
        "qkv_bias": bell_draw(key_list[4], (D + 2 * HEAD_DIM,), 0.3, 1.8, (), jnp.float32),
        "out_weight": bell_draw(key_list[5], (D, D), (max(1, D * 64 // LENGTH)) ** -0.5, 0.875),
        "ln2_gain": jnp.clip(1.0 + 0.1 * jax.random.normal(key_list[6], (D,), jnp.float32), 0.5, 1.5),
        "ln2_bias": bell_draw(key_list[7], (D,), 0.3, 1.8, (), jnp.float32),
        "fc1_weight": bell_draw(key_list[8], (D, FF), D ** -0.5, 0.21875),
        "fc1_bias": bell_draw(key_list[9], (FF,), 0.3, 1.8, (), jnp.float32),
        "fc2_weight": bell_draw(key_list[10], (FF, D), FF ** -0.5, 0.109375),
        "out_bias": bell_draw(key_list[11], (D,), 0.3, 1.8, (), jnp.float32),
        "output_grad": bell_draw(key_list[12], (SEQS, LENGTH, D), 1.0, 6.0, ((0, 4), (1, 8))),
        "key_value_grad": bell_draw(key_list[13], (SEQS, LENGTH, 2 * HEAD_DIM), 1.0, 6.0, ((0, 4), (1, 8))),
    }


@jax.custom_vjp
def low(v):
    return lax.optimization_barrier(v.astype(jnp.bfloat16)).astype(jnp.float32)

@jax.custom_vjp
def low_back(v):
    return v

def low_keep(v):
    return (low(v), None)

def low_pass(kept, grad):
    return (grad,)

def back_keep(v):
    return (v, None)

def back_low(kept, grad):
    return (low(grad),)
low.defvjp(low_keep, low_pass)
low_back.defvjp(back_keep, back_low)
norm_eps = 1e-05
masked_value = -1e+30

def normalize(rows):
    centre = lax.optimization_barrier(jnp.mean(rows, axis=-1, keepdims=True))
    centred = rows - centre
    spread = lax.optimization_barrier(jnp.mean(centred * centred, axis=-1, keepdims=True))
    return centred * lax.rsqrt(spread + norm_eps)

def rotate(values, cosine, sine):
    half = ROT // 2
    first = values[..., :half]
    second = values[..., half:2 * half]
    return jnp.concatenate([first * cosine - second * sine, second * cosine + first * sine, values[..., 2 * half:]], axis=-1)

def layer(params, inputs):
    ln1_gain, ln1_bias, qkv_weight, qkv_bias, out_weight, ln2_gain, ln2_bias, fc1_weight, fc1_bias, fc2_weight, out_bias = params
    highest = lax.Precision.HIGHEST
    normed = normalize(inputs)
    first_in = low(normed * ln1_gain + ln1_bias)
    projected = low_back(jnp.dot(first_in, qkv_weight, precision=highest) + qkv_bias)
    half = ROT // 2
    places = jnp.arange(LENGTH, dtype=jnp.float32) * 0.25
    freqs = 10000.0 ** (-jnp.arange(half, dtype=jnp.float32) / half)
    angles = places[:, None] * freqs[None, :]
    cosine = jnp.cos(angles)
    sine = jnp.sin(angles)
    query_heads = projected[:, :D].reshape(LENGTH, HEADS, HEAD_DIM)
    queries = low(rotate(query_heads, cosine[:, None, :], sine[:, None, :]) * (1.0 / math.sqrt(HEAD_DIM)))
    queries = queries.reshape(LENGTH * HEADS, HEAD_DIM)
    keys = low(rotate(projected[:, D:D + HEAD_DIM], cosine, sine))
    values = low(projected[:, D + HEAD_DIM:])
    key_value = jnp.concatenate([keys, values], axis=-1)
    block_tokens = min(LENGTH, 512)
    block_rows = block_tokens * HEADS

    def attend_block(first):
        rows = lax.dynamic_slice_in_dim(queries, first * HEADS, block_rows, 0)
        scores = low_back(jnp.dot(rows, keys.T, precision=highest))
        query_place = first + jnp.arange(block_rows) // HEADS
        allowed = jnp.arange(LENGTH)[None, :] <= query_place[:, None]
        scores = jnp.where(allowed, scores, masked_value)
        top = lax.optimization_barrier(jnp.max(scores, axis=-1, keepdims=True))
        expd = jnp.where(allowed, jnp.exp(scores - top), 0.0)
        total = lax.optimization_barrier(jnp.sum(expd, axis=-1, keepdims=True))
        weights = low(expd / total)
        return jnp.dot(weights, values, precision=highest)
    starts = (jnp.arange(LENGTH // block_tokens) * block_tokens).astype(jnp.int32)
    attn_rows = lax.map(jax.checkpoint(attend_block), starts)
    attn_out = low_back(low(attn_rows.reshape(LENGTH, D)))
    mixed_attn = jnp.dot(attn_out, out_weight, precision=highest)
    second_in = low(normed * ln2_gain + ln2_bias)
    hidden_pre = low_back(jnp.dot(second_in, fc1_weight, precision=highest) + fc1_bias)
    hidden_act = low(jax.nn.gelu(hidden_pre, approximate=False))
    mixed_mlp = jnp.dot(hidden_act, fc2_weight, precision=highest)
    output = inputs + mixed_attn + mixed_mlp + out_bias
    return (output, key_value)

def reference(tokens, ln1_gain, ln1_bias, qkv_weight, qkv_bias, out_weight, ln2_gain, ln2_bias, fc1_weight, fc1_bias, fc2_weight, out_bias, output_grad, key_value_grad):
    params = tuple((item.astype(jnp.float32) for item in (ln1_gain, ln1_bias, qkv_weight, qkv_bias, out_weight, ln2_gain, ln2_bias, fc1_weight, fc1_bias, fc2_weight, out_bias)))
    zero_grads = tuple((jnp.zeros_like(item) for item in params))

    def one_sequence(totals, items):
        inputs, grad_out, grad_kv = items
        (output, key_value), pull = jax.vjp(layer, params, inputs.astype(jnp.float32))
        param_grads, input_grad = pull((grad_out.astype(jnp.float32), grad_kv.astype(jnp.float32)))
        totals = tuple((total + part for total, part in zip(totals, param_grads)))
        return (totals, (output.astype(jnp.bfloat16), key_value.astype(jnp.bfloat16), input_grad.astype(jnp.bfloat16)))
    totals, (output, key_value, tokens_grad) = lax.scan(one_sequence, zero_grads, (tokens, output_grad, key_value_grad))
    return (output, key_value, tokens_grad, totals[0], totals[1], totals[2], totals[3], totals[4], totals[5], totals[6], totals[7], totals[8], totals[9], totals[10])
```

```python
import functools
import math

import jax
import jax.numpy as jnp
from jax import lax
from jax.experimental import pallas as pl
from jax.experimental.pallas import tpu as pltpu
from jax.sharding import PartitionSpec as P

D = 768
HEADS = 12
HEAD_DIM = 64
ROT = 16
PAIRS = HEADS // 2
SCALE = 1.0 / math.sqrt(HEAD_DIM)
NORM_EPS = 1e-05
MASKED = -1e30
F32 = jnp.float32
BF16 = jnp.bfloat16
VMEM_BYTES = 56 * 1024 * 1024


def dot(a, b):
    return lax.dot_general(a, b, (((1,), (0,)), ((), ())), preferred_element_type=F32)


def dot_nt(a, b):
    return lax.dot_general(a, b, (((1,), (1,)), ((), ())), preferred_element_type=F32)


def dot_tn(a, b):
    return lax.dot_general(a, b, (((0,), (0,)), ((), ())), preferred_element_type=F32)


def params():
    return pltpu.CompilerParams(vmem_limit_bytes=VMEM_BYTES)


def flipped(block, axis, bits):
    return lax.ppermute(block, axis, [(i, i ^ bits) for i in range(lax.axis_size(axis))])


def later(block, distance):
    size = lax.axis_size("seq")
    return lax.ppermute(block, "seq", [(i, i + distance) for i in range(size - distance)])


def earlier(block, distance):
    size = lax.axis_size("seq")
    return lax.ppermute(block, "seq", [(i + distance, i) for i in range(size - distance)])


def take(block, index, axis):
    return lax.dynamic_index_in_dim(block, index, axis, keepdims=False)


def added(a, b):
    return (a.astype(F32) + b.astype(F32)).astype(BF16)


def tree_sum(parts):
    parts = [p.astype(F32) for p in parts]
    while len(parts) > 1:
        parts = [parts[i] + parts[i + 1] for i in range(0, len(parts), 2)]
    return parts[0]


def normalize(rows):
    centre = jnp.mean(rows, axis=-1, keepdims=True)
    centred = rows - centre
    spread = jnp.mean(centred * centred, axis=-1, keepdims=True)
    inverse = lax.rsqrt(spread + NORM_EPS)
    return centred * inverse, inverse


def rotary_tables(first, count):
    lane = jnp.arange(128) % HEAD_DIM
    half = ROT // 2
    freqs = 10000.0 ** (-(lane % half).astype(F32) / half)
    places = (first + jnp.arange(count)).astype(F32) * 0.25
    angles = places[:, None] * freqs[None, :]
    cosine, sine = jnp.cos(angles), jnp.sin(angles)
    return jnp.stack(
        [
            jnp.where(lane < ROT, cosine, 1.0),
            jnp.where((lane >= half) & (lane < ROT), sine, 0.0),
            jnp.where(lane < half, -sine, 0.0),
        ]
    )


def turn(values, tables, sign):
    moved = pltpu.roll(values, ROT // 2, 1) * tables[1] + pltpu.roll(values, 128 - ROT // 2, 1) * tables[2]
    return values * tables[0] + (moved if sign > 0 else -moved)


def repeated(tables_ref, count):
    return [jnp.concatenate([tables_ref[i]] * count, axis=0) for i in range(3)]


def key_tables(tables):
    low = lax.broadcasted_iota(jnp.int32, (1, 128), 1) < HEAD_DIM
    return [jnp.where(low, tables[0], 1.0), jnp.where(low, tables[1], 0.0), jnp.where(low, tables[2], 0.0)]


def project_kernel(copies, x_ref, gain_ref, bias_ref, weight_ref, add_ref, tables_ref, q_ref, kv_ref):
    normed, _ = normalize(x_ref[...].astype(F32))
    first_in = (normed * gain_ref[...] + bias_ref[...]).astype(BF16)
    tables = repeated(tables_ref, copies)
    for p in range(PAIRS + 1):
        columns = slice(p * 128, (p + 1) * 128)
        part = dot(first_in, weight_ref[:, columns]) + add_ref[:, columns]
        if p < PAIRS:
            q_ref[:, columns] = (turn(part, tables, 1) * SCALE).astype(BF16)
        else:
            kv_ref[...] = turn(part, key_tables(tables), 1).astype(BF16)


def project(x, gain, bias, weight, add, tables, span):
    rows = x.shape[0]
    block = 2 * span
    whole = lambda a: pl.BlockSpec(a.shape, lambda i: (0,) * a.ndim)
    row = lambda width: pl.BlockSpec((block, width), lambda i: (i, 0))
    return pl.pallas_call(
        functools.partial(project_kernel, block // span),
        grid=(rows // block,),
        in_specs=[row(D), whole(gain), whole(bias), whole(weight), whole(add), whole(tables)],
        out_specs=[row(D), row(128)],
        out_shape=[jax.ShapeDtypeStruct((rows, D), BF16), jax.ShapeDtypeStruct((rows, 128), BF16)],
        compiler_params=params(),
        cost_estimate=pl.CostEstimate(flops=2 * rows * D * 896, bytes_accessed=4 * 1024 * 1024, transcendentals=0),
        name="project",
    )(x, gain, bias, weight, add, tables)


def gelu_parts(h):
    t = pl.reciprocal(1.0 + (0.3275911 / math.sqrt(2.0)) * jnp.abs(h))
    e = jnp.exp(-0.5 * h * h)
    poly = 0.5 * 1.061405429
    for coefficient in (-1.453152027, 1.421413741, -0.284496736, 0.254829592):
        poly = poly * t + 0.5 * coefficient
    tail = poly * t * e
    cdf = jnp.where(h >= 0.0, 1.0 - tail, tail)
    return h * cdf, cdf + h * e * (1.0 / math.sqrt(2.0 * math.pi))


def feed_kernel(
    core_ref,
    x_ref,
    g_ref,
    gain_ref,
    bias_ref,
    w1_ref,
    b1_ref,
    w2_ref,
    wo_ref,
    mlp_ref,
    back_ref,
    attn_grad_ref,
    send1_ref,
    keep1_ref,
    send2_ref,
    keep2_ref,
    b1_grad_ref,
    small_ref,
    in_ref,
    in_t_ref,
    g_cut_ref,
):
    step = pl.program_id(0)
    steps = pl.num_programs(0)
    half = D // 2

    @pl.when(step == 0)
    def _():
        normed, _ = normalize(x_ref[...].astype(F32))
        second_in = normed * gain_ref[...] + bias_ref[...]
        in_ref[...] = second_in.astype(BF16)
        in_t_ref[...] = second_in.T.astype(BF16)
        g = g_ref[...]
        own = core_ref[0] == 0
        g_cut_ref[:, :half] = jnp.where(own, g[:, half:], g[:, :half])
        g_cut_ref[:, half:] = jnp.where(own, g[:, :half], g[:, half:])
        attn_grad_ref[...] = dot_nt(g, wo_ref[...]).astype(BF16)

    second_in = in_ref[...]
    g = g_ref[...]
    w1 = w1_ref[...]
    w2 = w2_ref[...]
    act, slope = gelu_parts(dot(second_in, w1) + b1_ref[...])
    act = act.astype(BF16)
    pre = dot_nt(g, w2) * slope
    pre16 = pre.astype(BF16)
    b1_grad_ref[...] = jnp.sum(pre, axis=0, keepdims=True)
    mlp = dot(act, w2)
    back = dot_nt(pre16, w1)
    grad2 = dot_tn(act, g_cut_ref[...]).astype(BF16)
    send2_ref[...] = grad2[:, :half]
    keep2_ref[...] = grad2[:, half:]
    grad1 = dot(in_t_ref[...], pre16).astype(BF16)

    @pl.when(step < steps // 2)
    def _():
        send1_ref[...] = grad1

    @pl.when(step >= steps // 2)
    def _():
        keep1_ref[...] = grad1

    @pl.when(step == 0)
    def _():
        mlp_ref[...] = mlp
        back_ref[...] = back

    @pl.when(step > 0)
    def _():
        mlp_ref[...] += mlp
        back_ref[...] += back

    @pl.when(step == steps - 1)
    def _():
        normed, _ = normalize(x_ref[...].astype(F32))
        second_grad = back_ref[...]
        small_ref[0:1] = jnp.sum(second_grad * normed, axis=0, keepdims=True)
        small_ref[1:2] = jnp.sum(second_grad, axis=0, keepdims=True)
        small_ref[2:3] = jnp.sum(g_ref[...].astype(F32), axis=0, keepdims=True)


def feed(core, x, g, gain, bias, w1, b1, w2, wo):
    rows = x.shape[0]
    ff = w1.shape[1]
    chunk = 512
    steps = ff // chunk
    half = steps // 2
    at = lambda i, core: (i + half * (1 - core[0])) % steps
    whole = lambda a: pl.BlockSpec(a.shape, lambda i, core: (0,) * a.ndim)
    fixed = lambda *shape: pl.BlockSpec(shape, lambda i, core: (0, 0))
    spec = pltpu.PrefetchScalarGridSpec(
        num_scalar_prefetch=1,
        grid=(steps,),
        in_specs=[
            whole(x),
            whole(g),
            whole(gain),
            whole(bias),
            pl.BlockSpec((D, chunk), lambda i, core: (0, at(i, core))),
            pl.BlockSpec((1, chunk), lambda i, core: (0, at(i, core))),
            pl.BlockSpec((chunk, D), lambda i, core: (at(i, core), 0)),
            whole(wo),
        ],
        out_specs=[
            fixed(rows, D),
            fixed(rows, D),
            fixed(rows, D),
            pl.BlockSpec((D, chunk), lambda i, core: (0, jnp.minimum(i, half - 1))),
            pl.BlockSpec((D, chunk), lambda i, core: (0, jnp.maximum(i - half, 0))),
            pl.BlockSpec((chunk, D // 2), lambda i, core: (at(i, core), 0)),
            pl.BlockSpec((chunk, D // 2), lambda i, core: (at(i, core), 0)),
            pl.BlockSpec((1, chunk), lambda i, core: (0, at(i, core))),
            fixed(8, D),
        ],
        scratch_shapes=[pltpu.VMEM((rows, D), BF16), pltpu.VMEM((D, rows), BF16), pltpu.VMEM((rows, D), BF16)],
    )
    shape = jax.ShapeDtypeStruct
    return pl.pallas_call(
        feed_kernel,
        grid_spec=spec,
        out_shape=[
            shape((rows, D), F32),
            shape((rows, D), F32),
            shape((rows, D), BF16),
            shape((D, ff // 2), BF16),
            shape((D, ff // 2), BF16),
            shape((ff, D // 2), BF16),
            shape((ff, D // 2), BF16),
            shape((1, ff), F32),
            shape((8, D), F32),
        ],
        compiler_params=params(),
        cost_estimate=pl.CostEstimate(
            flops=12 * rows * D * ff + 2 * rows * D * D, bytes_accessed=26 * 1024 * 1024, transcendentals=2 * rows * ff
        ),
        name="feed_forward",
    )(core, x, g, gain, bias, w1, b1, w2, wo)


def attention_kernel(groups, span, block, count, own_ref, *refs):
    kv_refs, refs = refs[:count], refs[count:]
    q_ref, do_ref, out_ref, dq_ref = refs[:4]
    dkv_refs, refs = refs[4 : 4 + count], refs[4 + count :]
    kv_scr, e_ref, kv_t_ref, max_ref, acc_ref, ext_ref = refs
    rows = groups * span
    per = block // span
    own = own_ref[0]
    used = (own + per) // per
    group, group_count = pl.program_id(1), pl.num_programs(1)
    low = lax.broadcasted_iota(jnp.int32, (1, 128), 1) < HEAD_DIM
    lanes = lax.broadcasted_iota(jnp.int32, (rows, 128), 1)

    def stacked(ref):
        return jnp.concatenate([ref[:, p * 128 : (p + 1) * 128] for p in range(groups)], axis=0)

    @pl.when(group == 0)
    def _():
        for i in range(count):
            kv_scr[i * span : (i + 1) * span] = kv_refs[i][...]

    q = stacked(q_ref)
    do = stacked(do_ref)

    def load(b):
        kv = kv_scr[pl.ds(pl.multiple_of(b * block, block), block)]
        swapped = pltpu.roll(kv.astype(F32), HEAD_DIM, 1).astype(BF16)
        return kv, swapped, jnp.zeros_like(kv)

    def absent(b):
        row = lax.broadcasted_iota(jnp.int32, (block, 128), 0) + b * block
        lane = lax.broadcasted_iota(jnp.int32, (block, 128), 1)
        mask = jnp.where(row >= (own + 1) * span, MASKED, 0.0)
        return jnp.where(lane < 2, -1.0, jnp.where(lane == 2, mask, 0.0)).astype(BF16)

    def key_tiles(b):
        kv, swapped, zero = load(b)
        ext = absent(b)
        return [
            jnp.concatenate([jnp.where(low, kv, zero), ext], axis=1),
            jnp.concatenate([jnp.where(low, zero, swapped), ext], axis=1),
        ]

    def value_tiles(b):
        kv, swapped, zero = load(b)
        ext = absent(b)
        return [
            jnp.concatenate([jnp.where(low, swapped, zero), ext], axis=1),
            jnp.concatenate([jnp.where(low, zero, kv), ext], axis=1),
        ]

    def seen():
        token = lax.broadcasted_iota(jnp.int32, (rows, block), 0) % span
        key = lax.broadcasted_iota(jnp.int32, (rows, block), 1)
        return (key <= token) | (key >= span)

    def extended(values):
        high = values.astype(BF16).astype(F32)
        rest = jnp.where(lanes == 1, values - high, jnp.where(lanes == 2, 1.0, 0.0))
        return jnp.where(lanes == 0, high, rest).astype(BF16)

    def over_blocks(step):
        step(0, True)

        def body(b, carry):
            step(b, False)
            return carry

        lax.fori_loop(1, used, body, 0)

    plain = jnp.concatenate([q, jnp.where(lanes == 2, 1.0, 0.0).astype(BF16)], axis=1)

    def maxima(b, diagonal):
        keys = key_tiles(b)
        for h in range(2):
            scores = dot_nt(plain, keys[h])
            if diagonal:
                scores = jnp.where(seen(), scores, MASKED)
            top = functools.reduce(jnp.maximum, [scores[:, i : i + 128] for i in range(0, block, 128)])
            max_ref[h] = top if diagonal else jnp.maximum(max_ref[h], top)

    over_blocks(maxima)
    for h in range(2):
        top = jnp.max(max_ref[h], axis=1, keepdims=True)
        ext_ref[h] = jnp.concatenate([q, extended(jnp.broadcast_to(top, (rows, 128)))], axis=1)

    def forward(b, diagonal):
        keys = key_tiles(b)
        kv, swapped, _ = load(b)
        one = jnp.ones_like(kv)
        values = (jnp.where(low, swapped, one), jnp.where(low, one, kv))
        for h in range(2):
            expd = jnp.exp(dot_nt(ext_ref[h], keys[h]))
            if diagonal:
                expd = jnp.where(seen(), expd, 0.0)
            expd = expd.astype(BF16)
            e_ref[b, h] = expd
            mixed = dot(expd, values[h])
            acc_ref[h] = mixed if diagonal else acc_ref[h] + mixed

    over_blocks(forward)
    first, second = acc_ref[0], acc_ref[1]
    total = jnp.where(low, pltpu.roll(first, HEAD_DIM, 1), pltpu.roll(second, HEAD_DIM, 1))
    inverse = 1.0 / total
    out = jnp.where(low, first, second) * inverse
    for p in range(groups):
        out_ref[:, p * 128 : (p + 1) * 128] = out[p * span : (p + 1) * span].astype(BF16)
    do32 = do.astype(F32)
    product = do32 * out
    high = product.astype(BF16)
    rest = (product - high.astype(F32)).astype(BF16)
    place = lax.broadcasted_iota(jnp.int32, (128, 128), 0)
    for h in range(2):
        ones = jnp.where((place < HEAD_DIM) == (h == 0), 1.0, 0.0).astype(BF16)
        delta = dot(high, ones) + dot(rest, ones)
        ext_ref[h] = jnp.concatenate([do, extended(delta)], axis=1)
    do_t = (do32 * inverse).T.astype(BF16)
    q_t = (q.astype(F32) * inverse).T.astype(BF16)

    def backward(b, start):
        values = value_tiles(b)
        kv, swapped, zero = load(b)
        keys = (jnp.where(low, kv, zero), jnp.where(low, zero, swapped))
        dq = dk = dv = 0.0
        for h in range(2):
            expd = e_ref[b, h]
            head = slice(h * HEAD_DIM, (h + 1) * HEAD_DIM)
            dscore = (expd.astype(F32) * dot_nt(ext_ref[h], values[h])).astype(BF16)
            dq = dq + dot(dscore, keys[h])
            dk = dk + dot(q_t[head], dscore)
            dv = dv + dot(do_t[head], expd)
        acc_ref[0] = dq if start else acc_ref[0] + dq
        both = jnp.concatenate([dk, dv], axis=0)
        kv_t_ref[b] = jnp.where(group == 0, both, kv_t_ref[b] + both)

    over_blocks(backward)
    dq = acc_ref[0] * inverse
    for p in range(groups):
        dq_ref[:, p * 128 : (p + 1) * 128] = dq[p * span : (p + 1) * span]

    @pl.when(group == group_count - 1)
    def _():
        for b in range(count // per):

            @pl.when(b < used)
            def _(b=b):
                both = kv_t_ref[b].T.astype(BF16)
                for i in range(per):
                    dkv_refs[b * per + i][...] = both[i * span : (i + 1) * span]


def attention(own, kvs, q, do):
    count = len(kvs)
    seqs, span, _ = q.shape
    block = max(256, span)
    blocks = count * span // block
    groups = PAIRS if blocks * PAIRS * span * block * 4 <= 16 * 1024 * 1024 else 2
    rows = groups * span
    wide = pl.BlockSpec((None, span, groups * 128), lambda s, i: (s, 0, i))
    narrow = pl.BlockSpec((None, span, 128), lambda s, i: (s, 0, 0))
    shape = jax.ShapeDtypeStruct
    result = pl.pallas_call(
        functools.partial(attention_kernel, groups, span, block, count),
        grid=(seqs, PAIRS // groups),
        in_specs=[pl.BlockSpec(memory_space=pltpu.SMEM)] + [narrow] * count + [wide, wide],
        out_specs=[wide, wide] + [narrow] * count,
        out_shape=[shape(q.shape, BF16), shape(q.shape, F32)] + [shape((seqs, span, 128), BF16)] * count,
        scratch_shapes=[
            pltpu.VMEM((count * span, 128), BF16),
            pltpu.VMEM((blocks, 2, rows, block), BF16),
            pltpu.VMEM((blocks, 128, block), F32),
            pltpu.VMEM((2, rows, 128), F32),
            pltpu.VMEM((2, rows, 128), F32),
            pltpu.VMEM((2, rows, 256), BF16),
        ],
        compiler_params=params(),
        cost_estimate=pl.CostEstimate(
            flops=2 * 7 * seqs * 2 * PAIRS * span * count * span * 256,
            bytes_accessed=8 * 1024 * 1024,
            transcendentals=seqs * HEADS * span * count * span,
        ),
        name="attention",
    )(own, *kvs, q, do)
    return result[0], result[1], result[2:]


def mix_kernel(
    copies,
    core_ref,
    x_ref,
    g_ref,
    mlp_ref,
    out_ref,
    dq_ref,
    gain_ref,
    bias_ref,
    add_ref,
    wo_ref,
    wq_ref,
    tables_ref,
    output_ref,
    send_ref,
    keep_ref,
    first_ref,
    small_ref,
):
    half = D // 2
    x = x_ref[...].astype(F32)
    attn = out_ref[...]
    output_ref[...] = (x + (mlp_ref[...] + dot(attn, wo_ref[...])) + add_ref[...]).astype(BF16)
    normed, _ = normalize(x)
    first_in = (normed * gain_ref[...] + bias_ref[...]).astype(BF16)
    tables = repeated(tables_ref, copies)
    parts = []
    for p in range(PAIRS):
        parts.append(turn(dq_ref[:, p * 128 : (p + 1) * 128] * SCALE, tables, -1).astype(BF16))
    grad = jnp.concatenate(parts, axis=1)
    small_ref[...] = jnp.sum(grad.astype(F32), axis=0, keepdims=True)
    first_ref[...] = dot_nt(grad, wq_ref[...])
    attn_t = attn.astype(F32).T.astype(BF16)
    first_t = first_in.astype(F32).T.astype(BF16)
    own = core_ref[0] == 0
    g = g_ref[...]
    for left, right, at in ((attn_t, g, 0), (first_t, grad, half)):
        lower, upper = right[:, :half], right[:, half:]
        send_ref[:, at : at + half] = dot(left, jnp.where(own, upper, lower)).astype(BF16)
        keep_ref[:, at : at + half] = dot(left, jnp.where(own, lower, upper)).astype(BF16)


def mix(core, x, g, mlp, out, dq, gain, bias, add, wo, wq, tables):
    rows = x.shape[0]
    shape = jax.ShapeDtypeStruct
    vmem = pl.BlockSpec(memory_space=pltpu.VMEM)
    return pl.pallas_call(
        functools.partial(mix_kernel, rows // tables.shape[1]),
        in_specs=[pl.BlockSpec(memory_space=pltpu.SMEM)] + [vmem] * 11,
        out_specs=[vmem] * 5,
        out_shape=[
            shape((rows, D), BF16),
            shape((D, D), BF16),
            shape((D, D), BF16),
            shape((rows, D), F32),
            shape((1, D), F32),
        ],
        compiler_params=params(),
        cost_estimate=pl.CostEstimate(flops=8 * rows * D * D, bytes_accessed=16 * 1024 * 1024, transcendentals=0),
        name="mix",
    )(core, x, g, mlp, out, dq, gain, bias, add, wo, wq, tables)


def finish_kernel(
    copies,
    count,
    own_ref,
    *refs,
):
    kv_refs, refs = refs[:count], refs[count:]
    (
        extra_ref,
        x_ref,
        g_ref,
        first_ref,
        back_ref,
        gain_ref,
        bias_ref,
        gain2_ref,
        wkv_ref,
        tables_ref,
        tokens_ref,
        weight_ref,
        small_ref,
    ) = refs
    total = extra_ref[...].astype(F32) + kv_refs[0][...].astype(F32)
    for i in range(1, count):
        total += jnp.where(own_ref[0] + i < count, kv_refs[i][...].astype(F32), 0.0)
    tables = repeated(tables_ref, copies)
    grad = turn(total, key_tables(tables), -1).astype(BF16)
    x = x_ref[...].astype(F32)
    normed, inverse = normalize(x)
    first_in = normed * gain_ref[...] + bias_ref[...]
    weight_ref[...] = dot(first_in.T.astype(BF16), grad)
    first_grad = first_ref[...] + dot_nt(grad, wkv_ref[...])
    small_ref[...] = jnp.zeros_like(small_ref)
    small_ref[0:1] = jnp.sum(first_grad * normed, axis=0, keepdims=True)
    small_ref[1:2] = jnp.sum(first_grad, axis=0, keepdims=True)
    small_ref[2:3, :128] = jnp.sum(grad.astype(F32), axis=0, keepdims=True)
    normed_grad = first_grad * gain_ref[...] + back_ref[...] * gain2_ref[...]
    mean = jnp.mean(normed_grad, axis=-1, keepdims=True)
    along = jnp.mean(normed_grad * normed, axis=-1, keepdims=True)
    tokens_ref[...] = (g_ref[...].astype(F32) + inverse * (normed_grad - mean - normed * along)).astype(BF16)


def finish(own, kv_parts, extra, x, g, first, back, gain, bias, gain2, wkv, tables):
    rows = x.shape[0]
    count = len(kv_parts)
    shape = jax.ShapeDtypeStruct
    vmem = pl.BlockSpec(memory_space=pltpu.VMEM)
    return pl.pallas_call(
        functools.partial(finish_kernel, rows // tables.shape[1], count),
        in_specs=[pl.BlockSpec(memory_space=pltpu.SMEM)] + [vmem] * (count + 10),
        out_specs=[vmem] * 3,
        out_shape=[shape((rows, D), BF16), shape((D, 128), F32), shape((8, D), F32)],
        compiler_params=params(),
        cost_estimate=pl.CostEstimate(flops=4 * rows * D * 128, bytes_accessed=10 * 1024 * 1024, transcendentals=0),
        name="finish",
    )(own, *kv_parts, extra, x, g, first, back, gain, bias, gain2, wkv, tables)


def local(
    tokens,
    ln1_gain,
    ln1_bias,
    qkv_weight,
    qkv_bias,
    out_weight,
    ln2_gain,
    ln2_bias,
    fc1_weight,
    fc1_bias,
    fc2_weight,
    out_bias,
    output_grad,
    key_value_grad,
):
    seqs, span, _ = tokens.shape
    rows = seqs * span
    count = lax.axis_size("seq")
    depth = count // 2
    own = lax.axis_index("seq")
    y, z = own % 2, own // 2
    batch = lax.axis_index("batch")
    core, xs = batch % 2, batch // 2
    own1 = own.reshape(1).astype(jnp.int32)
    core1 = core.reshape(1).astype(jnp.int32)
    row = lambda v: v.reshape(1, -1)
    x = tokens.reshape(rows, D)
    g = output_grad.reshape(rows, D)
    tables = rotary_tables(own * span, span)

    q, kv = project(x, row(ln1_gain), row(ln1_bias), qkv_weight, row(qkv_bias), tables, span)
    kv3 = kv.reshape(seqs, span, 128)
    kvs = [kv3] + [later(kv3, i) for i in range(1, count)]

    mlp, back, attn_grad, send1, keep1, send2, keep2, b1_grad, small2 = feed(
        core1, x, g, row(ln2_gain), row(ln2_bias), fc1_weight, row(fc1_bias), fc2_weight, out_weight
    )

    def halves(keep, come, index, axis):
        mine = added(take(keep, index, axis), take(come, index, axis))
        theirs = added(take(keep, 1 - index, axis), take(come, 1 - index, axis))
        return mine, theirs

    def along_z(keep, come):
        parts = [added(take(keep, z ^ i, 0), take(come, z ^ i, 0)) for i in range(depth)]
        return tree_sum([parts[0]] + [flipped(parts[i], "seq", 2 * i) for i in range(1, depth)])

    def both(own_part, index, axis, flip):
        other = flip(own_part)
        first = jnp.where(index == 0, own_part, other)
        second = jnp.where(index == 0, other, own_part)
        return jnp.concatenate([first, second], axis=axis)

    over_core = lambda v: flipped(v, "batch", 1)
    over_x = lambda v: flipped(v, "batch", 2)
    over_y = lambda v: flipped(v, "seq", 1)

    def x_y_z(keep, come, per, width):
        cut = lambda v: v.reshape(count * per, 2, width)
        mine, theirs = halves(cut(keep), cut(come), xs, 1)
        come = over_x(theirs)
        cut = lambda v: v.reshape(depth, 2, per, width)
        mine, theirs = halves(cut(mine), cut(come), y, 1)
        part = along_z(mine, over_y(theirs)).astype(BF16)
        return both(part, xs, 1, over_x)

    def y_z_x(keep, come, per, width):
        cut = lambda v: v.reshape(depth, 2, per, width)
        mine, theirs = halves(cut(keep), cut(come), y, 1)
        part = along_z(mine, over_y(theirs)).astype(BF16)
        return added(part, over_x(part))

    come1, come2 = over_core(send1), over_core(send2)
    per1, per2 = D // count, fc1_weight.shape[1] // count
    sum1 = x_y_z(keep1, come1, per1, send1.shape[1] // 2)
    sum2 = y_z_x(keep2, come2, per2, D // 2)
    fc1_grad = both(sum1, core, 1, over_core).astype(F32)
    fc2_grad = both(sum2, core, 1, over_core).astype(F32)

    def everywhere(v):
        bit = 1
        while bit < lax.axis_size("batch"):
            v = v + flipped(v, "batch", bit)
            bit *= 2
        bit = 1
        while bit < count:
            v = v + flipped(v, "seq", bit)
            bit *= 2
        return v

    early = everywhere(jnp.concatenate([b1_grad.reshape(-1, D), small2[:3]], axis=0))

    out, dq, dkvs = attention(own1, kvs, q.reshape(seqs, span, D), attn_grad.reshape(seqs, span, D))
    kv_parts = [dkvs[0]] + [earlier(dkvs[i], i) for i in range(1, count)]
    flat = lambda v: v.reshape(rows, -1)
    output, send3, keep3, first, q_small = mix(
        core1, x, g, mlp, flat(out), flat(dq), row(ln1_gain), row(ln1_bias), row(out_bias), out_weight,
        qkv_weight[:, :D], tables,
    )
    sum3 = x_y_z(keep3, over_core(send3), per1, D // 2)
    out_grad = both(sum3[:, : D // 2], core, 1, over_core)
    q_grad = both(sum3[:, D // 2 :], core, 1, over_core)

    tokens_grad, kv_weight, small1 = finish(
        own1, [flat(v) for v in kv_parts], flat(key_value_grad), x, g, first, back, row(ln1_gain), row(ln1_bias),
        row(ln2_gain), qkv_weight[:, D:], tables,
    )
    shards = kv_weight.astype(BF16).reshape(count, per1, 128)
    kv_sum = tree_sum(
        [take(shards, own, 0)] + [flipped(take(shards, own ^ i, 0), "seq", i) for i in range(1, count)]
    ).astype(BF16)
    kv_sum = tree_sum([kv_sum] + [flipped(kv_sum, "batch", i) for i in range(1, lax.axis_size("batch"))])
    late = everywhere(jnp.concatenate([small1[:3], q_small], axis=0))

    qkv_grad = jnp.concatenate([q_grad.astype(F32), kv_sum], axis=1)
    b1_rows = b1_grad.size // D
    return (
        output.reshape(tokens.shape),
        kv3,
        tokens_grad.reshape(tokens.shape),
        late[0],
        late[1],
        qkv_grad,
        jnp.concatenate([late[3], late[2, :128]]),
        out_grad.astype(F32),
        early[b1_rows],
        early[b1_rows + 1],
        fc1_grad,
        early[:b1_rows].reshape(-1),
        fc2_grad,
        early[b1_rows + 2],
    )


def solution(mesh):
    part = P("batch", "seq", None)
    whole = P()
    split = P("seq", None)
    return jax.shard_map(
        local,
        mesh=mesh,
        in_specs=(part,) + (whole,) * 11 + (part, part),
        out_specs=(
            part, part, part, whole, whole, split, whole, split, whole, whole, split, whole, split, whole,
        ),
        check_vma=False,
    )
```

```python
import functools
import math

import jax
import jax.numpy as jnp
from jax import lax
from jax.experimental import pallas as pl
from jax.experimental.pallas import tpu as pltpu
from jax.sharding import PartitionSpec as P

D = 768
HEADS = 12
HEAD_DIM = 64
ROT = 16
PAIRS = HEADS // 2
SCALE = 1.0 / math.sqrt(HEAD_DIM)
NORM_EPS = 1e-05
MASKED = -1e30
F32 = jnp.float32
BF16 = jnp.bfloat16
VMEM_BYTES = 56 * 1024 * 1024


def dot(a, b):
    return lax.dot_general(a, b, (((1,), (0,)), ((), ())), preferred_element_type=F32)


def dot_nt(a, b):
    return lax.dot_general(a, b, (((1,), (1,)), ((), ())), preferred_element_type=F32)


def dot_tn(a, b):
    return lax.dot_general(a, b, (((0,), (0,)), ((), ())), preferred_element_type=F32)


def params():
    return pltpu.CompilerParams(vmem_limit_bytes=VMEM_BYTES)


def flipped(block, axis, bits):
    return lax.ppermute(block, axis, [(i, i ^ bits) for i in range(lax.axis_size(axis))])


def along(block, distance):
    size = lax.axis_size("seq")
    return lax.ppermute(block, "seq", [(i, (i + 2 * distance) % size) for i in range(size)])


def to_owner(block, distance):
    size = lax.axis_size("seq")
    half = size // 4
    route = []
    for b in range(lax.axis_size("batch")):
        for i in range(size):
            j = i ^ (2 * distance)
            if (j // 2) // half == b % 2:
                route.append((b * size + i, b * size + j))
    return lax.ppermute(block, ("batch", "seq"), route)


def after(values, *others):
    return lax.optimization_barrier((tuple(values), others))[0]


def tree_sum(parts):
    parts = [p.astype(F32) for p in parts]
    while len(parts) > 1:
        parts = [sum(parts[i : i + 2][1:], parts[i]) for i in range(0, len(parts), 2)]
    return parts[0]


def take(block, index, axis):
    return lax.dynamic_index_in_dim(block, index, axis, keepdims=False)


def normalize(rows):
    centre = jnp.mean(rows, axis=-1, keepdims=True)
    centred = rows - centre
    spread = jnp.mean(centred * centred, axis=-1, keepdims=True)
    inverse = lax.rsqrt(spread + NORM_EPS)
    return centred * inverse, inverse


def rotary_tables(first, count):
    lane = jnp.arange(128) % HEAD_DIM
    half = ROT // 2
    freqs = 10000.0 ** (-(lane % half).astype(F32) / half)
    places = (first + jnp.arange(count)).astype(F32) * 0.25
    angles = places[:, None] * freqs[None, :]
    cosine, sine = jnp.cos(angles), jnp.sin(angles)
    return jnp.stack(
        [
            jnp.where(lane < ROT, cosine, 1.0),
            jnp.where((lane >= half) & (lane < ROT), sine, 0.0),
            jnp.where(lane < half, -sine, 0.0),
        ]
    )


def turn(values, tables, sign):
    moved = pltpu.roll(values, ROT // 2, 1) * tables[1] + pltpu.roll(values, 128 - ROT // 2, 1) * tables[2]
    return values * tables[0] + (moved if sign > 0 else -moved)


def repeated(tables_ref, count):
    return [jnp.concatenate([tables_ref[i]] * count, axis=0) for i in range(3)]


def key_tables(tables):
    low = lax.broadcasted_iota(jnp.int32, (1, 128), 1) < HEAD_DIM
    return [jnp.where(low, tables[0], 1.0), jnp.where(low, tables[1], 0.0), jnp.where(low, tables[2], 0.0)]

VMEM = pl.BlockSpec(memory_space=pltpu.VMEM)
SMEM = pl.BlockSpec(memory_space=pltpu.SMEM)
SHAPE = jax.ShapeDtypeStruct


def cost(share):
    return pl.CostEstimate(flops=int(share * 3e9), bytes_accessed=0, transcendentals=0)


def wide(ref):
    return ref[...].reshape(1, -1)


def add_split(place, items):
    def kernel(place_ref, *refs):
        sources, results = refs[: 2 * len(items)], refs[2 * len(items) :]
        for n, (_, _, which) in enumerate(items):
            a, b = sources[2 * n], sources[2 * n + 1]
            own = place_ref[which]
            for m in range(a.shape[0]):
                for result, at in ((results[2 * n], 1 - own), (results[2 * n + 1], own)):
                    result[m] = (a[m, at].astype(F32) + b[m, at].astype(F32)).astype(BF16)

    shapes = []
    for a, _, _ in items:
        shapes += [SHAPE((a.shape[0],) + a.shape[2:], BF16)] * 2
    arrays = [v for item in items for v in item[:2]]
    return pl.pallas_call(
        kernel,
        in_specs=[SMEM] + [VMEM] * len(arrays),
        out_specs=[VMEM] * len(shapes),
        out_shape=shapes,
        compiler_params=params(),
        cost_estimate=cost(1.2),
        name="add_split",
    )(place, *arrays)


def add_cut(place, items):
    def kernel(place_ref, *refs):
        sources, results = refs[: 2 * len(items)], refs[2 * len(items) :]
        start = 0
        for n, (first, _) in enumerate(items):
            a, b = sources[2 * n], sources[2 * n + 1]
            count = first.shape[0]
            for i in range(count):
                at = lax.rem(place_ref[3] ^ i, count)
                results[start + i][...] = (a[at].astype(F32) + b[at].astype(F32)).astype(BF16)
            start += count

    shapes = []
    for a, _ in items:
        shapes += [SHAPE(a.shape[1:], BF16)] * a.shape[0]
    arrays = [v for item in items for v in item]
    return pl.pallas_call(
        kernel,
        in_specs=[SMEM] + [VMEM] * len(arrays),
        out_specs=[VMEM] * len(shapes),
        out_shape=shapes,
        compiler_params=params(),
        cost_estimate=cost(0.8),
        name="add_cut",
    )(place, *arrays)


def sum_split(place, parts):
    def kernel(place_ref, *refs):
        sources, results = refs[:-2], refs[-2:]
        y = place_ref[2]
        for result, at in ((results[0], 1 - y), (results[1], y)):
            result[...] = tree_sum([ref[at] for ref in sources]).astype(BF16)

    return pl.pallas_call(
        kernel,
        in_specs=[SMEM] + [VMEM] * len(parts),
        out_specs=[VMEM] * 2,
        out_shape=[SHAPE(parts[0].shape[1:], BF16)] * 2,
        compiler_params=params(),
        cost_estimate=cost(1.6),
        name="sum_split",
    )(place, *parts)


def project_kernel(copies, x_ref, gain_ref, bias_ref, weight_ref, add_ref, tables_ref, q_ref, kv_ref):
    normed, _ = normalize(x_ref[...].astype(F32))
    first_in = (normed * wide(gain_ref) + wide(bias_ref)).astype(BF16)
    tables = repeated(tables_ref, copies)
    bias = wide(add_ref)
    for p in (PAIRS,) + tuple(range(PAIRS)):
        columns = slice(p * 128, (p + 1) * 128)
        part = dot(first_in, weight_ref[:, columns]) + bias[:, columns]
        if p < PAIRS:
            q_ref[:, columns] = (turn(part, tables, 1) * SCALE).astype(BF16)
        else:
            kv_ref[...] = turn(part, key_tables(tables), 1).astype(BF16)


def project(x, gain, bias, weight, add, tables):
    rows = x.shape[0]
    return pl.pallas_call(
        functools.partial(project_kernel, rows // tables.shape[1]),
        in_specs=[VMEM] * 6,
        out_specs=[VMEM] * 2,
        out_shape=[SHAPE((rows, D), BF16), SHAPE((rows, 128), BF16)],
        compiler_params=params(),
        cost_estimate=cost(2),
        name="project",
    )(x, gain, bias, weight, add, tables)


def gelu_parts(h):
    t = pl.reciprocal(1.0 + (0.3275911 / math.sqrt(2.0)) * jnp.abs(h))
    e = jnp.exp(-0.5 * h * h)
    poly = 0.5 * 1.061405429
    for coefficient in (-1.453152027, 1.421413741, -0.284496736, 0.254829592):
        poly = poly * t + 0.5 * coefficient
    tail = poly * t * e
    cdf = jnp.where(h >= 0.0, 1.0 - tail, tail)
    return h * cdf, cdf + h * e * (1.0 / math.sqrt(2.0 * math.pi))


def forward_kernel(
    place_ref,
    x_ref,
    xx_ref,
    g_ref,
    gg_ref,
    gain_ref,
    bias_ref,
    w1_ref,
    b1_ref,
    w2_ref,
    own_ref,
    other_ref,
    slope_ref,
    in_t_ref,
    *refs,
):
    grad_refs, (in_scr, g_scr, acc_scr) = refs[:-3], refs[-3:]
    step, steps = pl.program_id(0), pl.num_programs(0)
    rows = x_ref.shape[0]

    @pl.when(step == 0)
    def _():
        for i, (tokens, grads) in enumerate(((x_ref, g_ref), (xx_ref, gg_ref))):
            at = slice(i * rows, (i + 1) * rows)
            normed, _ = normalize(tokens[...].astype(F32))
            second_in = normed * wide(gain_ref) + wide(bias_ref)
            in_scr[at] = second_in.astype(BF16)
            in_t_ref[:, at] = second_in.T.astype(BF16)
            g_scr[at] = grads[...]

    w2 = w2_ref[...]
    act, slope = gelu_parts(dot(in_scr[...], w1_ref[...]) + b1_ref[...])
    act = act.astype(BF16)
    slope_ref[...] = slope.astype(BF16)
    grad = dot_tn(act, g_scr[...]).astype(BF16)
    if len(grad_refs) == 1:
        grad_refs[0][...] = grad
    for i in range(len(grad_refs) if len(grad_refs) > 1 else 0):

        @pl.when(step == steps - 1 - i)
        def _(i=i):
            grad_refs[i][...] = grad

    mlp = dot(act, w2)

    @pl.when(step == 0)
    def _():
        acc_scr[...] = mlp

    @pl.when((step > 0) & (step < steps - 1))
    def _():
        acc_scr[...] += mlp

    @pl.when(step == steps - 1)
    def _():
        total = acc_scr[...] + mlp
        own_ref[...] = total[:rows]
        other_ref[...] = total[rows:].astype(BF16)


CHUNK = 512


def feed_forward(place, depth, x, xx, g, gg, gain, bias, w1, b1, w2):
    rows = x.shape[0]
    half = w1.shape[1] // 2
    pieces = depth // 2
    aligned = half % (pieces * 256) == 0
    chunk = half // pieces if aligned else CHUNK
    steps = half // chunk
    whole = lambda a: pl.BlockSpec(a.shape, lambda i, place: (0,) * a.ndim)
    fixed = lambda *shape: pl.BlockSpec(shape, lambda i, place: (0, 0))
    if aligned:
        piece = lambda i, place: (place[3] ^ (steps - 1 - i)) % steps
        grad_specs = [fixed(chunk, D)] * pieces
        grad_shapes = [SHAPE((chunk, D), BF16)] * pieces
    else:
        piece = lambda i, place: i
        grad_specs = [pl.BlockSpec((chunk, D), lambda i, place: (i, 0))]
        grad_shapes = [SHAPE((half, D), BF16)]
    at = lambda i, place: place[0] * steps + piece(i, place)
    spec = pltpu.PrefetchScalarGridSpec(
        num_scalar_prefetch=1,
        grid=(steps,),
        in_specs=[
            whole(x),
            whole(xx),
            whole(g),
            whole(gg),
            whole(gain),
            whole(bias),
            pl.BlockSpec((D, chunk), lambda i, place: (0, at(i, place))),
            pl.BlockSpec((1, chunk), lambda i, place: (0, at(i, place))),
            pl.BlockSpec((chunk, D), lambda i, place: (at(i, place), 0)),
        ],
        out_specs=[
            fixed(rows, D),
            fixed(rows, D),
            pl.BlockSpec((2 * rows, chunk), lambda i, place: (0, piece(i, place))),
            fixed(D, 2 * rows),
        ]
        + grad_specs,
        scratch_shapes=[
            pltpu.VMEM((2 * rows, D), BF16),
            pltpu.VMEM((2 * rows, D), BF16),
            pltpu.VMEM((2 * rows, D), F32),
        ],
    )
    result = pl.pallas_call(
        forward_kernel,
        grid_spec=spec,
        out_shape=[
            SHAPE((rows, D), F32),
            SHAPE((rows, D), BF16),
            SHAPE((2 * rows, half), BF16),
            SHAPE((D, 2 * rows), BF16),
        ]
        + grad_shapes,
        compiler_params=params(),
        cost_estimate=cost(8),
        name="feed_forward",
    )(place, x, xx, g, gg, gain, bias, w1, b1, w2)
    grads = result[4:]
    if not aligned:
        cut = grads[0].reshape(pieces, -1, D)
        grads = [take(cut, (place[3] ^ i) % pieces, 0) for i in range(pieces)]
    return result[:4], grads


def backward_kernel(
    place_ref,
    g_ref,
    gg_ref,
    slope_ref,
    in_theirs_ref,
    in_mine_ref,
    w1_ref,
    w2_ref,
    wo_ref,
    own_ref,
    other_ref,
    attn_grad_ref,
    theirs_ref,
    mine_ref,
    b1_grad_ref,
    g_scr,
    acc_scr,
):
    step, steps = pl.program_id(0), pl.num_programs(0)
    rows = g_ref.shape[0]

    @pl.when(step == 0)
    def _():
        g_scr[:rows] = g_ref[...]
        g_scr[rows:] = gg_ref[...]
        attn_grad_ref[...] = dot_nt(g_ref[...], wo_ref[...]).astype(BF16)

    w1 = w1_ref[...]
    pre = dot_nt(g_scr[...], w2_ref[...]) * slope_ref[...].astype(F32)
    pre16 = pre.astype(BF16)
    b1_grad_ref[...] = jnp.sum(pre, axis=0, keepdims=True)
    for source, result in ((in_theirs_ref, theirs_ref), (in_mine_ref, mine_ref)):
        left = source[...].reshape(-1, 2 * rows)
        result[...] = dot(left, pre16).astype(BF16).reshape(result.shape)
    back = dot_nt(pre16, w1)

    @pl.when(step == 0)
    def _():
        acc_scr[...] = back

    @pl.when((step > 0) & (step < steps - 1))
    def _():
        acc_scr[...] += back

    @pl.when(step == steps - 1)
    def _():
        total = acc_scr[...] + back
        own_ref[...] = total[:rows]
        other_ref[...] = total[rows:].astype(BF16)


def feed_backward(place, count, g, gg, slope, in_t, w1, w2, wo):
    rows = g.shape[0]
    half = w1.shape[1] // 2
    steps = half // CHUNK
    per = D // count // 2
    in_t = in_t.reshape(count, 2, per, 2 * rows)
    whole = lambda a: pl.BlockSpec(a.shape, lambda i, place: (0,) * a.ndim)
    fixed = lambda *shape: pl.BlockSpec(shape, lambda i, place: (0, 0))
    at = lambda i, place: place[0] * steps + i
    cut = pl.BlockSpec((count, per, CHUNK), lambda i, place: (0, 0, i))
    spec = pltpu.PrefetchScalarGridSpec(
        num_scalar_prefetch=1,
        grid=(steps,),
        in_specs=[
            whole(g),
            whole(gg),
            pl.BlockSpec((2 * rows, CHUNK), lambda i, place: (0, i)),
            pl.BlockSpec((count, None, per, 2 * rows), lambda i, place: (0, 1 - place[1], 0, 0)),
            pl.BlockSpec((count, None, per, 2 * rows), lambda i, place: (0, place[1], 0, 0)),
            pl.BlockSpec((D, CHUNK), lambda i, place: (0, at(i, place))),
            pl.BlockSpec((CHUNK, D), lambda i, place: (at(i, place), 0)),
            whole(wo),
        ],
        out_specs=[
            fixed(rows, D),
            fixed(rows, D),
            fixed(rows, D),
            cut,
            cut,
            pl.BlockSpec((1, CHUNK), lambda i, place: (0, i)),
        ],
        scratch_shapes=[pltpu.VMEM((2 * rows, D), BF16), pltpu.VMEM((2 * rows, D), F32)],
    )
    return pl.pallas_call(
        backward_kernel,
        grid_spec=spec,
        out_shape=[
            SHAPE((rows, D), F32),
            SHAPE((rows, D), BF16),
            SHAPE((rows, D), BF16),
            SHAPE((count, per, half), BF16),
            SHAPE((count, per, half), BF16),
            SHAPE((1, half), F32),
        ],
        compiler_params=params(),
        cost_estimate=cost(6.4),
        name="feed_backward",
    )(place, g, gg, slope, in_t, in_t, w1, w2, wo)


def present(slot, y, z):
    back = slot // 2
    return (back <= z) & ((slot % 2 == 0) | (back >= 1) | (y == 1))


def whole_kernel(span, depth, place_ref, *refs):
    even_ref, odd_ref, q_ref, do_ref, out_ref, dq_ref, even_out_ref, odd_out_ref = refs
    y, z = place_ref[2], place_ref[3]
    rows = PAIRS * span
    low = lax.broadcasted_iota(jnp.int32, (1, 128), 1) < HEAD_DIM

    def stacked(ref):
        return jnp.concatenate([ref[:, p * 128 : (p + 1) * 128] for p in range(PAIRS)], axis=0)

    blocks = [ref[k] for k in range(depth) for ref in (even_ref, odd_ref)]
    kv = jnp.concatenate(blocks, axis=0)
    swapped = pltpu.roll(kv.astype(F32), HEAD_DIM, 1).astype(BF16)
    zero, one = jnp.zeros_like(kv), jnp.ones_like(kv)
    keys = (jnp.where(low, kv, zero), jnp.where(low, zero, swapped))
    values = (jnp.where(low, swapped, zero), jnp.where(low, zero, kv))
    summing = (jnp.where(low, swapped, one), jnp.where(low, one, kv))
    slot = lax.broadcasted_iota(jnp.int32, (1, (2 * depth - 1) * span), 1) // span + 1
    absent = jnp.where(present(slot, y, z), 0.0, MASKED)
    token = lax.broadcasted_iota(jnp.int32, (rows, span), 0) % span
    seen = lax.broadcasted_iota(jnp.int32, (rows, span), 1) <= token
    q = stacked(q_ref)
    do = stacked(do_ref)
    do32 = do.astype(F32)

    expd, mixed = [], []
    for h in range(2):
        scores = dot_nt(q, keys[h])
        scores = jnp.concatenate([jnp.where(seen, scores[:, :span], MASKED), scores[:, span:] + absent], axis=1)
        top = jnp.max(scores, axis=1, keepdims=True)
        expd.append(jnp.exp(scores - top).astype(BF16))
        mixed.append(dot(expd[h], summing[h]))
    total = jnp.where(low, pltpu.roll(mixed[0], HEAD_DIM, 1), pltpu.roll(mixed[1], HEAD_DIM, 1))
    inverse = 1.0 / total
    out = jnp.where(low, mixed[0], mixed[1]) * inverse
    for p in range(PAIRS):
        out_ref[:, p * 128 : (p + 1) * 128] = out[p * span : (p + 1) * span].astype(BF16)
    product = do32 * out
    do_t = (do32 * inverse).T.astype(BF16)
    q_t = (q.astype(F32) * inverse).T.astype(BF16)
    dq = dk = dv = 0.0
    for h in range(2):
        head = slice(h * HEAD_DIM, (h + 1) * HEAD_DIM)
        delta = jnp.sum(jnp.where(low == (h == 0), product, 0.0), axis=1, keepdims=True)
        dprob = dot_nt(do, values[h])
        dscore = (expd[h].astype(F32) * (dprob - delta)).astype(BF16)
        dq = dq + dot(dscore, keys[h])
        dk = dk + dot(q_t[head], dscore)
        dv = dv + dot(do_t[head], expd[h])
    dq = dq * inverse
    for p in range(PAIRS):
        dq_ref[:, p * 128 : (p + 1) * 128] = dq[p * span : (p + 1) * span]
    both = jnp.concatenate([dk, dv], axis=0).T.astype(BF16)
    for k in range(depth):
        even_out_ref[k] = both[2 * k * span : (2 * k + 1) * span]
        odd_out_ref[k] = both[(2 * k + 1) * span : (2 * k + 2) * span]


def loop_kernel(groups, span, block, count, place_ref, *refs):
    even_ref, odd_ref, q_ref, do_ref, out_ref, dq_ref, even_out_ref, odd_out_ref = refs[:8]
    kv_scr, e_ref, kv_t_ref, max_ref, acc_ref, ext_ref = refs[8:]
    depth = count // 2
    rows = groups * span
    per = block // span
    y, z = place_ref[2], place_ref[3]
    used = (2 * (z + 1) + per - 1) // per
    group, group_count = pl.program_id(1), pl.num_programs(1)
    low = lax.broadcasted_iota(jnp.int32, (1, 128), 1) < HEAD_DIM
    lanes = lax.broadcasted_iota(jnp.int32, (rows, 128), 1)

    def stacked(ref):
        return jnp.concatenate([ref[:, p * 128 : (p + 1) * 128] for p in range(groups)], axis=0)

    @pl.when(group == 0)
    def _():
        for i in range(count):
            kv_scr[i * span : (i + 1) * span] = (odd_ref if i % 2 else even_ref)[i // 2]

    q = stacked(q_ref)
    do = stacked(do_ref)

    def load(b):
        kv = kv_scr[pl.ds(pl.multiple_of(b * block, block), block)]
        swapped = pltpu.roll(kv.astype(F32), HEAD_DIM, 1).astype(BF16)
        return kv, swapped, jnp.zeros_like(kv)

    def absent(b):
        row = lax.broadcasted_iota(jnp.int32, (block, 128), 0) + b * block
        lane = lax.broadcasted_iota(jnp.int32, (block, 128), 1)
        mask = jnp.where(present(row // span, y, z), 0.0, MASKED)
        return jnp.where(lane < 2, -1.0, jnp.where(lane == 2, mask, 0.0)).astype(BF16)

    def key_tiles(b):
        kv, swapped, zero = load(b)
        ext = absent(b)
        return [
            jnp.concatenate([jnp.where(low, kv, zero), ext], axis=1),
            jnp.concatenate([jnp.where(low, zero, swapped), ext], axis=1),
        ]

    def value_tiles(b):
        kv, swapped, zero = load(b)
        ext = absent(b)
        return [
            jnp.concatenate([jnp.where(low, swapped, zero), ext], axis=1),
            jnp.concatenate([jnp.where(low, zero, kv), ext], axis=1),
        ]

    def seen():
        token = lax.broadcasted_iota(jnp.int32, (rows, block), 0) % span
        key = lax.broadcasted_iota(jnp.int32, (rows, block), 1)
        return (key <= token) | (key >= span)

    def extended(values):
        high = values.astype(BF16).astype(F32)
        rest = jnp.where(lanes == 1, values - high, jnp.where(lanes == 2, 1.0, 0.0))
        return jnp.where(lanes == 0, high, rest).astype(BF16)

    def over_blocks(step):
        step(0, True)

        def body(b, carry):
            step(b, False)
            return carry

        lax.fori_loop(1, used, body, 0)

    plain = jnp.concatenate([q, jnp.where(lanes == 2, 1.0, 0.0).astype(BF16)], axis=1)

    def maxima(b, diagonal):
        keys = key_tiles(b)
        for h in range(2):
            scores = dot_nt(plain, keys[h])
            if diagonal:
                scores = jnp.where(seen(), scores, MASKED)
            top = functools.reduce(jnp.maximum, [scores[:, i : i + 128] for i in range(0, block, 128)])
            max_ref[h] = top if diagonal else jnp.maximum(max_ref[h], top)

    over_blocks(maxima)
    for h in range(2):
        top = jnp.max(max_ref[h], axis=1, keepdims=True)
        ext_ref[h] = jnp.concatenate([q, extended(jnp.broadcast_to(top, (rows, 128)))], axis=1)

    def forward(b, diagonal):
        keys = key_tiles(b)
        kv, swapped, _ = load(b)
        one = jnp.ones_like(kv)
        values = (jnp.where(low, swapped, one), jnp.where(low, one, kv))
        for h in range(2):
            expd = jnp.exp(dot_nt(ext_ref[h], keys[h]))
            if diagonal:
                expd = jnp.where(seen(), expd, 0.0)
            expd = expd.astype(BF16)
            e_ref[b, h] = expd
            mixed = dot(expd, values[h])
            acc_ref[h] = mixed if diagonal else acc_ref[h] + mixed

    over_blocks(forward)
    first, second = acc_ref[0], acc_ref[1]
    total = jnp.where(low, pltpu.roll(first, HEAD_DIM, 1), pltpu.roll(second, HEAD_DIM, 1))
    inverse = 1.0 / total
    out = jnp.where(low, first, second) * inverse
    for p in range(groups):
        out_ref[:, p * 128 : (p + 1) * 128] = out[p * span : (p + 1) * span].astype(BF16)
    do32 = do.astype(F32)
    product = do32 * out
    high = product.astype(BF16)
    rest = (product - high.astype(F32)).astype(BF16)
    place = lax.broadcasted_iota(jnp.int32, (128, 128), 0)
    for h in range(2):
        ones = jnp.where((place < HEAD_DIM) == (h == 0), 1.0, 0.0).astype(BF16)
        delta = dot(high, ones) + dot(rest, ones)
        ext_ref[h] = jnp.concatenate([do, extended(delta)], axis=1)
    do_t = (do32 * inverse).T.astype(BF16)
    q_t = (q.astype(F32) * inverse).T.astype(BF16)

    def backward(b, start):
        values = value_tiles(b)
        kv, swapped, zero = load(b)
        keys = (jnp.where(low, kv, zero), jnp.where(low, zero, swapped))
        dq = dk = dv = 0.0
        for h in range(2):
            expd = e_ref[b, h]
            head = slice(h * HEAD_DIM, (h + 1) * HEAD_DIM)
            dscore = (expd.astype(F32) * dot_nt(ext_ref[h], values[h])).astype(BF16)
            dq = dq + dot(dscore, keys[h])
            dk = dk + dot(q_t[head], dscore)
            dv = dv + dot(do_t[head], expd)
        acc_ref[0] = dq if start else acc_ref[0] + dq
        both = jnp.concatenate([dk, dv], axis=0)
        kv_t_ref[b] = jnp.where(group == 0, both, kv_t_ref[b] + both)

    over_blocks(backward)
    dq = acc_ref[0] * inverse
    for p in range(groups):
        dq_ref[:, p * 128 : (p + 1) * 128] = dq[p * span : (p + 1) * span]

    @pl.when(group == group_count - 1)
    def _():
        for b in range(count // per):
            used_block = jnp.where(b < used, kv_t_ref[b], 0.0).T.astype(BF16)
            for i in range(per):
                slot = b * per + i
                result = odd_out_ref if slot % 2 else even_out_ref
                result[slot // 2] = used_block[i * span : (i + 1) * span]


def attention(place, evens, odds, q, do):
    depth = evens.shape[0]
    count = 2 * depth
    seqs, span, _ = q.shape
    single = count * span <= 1024
    groups = PAIRS if single else 2
    wide_spec = pl.BlockSpec((None, span, groups * 128), lambda s, i: (s, 0, i))
    pieces = pl.BlockSpec((depth, None, span, 128), lambda s, i: (0, s, 0, 0))
    if single:
        kernel, scratch = functools.partial(whole_kernel, span, depth), []
    else:
        block = max(512, span)
        blocks = count * span // block
        rows = groups * span
        kernel = functools.partial(loop_kernel, groups, span, block, count)
        scratch = [
            pltpu.VMEM((count * span, 128), BF16),
            pltpu.VMEM((blocks, 2, rows, block), BF16),
            pltpu.VMEM((blocks, 128, block), F32),
            pltpu.VMEM((2, rows, 128), F32),
            pltpu.VMEM((2, rows, 128), F32),
            pltpu.VMEM((2, rows, 256), BF16),
        ]
    return pl.pallas_call(
        kernel,
        grid=(seqs, PAIRS // groups),
        in_specs=[SMEM, pieces, pieces, wide_spec, wide_spec],
        out_specs=[wide_spec] * 2 + [pieces] * 2,
        out_shape=[SHAPE((seqs, span, D), BF16), SHAPE((seqs, span, D), F32)]
        + [SHAPE((depth, seqs, span, 128), BF16)] * 2,
        scratch_shapes=scratch,
        compiler_params=params(),
        cost_estimate=cost(10),
        name="attention",
    )(place, evens, odds, q, do)


def mix_kernel(
    copies,
    calls,
    place_ref,
    *refs,
):
    outs, dqs, refs = refs[:calls], refs[calls : 2 * calls], refs[2 * calls :]
    (
        x_ref,
        g_ref,
        mlp_ref,
        mlp2_ref,
        gain_ref,
        bias_ref,
        add_ref,
        wo_ref,
        wqkv_ref,
        tables_ref,
        output_ref,
        send_ref,
        keep_ref,
        first_ref,
        small_ref,
    ) = refs
    half = D // 2
    x = x_ref[...].astype(F32)
    g = g_ref[...]
    attn = jnp.concatenate([r[...] for r in outs], axis=0)
    normed, _ = normalize(x)
    first_in = normed * wide(gain_ref) + wide(bias_ref)
    tables = repeated(tables_ref, copies)
    parts = []
    for p in range(PAIRS):
        dq = jnp.concatenate([r[:, p * 128 : (p + 1) * 128] for r in dqs], axis=0)
        parts.append(turn(dq * SCALE, tables, -1).astype(BF16))
    grad = jnp.concatenate(parts, axis=1)
    attn_t = attn.astype(F32).T.astype(BF16)
    first_t = first_in.T.astype(BF16)
    own = place_ref[0] == 0
    for i, (left, right) in enumerate(((attn_t, g), (first_t, grad))):
        lower, upper = right[:, :half], right[:, half:]
        send_ref[i] = dot(left, jnp.where(own, upper, lower)).astype(BF16)
        keep_ref[i] = dot(left, jnp.where(own, lower, upper)).astype(BF16)
    small_ref[...] = jnp.zeros_like(small_ref)
    small_ref[0:1] = jnp.sum(grad.astype(F32), axis=0, keepdims=True)
    small_ref[1:2] = jnp.sum(g.astype(F32), axis=0, keepdims=True)
    mlp = mlp_ref[...] + mlp2_ref[...].astype(F32)
    output_ref[...] = (x + (mlp + dot(attn, wo_ref[...])) + wide(add_ref)).astype(BF16)
    first_ref[...] = dot_nt(grad, wqkv_ref[:, :D])


def mix(place, outs, dqs, x, g, mlp, mlp2, gain, bias, add, wo, wqkv, tables):
    rows = x.shape[0]
    calls = len(outs)
    return pl.pallas_call(
        functools.partial(mix_kernel, rows // tables.shape[1], calls),
        in_specs=[SMEM] + [VMEM] * (2 * calls + 10),
        out_specs=[VMEM] * 5,
        out_shape=[
            SHAPE((rows, D), BF16),
            SHAPE((2, D, D // 2), BF16),
            SHAPE((2, D, D // 2), BF16),
            SHAPE((rows, D), F32),
            SHAPE((8, D), F32),
        ],
        compiler_params=params(),
        cost_estimate=cost(3.2),
        name="mix",
    )(place, *outs, *dqs, x, g, mlp, mlp2, gain, bias, add, wo, wqkv, tables)


def finish_kernel(copies, groups, *refs):
    sums = []
    for group in groups:
        total = refs[0][...].astype(F32)
        for ref in refs[1:group]:
            total += ref[...].astype(F32)
        sums.append(total)
        refs = refs[group:]
    (
        extra_ref,
        x_ref,
        g_ref,
        first_ref,
        back_ref,
        back2_ref,
        gain_ref,
        bias_ref,
        gain2_ref,
        wqkv_ref,
        tables_ref,
        tokens_ref,
        weight_ref,
        small_ref,
    ) = refs
    total = jnp.concatenate(sums, axis=0) + extra_ref[...].astype(F32)
    tables = repeated(tables_ref, copies)
    grad = turn(total, key_tables(tables), -1).astype(BF16)
    x = x_ref[...].astype(F32)
    normed, inverse = normalize(x)
    gain = wide(gain_ref)
    first_in = normed * gain + wide(bias_ref)
    weight_ref[...] = dot(first_in.T.astype(BF16), grad).astype(BF16)
    first_grad = first_ref[...] + dot_nt(grad, wqkv_ref[:, D:])
    second_grad = back_ref[...] + back2_ref[...].astype(F32)
    small_ref[...] = jnp.zeros_like(small_ref)
    for i, rows in enumerate((first_grad * normed, first_grad, second_grad * normed, second_grad)):
        small_ref[i : i + 1] = jnp.sum(rows, axis=0, keepdims=True)
    small_ref[4:5, :128] = jnp.sum(grad.astype(F32), axis=0, keepdims=True)
    normed_grad = first_grad * gain + second_grad * wide(gain2_ref)
    mean = jnp.mean(normed_grad, axis=-1, keepdims=True)
    along_rows = jnp.mean(normed_grad * normed, axis=-1, keepdims=True)
    tokens_ref[...] = (g_ref[...].astype(F32) + inverse * (normed_grad - mean - normed * along_rows)).astype(BF16)


def finish(kv_parts, extra, x, g, first, back, back2, gain, bias, gain2, wqkv, tables):
    rows = x.shape[0]
    groups = [len(parts) for parts in kv_parts]
    arrays = [v for parts in kv_parts for v in parts]
    return pl.pallas_call(
        functools.partial(finish_kernel, rows // tables.shape[1], groups),
        in_specs=[VMEM] * (len(arrays) + 11),
        out_specs=[VMEM] * 3,
        out_shape=[SHAPE((rows, D), BF16), SHAPE((D, 128), BF16), SHAPE((8, D), F32)],
        compiler_params=params(),
        cost_estimate=cost(2.4),
        name="finish",
    )(*arrays, extra, x, g, first, back, back2, gain, bias, gain2, wqkv, tables)


def local(
    tokens,
    ln1_gain,
    ln1_bias,
    qkv_weight,
    qkv_bias,
    out_weight,
    ln2_gain,
    ln2_bias,
    fc1_weight,
    fc1_bias,
    fc2_weight,
    out_bias,
    output_grad,
    key_value_grad,
):
    seqs, span, _ = tokens.shape
    rows = seqs * span
    ff = fc1_weight.shape[1]
    count = lax.axis_size("seq")
    batches = lax.axis_size("batch")
    depth = count // 2
    half_depth = depth // 2
    per1, per2 = D // count, ff // count
    own = lax.axis_index("seq").astype(jnp.int32)
    batch = lax.axis_index("batch").astype(jnp.int32)
    y, z = own & 1, own >> 1
    core, xs = batch & 1, batch >> 1
    place = jnp.stack([core, xs, y, z])
    x = tokens.reshape(rows, D)
    g = output_grad.reshape(rows, D)
    over_core = lambda v: flipped(v, "batch", 1)
    over_x = lambda v: flipped(v, "batch", 2)
    over_y = lambda v: flipped(v, "seq", 1)
    flat = lambda v: v.reshape(rows, -1)

    def pair(mine, other, index, axis):
        first = jnp.where(index == 0, mine, other)
        second = jnp.where(index == 0, other, mine)
        return jnp.concatenate([first, second], axis=axis)

    def summed(*parts):
        return tree_sum(parts).astype(BF16)

    x_other, g_other = over_core(x), over_core(g)
    tables = rotary_tables(own * span, span)
    q, kv = project(x, ln1_gain, ln1_bias, qkv_weight, qkv_bias, tables)
    kv3 = kv.reshape(seqs, span, 128)
    evens = [kv3] + [along(kv3, k) for k in range(1, depth)]

    x_fed, g_fed = after((x, g), kv)
    (mlp, mlp_other, slope, in_t), grads2 = feed_forward(
        place, depth, x_fed, x_other, g_fed, g_other, ln2_gain, ln2_bias, fc1_weight, fc1_bias.reshape(1, -1), fc2_weight
    )
    parts2 = [grads2[0]] + [to_owner(grads2[i % half_depth], i) for i in range(1, depth)]
    mlp_come = over_core(mlp_other)
    evens = [kv3] + list(after(evens[1:], slope))
    evens = jnp.stack(evens)
    odds = over_y(evens)
    back, back_other, attn_grad, theirs1, mine1, b1_grad = feed_backward(
        place, count, g, g_other, slope, in_t, fc1_weight, fc2_weight, out_weight
    )
    come1 = over_x(theirs1)
    back_come = over_core(back_other)

    q3, do3 = q.reshape(seqs, span, D), attn_grad.reshape(seqs, span, D)
    out, dq, even, odd = attention(place, evens, odds, q3, do3)
    odd = over_y(odd)

    cut = lambda v: v.reshape(depth, 2, per1 // 2, ff // 2)
    mine1, come1 = after((mine1, come1), out)
    theirs1, mine1 = add_split(place, [(cut(mine1), cut(come1), 2)])
    come1 = over_y(theirs1)

    g_mix, mlp_come = after((g, mlp_come), theirs1)
    output, send, keep, first, small_mix = mix(
        place, [flat(out)], [flat(dq)], x, g_mix, mlp, mlp_come, ln1_gain, ln1_bias, out_bias, out_weight, qkv_weight, tables
    )
    come = over_core(send)
    even, odd = after((even, odd), send)
    kv_sums = [summed(even[k], odd[k]) for k in range(depth)]
    got = [along(kv_sums[k], -k) for k in range(1, depth)]

    parts2 = after(parts2, *kv_sums)
    theirs2, mine2 = sum_split(place, [v.reshape(2, per2, D) for v in parts2])
    come2 = over_y(theirs2)

    mine1, come1 = after((mine1, come1), theirs2)
    cuts1 = add_cut(place, [(mine1, come1)])
    parts1 = [cuts1[0]] + [flipped(cuts1[i], "seq", 2 * i) for i in range(1, depth)]

    keep, come = after((keep, come), cuts1[0])
    cut_o = lambda v: v[0].reshape(depth, 2, per1, D // 2)
    cut_q = lambda v: v[1].reshape(count, 2, per1 // 2, D // 2)
    theirs_o, mine_o, theirs_q, mine_q = add_split(
        place, [(cut_o(keep), cut_o(come), 2), (cut_q(keep), cut_q(come), 1)]
    )
    come_o, come_q = over_y(theirs_o), over_x(theirs_q)

    mine2, come2 = after((mine2, come2), theirs_o)
    sum2 = summed(mine2, come2)
    other2 = over_x(sum2)

    got = after(got, sum2)
    kv_parts = [[v.reshape(-1, 128) for v in (kv_sums[0], *got)]]
    tokens_grad, kv_weight, small = finish(
        kv_parts, flat(key_value_grad), x, g, first, back, back_come, ln1_gain, ln1_bias, ln2_gain, qkv_weight, tables
    )

    b1_half = b1_grad.reshape(-1, 128)
    empty = jnp.zeros_like(b1_half)
    vector = jnp.concatenate(
        [
            jnp.where(core == 0, b1_half, empty),
            jnp.where(core == 0, empty, b1_half),
            small_mix[:2].reshape(-1, 128),
            small[:4].reshape(-1, 128),
            small[4:5, :128],
        ]
    )
    lines = vector.shape[0]

    def packed(weight, vector):
        high = vector.astype(BF16)
        rest = (vector - high.astype(F32)).astype(BF16)
        return jnp.concatenate([weight.astype(BF16), high, rest])

    def unpacked(message):
        message = message.astype(F32)
        return jnp.concatenate([message[:per1], message[per1 : per1 + lines] + message[per1 + lines :]])

    shards = kv_weight.reshape(depth, 2, per1, 128)
    vector16 = packed(kv_weight[:0], vector)
    late_send = jnp.concatenate([take(shards, 1 - y, 1).reshape(-1, 128), vector16])
    late_keep = jnp.concatenate([take(shards, y, 1).reshape(-1, 128), vector16])
    late_come = over_y(late_send)

    mine_o, come_o, mine_q, come_q = after((mine_o, come_o, mine_q, come_q), late_send)
    cuts_o = add_cut(place, [(mine_o, come_o)])
    parts_o = [cuts_o[0]] + [flipped(cuts_o[i], "seq", 2 * i) for i in range(1, depth)]
    cut_q = lambda v: v.reshape(depth, 2, per1 // 2, D // 2)
    theirs_q, mine_q = add_split(place, [(cut_q(mine_q), cut_q(come_q), 2)])
    come_q = over_y(theirs_q)

    late_keep, late_come = after((late_keep, late_come), theirs_q, cuts_o[0])
    unpack = lambda v, at: v[at : at + lines].astype(F32) + v[at + lines :].astype(F32)
    shards = late_keep[: depth * per1].astype(F32) + late_come[: depth * per1].astype(F32)
    shards = shards.reshape(depth, per1, 128)
    vector = unpack(late_keep, depth * per1) + unpack(late_come, depth * per1)
    messages = [packed(take(shards, z ^ i, 0), vector) for i in range(depth)]
    got = [flipped(messages[i], "seq", 2 * i) for i in range(1, depth)]

    sum2, other2 = after((sum2, other2), *messages)
    sum2 = summed(sum2, other2)
    other2 = over_core(sum2)
    parts1 = after(parts1, sum2)
    sum1 = summed(*parts1)
    other1 = over_x(sum1)

    got = after(got, sum1)
    total = tree_sum([unpacked(v) for v in [messages[0], *got]])
    message = packed(total[:per1], total[per1:])
    got = [flipped(message, "batch", i) for i in range(1, batches)]

    parts_o = after(parts_o, message)
    sum_o = summed(*parts_o)
    other_o = over_x(sum_o)
    mine_q, come_q = after((mine_q, come_q), sum_o)
    cuts_q = add_cut(place, [(mine_q, come_q)])
    parts_q = [cuts_q[0]] + [flipped(cuts_q[i], "seq", 2 * i) for i in range(1, depth)]

    sum1, other1 = after((sum1, other1), cuts_q[0])
    sum1 = pair(sum1, other1, xs, 0)
    other1 = over_core(sum1)
    sum_o, other_o = after((sum_o, other_o), sum1)
    sum_o = summed(sum_o, other_o)
    other_o = over_core(sum_o)
    owner = z // half_depth == core
    (other2,) = after((other2,), sum_o)
    fc2_grad = jnp.where(owner, sum2, other2).astype(F32)
    parts_q = after(parts_q, fc2_grad)
    sum_q = summed(*parts_q)
    other_q = over_x(sum_q)
    got = after(got, sum_q)
    total = tree_sum([unpacked(v) for v in [message, *got]])
    (other1,) = after((other1,), total)
    fc1_grad = pair(sum1, other1, core, 1).astype(F32)
    sum_q, other_q = after((sum_q, other_q), fc1_grad)
    sum_q = pair(sum_q, other_q, xs, 0)
    other_q = over_core(sum_q)
    (other_o,) = after((other_o,), sum_q)
    out_grad = pair(sum_o, other_o, core, 1).astype(F32)
    q_grad = pair(sum_q, other_q, core, 1).astype(F32)

    vector = total[per1:]
    b1_lines, d_lines = ff // 128, D // 128
    row = lambda i: vector[b1_lines + i * d_lines : b1_lines + (i + 1) * d_lines].reshape(-1)
    return (
        output.reshape(tokens.shape),
        kv3,
        tokens_grad.reshape(tokens.shape),
        row(2),
        row(3),
        jnp.concatenate([q_grad, total[:per1]], axis=1),
        jnp.concatenate([row(0), vector[-1]]),
        out_grad,
        row(4),
        row(5),
        fc1_grad,
        vector[:b1_lines].reshape(-1),
        fc2_grad,
        row(1),
    )


def solution(mesh):
    part = P("batch", "seq", None)
    whole = P()
    split = P("seq", None)
    return jax.shard_map(
        local,
        mesh=mesh,
        in_specs=(part,) + (whole,) * 11 + (part, part),
        out_specs=(
            part, part, part, whole, whole, split, whole, split, whole, whole, split, whole, split, whole,
        ),
        check_vma=False,
    )
```

```python
import functools
import math

import jax
import jax.numpy as jnp
from jax import lax
from jax.experimental import pallas as pl
from jax.experimental.pallas import tpu as pltpu
from jax.sharding import PartitionSpec as P

D = 768
HEADS = 12
HEAD_DIM = 64
ROT = 16
PAIRS = HEADS // 2
SCALE = 1.0 / math.sqrt(HEAD_DIM)
NORM_EPS = 1e-05
MASKED = -1e30
F32 = jnp.float32
BF16 = jnp.bfloat16
VMEM_BYTES = 56 * 1024 * 1024


def dot(a, b):
    return lax.dot_general(a, b, (((1,), (0,)), ((), ())), preferred_element_type=F32)


def dot_nt(a, b):
    return lax.dot_general(a, b, (((1,), (1,)), ((), ())), preferred_element_type=F32)


def dot_tn(a, b):
    return lax.dot_general(a, b, (((0,), (0,)), ((), ())), preferred_element_type=F32)


def params():
    return pltpu.CompilerParams(vmem_limit_bytes=VMEM_BYTES)


def flipped(block, axis, bits):
    return lax.ppermute(block, axis, [(i, i ^ bits) for i in range(lax.axis_size(axis))])


def along(block, distance):
    size = lax.axis_size("seq")
    return lax.ppermute(block, "seq", [(i, (i + 2 * distance) % size) for i in range(size)])


def to_owner(block):
    size = lax.axis_size("seq")
    route = []
    for b in range(lax.axis_size("batch")):
        for i in range(size):
            j = i ^ (size // 2)
            if j // (size // 2) == b % 2:
                route.append((b * size + i, b * size + j))
    return lax.ppermute(block, ("batch", "seq"), route)


def after(values, *others):
    return lax.optimization_barrier((tuple(values), others))[0]


def tree_sum(parts):
    parts = [p.astype(F32) for p in parts]
    while len(parts) > 1:
        parts = [sum(parts[i : i + 2][1:], parts[i]) for i in range(0, len(parts), 2)]
    return parts[0]


def take(block, index, axis):
    return lax.dynamic_index_in_dim(block, index, axis, keepdims=False)


def normalize(rows):
    centre = jnp.mean(rows, axis=-1, keepdims=True)
    centred = rows - centre
    spread = jnp.mean(centred * centred, axis=-1, keepdims=True)
    inverse = lax.rsqrt(spread + NORM_EPS)
    return centred * inverse, inverse


def rotary_tables(first, count):
    lane = jnp.arange(128) % HEAD_DIM
    half = ROT // 2
    freqs = 10000.0 ** (-(lane % half).astype(F32) / half)
    places = (first + jnp.arange(count)).astype(F32) * 0.25
    angles = places[:, None] * freqs[None, :]
    cosine, sine = jnp.cos(angles), jnp.sin(angles)
    return jnp.stack(
        [
            jnp.where(lane < ROT, cosine, 1.0),
            jnp.where((lane >= half) & (lane < ROT), sine, 0.0),
            jnp.where(lane < half, -sine, 0.0),
        ]
    )


def turn(values, tables, sign):
    moved = pltpu.roll(values, ROT // 2, 1) * tables[1] + pltpu.roll(values, 128 - ROT // 2, 1) * tables[2]
    return values * tables[0] + (moved if sign > 0 else -moved)


def repeated(tables_ref, count):
    return [jnp.concatenate([tables_ref[i]] * count, axis=0) for i in range(3)]


def key_tables(tables):
    low = lax.broadcasted_iota(jnp.int32, (1, 128), 1) < HEAD_DIM
    return [jnp.where(low, tables[0], 1.0), jnp.where(low, tables[1], 0.0), jnp.where(low, tables[2], 0.0)]

VMEM = pl.BlockSpec(memory_space=pltpu.VMEM)
SMEM = pl.BlockSpec(memory_space=pltpu.SMEM)
SHAPE = jax.ShapeDtypeStruct


def cost(share):
    return pl.CostEstimate(flops=int(share * 3e9), bytes_accessed=0, transcendentals=0)


def wide(ref):
    return ref[...].reshape(1, -1)


def add_split(place, items):
    def kernel(place_ref, *refs):
        sources, results = refs[: 2 * len(items)], refs[2 * len(items) :]
        for n, (_, _, which) in enumerate(items):
            a, b = sources[2 * n], sources[2 * n + 1]
            own = place_ref[which] if which < 3 else lax.rem(lax.shift_right_logical(place_ref[3], which - 3), 2)
            for m in range(a.shape[0]):
                for result, at in ((results[2 * n], 1 - own), (results[2 * n + 1], own)):
                    result[m] = (a[m, at].astype(F32) + b[m, at].astype(F32)).astype(BF16)

    shapes = []
    for a, _, _ in items:
        shapes += [SHAPE((a.shape[0],) + a.shape[2:], BF16)] * 2
    arrays = [v for item in items for v in item[:2]]
    return pl.pallas_call(
        kernel,
        in_specs=[SMEM] + [VMEM] * len(arrays),
        out_specs=[VMEM] * len(shapes),
        out_shape=shapes,
        compiler_params=params(),
        cost_estimate=cost(1.2),
        name="add_split",
    )(place, *arrays)


def project_kernel(copies, x_ref, gain_ref, bias_ref, weight_ref, add_ref, tables_ref, q_ref, kv_ref):
    normed, _ = normalize(x_ref[...].astype(F32))
    first_in = (normed * wide(gain_ref) + wide(bias_ref)).astype(BF16)
    tables = repeated(tables_ref, copies)
    bias = wide(add_ref)
    for p in (PAIRS,) + tuple(range(PAIRS)):
        columns = slice(p * 128, (p + 1) * 128)
        part = dot(first_in, weight_ref[:, columns]) + bias[:, columns]
        if p < PAIRS:
            q_ref[:, columns] = (turn(part, tables, 1) * SCALE).astype(BF16)
        else:
            kv_ref[...] = turn(part, key_tables(tables), 1).astype(BF16)


def project(x, gain, bias, weight, add, tables):
    rows = x.shape[0]
    return pl.pallas_call(
        functools.partial(project_kernel, rows // tables.shape[1]),
        in_specs=[VMEM] * 6,
        out_specs=[VMEM] * 2,
        out_shape=[SHAPE((rows, D), BF16), SHAPE((rows, 128), BF16)],
        compiler_params=params(),
        cost_estimate=cost(2),
        name="project",
    )(x, gain, bias, weight, add, tables)


def gelu_parts(h):
    t = pl.reciprocal(1.0 + (0.3275911 / math.sqrt(2.0)) * jnp.abs(h))
    e = jnp.exp(-0.5 * h * h)
    poly = 0.5 * 1.061405429
    for coefficient in (-1.453152027, 1.421413741, -0.284496736, 0.254829592):
        poly = poly * t + 0.5 * coefficient
    tail = poly * t * e
    cdf = jnp.where(h >= 0.0, 1.0 - tail, tail)
    return h * cdf, cdf + h * e * (1.0 / math.sqrt(2.0 * math.pi))


def forward_kernel(
    place_ref,
    x_ref,
    xx_ref,
    g_ref,
    gg_ref,
    gain_ref,
    bias_ref,
    w1_ref,
    b1_ref,
    w2_ref,
    own_ref,
    other_ref,
    slope_ref,
    in_t_ref,
    *refs,
):
    grad_refs, (in_scr, g_scr, acc_scr) = refs[:-3], refs[-3:]
    step, steps = pl.program_id(0), pl.num_programs(0)
    rows = x_ref.shape[0]

    @pl.when(step == 0)
    def _():
        for i, (tokens, grads) in enumerate(((x_ref, g_ref), (xx_ref, gg_ref))):
            at = slice(i * rows, (i + 1) * rows)
            normed, _ = normalize(tokens[...].astype(F32))
            second_in = normed * wide(gain_ref) + wide(bias_ref)
            in_scr[at] = second_in.astype(BF16)
            in_t_ref[:, at] = second_in.T.astype(BF16)
            g_scr[at] = grads[...]

    w2 = w2_ref[...]
    act, slope = gelu_parts(dot(in_scr[...], w1_ref[...]) + b1_ref[...])
    act = act.astype(BF16)
    slope_ref[...] = slope.astype(BF16)
    grad = dot_tn(act, g_scr[...]).astype(BF16)
    if len(grad_refs) == 1:
        grad_refs[0][...] = grad
    for i in range(len(grad_refs) if len(grad_refs) > 1 else 0):

        @pl.when(step == i)
        def _(i=i):
            grad_refs[i][...] = grad

    mlp = dot(act, w2)

    @pl.when(step == 0)
    def _():
        acc_scr[...] = mlp

    @pl.when((step > 0) & (step < steps - 1))
    def _():
        acc_scr[...] += mlp

    @pl.when(step == steps - 1)
    def _():
        total = acc_scr[...] + mlp
        own_ref[...] = total[:rows].astype(BF16)
        other_ref[...] = total[rows:].astype(BF16)


CHUNK = 512


def feed_forward(place, depth, x, xx, g, gg, gain, bias, w1, b1, w2):
    rows = x.shape[0]
    half = w1.shape[1] // 2
    pieces = depth // 2
    aligned = pieces == 2 and half % 512 == 0
    chunk = half // pieces if aligned else CHUNK
    steps = half // chunk
    whole = lambda a: pl.BlockSpec(a.shape, lambda i, place: (0,) * a.ndim)
    fixed = lambda *shape: pl.BlockSpec(shape, lambda i, place: (0, 0))
    if aligned:
        piece = lambda i, place: (place[3] ^ (1 - i)) & 1
        grad_specs = [fixed(chunk, D)] * pieces
        grad_shapes = [SHAPE((chunk, D), BF16)] * pieces
    else:
        piece = lambda i, place: i
        grad_specs = [pl.BlockSpec((chunk, D), lambda i, place: (i, 0))]
        grad_shapes = [SHAPE((half, D), BF16)]
    at = lambda i, place: place[0] * steps + piece(i, place)
    spec = pltpu.PrefetchScalarGridSpec(
        num_scalar_prefetch=1,
        grid=(steps,),
        in_specs=[
            whole(x),
            whole(xx),
            whole(g),
            whole(gg),
            whole(gain),
            whole(bias),
            pl.BlockSpec((D, chunk), lambda i, place: (0, at(i, place))),
            pl.BlockSpec((1, chunk), lambda i, place: (0, at(i, place))),
            pl.BlockSpec((chunk, D), lambda i, place: (at(i, place), 0)),
        ],
        out_specs=[
            fixed(rows, D),
            fixed(rows, D),
            pl.BlockSpec((2 * rows, chunk), lambda i, place: (0, piece(i, place))),
            fixed(D, 2 * rows),
        ]
        + grad_specs,
        scratch_shapes=[
            pltpu.VMEM((2 * rows, D), BF16),
            pltpu.VMEM((2 * rows, D), BF16),
            pltpu.VMEM((2 * rows, D), F32),
        ],
    )
    result = pl.pallas_call(
        forward_kernel,
        grid_spec=spec,
        out_shape=[
            SHAPE((rows, D), BF16),
            SHAPE((rows, D), BF16),
            SHAPE((2 * rows, half), BF16),
            SHAPE((D, 2 * rows), BF16),
        ]
        + grad_shapes,
        compiler_params=params(),
        cost_estimate=cost(8),
        name="feed_forward",
    )(place, x, xx, g, gg, gain, bias, w1, b1, w2)
    grads = result[4:]
    if not aligned:
        cut = grads[0].reshape(pieces // 2, 2, -1, D)
        low = place[3] & 1
        grads = [take(cut, 1 - low, 1), take(cut, low, 1)]
    return result[:4], grads


def backward_kernel(
    place_ref,
    g_ref,
    gg_ref,
    slope_ref,
    in_theirs_ref,
    in_mine_ref,
    w1_ref,
    w2_ref,
    wo_ref,
    own_ref,
    other_ref,
    attn_grad_ref,
    theirs_ref,
    mine_ref,
    b1_grad_ref,
    g_scr,
    acc_scr,
):
    step, steps = pl.program_id(0), pl.num_programs(0)
    rows = g_ref.shape[0]

    @pl.when(step == 0)
    def _():
        g_scr[:rows] = g_ref[...]
        g_scr[rows:] = gg_ref[...]
        attn_grad_ref[...] = dot_nt(g_ref[...], wo_ref[...]).astype(BF16)

    w1 = w1_ref[...]
    pre = dot_nt(g_scr[...], w2_ref[...]) * slope_ref[...].astype(F32)
    pre16 = pre.astype(BF16)
    b1_grad_ref[...] = jnp.sum(pre, axis=0, keepdims=True)
    for source, result in ((in_theirs_ref, theirs_ref), (in_mine_ref, mine_ref)):
        left = source[...].reshape(-1, 2 * rows)
        result[...] = dot(left, pre16).astype(BF16).reshape(result.shape)
    back = dot_nt(pre16, w1)

    @pl.when(step == 0)
    def _():
        acc_scr[...] = back

    @pl.when((step > 0) & (step < steps - 1))
    def _():
        acc_scr[...] += back

    @pl.when(step == steps - 1)
    def _():
        total = acc_scr[...] + back
        own_ref[...] = total[:rows].astype(BF16)
        other_ref[...] = total[rows:].astype(BF16)


def feed_backward(place, count, g, gg, slope, in_t, w1, w2, wo):
    rows = g.shape[0]
    half = w1.shape[1] // 2
    steps = half // CHUNK
    per = D // count // 2
    in_t = in_t.reshape(count, 2, per, 2 * rows)
    whole = lambda a: pl.BlockSpec(a.shape, lambda i, place: (0,) * a.ndim)
    fixed = lambda *shape: pl.BlockSpec(shape, lambda i, place: (0, 0))
    at = lambda i, place: place[0] * steps + i
    cut = pl.BlockSpec((count, per, CHUNK), lambda i, place: (0, 0, i))
    spec = pltpu.PrefetchScalarGridSpec(
        num_scalar_prefetch=1,
        grid=(steps,),
        in_specs=[
            whole(g),
            whole(gg),
            pl.BlockSpec((2 * rows, CHUNK), lambda i, place: (0, i)),
            pl.BlockSpec((count, None, per, 2 * rows), lambda i, place: (0, 1 - place[1], 0, 0)),
            pl.BlockSpec((count, None, per, 2 * rows), lambda i, place: (0, place[1], 0, 0)),
            pl.BlockSpec((D, CHUNK), lambda i, place: (0, at(i, place))),
            pl.BlockSpec((CHUNK, D), lambda i, place: (at(i, place), 0)),
            whole(wo),
        ],
        out_specs=[
            fixed(rows, D),
            fixed(rows, D),
            fixed(rows, D),
            cut,
            cut,
            pl.BlockSpec((1, CHUNK), lambda i, place: (0, i)),
        ],
        scratch_shapes=[pltpu.VMEM((2 * rows, D), BF16), pltpu.VMEM((2 * rows, D), F32)],
    )
    return pl.pallas_call(
        backward_kernel,
        grid_spec=spec,
        out_shape=[
            SHAPE((rows, D), BF16),
            SHAPE((rows, D), BF16),
            SHAPE((rows, D), BF16),
            SHAPE((count, per, half), BF16),
            SHAPE((count, per, half), BF16),
            SHAPE((1, half), F32),
        ],
        compiler_params=params(),
        cost_estimate=cost(6.4),
        name="feed_backward",
    )(place, g, gg, slope, in_t, in_t, w1, w2, wo)


def present(slot, y, z):
    back = slot // 2
    return (back <= z) & ((slot % 2 == 0) | (back >= 1) | (y == 1))


def whole_kernel(span, depth, place_ref, *refs):
    even_ref, odd_ref, q_ref, do_ref, out_ref, dq_ref, even_out_ref, odd_out_ref = refs
    y, z = place_ref[2], place_ref[3]
    rows = PAIRS * span
    low = lax.broadcasted_iota(jnp.int32, (1, 128), 1) < HEAD_DIM

    def stacked(ref):
        return jnp.concatenate([ref[:, p * 128 : (p + 1) * 128] for p in range(PAIRS)], axis=0)

    blocks = [ref[k] for k in range(depth) for ref in (even_ref, odd_ref)]
    kv = jnp.concatenate(blocks, axis=0)
    swapped = pltpu.roll(kv.astype(F32), HEAD_DIM, 1).astype(BF16)
    zero, one = jnp.zeros_like(kv), jnp.ones_like(kv)
    keys = (jnp.where(low, kv, zero), jnp.where(low, zero, swapped))
    values = (jnp.where(low, swapped, zero), jnp.where(low, zero, kv))
    summing = (jnp.where(low, swapped, one), jnp.where(low, one, kv))
    slot = lax.broadcasted_iota(jnp.int32, (1, (2 * depth - 1) * span), 1) // span + 1
    absent = jnp.where(present(slot, y, z), 0.0, MASKED)
    token = lax.broadcasted_iota(jnp.int32, (rows, span), 0) % span
    seen = lax.broadcasted_iota(jnp.int32, (rows, span), 1) <= token
    q = stacked(q_ref)
    do = stacked(do_ref)
    do32 = do.astype(F32)

    expd, mixed = [], []
    for h in range(2):
        scores = dot_nt(q, keys[h])
        scores = jnp.concatenate([jnp.where(seen, scores[:, :span], MASKED), scores[:, span:] + absent], axis=1)
        top = jnp.max(scores, axis=1, keepdims=True)
        expd.append(jnp.exp(scores - top).astype(BF16))
        mixed.append(dot(expd[h], summing[h]))
    total = jnp.where(low, pltpu.roll(mixed[0], HEAD_DIM, 1), pltpu.roll(mixed[1], HEAD_DIM, 1))
    inverse = 1.0 / total
    out = jnp.where(low, mixed[0], mixed[1]) * inverse
    for p in range(PAIRS):
        out_ref[:, p * 128 : (p + 1) * 128] = out[p * span : (p + 1) * span].astype(BF16)
    product = do32 * out
    do_t = (do32 * inverse).T.astype(BF16)
    q_t = (q.astype(F32) * inverse).T.astype(BF16)
    dq = dk = dv = 0.0
    for h in range(2):
        head = slice(h * HEAD_DIM, (h + 1) * HEAD_DIM)
        delta = jnp.sum(jnp.where(low == (h == 0), product, 0.0), axis=1, keepdims=True)
        dprob = dot_nt(do, values[h])
        dscore = (expd[h].astype(F32) * (dprob - delta)).astype(BF16)
        dq = dq + dot(dscore, keys[h])
        dk = dk + dot(q_t[head], dscore)
        dv = dv + dot(do_t[head], expd[h])
    dq = dq * inverse
    for p in range(PAIRS):
        dq_ref[:, p * 128 : (p + 1) * 128] = dq[p * span : (p + 1) * span].astype(BF16)
    both = jnp.concatenate([dk, dv], axis=0).T.astype(BF16)
    for k in range(depth):
        even_out_ref[k] = both[2 * k * span : (2 * k + 1) * span]
        odd_out_ref[k] = both[(2 * k + 1) * span : (2 * k + 2) * span]


def loop_kernel(groups, span, block, count, place_ref, *refs):
    even_ref, odd_ref, q_ref, do_ref, out_ref, dq_ref, even_out_ref, odd_out_ref = refs[:8]
    kv_scr, e_ref, kv_t_ref, max_ref, acc_ref, ext_ref = refs[8:]
    depth = count // 2
    rows = groups * span
    per = block // span
    y, z = place_ref[2], place_ref[3]
    used = (2 * (z + 1) + per - 1) // per
    group, group_count = pl.program_id(1), pl.num_programs(1)
    low = lax.broadcasted_iota(jnp.int32, (1, 128), 1) < HEAD_DIM
    lanes = lax.broadcasted_iota(jnp.int32, (rows, 128), 1)

    def stacked(ref):
        return jnp.concatenate([ref[:, p * 128 : (p + 1) * 128] for p in range(groups)], axis=0)

    @pl.when(group == 0)
    def _():
        for i in range(count):
            kv_scr[i * span : (i + 1) * span] = (odd_ref if i % 2 else even_ref)[i // 2]

    q = stacked(q_ref)
    do = stacked(do_ref)

    def load(b):
        kv = kv_scr[pl.ds(pl.multiple_of(b * block, block), block)]
        swapped = pltpu.roll(kv.astype(F32), HEAD_DIM, 1).astype(BF16)
        return kv, swapped, jnp.zeros_like(kv)

    def absent(b):
        row = lax.broadcasted_iota(jnp.int32, (block, 128), 0) + b * block
        lane = lax.broadcasted_iota(jnp.int32, (block, 128), 1)
        mask = jnp.where(present(row // span, y, z), 0.0, MASKED)
        return jnp.where(lane < 2, -1.0, jnp.where(lane == 2, mask, 0.0)).astype(BF16)

    def key_tiles(b):
        kv, swapped, zero = load(b)
        ext = absent(b)
        return [
            jnp.concatenate([jnp.where(low, kv, zero), ext], axis=1),
            jnp.concatenate([jnp.where(low, zero, swapped), ext], axis=1),
        ]

    def value_tiles(b):
        kv, swapped, zero = load(b)
        ext = absent(b)
        return [
            jnp.concatenate([jnp.where(low, swapped, zero), ext], axis=1),
            jnp.concatenate([jnp.where(low, zero, kv), ext], axis=1),
        ]

    def seen():
        token = lax.broadcasted_iota(jnp.int32, (rows, block), 0) % span
        key = lax.broadcasted_iota(jnp.int32, (rows, block), 1)
        return (key <= token) | (key >= span)

    def extended(values):
        high = values.astype(BF16).astype(F32)
        rest = jnp.where(lanes == 1, values - high, jnp.where(lanes == 2, 1.0, 0.0))
        return jnp.where(lanes == 0, high, rest).astype(BF16)

    def over_blocks(step):
        step(0, True)

        def body(b, carry):
            step(b, False)
            return carry

        lax.fori_loop(1, used, body, 0)

    plain = jnp.concatenate([q, jnp.where(lanes == 2, 1.0, 0.0).astype(BF16)], axis=1)

    def maxima(b, diagonal):
        keys = key_tiles(b)
        for h in range(2):
            scores = dot_nt(plain, keys[h])
            if diagonal:
                scores = jnp.where(seen(), scores, MASKED)
            top = functools.reduce(jnp.maximum, [scores[:, i : i + 128] for i in range(0, block, 128)])
            max_ref[h] = top if diagonal else jnp.maximum(max_ref[h], top)

    over_blocks(maxima)
    for h in range(2):
        top = jnp.max(max_ref[h], axis=1, keepdims=True)
        ext_ref[h] = jnp.concatenate([q, extended(jnp.broadcast_to(top, (rows, 128)))], axis=1)

    def forward(b, diagonal):
        keys = key_tiles(b)
        kv, swapped, _ = load(b)
        one = jnp.ones_like(kv)
        values = (jnp.where(low, swapped, one), jnp.where(low, one, kv))
        for h in range(2):
            expd = jnp.exp(dot_nt(ext_ref[h], keys[h]))
            if diagonal:
                expd = jnp.where(seen(), expd, 0.0)
            expd = expd.astype(BF16)
            e_ref[b, h] = expd
            mixed = dot(expd, values[h])
            acc_ref[h] = mixed if diagonal else acc_ref[h] + mixed

    over_blocks(forward)
    first, second = acc_ref[0], acc_ref[1]
    total = jnp.where(low, pltpu.roll(first, HEAD_DIM, 1), pltpu.roll(second, HEAD_DIM, 1))
    inverse = 1.0 / total
    out = jnp.where(low, first, second) * inverse
    for p in range(groups):
        out_ref[:, p * 128 : (p + 1) * 128] = out[p * span : (p + 1) * span].astype(BF16)
    do32 = do.astype(F32)
    product = do32 * out
    high = product.astype(BF16)
    rest = (product - high.astype(F32)).astype(BF16)
    place = lax.broadcasted_iota(jnp.int32, (128, 128), 0)
    for h in range(2):
        ones = jnp.where((place < HEAD_DIM) == (h == 0), 1.0, 0.0).astype(BF16)
        delta = dot(high, ones) + dot(rest, ones)
        ext_ref[h] = jnp.concatenate([do, extended(delta)], axis=1)
    do_t = (do32 * inverse).T.astype(BF16)
    q_t = (q.astype(F32) * inverse).T.astype(BF16)

    def backward(b, start):
        values = value_tiles(b)
        kv, swapped, zero = load(b)
        keys = (jnp.where(low, kv, zero), jnp.where(low, zero, swapped))
        dq = dk = dv = 0.0
        for h in range(2):
            expd = e_ref[b, h]
            head = slice(h * HEAD_DIM, (h + 1) * HEAD_DIM)
            dscore = (expd.astype(F32) * dot_nt(ext_ref[h], values[h])).astype(BF16)
            dq = dq + dot(dscore, keys[h])
            dk = dk + dot(q_t[head], dscore)
            dv = dv + dot(do_t[head], expd)
        acc_ref[0] = dq if start else acc_ref[0] + dq
        both = jnp.concatenate([dk, dv], axis=0)
        kv_t_ref[b] = jnp.where(group == 0, both, kv_t_ref[b] + both)

    over_blocks(backward)
    dq = acc_ref[0] * inverse
    for p in range(groups):
        dq_ref[:, p * 128 : (p + 1) * 128] = dq[p * span : (p + 1) * span].astype(BF16)

    @pl.when(group == group_count - 1)
    def _():
        for b in range(count // per):
            used_block = jnp.where(b < used, kv_t_ref[b], 0.0).T.astype(BF16)
            for i in range(per):
                slot = b * per + i
                result = odd_out_ref if slot % 2 else even_out_ref
                result[slot // 2] = used_block[i * span : (i + 1) * span]


def attention(place, evens, odds, q, do):
    depth = evens.shape[0]
    count = 2 * depth
    seqs, span, _ = q.shape
    single = count * span <= 1024
    groups = PAIRS if single else 2
    wide_spec = pl.BlockSpec((None, span, groups * 128), lambda s, i: (s, 0, i))
    pieces = pl.BlockSpec((depth, None, span, 128), lambda s, i: (0, s, 0, 0))
    if single:
        kernel, scratch = functools.partial(whole_kernel, span, depth), []
    else:
        block = max(512, span)
        blocks = count * span // block
        rows = groups * span
        kernel = functools.partial(loop_kernel, groups, span, block, count)
        scratch = [
            pltpu.VMEM((count * span, 128), BF16),
            pltpu.VMEM((blocks, 2, rows, block), BF16),
            pltpu.VMEM((blocks, 128, block), F32),
            pltpu.VMEM((2, rows, 128), F32),
            pltpu.VMEM((2, rows, 128), F32),
            pltpu.VMEM((2, rows, 256), BF16),
        ]
    return pl.pallas_call(
        kernel,
        grid=(seqs, PAIRS // groups),
        in_specs=[SMEM, pieces, pieces, wide_spec, wide_spec],
        out_specs=[wide_spec] * 2 + [pieces] * 2,
        out_shape=[SHAPE((seqs, span, D), BF16), SHAPE((seqs, span, D), BF16)]
        + [SHAPE((depth, seqs, span, 128), BF16)] * 2,
        scratch_shapes=scratch,
        compiler_params=params(),
        cost_estimate=cost(10),
        name="attention",
    )(place, evens, odds, q, do)


def weights_kernel(
    copies, place_ref, dq_ref, attn_ref, g_ref, x_ref, gain_ref, bias_ref, tables_ref, send_ref, keep_ref, grad_ref, small_ref
):
    half = D // 2
    own = place_ref[0] == 0

    def products(left, right):
        lower, upper = right[:, :half], right[:, half:]
        send_ref[0] = dot(left, jnp.where(own, upper, lower)).astype(BF16)
        keep_ref[0] = dot(left, jnp.where(own, lower, upper)).astype(BF16)

    @pl.when(pl.program_id(0) == 0)
    def _():
        g = g_ref[...]
        small_ref[1:2] = jnp.sum(g.astype(F32), axis=0, keepdims=True)
        products(attn_ref[...].astype(F32).T.astype(BF16), g)

    @pl.when(pl.program_id(0) == 1)
    def _():
        tables = repeated(tables_ref, copies)
        for p in range(PAIRS):
            columns = slice(p * 128, (p + 1) * 128)
            grad_ref[:, columns] = turn(dq_ref[:, columns].astype(F32) * SCALE, tables, -1).astype(BF16)
        grad = grad_ref[...]
        small_ref[0:1] = jnp.sum(grad.astype(F32), axis=0, keepdims=True)
        normed, _ = normalize(x_ref[...].astype(F32))
        first_in = normed * wide(gain_ref) + wide(bias_ref)
        products(first_in.T.astype(BF16), grad)


def weights(place, dq, attn, g, x, gain, bias, tables):
    rows = x.shape[0]
    whole = lambda a: pl.BlockSpec(a.shape, lambda i: (0,) * a.ndim)
    fixed = lambda *shape: pl.BlockSpec(shape, lambda i: (0, 0))
    part = pl.BlockSpec((1, D, D // 2), lambda i: (i, 0, 0))
    arrays = (dq, attn, g, x, gain, bias, tables)
    return pl.pallas_call(
        functools.partial(weights_kernel, rows // tables.shape[1]),
        grid=(2,),
        in_specs=[SMEM] + [whole(a) for a in arrays],
        out_specs=[part, part, fixed(rows, D), fixed(8, D)],
        out_shape=[
            SHAPE((2, D, D // 2), BF16),
            SHAPE((2, D, D // 2), BF16),
            SHAPE((rows, D), BF16),
            SHAPE((8, D), F32),
        ],
        compiler_params=params(),
        cost_estimate=cost(2.4),
        name="weights",
    )(place, *arrays)


def mix_kernel(x_ref, mlp_ref, mlp2_ref, attn_ref, grad_ref, add_ref, wo_ref, wq_ref, output_ref, first_ref):
    first_ref[...] = dot_nt(grad_ref[...], wq_ref[...]).astype(BF16)
    mlp = mlp_ref[...].astype(F32) + mlp2_ref[...].astype(F32)
    x = x_ref[...].astype(F32)
    output_ref[...] = (x + (mlp + dot(attn_ref[...], wo_ref[...])) + wide(add_ref)).astype(BF16)


def mix(x, mlp, mlp2, attn, grad, add, wo, wqkv):
    rows = x.shape[0]
    row = pl.BlockSpec((rows // 2, D), lambda i: (i, 0))
    square = pl.BlockSpec((D, D), lambda i: (0, 0))
    return pl.pallas_call(
        mix_kernel,
        grid=(2,),
        in_specs=[row] * 5 + [pl.BlockSpec((D,), lambda i: (0,)), square, square],
        out_specs=[row] * 2,
        out_shape=[SHAPE((rows, D), BF16)] * 2,
        compiler_params=params(),
        cost_estimate=cost(2.4),
        name="mix",
    )(x, mlp, mlp2, attn, grad, add, wo, wqkv)


def two_terms(values):
    high = values.astype(BF16)
    return high, (values - high.astype(F32)).astype(BF16)


def message_lines(ff):
    return -(-(ff // 128 + 6 * (D // 128) + 1) // 16) * 16


def finish_kernel(
    copies,
    count,
    lines,
    place_ref,
    *refs,
):
    kv_refs, refs = refs[:count], refs[count:]
    (
        extra_ref,
        x_ref,
        g_ref,
        first_ref,
        back_ref,
        back2_ref,
        gain_ref,
        bias_ref,
        gain2_ref,
        wkv_ref,
        tables_ref,
        b1_ref,
        early_ref,
        tokens_ref,
        message_ref,
        vector_scr,
    ) = refs
    total = extra_ref[...].astype(F32)
    for ref in kv_refs:
        total += ref[...].astype(F32)
    tables = repeated(tables_ref, copies)
    grad = turn(total, key_tables(tables), -1).astype(BF16)
    x = x_ref[...].astype(F32)
    normed, inverse = normalize(x)
    gain = wide(gain_ref)
    first_in = normed * gain + wide(bias_ref)
    first_grad = first_ref[...].astype(F32) + dot_nt(grad, wkv_ref[...])
    second_grad = back_ref[...].astype(F32) + back2_ref[...].astype(F32)

    vector_scr[...] = jnp.zeros_like(vector_scr)
    b1 = b1_ref[...]
    b1_lines = b1.shape[1] // 128
    for i in range(b1_lines):
        vector_scr[pl.ds(place_ref[0] * b1_lines + i, 1)] = b1[:, i * 128 : (i + 1) * 128]
    at = 2 * b1_lines
    sums = [early_ref[0:1], early_ref[1:2]]
    for rows in (first_grad * normed, first_grad, second_grad * normed, second_grad):
        sums.append(jnp.sum(rows, axis=0, keepdims=True))
    sums.append(jnp.sum(grad.astype(F32), axis=0, keepdims=True))
    for row in sums:
        for i in range(row.shape[1] // 128):
            vector_scr[at : at + 1] = row[:, i * 128 : (i + 1) * 128]
            at += 1
    high, rest = two_terms(vector_scr[...])
    weight = dot(first_in.T.astype(BF16), grad).astype(BF16)
    places = message_ref.shape[0]
    per = weight.shape[0] // places
    for i in range(places):
        message_ref[i, :lines] = high
        message_ref[i, lines : 2 * lines] = rest
        message_ref[i, 2 * lines :] = weight[i * per : (i + 1) * per]

    normed_grad = first_grad * gain + second_grad * wide(gain2_ref)
    mean = jnp.mean(normed_grad, axis=-1, keepdims=True)
    along_rows = jnp.mean(normed_grad * normed, axis=-1, keepdims=True)
    tokens_ref[...] = (g_ref[...].astype(F32) + inverse * (normed_grad - mean - normed * along_rows)).astype(BF16)


def finish(place, places, ff, kv_parts, extra, x, g, first, back, back2, gain, bias, gain2, wqkv, tables, b1, early):
    rows = x.shape[0]
    lines = message_lines(ff)
    whole = lambda a: pl.BlockSpec(a.shape, lambda i: (0,) * a.ndim)
    before = (*kv_parts, extra, x, g, first, back, back2, gain, bias, gain2)
    after_it = (tables, b1, early)
    return pl.pallas_call(
        functools.partial(finish_kernel, rows // tables.shape[1], len(kv_parts), lines),
        grid=(1,),
        in_specs=[SMEM]
        + [whole(a) for a in before]
        + [pl.BlockSpec((D, 128), lambda i: (0, D // 128))]
        + [whole(a) for a in after_it],
        out_specs=[
            pl.BlockSpec((rows, D), lambda i: (0, 0)),
            pl.BlockSpec((places, 2 * lines + D // places, 128), lambda i: (0, 0, 0)),
        ],
        out_shape=[SHAPE((rows, D), BF16), SHAPE((places, 2 * lines + D // places, 128), BF16)],
        scratch_shapes=[pltpu.VMEM((lines, 128), F32)],
        compiler_params=params(),
        cost_estimate=cost(2.4),
        name="finish",
    )(place, *before, wqkv, *after_it)


def gather_sums(messages, lines):
    rows = messages.shape[1]

    def kernel(refs, result):
        total = tree_sum([refs[i] for i in range(messages.shape[0])])
        high, rest = two_terms(total[:lines] + total[lines : 2 * lines])
        result[:lines] = high
        result[lines : 2 * lines] = rest
        result[2 * lines :] = total[2 * lines :].astype(BF16)

    return pl.pallas_call(
        kernel,
        in_specs=[VMEM],
        out_specs=VMEM,
        out_shape=SHAPE((rows, 128), BF16),
        compiler_params=params(),
        cost_estimate=cost(0.6),
        name="gather_sums",
    )(messages)


def last_sums(messages, lines, widths):
    rows = messages[0].shape[0] - 2 * lines

    def kernel(*refs):
        sources, results = refs[: len(messages)], refs[len(messages) :]
        total = tree_sum([ref[...] for ref in sources])
        vector = total[:lines] + total[lines : 2 * lines]
        at = 0
        for result, width in zip(results[:-1], widths):
            for i in range(width // 128):
                result[i * 128 : (i + 1) * 128] = vector[at + i]
            at += width // 128
        results[-1][...] = total[2 * lines :]

    return pl.pallas_call(
        kernel,
        in_specs=[VMEM] * len(messages),
        out_specs=[VMEM] * (len(widths) + 1),
        out_shape=[SHAPE((width,), F32) for width in widths] + [SHAPE((rows, 128), F32)],
        compiler_params=params(),
        cost_estimate=cost(0.6),
        name="last_sums",
    )(*messages)


def local(
    tokens,
    ln1_gain,
    ln1_bias,
    qkv_weight,
    qkv_bias,
    out_weight,
    ln2_gain,
    ln2_bias,
    fc1_weight,
    fc1_bias,
    fc2_weight,
    out_bias,
    output_grad,
    key_value_grad,
):
    seqs, span, _ = tokens.shape
    rows = seqs * span
    ff = fc1_weight.shape[1]
    count = lax.axis_size("seq")
    batches = lax.axis_size("batch")
    depth = count // 2
    half_depth = depth // 2
    per1, per2 = D // count, ff // count
    own = lax.axis_index("seq").astype(jnp.int32)
    batch = lax.axis_index("batch").astype(jnp.int32)
    y, z = own & 1, own >> 1
    core, xs = batch & 1, batch >> 1
    place = jnp.stack([core, xs, y, z])
    x = tokens.reshape(rows, D)
    g = output_grad.reshape(rows, D)
    over_core = lambda v: flipped(v, "batch", 1)
    over_x = lambda v: flipped(v, "batch", 2)
    over_y = lambda v: flipped(v, "seq", 1)
    over_z = lambda v, bit: flipped(v, "seq", 2 << bit)
    z_bits = depth.bit_length() - 1
    flat = lambda v: v.reshape(rows, -1)

    def pair(mine, other, index, axis):
        first = jnp.where(index == 0, mine, other)
        second = jnp.where(index == 0, other, mine)
        return jnp.concatenate([first, second], axis=axis)

    def summed(*parts):
        return tree_sum(parts).astype(BF16)

    x_other, g_other = over_core(x), over_core(g)
    tables = rotary_tables(own * span, span)
    q, kv = project(x, ln1_gain, ln1_bias, qkv_weight, qkv_bias, tables)
    kv3 = kv.reshape(seqs, span, 128)
    evens = [kv3] + [along(kv3, k) for k in range(1, depth)]

    x_fed, g_fed = after((x, g), kv)
    (mlp, mlp_other, slope, in_t), grads2 = feed_forward(
        place, depth, x_fed, x_other, g_fed, g_other, ln2_gain, ln2_bias, fc1_weight, fc1_bias.reshape(1, -1), fc2_weight
    )
    theirs2, mine2 = grads2
    come2 = over_z(theirs2, 0)
    mlp_come = over_core(mlp_other)
    evens = [kv3] + list(after(evens[1:], slope))
    evens = jnp.stack(evens)
    odds = over_y(evens)
    back, back_other, attn_grad, theirs1, mine1, b1_grad = feed_backward(
        place, count, g, g_other, slope, in_t, fc1_weight, fc2_weight, out_weight
    )
    come1 = over_x(theirs1)
    back_come = over_core(back_other)

    q3, do3 = q.reshape(seqs, span, D), attn_grad.reshape(seqs, span, D)
    out, dq, even, odd = attention(place, evens, odds, q3, do3)
    odd = over_y(odd)

    def halved(a, parts, height):
        return a.reshape(parts, 2, height, a.shape[-1])

    g_weights, x_weights, come1, mlp_come, back_come = after((g, x, come1, mlp_come, back_come), out)
    send, keep, q_rows, early = weights(place, flat(dq), flat(out), g_weights, x_weights, ln1_gain, ln1_bias, tables)
    come3 = over_core(send)

    mine2, come2 = after((mine2, come2), send)
    height = per2 // 2
    view = lambda v: halved(v, half_depth, height)
    theirs2, mine2 = add_split(place, [(view(mine2), view(come2), 1)])
    come2 = over_x(theirs2)

    even, odd = after((even, odd), theirs2)
    kv_sums = [summed(even[k], odd[k]) for k in range(depth)]
    got = [along(kv_sums[k], -k) for k in range(1, depth)]

    mine1, come1 = after((mine1, come1), *kv_sums)
    view = lambda v: halved(v, depth, per1 // 2)
    theirs1, mine1 = add_split(place, [(view(mine1), view(come1), 2)])
    come1 = over_y(theirs1)

    x_mix, mlp_come = after((x, mlp_come), theirs1)
    output, first = mix(x_mix, mlp, mlp_come, flat(out), q_rows, out_bias, out_weight, qkv_weight)

    keep, come3 = after((keep, come3), first)
    view = lambda v: halved(v, 2 * depth, per1)
    theirs3, mine3 = add_split(place, [(view(keep), view(come3), 2)])
    come3 = over_y(theirs3)

    mine2, come2 = after((mine2, come2), theirs3)
    view = lambda v: halved(v, half_depth // 2, height)
    theirs2, mine2 = add_split(place, [(view(mine2), view(come2), 2)])
    come2 = over_y(theirs2)

    got = after(got, theirs2)
    lines = message_lines(ff)
    tokens_grad, messages = finish(
        place, count, ff, [flat(v) for v in (kv_sums[0], *got)], flat(key_value_grad), x, g, first, back, back_come,
        ln1_gain, ln1_bias, ln2_gain, qkv_weight, tables, b1_grad, early,
    )
    messages = lax.all_to_all(messages, "seq", 0, 0, tiled=True)

    mine3, come3 = after((mine3, come3), tokens_grad)
    view = lambda v: halved(v, depth, per1)
    theirs3, mine3 = add_split(place, [(view(mine3), view(come3), 3)])
    come3 = over_z(theirs3, 0)
    mine1, come1 = after((mine1, come1), theirs3)
    view = lambda v: halved(v, depth // 2, per1 // 2)
    theirs1, mine1 = add_split(place, [(view(mine1), view(come1), 3)])
    come1 = over_z(theirs1, 0)
    mine2, come2 = after((mine2, come2), theirs1)
    for bit in range(1, z_bits - 1):
        view = lambda v: halved(v, half_depth >> (bit + 1), height)
        theirs2, mine2 = add_split(place, [(view(mine2), view(come2), 3 + bit)])
        come2 = over_z(theirs2, bit)
    sum2 = summed(mine2, come2).reshape(height, D)
    come2 = to_owner(sum2)

    (messages,) = after((messages,), sum2)
    message = gather_sums(messages, lines)
    got = [flipped(message, "batch", i) for i in range(1, batches)]

    mine3, come3 = after((mine3, come3), message)
    for bit in range(1, z_bits):
        view = lambda v: halved(v, 2 * (depth >> (bit + 1)), per1)
        theirs3, mine3 = add_split(place, [(view(mine3), view(come3), 3 + bit)])
        come3 = over_z(theirs3, bit)
    mine1, come1 = after((mine1, come1), theirs3)
    for bit in range(1, z_bits):
        view = lambda v: halved(v, depth >> (bit + 1), per1 // 2)
        theirs1, mine1 = add_split(place, [(view(mine1), view(come1), 3 + bit)])
        come1 = over_z(theirs1, bit)

    sum2, come2 = after((sum2, come2), theirs1)
    sum2 = summed(sum2, come2)
    other2 = over_x(sum2)
    got = after(got, sum2)
    widths = (ff,) + (D,) * 6 + (128,)
    b1_sum, q_sum, out_sum, gain1, bias1, gain2, bias2, kv_bias, kv_sum = last_sums([message, *got], lines, widths)
    mine3, come3 = after((mine3, come3), kv_sum)
    sum3 = summed(mine3, come3)
    other3 = over_x(sum3)
    mine1, come1 = after((mine1, come1), sum3)
    sum1 = summed(mine1, come1).reshape(per1 // 2, -1)
    other1 = over_x(sum1)

    sum2, other2 = after((sum2, other2), sum1)
    sum2 = pair(sum2, other2, xs, 0)
    other2 = over_core(sum2)
    sum3, other3 = after((sum3, other3), sum2)
    sum3 = summed(sum3, other3)
    other3 = over_core(sum3)
    sum1, other1 = after((sum1, other1), sum3)
    sum1 = pair(sum1, other1, xs, 0)
    other1 = over_core(sum1)

    owner = (z >> (z_bits - 1)) == core
    (other2,) = after((other2,), sum1)
    fc2_grad = jnp.where(owner, sum2, other2).astype(F32)
    (other3,) = after((other3,), fc2_grad)
    both3 = pair(sum3, other3, core, 2).astype(F32)
    (other1,) = after((other1,), both3)
    fc1_grad = pair(sum1, other1, core, 1).astype(F32)
    return (
        output.reshape(tokens.shape),
        kv3,
        tokens_grad.reshape(tokens.shape),
        gain1,
        bias1,
        jnp.concatenate([both3[1], kv_sum], axis=1),
        jnp.concatenate([q_sum, kv_bias]),
        both3[0],
        gain2,
        bias2,
        fc1_grad,
        b1_sum,
        fc2_grad,
        out_sum,
    )


def solution(mesh):
    part = P("batch", "seq", None)
    whole = P()
    split = P("seq", None)
    return jax.shard_map(
        local,
        mesh=mesh,
        in_specs=(part,) + (whole,) * 11 + (part, part),
        out_specs=(
            part, part, part, whole, whole, split, whole, split, whole, whole, split, whole, split, whole,
        ),
        check_vma=False,
    )
```

```python
import functools
import math

import jax
import jax.numpy as jnp
from jax import lax
from jax.experimental import pallas as pl
from jax.experimental.pallas import tpu as pltpu
from jax.sharding import PartitionSpec as P

D = 768
HEADS = 12
HEAD_DIM = 64
ROT = 16
PAIRS = HEADS // 2
SCALE = 1.0 / math.sqrt(HEAD_DIM)
NORM_EPS = 1e-05
MASKED = -1e30
F32 = jnp.float32
BF16 = jnp.bfloat16
VMEM_BYTES = 56 * 1024 * 1024


def dot(a, b):
    return lax.dot_general(a, b, (((1,), (0,)), ((), ())), preferred_element_type=F32)


def dot_nt(a, b):
    return lax.dot_general(a, b, (((1,), (1,)), ((), ())), preferred_element_type=F32)


def dot_tn(a, b):
    return lax.dot_general(a, b, (((0,), (0,)), ((), ())), preferred_element_type=F32)


def params():
    return pltpu.CompilerParams(vmem_limit_bytes=VMEM_BYTES)


def flipped(block, axis, bits):
    return lax.ppermute(block, axis, [(i, i ^ bits) for i in range(lax.axis_size(axis))])


def along(block, distance):
    size = lax.axis_size("seq")
    return lax.ppermute(block, "seq", [(i, (i + 2 * distance) % size) for i in range(size)])


def to_owner(block):
    size = lax.axis_size("seq")
    route = []
    for b in range(lax.axis_size("batch")):
        for i in range(size):
            j = i ^ (size // 2)
            if j // (size // 2) == b % 2:
                route.append((b * size + i, b * size + j))
    return lax.ppermute(block, ("batch", "seq"), route)


def after(values, *others):
    return lax.optimization_barrier((tuple(values), others))[0]


def tree_sum(parts):
    parts = [p.astype(F32) for p in parts]
    while len(parts) > 1:
        parts = [sum(parts[i : i + 2][1:], parts[i]) for i in range(0, len(parts), 2)]
    return parts[0]


def take(block, index, axis):
    return lax.dynamic_index_in_dim(block, index, axis, keepdims=False)


def normalize(rows):
    centre = jnp.mean(rows, axis=-1, keepdims=True)
    centred = rows - centre
    spread = jnp.mean(centred * centred, axis=-1, keepdims=True)
    inverse = lax.rsqrt(spread + NORM_EPS)
    return centred * inverse, inverse


def rotary_tables(first, count):
    lane = jnp.arange(128) % HEAD_DIM
    half = ROT // 2
    freqs = 10000.0 ** (-(lane % half).astype(F32) / half)
    places = (first + jnp.arange(count)).astype(F32) * 0.25
    angles = places[:, None] * freqs[None, :]
    cosine, sine = jnp.cos(angles), jnp.sin(angles)
    return jnp.stack(
        [
            jnp.where(lane < ROT, cosine, 1.0),
            jnp.where((lane >= half) & (lane < ROT), sine, 0.0),
            jnp.where(lane < half, -sine, 0.0),
        ]
    )


def turn(values, tables, sign):
    moved = pltpu.roll(values, ROT // 2, 1) * tables[1] + pltpu.roll(values, 128 - ROT // 2, 1) * tables[2]
    return values * tables[0] + (moved if sign > 0 else -moved)


def repeated(tables_ref, count):
    return [jnp.concatenate([tables_ref[i]] * count, axis=0) for i in range(3)]


def key_tables(tables):
    low = lax.broadcasted_iota(jnp.int32, (1, 128), 1) < HEAD_DIM
    return [jnp.where(low, tables[0], 1.0), jnp.where(low, tables[1], 0.0), jnp.where(low, tables[2], 0.0)]

VMEM = pl.BlockSpec(memory_space=pltpu.VMEM)
SMEM = pl.BlockSpec(memory_space=pltpu.SMEM)
SHAPE = jax.ShapeDtypeStruct


def cost(share):
    return pl.CostEstimate(flops=int(share * 3e9), bytes_accessed=0, transcendentals=0)


def wide(ref):
    return ref[...].reshape(1, -1)


def add_split(place, items):
    def kernel(place_ref, *refs):
        sources, results = refs[: 2 * len(items)], refs[2 * len(items) :]
        for n, (_, _, which) in enumerate(items):
            a, b = sources[2 * n], sources[2 * n + 1]
            own = place_ref[which] if which < 3 else lax.rem(lax.shift_right_logical(place_ref[3], which - 3), 2)
            for m in range(a.shape[0]):
                for result, at in ((results[2 * n], 1 - own), (results[2 * n + 1], own)):
                    result[m] = (a[m, at].astype(F32) + b[m, at].astype(F32)).astype(BF16)

    shapes = []
    for a, _, _ in items:
        shapes += [SHAPE((a.shape[0],) + a.shape[2:], BF16)] * 2
    arrays = [v for item in items for v in item[:2]]
    return pl.pallas_call(
        kernel,
        in_specs=[SMEM] + [VMEM] * len(arrays),
        out_specs=[VMEM] * len(shapes),
        out_shape=shapes,
        compiler_params=params(),
        cost_estimate=cost(1.2),
        name="add_split",
    )(place, *arrays)


def keys_kernel(copies, x_ref, gain_ref, bias_ref, weight_ref, add_ref, tables_ref, kv_ref, first_ref):
    normed, _ = normalize(x_ref[...].astype(F32))
    first_in = (normed * wide(gain_ref) + wide(bias_ref)).astype(BF16)
    first_ref[...] = first_in
    part = dot(first_in, weight_ref[...]) + wide(add_ref)[:, D:]
    kv_ref[...] = turn(part, key_tables(repeated(tables_ref, copies)), 1).astype(BF16)


def queries_kernel(copies, first_ref, weight_ref, add_ref, tables_ref, q_ref):
    first_in = first_ref[...]
    tables = repeated(tables_ref, copies)
    bias = wide(add_ref)
    for p in range(PAIRS):
        columns = slice(p * 128, (p + 1) * 128)
        part = dot(first_in, weight_ref[:, columns]) + bias[:, columns]
        q_ref[:, columns] = (turn(part, tables, 1) * SCALE).astype(BF16)


def project_keys(x, gain, bias, weight, add, tables):
    rows = x.shape[0]
    whole = lambda a: pl.BlockSpec(a.shape, lambda i: (0,) * a.ndim)
    return pl.pallas_call(
        functools.partial(keys_kernel, rows // tables.shape[1]),
        grid=(1,),
        in_specs=[
            whole(x),
            whole(gain),
            whole(bias),
            pl.BlockSpec((D, 128), lambda i: (0, D // 128)),
            whole(add),
            whole(tables),
        ],
        out_specs=[pl.BlockSpec((rows, 128), lambda i: (0, 0)), pl.BlockSpec((rows, D), lambda i: (0, 0))],
        out_shape=[SHAPE((rows, 128), BF16), SHAPE((rows, D), BF16)],
        compiler_params=params(),
        cost_estimate=cost(1),
        name="project_keys",
    )(x, gain, bias, weight, add, tables)


def project_queries(first_in, weight, add, tables):
    rows = first_in.shape[0]
    whole = lambda a: pl.BlockSpec(a.shape, lambda i: (0,) * a.ndim)
    return pl.pallas_call(
        functools.partial(queries_kernel, rows // tables.shape[1]),
        grid=(1,),
        in_specs=[
            whole(first_in),
            pl.BlockSpec((D, D), lambda i: (0, 0)),
            whole(add),
            whole(tables),
        ],
        out_specs=pl.BlockSpec((rows, D), lambda i: (0, 0)),
        out_shape=SHAPE((rows, D), BF16),
        compiler_params=params(),
        cost_estimate=cost(2),
        name="project_queries",
    )(first_in, weight, add, tables)


def gelu_parts(h):
    t = pl.reciprocal(1.0 + (0.3275911 / math.sqrt(2.0)) * jnp.abs(h))
    e = jnp.exp(-0.5 * h * h)
    poly = 0.5 * 1.061405429
    for coefficient in (-1.453152027, 1.421413741, -0.284496736, 0.254829592):
        poly = poly * t + 0.5 * coefficient
    tail = poly * t * e
    cdf = jnp.where(h >= 0.0, 1.0 - tail, tail)
    return h * cdf, cdf + h * e * (1.0 / math.sqrt(2.0 * math.pi))


def feed_kernel(
    place_ref,
    x_ref,
    xx_ref,
    g_ref,
    gg_ref,
    gain_ref,
    bias_ref,
    w1_ref,
    b1_ref,
    w2_ref,
    wo_ref,
    mlp_ref,
    mlp2_ref,
    back_ref,
    back2_ref,
    attn_grad_ref,
    b1_grad_ref,
    theirs1_ref,
    mine1_ref,
    *refs,
):
    grad_refs, (in_scr, in_t_scr, g_scr, mlp_scr, back_scr) = refs[:-5], refs[-5:]
    step, steps = pl.program_id(0), pl.num_programs(0)
    rows = x_ref.shape[0]

    @pl.when(step == 0)
    def _():
        for i, (tokens, grads) in enumerate(((x_ref, g_ref), (xx_ref, gg_ref))):
            at = slice(i * rows, (i + 1) * rows)
            normed, _ = normalize(tokens[...].astype(F32))
            second_in = normed * wide(gain_ref) + wide(bias_ref)
            in_scr[at] = second_in.astype(BF16)
            in_t_scr[:, :, :, at] = second_in.T.astype(BF16).reshape(in_t_scr.shape[:3] + (rows,))
            g_scr[at] = grads[...]
        attn_grad_ref[...] = dot_nt(g_ref[...], wo_ref[...]).astype(BF16)

    g = g_scr[...]
    w1 = w1_ref[...]
    w2 = w2_ref[...]
    act, slope = gelu_parts(dot(in_scr[...], w1) + b1_ref[...])
    act = act.astype(BF16)
    pre = dot_nt(g, w2) * slope
    pre16 = pre.astype(BF16)
    b1_grad_ref[...] = jnp.sum(pre, axis=0, keepdims=True)
    mlp = dot(act, w2)
    grad = dot_tn(act, g).astype(BF16)
    if len(grad_refs) == 1:
        grad_refs[0][...] = grad
    for i in range(len(grad_refs) if len(grad_refs) > 1 else 0):

        @pl.when(step == i)
        def _(i=i):
            grad_refs[i][...] = grad

    back = dot_nt(pre16, w1)
    own = place_ref[1]
    for result, at in ((theirs1_ref, 1 - own), (mine1_ref, own)):
        left = in_t_scr[:, pl.ds(at, 1)].reshape(D // 2, 2 * rows)
        result[...] = dot(left, pre16).astype(BF16).reshape(result.shape)

    @pl.when(step == 0)
    def _():
        mlp_scr[...] = mlp
        back_scr[...] = back

    @pl.when((step > 0) & (step < steps - 1))
    def _():
        mlp_scr[...] += mlp
        back_scr[...] += back

    @pl.when(step == steps - 1)
    def _():
        for scr, last, own_ref, other_ref in ((mlp_scr, mlp, mlp_ref, mlp2_ref), (back_scr, back, back_ref, back2_ref)):
            total = (scr[...] + last).astype(BF16)
            own_ref[...] = total[:rows]
            other_ref[...] = total[rows:]


CHUNK = 512


def feed(place, count, x, xx, g, gg, gain, bias, w1, b1, w2, wo):
    rows = x.shape[0]
    half = w1.shape[1] // 2
    depth = count // 2
    per = D // count // 2
    pieces = depth // 2
    aligned = pieces == 2 and half % 512 == 0
    chunk = half // pieces if aligned else CHUNK
    steps = half // chunk
    single = pl.Buffered(1)
    whole = lambda a: pl.BlockSpec(a.shape, lambda i, place: (0,) * a.ndim, pipeline_mode=single)
    fixed = lambda *shape: pl.BlockSpec(shape, lambda i, place: (0, 0))
    if aligned:
        piece = lambda i, place: (place[3] ^ (1 - i)) & 1
        grad_specs = [fixed(chunk, D)] * pieces
        grad_shapes = [SHAPE((chunk, D), BF16)] * pieces
    else:
        piece = lambda i, place: i
        grad_specs = [pl.BlockSpec((chunk, D), lambda i, place: (i, 0))]
        grad_shapes = [SHAPE((half, D), BF16)]
    at = lambda i, place: place[0] * steps + piece(i, place)
    cut = pl.BlockSpec((count, per, chunk), lambda i, place: (0, 0, piece(i, place)))
    spec = pltpu.PrefetchScalarGridSpec(
        num_scalar_prefetch=1,
        grid=(steps,),
        in_specs=[
            whole(x),
            whole(xx),
            whole(g),
            whole(gg),
            whole(gain),
            whole(bias),
            pl.BlockSpec((D, chunk), lambda i, place: (0, at(i, place))),
            pl.BlockSpec((1, chunk), lambda i, place: (0, at(i, place))),
            pl.BlockSpec((chunk, D), lambda i, place: (at(i, place), 0)),
            whole(wo),
        ],
        out_specs=[fixed(rows, D)] * 5
        + [pl.BlockSpec((1, chunk), lambda i, place: (0, piece(i, place))), cut, cut]
        + grad_specs,
        scratch_shapes=[
            pltpu.VMEM((2 * rows, D), BF16),
            pltpu.VMEM((count, 2, per, 2 * rows), BF16),
            pltpu.VMEM((2 * rows, D), BF16),
            pltpu.VMEM((2 * rows, D), F32),
            pltpu.VMEM((2 * rows, D), F32),
        ],
    )
    result = pl.pallas_call(
        feed_kernel,
        grid_spec=spec,
        out_shape=[SHAPE((rows, D), BF16)] * 5
        + [SHAPE((1, half), F32), SHAPE((count, per, half), BF16), SHAPE((count, per, half), BF16)]
        + grad_shapes,
        compiler_params=params(),
        cost_estimate=cost(12),
        name="feed_forward",
    )(place, x, xx, g, gg, gain, bias, w1, b1, w2, wo)
    grads = result[8:]
    if not aligned:
        cut = grads[0].reshape(pieces // 2, 2, -1, D)
        low = place[3] & 1
        grads = [take(cut, 1 - low, 1), take(cut, low, 1)]
    return result[:8], grads


def present(slot, y, z):
    back = slot // 2
    return (back <= z) & ((slot % 2 == 0) | (back >= 1) | (y == 1))


def whole_kernel(span, depth, place_ref, *refs):
    pair_refs, (q_ref, do_ref, tables_ref, out_ref, dq_ref, even_out_ref, odd_out_ref) = refs[:depth], refs[depth:]
    y, z = place_ref[2], place_ref[3]
    tables = [tables_ref[i] for i in range(3)]
    rows = PAIRS * span
    low = lax.broadcasted_iota(jnp.int32, (1, 128), 1) < HEAD_DIM

    def stacked(ref):
        return jnp.concatenate([ref[:, p * 128 : (p + 1) * 128] for p in range(PAIRS)], axis=0)

    blocks = [ref[i] for ref in pair_refs for i in range(2)]
    kv = jnp.concatenate(blocks, axis=0)
    swapped = pltpu.roll(kv.astype(F32), HEAD_DIM, 1).astype(BF16)
    zero, one = jnp.zeros_like(kv), jnp.ones_like(kv)
    keys = (jnp.where(low, kv, zero), jnp.where(low, zero, swapped))
    values = (jnp.where(low, swapped, zero), jnp.where(low, zero, kv))
    summing = (jnp.where(low, swapped, one), jnp.where(low, one, kv))
    slot = lax.broadcasted_iota(jnp.int32, (1, (2 * depth - 1) * span), 1) // span + 1
    absent = jnp.where(present(slot, y, z), 0.0, MASKED)
    token = lax.broadcasted_iota(jnp.int32, (rows, span), 0) % span
    seen = lax.broadcasted_iota(jnp.int32, (rows, span), 1) <= token
    q = stacked(q_ref)
    do = stacked(do_ref)
    do32 = do.astype(F32)

    expd, mixed = [], []
    for h in range(2):
        scores = dot_nt(q, keys[h])
        scores = jnp.concatenate([jnp.where(seen, scores[:, :span], MASKED), scores[:, span:] + absent], axis=1)
        top = jnp.max(scores, axis=1, keepdims=True)
        expd.append(jnp.exp(scores - top).astype(BF16))
        mixed.append(dot(expd[h], summing[h]))
    total = jnp.where(low, pltpu.roll(mixed[0], HEAD_DIM, 1), pltpu.roll(mixed[1], HEAD_DIM, 1))
    inverse = 1.0 / total
    out = jnp.where(low, mixed[0], mixed[1]) * inverse
    for p in range(PAIRS):
        out_ref[:, p * 128 : (p + 1) * 128] = out[p * span : (p + 1) * span].astype(BF16)
    product = do32 * out
    do_t = (do32 * inverse).T.astype(BF16)
    q_t = (q.astype(F32) * inverse).T.astype(BF16)
    dq = dk = dv = 0.0
    for h in range(2):
        head = slice(h * HEAD_DIM, (h + 1) * HEAD_DIM)
        delta = jnp.sum(jnp.where(low == (h == 0), product, 0.0), axis=1, keepdims=True)
        dprob = dot_nt(do, values[h])
        dscore = (expd[h].astype(F32) * (dprob - delta)).astype(BF16)
        dq = dq + dot(dscore, keys[h])
        dk = dk + dot(q_t[head], dscore)
        dv = dv + dot(do_t[head], expd[h])
    dq = dq * (inverse * SCALE)
    for p in range(PAIRS):
        dq_ref[:, p * 128 : (p + 1) * 128] = turn(dq[p * span : (p + 1) * span], tables, -1).astype(BF16)
    both = jnp.concatenate([dk, dv], axis=0).T.astype(BF16)
    for k in range(depth):
        even_out_ref[k] = both[2 * k * span : (2 * k + 1) * span]
        odd_out_ref[k] = both[(2 * k + 1) * span : (2 * k + 2) * span]


def loop_kernel(groups, span, block, count, place_ref, *refs):
    depth = count // 2
    pair_refs, refs = refs[:depth], refs[depth:]
    q_ref, do_ref, tables_ref, out_ref, dq_ref, even_out_ref, odd_out_ref = refs[:7]
    kv_scr, e_ref, kv_t_ref, max_ref, acc_ref, ext_ref = refs[7:]
    tables = [tables_ref[i] for i in range(3)]
    rows = groups * span
    per = block // span
    y, z = place_ref[2], place_ref[3]
    used = (2 * (z + 1) + per - 1) // per
    group, group_count = pl.program_id(1), pl.num_programs(1)
    low = lax.broadcasted_iota(jnp.int32, (1, 128), 1) < HEAD_DIM
    lanes = lax.broadcasted_iota(jnp.int32, (rows, 128), 1)

    def stacked(ref):
        return jnp.concatenate([ref[:, p * 128 : (p + 1) * 128] for p in range(groups)], axis=0)

    @pl.when(group == 0)
    def _():
        for i in range(count):
            kv_scr[i * span : (i + 1) * span] = pair_refs[i // 2][i % 2]

    q = stacked(q_ref)
    do = stacked(do_ref)

    def load(b):
        kv = kv_scr[pl.ds(pl.multiple_of(b * block, block), block)]
        swapped = pltpu.roll(kv.astype(F32), HEAD_DIM, 1).astype(BF16)
        return kv, swapped, jnp.zeros_like(kv)

    def absent(b):
        row = lax.broadcasted_iota(jnp.int32, (block, 128), 0) + b * block
        lane = lax.broadcasted_iota(jnp.int32, (block, 128), 1)
        mask = jnp.where(present(row // span, y, z), 0.0, MASKED)
        return jnp.where(lane < 2, -1.0, jnp.where(lane == 2, mask, 0.0)).astype(BF16)

    def key_tiles(b):
        kv, swapped, zero = load(b)
        ext = absent(b)
        return [
            jnp.concatenate([jnp.where(low, kv, zero), ext], axis=1),
            jnp.concatenate([jnp.where(low, zero, swapped), ext], axis=1),
        ]

    def value_tiles(b):
        kv, swapped, zero = load(b)
        ext = absent(b)
        return [
            jnp.concatenate([jnp.where(low, swapped, zero), ext], axis=1),
            jnp.concatenate([jnp.where(low, zero, kv), ext], axis=1),
        ]

    def seen():
        token = lax.broadcasted_iota(jnp.int32, (rows, block), 0) % span
        key = lax.broadcasted_iota(jnp.int32, (rows, block), 1)
        return (key <= token) | (key >= span)

    def extended(values):
        high = values.astype(BF16).astype(F32)
        rest = jnp.where(lanes == 1, values - high, jnp.where(lanes == 2, 1.0, 0.0))
        return jnp.where(lanes == 0, high, rest).astype(BF16)

    def over_blocks(step):
        step(0, True)

        def body(b, carry):
            step(b, False)
            return carry

        lax.fori_loop(1, used, body, 0)

    plain = jnp.concatenate([q, jnp.where(lanes == 2, 1.0, 0.0).astype(BF16)], axis=1)

    def maxima(b, diagonal):
        keys = key_tiles(b)
        for h in range(2):
            scores = dot_nt(plain, keys[h])
            if diagonal:
                scores = jnp.where(seen(), scores, MASKED)
            top = functools.reduce(jnp.maximum, [scores[:, i : i + 128] for i in range(0, block, 128)])
            max_ref[h] = top if diagonal else jnp.maximum(max_ref[h], top)

    over_blocks(maxima)
    for h in range(2):
        top = jnp.max(max_ref[h], axis=1, keepdims=True)
        ext_ref[h] = jnp.concatenate([q, extended(jnp.broadcast_to(top, (rows, 128)))], axis=1)

    def forward(b, diagonal):
        keys = key_tiles(b)
        kv, swapped, _ = load(b)
        one = jnp.ones_like(kv)
        values = (jnp.where(low, swapped, one), jnp.where(low, one, kv))
        for h in range(2):
            expd = jnp.exp(dot_nt(ext_ref[h], keys[h]))
            if diagonal:
                expd = jnp.where(seen(), expd, 0.0)
            expd = expd.astype(BF16)
            e_ref[b, h] = expd
            mixed = dot(expd, values[h])
            acc_ref[h] = mixed if diagonal else acc_ref[h] + mixed

    over_blocks(forward)
    first, second = acc_ref[0], acc_ref[1]
    total = jnp.where(low, pltpu.roll(first, HEAD_DIM, 1), pltpu.roll(second, HEAD_DIM, 1))
    inverse = 1.0 / total
    out = jnp.where(low, first, second) * inverse
    for p in range(groups):
        out_ref[:, p * 128 : (p + 1) * 128] = out[p * span : (p + 1) * span].astype(BF16)
    do32 = do.astype(F32)
    product = do32 * out
    high = product.astype(BF16)
    rest = (product - high.astype(F32)).astype(BF16)
    place = lax.broadcasted_iota(jnp.int32, (128, 128), 0)
    for h in range(2):
        ones = jnp.where((place < HEAD_DIM) == (h == 0), 1.0, 0.0).astype(BF16)
        delta = dot(high, ones) + dot(rest, ones)
        ext_ref[h] = jnp.concatenate([do, extended(delta)], axis=1)
    do_t = (do32 * inverse).T.astype(BF16)
    q_t = (q.astype(F32) * inverse).T.astype(BF16)

    def backward(b, start):
        values = value_tiles(b)
        kv, swapped, zero = load(b)
        keys = (jnp.where(low, kv, zero), jnp.where(low, zero, swapped))
        dq = dk = dv = 0.0
        for h in range(2):
            expd = e_ref[b, h]
            head = slice(h * HEAD_DIM, (h + 1) * HEAD_DIM)
            dscore = (expd.astype(F32) * dot_nt(ext_ref[h], values[h])).astype(BF16)
            dq = dq + dot(dscore, keys[h])
            dk = dk + dot(q_t[head], dscore)
            dv = dv + dot(do_t[head], expd)
        acc_ref[0] = dq if start else acc_ref[0] + dq
        both = jnp.concatenate([dk, dv], axis=0)
        kv_t_ref[b] = jnp.where(group == 0, both, kv_t_ref[b] + both)

    over_blocks(backward)
    dq = acc_ref[0] * (inverse * SCALE)
    for p in range(groups):
        dq_ref[:, p * 128 : (p + 1) * 128] = turn(dq[p * span : (p + 1) * span], tables, -1).astype(BF16)

    @pl.when(group == group_count - 1)
    def _():
        for b in range(count // per):
            used_block = jnp.where(b < used, kv_t_ref[b], 0.0).T.astype(BF16)
            for i in range(per):
                slot = b * per + i
                result = odd_out_ref if slot % 2 else even_out_ref
                result[slot // 2] = used_block[i * span : (i + 1) * span]


def attention(place, pairs, q, do, tables):
    depth = len(pairs)
    count = 2 * depth
    seqs, span, _ = q.shape
    single = count * span <= 1024
    groups = PAIRS if single else 2
    wide_spec = pl.BlockSpec((None, span, groups * 128), lambda s, i: (s, 0, i))
    pieces = pl.BlockSpec((depth, None, span, 128), lambda s, i: (0, s, 0, 0))
    two = pl.BlockSpec((2, None, span, 128), lambda s, i: (0, s, 0, 0))
    if single:
        kernel, scratch = functools.partial(whole_kernel, span, depth), []
    else:
        block = max(512, span)
        blocks = count * span // block
        rows = groups * span
        kernel = functools.partial(loop_kernel, groups, span, block, count)
        scratch = [
            pltpu.VMEM((count * span, 128), BF16),
            pltpu.VMEM((blocks, 2, rows, block), BF16),
            pltpu.VMEM((blocks, 128, block), F32),
            pltpu.VMEM((2, rows, 128), F32),
            pltpu.VMEM((2, rows, 128), F32),
            pltpu.VMEM((2, rows, 256), BF16),
        ]
    return pl.pallas_call(
        kernel,
        grid=(seqs, PAIRS // groups),
        in_specs=[SMEM] + [two] * depth + [wide_spec, wide_spec, pl.BlockSpec(tables.shape, lambda s, i: (0, 0, 0))],
        out_specs=[wide_spec] * 2 + [pieces] * 2,
        out_shape=[SHAPE((seqs, span, D), BF16), SHAPE((seqs, span, D), BF16)]
        + [SHAPE((depth, seqs, span, 128), BF16)] * 2,
        scratch_shapes=scratch,
        compiler_params=params(),
        cost_estimate=cost(10),
        name="attention",
    )(place, *pairs, q, do, tables)


def weights_kernel(place_ref, attn_ref, g_ref, first_in_ref, grad_ref, send_ref, keep_ref, small_ref):
    half = D // 2
    own = place_ref[0] == 0

    def products(left, right, line):
        small_ref[line : line + 1] = jnp.sum(right.astype(F32), axis=0, keepdims=True)
        result = dot_tn(left, right).astype(BF16)
        lower, upper = result[:, :half], result[:, half:]
        send_ref[0] = jnp.where(own, upper, lower)
        keep_ref[0] = jnp.where(own, lower, upper)

    @pl.when(pl.program_id(0) == 0)
    def _():
        products(attn_ref[...], g_ref[...], 1)

    @pl.when(pl.program_id(0) == 1)
    def _():
        products(first_in_ref[...], grad_ref[...], 0)


def weights(place, attn, g, first_in, grad):
    rows = attn.shape[0]
    whole = pl.BlockSpec((rows, D), lambda i: (0, 0))
    part = pl.BlockSpec((1, D, D // 2), lambda i: (i, 0, 0))
    return pl.pallas_call(
        weights_kernel,
        grid=(2,),
        in_specs=[SMEM] + [whole] * 4,
        out_specs=[part, part, pl.BlockSpec((8, D), lambda i: (0, 0))],
        out_shape=[SHAPE((2, D, D // 2), BF16), SHAPE((2, D, D // 2), BF16), SHAPE((8, D), F32)],
        compiler_params=params(),
        cost_estimate=cost(2.4),
        name="weights",
    )(place, attn, g, first_in, grad)


def mix_kernel(x_ref, mlp_ref, mlp2_ref, attn_ref, grad_ref, add_ref, wo_ref, wq_ref, output_ref, first_ref):
    first_ref[...] = dot_nt(grad_ref[...], wq_ref[...]).astype(BF16)
    mlp = mlp_ref[...].astype(F32) + mlp2_ref[...].astype(F32)
    x = x_ref[...].astype(F32)
    output_ref[...] = (x + (mlp + dot(attn_ref[...], wo_ref[...])) + wide(add_ref)).astype(BF16)


def mix(x, mlp, mlp2, attn, grad, add, wo, wqkv):
    rows = x.shape[0]
    row = pl.BlockSpec((rows // 2, D), lambda i: (i, 0))
    square = pl.BlockSpec((D, D), lambda i: (0, 0))
    return pl.pallas_call(
        mix_kernel,
        grid=(2,),
        in_specs=[row] * 5 + [pl.BlockSpec((D,), lambda i: (0,)), square, square],
        out_specs=[row] * 2,
        out_shape=[SHAPE((rows, D), BF16)] * 2,
        compiler_params=params(),
        cost_estimate=cost(2.4),
        name="mix",
    )(x, mlp, mlp2, attn, grad, add, wo, wqkv)


def two_terms(values):
    high = values.astype(BF16)
    return high, (values - high.astype(F32)).astype(BF16)


def message_lines(ff):
    return -(-(ff // 128 + 6 * (D // 128) + 1) // 16) * 16


def finish_kernel(
    copies,
    count,
    lines,
    place_ref,
    *refs,
):
    kv_refs, refs = refs[:count], refs[count:]
    (
        extra_ref,
        x_ref,
        g_ref,
        first_ref,
        back_ref,
        back2_ref,
        gain_ref,
        bias_ref,
        gain2_ref,
        wkv_ref,
        tables_ref,
        b1_ref,
        early_ref,
        tokens_ref,
        message_ref,
        vector_scr,
    ) = refs
    total = extra_ref[...].astype(F32)
    for ref in kv_refs:
        total += ref[...].astype(F32)
    tables = repeated(tables_ref, copies)
    grad = turn(total, key_tables(tables), -1).astype(BF16)
    x = x_ref[...].astype(F32)
    normed, inverse = normalize(x)
    gain = wide(gain_ref)
    first_in = normed * gain + wide(bias_ref)
    first_grad = first_ref[...].astype(F32) + dot_nt(grad, wkv_ref[...])
    second_grad = back_ref[...].astype(F32) + back2_ref[...].astype(F32)

    vector_scr[...] = jnp.zeros_like(vector_scr)
    b1 = b1_ref[...]
    b1_lines = b1.shape[1] // 128
    for i in range(b1_lines):
        vector_scr[pl.ds(place_ref[0] * b1_lines + i, 1)] = b1[:, i * 128 : (i + 1) * 128]
    at = 2 * b1_lines
    sums = [early_ref[0:1], early_ref[1:2]]
    for rows in (first_grad * normed, first_grad, second_grad * normed, second_grad):
        sums.append(jnp.sum(rows, axis=0, keepdims=True))
    sums.append(jnp.sum(grad.astype(F32), axis=0, keepdims=True))
    for row in sums:
        for i in range(row.shape[1] // 128):
            vector_scr[at : at + 1] = row[:, i * 128 : (i + 1) * 128]
            at += 1
    high, rest = two_terms(vector_scr[...])
    weight = dot(first_in.T.astype(BF16), grad).astype(BF16)
    places = message_ref.shape[0]
    per = weight.shape[0] // places
    for i in range(places):
        message_ref[i, :lines] = high
        message_ref[i, lines : 2 * lines] = rest
        message_ref[i, 2 * lines :] = weight[i * per : (i + 1) * per]

    normed_grad = first_grad * gain + second_grad * wide(gain2_ref)
    mean = jnp.mean(normed_grad, axis=-1, keepdims=True)
    along_rows = jnp.mean(normed_grad * normed, axis=-1, keepdims=True)
    tokens_ref[...] = (g_ref[...].astype(F32) + inverse * (normed_grad - mean - normed * along_rows)).astype(BF16)


def finish(place, places, ff, kv_parts, extra, x, g, first, back, back2, gain, bias, gain2, wqkv, tables, b1, early):
    rows = x.shape[0]
    lines = message_lines(ff)
    whole = lambda a: pl.BlockSpec(a.shape, lambda i: (0,) * a.ndim)
    before = (*kv_parts, extra, x, g, first, back, back2, gain, bias, gain2)
    after_it = (tables, b1, early)
    return pl.pallas_call(
        functools.partial(finish_kernel, rows // tables.shape[1], len(kv_parts), lines),
        grid=(1,),
        in_specs=[SMEM]
        + [whole(a) for a in before]
        + [pl.BlockSpec((D, 128), lambda i: (0, D // 128))]
        + [whole(a) for a in after_it],
        out_specs=[
            pl.BlockSpec((rows, D), lambda i: (0, 0)),
            pl.BlockSpec((places, 2 * lines + D // places, 128), lambda i: (0, 0, 0)),
        ],
        out_shape=[SHAPE((rows, D), BF16), SHAPE((places, 2 * lines + D // places, 128), BF16)],
        scratch_shapes=[pltpu.VMEM((lines, 128), F32)],
        compiler_params=params(),
        cost_estimate=cost(2.4),
        name="finish",
    )(place, *before, wqkv, *after_it)


def gather_sums(messages, lines):
    rows = messages.shape[1]

    def kernel(refs, result):
        total = tree_sum([refs[i] for i in range(messages.shape[0])])
        high, rest = two_terms(total[:lines] + total[lines : 2 * lines])
        result[:lines] = high
        result[lines : 2 * lines] = rest
        result[2 * lines :] = total[2 * lines :].astype(BF16)

    return pl.pallas_call(
        kernel,
        in_specs=[VMEM],
        out_specs=VMEM,
        out_shape=SHAPE((rows, 128), BF16),
        compiler_params=params(),
        cost_estimate=cost(0.6),
        name="gather_sums",
    )(messages)


def last_sums(messages, lines, widths):
    rows = messages[0].shape[0] - 2 * lines

    def kernel(*refs):
        sources, results = refs[: len(messages)], refs[len(messages) :]
        total = tree_sum([ref[...] for ref in sources])
        vector = total[:lines] + total[lines : 2 * lines]
        at = 0
        for result, width in zip(results[:-1], widths):
            for i in range(width // 128):
                result[i * 128 : (i + 1) * 128] = vector[at + i]
            at += width // 128
        results[-1][...] = total[2 * lines :]

    return pl.pallas_call(
        kernel,
        in_specs=[VMEM] * len(messages),
        out_specs=[VMEM] * (len(widths) + 1),
        out_shape=[SHAPE((width,), F32) for width in widths] + [SHAPE((rows, 128), F32)],
        compiler_params=params(),
        cost_estimate=cost(0.6),
        name="last_sums",
    )(*messages)


def local(
    tokens,
    ln1_gain,
    ln1_bias,
    qkv_weight,
    qkv_bias,
    out_weight,
    ln2_gain,
    ln2_bias,
    fc1_weight,
    fc1_bias,
    fc2_weight,
    out_bias,
    output_grad,
    key_value_grad,
):
    seqs, span, _ = tokens.shape
    rows = seqs * span
    ff = fc1_weight.shape[1]
    count = lax.axis_size("seq")
    batches = lax.axis_size("batch")
    depth = count // 2
    half_depth = depth // 2
    per1, per2 = D // count, ff // count
    own = lax.axis_index("seq").astype(jnp.int32)
    batch = lax.axis_index("batch").astype(jnp.int32)
    y, z = own & 1, own >> 1
    core, xs = batch & 1, batch >> 1
    place = jnp.stack([core, xs, y, z])
    x = tokens.reshape(rows, D)
    g = output_grad.reshape(rows, D)
    over_core = lambda v: flipped(v, "batch", 1)
    over_x = lambda v: flipped(v, "batch", 2)
    over_y = lambda v: flipped(v, "seq", 1)
    over_z = lambda v, bit: flipped(v, "seq", 2 << bit)
    z_bits = depth.bit_length() - 1
    flat = lambda v: v.reshape(rows, -1)

    def pair(mine, other, index, axis):
        first = jnp.where(index == 0, mine, other)
        second = jnp.where(index == 0, other, mine)
        return jnp.concatenate([first, second], axis=axis)

    def summed(*parts):
        return tree_sum(parts).astype(BF16)

    x_other, g_other = over_core(x), over_core(g)
    tables = rotary_tables(own * span, span)
    kv, first_in = project_keys(x, ln1_gain, ln1_bias, qkv_weight, qkv_bias, tables)
    kv3 = kv.reshape(seqs, span, 128)
    kv_y = over_y(kv3)
    q = project_queries(first_in, qkv_weight, qkv_bias, tables)
    (kv_y,) = after((kv_y,), q)
    two = jnp.stack([kv3, kv_y])
    pairs = [two] + [along(two, k) for k in range(1, depth)]

    x_fed, g_fed = after((x, g), two)
    (mlp, mlp_other, back, back_other, attn_grad, b1_grad, theirs1, mine1), (theirs2, mine2) = feed(
        place, count, x_fed, x_other, g_fed, g_other, ln2_gain, ln2_bias, fc1_weight, fc1_bias.reshape(1, -1),
        fc2_weight, out_weight,
    )
    come1 = over_x(theirs1)
    come2 = over_z(theirs2, 0)
    mlp_come, back_come = over_core(mlp_other), over_core(back_other)

    q3, do3 = q.reshape(seqs, span, D), attn_grad.reshape(seqs, span, D)
    out, q_rows, even, odd = attention(place, pairs, q3, do3, tables)
    odd = over_y(odd)

    def halved(a, parts, height):
        return a.reshape(parts, 2, height, a.shape[-1])

    q_rows, come1, mlp_come, back_come = after((flat(q_rows), come1, mlp_come, back_come), out)
    send, keep, early = weights(place, flat(out), g, first_in, q_rows)
    come3 = over_core(send)

    mine2, come2 = after((mine2, come2), send)
    height = per2 // 2
    view = lambda v: halved(v, half_depth, height)
    theirs2, mine2 = add_split(place, [(view(mine2), view(come2), 1)])
    come2 = over_x(theirs2)

    even, odd = after((even, odd), theirs2)
    kv_sums = [summed(even[k], odd[k]) for k in range(depth)]
    got = [along(kv_sums[k], -k) for k in range(1, depth)]

    mine1, come1 = after((mine1, come1), *kv_sums)
    view = lambda v: halved(v, depth // 2, per1)
    theirs1, mine1 = add_split(place, [(view(mine1), view(come1), 3)])
    come1 = over_z(theirs1, 0)

    x_mix, mlp_come = after((x, mlp_come), theirs1)
    output, first = mix(x_mix, mlp, mlp_come, flat(out), q_rows, out_bias, out_weight, qkv_weight)

    keep, come3 = after((keep, come3), first)
    view = lambda v: halved(v, 2 * depth, per1)
    theirs3, mine3 = add_split(place, [(view(keep), view(come3), 2)])
    come3 = over_y(theirs3)

    mine2, come2 = after((mine2, come2), theirs3)
    view = lambda v: halved(v, half_depth // 2, height)
    theirs2, mine2 = add_split(place, [(view(mine2), view(come2), 2)])
    come2 = over_y(theirs2)

    got = after(got, theirs2)
    lines = message_lines(ff)
    tokens_grad, messages = finish(
        place, count, ff, [flat(v) for v in (kv_sums[0], *got)], flat(key_value_grad), x, g, first, back, back_come,
        ln1_gain, ln1_bias, ln2_gain, qkv_weight, tables, b1_grad, early,
    )
    messages = lax.all_to_all(messages, "seq", 0, 0, tiled=True)

    mine3, come3, mine1, come1 = after((mine3, come3, mine1, come1), tokens_grad)
    view3 = lambda v: halved(v, depth, per1)
    view1 = lambda v: halved(v, depth // 2, per1 // 2)
    theirs3, mine3, theirs1, mine1 = add_split(
        place, [(view3(mine3), view3(come3), 3), (view1(mine1), view1(come1), 2)]
    )
    come3, come1 = over_z(theirs3, 0), over_y(theirs1)
    mine2, come2 = after((mine2, come2), theirs1)
    for bit in range(1, z_bits - 1):
        view = lambda v: halved(v, half_depth >> (bit + 1), height)
        theirs2, mine2 = add_split(place, [(view(mine2), view(come2), 3 + bit)])
        come2 = over_z(theirs2, bit)
    sum2 = summed(mine2, come2).reshape(height, D)
    come2 = to_owner(sum2)

    (messages,) = after((messages,), sum2)
    message = gather_sums(messages, lines)
    got = [flipped(message, "batch", i) for i in range(1, batches)]

    mine3, come3, mine1, come1 = after((mine3, come3, mine1, come1), message)
    for bit in range(1, z_bits):
        parts = depth >> (bit + 1)
        view3 = lambda v: halved(v, 2 * parts, per1)
        view1 = lambda v: halved(v, parts, per1 // 2)
        theirs3, mine3, theirs1, mine1 = add_split(
            place, [(view3(mine3), view3(come3), 3 + bit), (view1(mine1), view1(come1), 3 + bit)]
        )
        come3, come1 = over_z(theirs3, bit), over_z(theirs1, bit)

    sum2, come2 = after((sum2, come2), theirs1)
    sum2 = summed(sum2, come2)
    other2 = over_x(sum2)
    got = after(got, sum2)
    widths = (ff,) + (D,) * 6 + (128,)
    b1_sum, q_sum, out_sum, gain1, bias1, gain2, bias2, kv_bias, kv_sum = last_sums([message, *got], lines, widths)
    mine3, come3 = after((mine3, come3), kv_sum)
    sum3 = summed(mine3, come3)
    other3 = over_x(sum3)
    mine1, come1 = after((mine1, come1), sum3)
    sum1 = summed(mine1, come1).reshape(per1 // 2, -1)
    other1 = over_x(sum1)

    sum2, other2 = after((sum2, other2), sum1)
    sum2 = pair(sum2, other2, xs, 0)
    other2 = over_core(sum2)
    sum3, other3 = after((sum3, other3), sum2)
    sum3 = summed(sum3, other3)
    other3 = over_core(sum3)
    sum1, other1 = after((sum1, other1), sum3)
    sum1 = pair(sum1, other1, xs, 0)
    other1 = over_core(sum1)

    owner = (z >> (z_bits - 1)) == core
    (other2,) = after((other2,), sum1)
    fc2_grad = jnp.where(owner, sum2, other2).astype(F32)
    (other3,) = after((other3,), fc2_grad)
    both3 = pair(sum3, other3, core, 2).astype(F32)
    (other1,) = after((other1,), both3)
    fc1_grad = pair(sum1, other1, core, 1).astype(F32)
    return (
        output.reshape(tokens.shape),
        kv3,
        tokens_grad.reshape(tokens.shape),
        gain1,
        bias1,
        jnp.concatenate([both3[1], kv_sum], axis=1),
        jnp.concatenate([q_sum, kv_bias]),
        both3[0],
        gain2,
        bias2,
        fc1_grad,
        b1_sum,
        fc2_grad,
        out_sum,
    )


def solution(mesh):
    part = P("batch", "seq", None)
    whole = P()
    split = P("seq", None)
    return jax.shard_map(
        local,
        mesh=mesh,
        in_specs=(part,) + (whole,) * 11 + (part, part),
        out_specs=(
            part, part, part, whole, whole, split, whole, split, whole, whole, split, whole, split, whole,
        ),
        check_vma=False,
    )
```

```python
import functools
import math

import jax
import jax.numpy as jnp
from jax import lax
from jax.experimental import pallas as pl
from jax.experimental.pallas import tpu as pltpu
from jax.sharding import PartitionSpec as P

D = 768
HEADS = 12
HEAD_DIM = 64
ROT = 16
PAIRS = HEADS // 2
SCALE = 1.0 / math.sqrt(HEAD_DIM)
NORM_EPS = 1e-05
MASKED = -1e30
F32 = jnp.float32
BF16 = jnp.bfloat16
VMEM_BYTES = 56 * 1024 * 1024


def dot(a, b):
    return lax.dot_general(a, b, (((1,), (0,)), ((), ())), preferred_element_type=F32)


def dot_nt(a, b):
    return lax.dot_general(a, b, (((1,), (1,)), ((), ())), preferred_element_type=F32)


def dot_tn(a, b):
    return lax.dot_general(a, b, (((0,), (0,)), ((), ())), preferred_element_type=F32)


def params():
    return pltpu.CompilerParams(vmem_limit_bytes=VMEM_BYTES)


def flipped(block, axis, bits):
    return lax.ppermute(block, axis, [(i, i ^ bits) for i in range(lax.axis_size(axis))])


def along(block, distance):
    size = lax.axis_size("seq")
    return lax.ppermute(block, "seq", [(i, (i + 2 * distance) % size) for i in range(size)])


def to_owner(block):
    size = lax.axis_size("seq")
    route = []
    for b in range(lax.axis_size("batch")):
        for i in range(size):
            j = i ^ (size // 2)
            if j // (size // 2) == b % 2:
                route.append((b * size + i, b * size + j))
    return lax.ppermute(block, ("batch", "seq"), route)


def after(values, *others):
    return lax.optimization_barrier((tuple(values), others))[0]


def tree_sum(parts):
    parts = [p.astype(F32) for p in parts]
    while len(parts) > 1:
        parts = [sum(parts[i : i + 2][1:], parts[i]) for i in range(0, len(parts), 2)]
    return parts[0]


def take(block, index, axis):
    return lax.dynamic_index_in_dim(block, index, axis, keepdims=False)


def normalize(rows):
    centre = jnp.mean(rows, axis=-1, keepdims=True)
    centred = rows - centre
    spread = jnp.mean(centred * centred, axis=-1, keepdims=True)
    inverse = lax.rsqrt(spread + NORM_EPS)
    return centred * inverse, inverse


def rotary_tables(first, count):
    lane = jnp.arange(128) % HEAD_DIM
    half = ROT // 2
    freqs = 10000.0 ** (-(lane % half).astype(F32) / half)
    places = (first + jnp.arange(count)).astype(F32) * 0.25
    angles = places[:, None] * freqs[None, :]
    cosine, sine = jnp.cos(angles), jnp.sin(angles)
    return jnp.stack(
        [
            jnp.where(lane < ROT, cosine, 1.0),
            jnp.where((lane >= half) & (lane < ROT), sine, 0.0),
            jnp.where(lane < half, -sine, 0.0),
        ]
    )


def turn(values, tables, sign):
    moved = pltpu.roll(values, ROT // 2, 1) * tables[1] + pltpu.roll(values, 128 - ROT // 2, 1) * tables[2]
    return values * tables[0] + (moved if sign > 0 else -moved)


def repeated(tables_ref, count):
    return [jnp.concatenate([tables_ref[i]] * count, axis=0) for i in range(3)]


def key_tables(tables):
    low = lax.broadcasted_iota(jnp.int32, (1, 128), 1) < HEAD_DIM
    return [jnp.where(low, tables[0], 1.0), jnp.where(low, tables[1], 0.0), jnp.where(low, tables[2], 0.0)]

VMEM = pl.BlockSpec(memory_space=pltpu.VMEM)
SMEM = pl.BlockSpec(memory_space=pltpu.SMEM)
SHAPE = jax.ShapeDtypeStruct


def cost(share):
    return pl.CostEstimate(flops=int(share * 3e9), bytes_accessed=0, transcendentals=0)


def wide(ref):
    return ref[...].reshape(1, -1)


def add_split(place, items):
    def kernel(place_ref, *refs):
        sources, results = refs[: 2 * len(items)], refs[2 * len(items) :]
        for n, (_, _, which) in enumerate(items):
            a, b = sources[2 * n], sources[2 * n + 1]
            own = place_ref[which] if which < 3 else lax.rem(lax.shift_right_logical(place_ref[3], which - 3), 2)
            for m in range(a.shape[0]):
                for result, at in ((results[2 * n], 1 - own), (results[2 * n + 1], own)):
                    result[m] = (a[m, at].astype(F32) + b[m, at].astype(F32)).astype(BF16)

    shapes = []
    for a, _, _ in items:
        shapes += [SHAPE((a.shape[0],) + a.shape[2:], BF16)] * 2
    arrays = [v for item in items for v in item[:2]]
    return pl.pallas_call(
        kernel,
        in_specs=[SMEM] + [VMEM] * len(arrays),
        out_specs=[VMEM] * len(shapes),
        out_shape=shapes,
        compiler_params=params(),
        cost_estimate=cost(1.2),
        name="add_split",
    )(place, *arrays)


def keys_kernel(copies, x_ref, gain_ref, bias_ref, weight_ref, add_ref, tables_ref, kv_ref, first_ref):
    normed, _ = normalize(x_ref[...].astype(F32))
    first_in = (normed * wide(gain_ref) + wide(bias_ref)).astype(BF16)
    first_ref[...] = first_in
    part = dot(first_in, weight_ref[...]) + wide(add_ref)[:, D:]
    kv_ref[...] = turn(part, key_tables(repeated(tables_ref, copies)), 1).astype(BF16)


def queries_kernel(copies, first_ref, weight_ref, add_ref, tables_ref, q_ref):
    first_in = first_ref[...]
    tables = repeated(tables_ref, copies)
    bias = wide(add_ref)
    for p in range(PAIRS):
        columns = slice(p * 128, (p + 1) * 128)
        part = dot(first_in, weight_ref[:, columns]) + bias[:, columns]
        q_ref[:, columns] = (turn(part, tables, 1) * SCALE).astype(BF16)


def project_keys(x, gain, bias, weight, add, tables):
    rows = x.shape[0]
    whole = lambda a: pl.BlockSpec(a.shape, lambda i: (0,) * a.ndim)
    return pl.pallas_call(
        functools.partial(keys_kernel, rows // tables.shape[1]),
        grid=(1,),
        in_specs=[
            whole(x),
            whole(gain),
            whole(bias),
            pl.BlockSpec((D, 128), lambda i: (0, D // 128)),
            whole(add),
            whole(tables),
        ],
        out_specs=[pl.BlockSpec((rows, 128), lambda i: (0, 0)), pl.BlockSpec((rows, D), lambda i: (0, 0))],
        out_shape=[SHAPE((rows, 128), BF16), SHAPE((rows, D), BF16)],
        compiler_params=params(),
        cost_estimate=cost(1),
        name="project_keys",
    )(x, gain, bias, weight, add, tables)


def project_queries(first_in, weight, add, tables):
    rows = first_in.shape[0]
    whole = lambda a: pl.BlockSpec(a.shape, lambda i: (0,) * a.ndim)
    return pl.pallas_call(
        functools.partial(queries_kernel, rows // tables.shape[1]),
        grid=(1,),
        in_specs=[
            whole(first_in),
            pl.BlockSpec((D, D), lambda i: (0, 0)),
            whole(add),
            whole(tables),
        ],
        out_specs=pl.BlockSpec((rows, D), lambda i: (0, 0)),
        out_shape=SHAPE((rows, D), BF16),
        compiler_params=params(),
        cost_estimate=cost(2),
        name="project_queries",
    )(first_in, weight, add, tables)


def gelu_parts(h):
    t = pl.reciprocal(1.0 + (0.3275911 / math.sqrt(2.0)) * jnp.abs(h))
    e = jnp.exp(-0.5 * h * h)
    poly = 0.5 * 1.061405429
    for coefficient in (-1.453152027, 1.421413741, -0.284496736, 0.254829592):
        poly = poly * t + 0.5 * coefficient
    tail = poly * t * e
    cdf = jnp.where(h >= 0.0, 1.0 - tail, tail)
    return h * cdf, cdf + h * e * (1.0 / math.sqrt(2.0 * math.pi))


def feed_kernel(
    place_ref,
    x_ref,
    xx_ref,
    g_ref,
    gg_ref,
    gain_ref,
    bias_ref,
    w1_ref,
    b1_ref,
    w2_ref,
    wo_ref,
    mlp_ref,
    mlp2_ref,
    back_ref,
    back2_ref,
    attn_grad_ref,
    b1_grad_ref,
    theirs1_ref,
    mine1_ref,
    *refs,
):
    grad_refs, (in_scr, in_t_scr, g_scr, mlp_scr, back_scr) = refs[:-5], refs[-5:]
    step, steps = pl.program_id(0), pl.num_programs(0)
    rows = x_ref.shape[0]

    @pl.when(step == 0)
    def _():
        for i, (tokens, grads) in enumerate(((x_ref, g_ref), (xx_ref, gg_ref))):
            at = slice(i * rows, (i + 1) * rows)
            normed, _ = normalize(tokens[...].astype(F32))
            second_in = normed * wide(gain_ref) + wide(bias_ref)
            in_scr[at] = second_in.astype(BF16)
            in_t_scr[:, :, :, at] = second_in.T.astype(BF16).reshape(in_t_scr.shape[:3] + (rows,))
            g_scr[at] = grads[...]
        attn_grad_ref[...] = dot_nt(g_ref[...], wo_ref[...]).astype(BF16)

    g = g_scr[...]
    w1 = w1_ref[...]
    w2 = w2_ref[...]
    act, slope = gelu_parts(dot(in_scr[...], w1) + b1_ref[...])
    act = act.astype(BF16)
    pre = dot_nt(g, w2) * slope
    pre16 = pre.astype(BF16)
    b1_grad_ref[...] = jnp.sum(pre, axis=0, keepdims=True)
    mlp = dot(act, w2)
    grad = dot_tn(act, g).astype(BF16)
    if len(grad_refs) == 1:
        grad_refs[0][...] = grad
    for i in range(len(grad_refs) if len(grad_refs) > 1 else 0):

        @pl.when(step == i)
        def _(i=i):
            grad_refs[i][...] = grad

    back = dot_nt(pre16, w1)
    own = place_ref[1]
    for result, at in ((theirs1_ref, 1 - own), (mine1_ref, own)):
        left = in_t_scr[:, pl.ds(at, 1)].reshape(D // 2, 2 * rows)
        result[...] = dot(left, pre16).astype(BF16).reshape(result.shape)

    @pl.when(step == 0)
    def _():
        mlp_scr[...] = mlp
        back_scr[...] = back

    @pl.when((step > 0) & (step < steps - 1))
    def _():
        mlp_scr[...] += mlp
        back_scr[...] += back

    @pl.when(step == steps - 1)
    def _():
        for scr, last, own_ref, other_ref in ((mlp_scr, mlp, mlp_ref, mlp2_ref), (back_scr, back, back_ref, back2_ref)):
            total = (scr[...] + last).astype(BF16)
            own_ref[...] = total[:rows]
            other_ref[...] = total[rows:]


CHUNK = 512


def feed(place, count, x, xx, g, gg, gain, bias, w1, b1, w2, wo):
    rows = x.shape[0]
    half = w1.shape[1] // 2
    depth = count // 2
    per = D // count // 2
    pieces = depth // 2
    aligned = pieces == 2 and half % 512 == 0
    chunk = half // pieces if aligned else CHUNK
    steps = half // chunk
    single = pl.Buffered(1)
    whole = lambda a: pl.BlockSpec(a.shape, lambda i, place: (0,) * a.ndim, pipeline_mode=single)
    fixed = lambda *shape: pl.BlockSpec(shape, lambda i, place: (0, 0))
    if aligned:
        piece = lambda i, place: (place[3] ^ (1 - i)) & 1
        grad_specs = [fixed(chunk, D)] * pieces
        grad_shapes = [SHAPE((chunk, D), BF16)] * pieces
    else:
        piece = lambda i, place: i
        grad_specs = [pl.BlockSpec((chunk, D), lambda i, place: (i, 0))]
        grad_shapes = [SHAPE((half, D), BF16)]
    at = lambda i, place: place[0] * steps + piece(i, place)
    cut = pl.BlockSpec((count, per, chunk), lambda i, place: (0, 0, piece(i, place)))
    spec = pltpu.PrefetchScalarGridSpec(
        num_scalar_prefetch=1,
        grid=(steps,),
        in_specs=[
            whole(x),
            whole(xx),
            whole(g),
            whole(gg),
            whole(gain),
            whole(bias),
            pl.BlockSpec((D, chunk), lambda i, place: (0, at(i, place))),
            pl.BlockSpec((1, chunk), lambda i, place: (0, at(i, place))),
            pl.BlockSpec((chunk, D), lambda i, place: (at(i, place), 0)),
            whole(wo),
        ],
        out_specs=[fixed(rows, D)] * 5
        + [pl.BlockSpec((1, chunk), lambda i, place: (0, piece(i, place))), cut, cut]
        + grad_specs,
        scratch_shapes=[
            pltpu.VMEM((2 * rows, D), BF16),
            pltpu.VMEM((count, 2, per, 2 * rows), BF16),
            pltpu.VMEM((2 * rows, D), BF16),
            pltpu.VMEM((2 * rows, D), F32),
            pltpu.VMEM((2 * rows, D), F32),
        ],
    )
    result = pl.pallas_call(
        feed_kernel,
        grid_spec=spec,
        out_shape=[SHAPE((rows, D), BF16)] * 5
        + [SHAPE((1, half), F32), SHAPE((count, per, half), BF16), SHAPE((count, per, half), BF16)]
        + grad_shapes,
        compiler_params=params(),
        cost_estimate=cost(12),
        name="feed_forward",
    )(place, x, xx, g, gg, gain, bias, w1, b1, w2, wo)
    grads = result[8:]
    if not aligned:
        cut = grads[0].reshape(pieces // 2, 2, -1, D)
        low = place[3] & 1
        grads = [take(cut, 1 - low, 1), take(cut, low, 1)]
    return result[:8], grads


def present(slot, y, z):
    back = slot // 2
    return (back <= z) & ((slot % 2 == 0) | (back >= 1) | (y == 1))


def whole_kernel(span, depth, place_ref, *refs):
    pair_refs, (q_ref, do_ref, tables_ref, out_ref, dq_ref, even_out_ref, odd_out_ref) = refs[:depth], refs[depth:]
    y, z = place_ref[2], place_ref[3]
    tables = [tables_ref[i] for i in range(3)]
    rows = PAIRS * span
    low = lax.broadcasted_iota(jnp.int32, (1, 128), 1) < HEAD_DIM

    def stacked(ref):
        return jnp.concatenate([ref[:, p * 128 : (p + 1) * 128] for p in range(PAIRS)], axis=0)

    blocks = [ref[i] for ref in pair_refs for i in range(2)]
    kv = jnp.concatenate(blocks, axis=0)
    swapped = pltpu.roll(kv.astype(F32), HEAD_DIM, 1).astype(BF16)
    zero, one = jnp.zeros_like(kv), jnp.ones_like(kv)
    keys = (jnp.where(low, kv, zero), jnp.where(low, zero, swapped))
    values = (jnp.where(low, swapped, zero), jnp.where(low, zero, kv))
    summing = (jnp.where(low, swapped, one), jnp.where(low, one, kv))
    slot = lax.broadcasted_iota(jnp.int32, (1, (2 * depth - 1) * span), 1) // span + 1
    absent = jnp.where(present(slot, y, z), 0.0, MASKED)
    token = lax.broadcasted_iota(jnp.int32, (rows, span), 0) % span
    seen = lax.broadcasted_iota(jnp.int32, (rows, span), 1) <= token
    q = stacked(q_ref)
    do = stacked(do_ref)
    do32 = do.astype(F32)

    expd, mixed = [], []
    for h in range(2):
        scores = dot_nt(q, keys[h])
        scores = jnp.concatenate([jnp.where(seen, scores[:, :span], MASKED), scores[:, span:] + absent], axis=1)
        top = jnp.max(scores, axis=1, keepdims=True)
        expd.append(jnp.exp(scores - top).astype(BF16))
        mixed.append(dot(expd[h], summing[h]))
    total = jnp.where(low, pltpu.roll(mixed[0], HEAD_DIM, 1), pltpu.roll(mixed[1], HEAD_DIM, 1))
    inverse = 1.0 / total
    out = jnp.where(low, mixed[0], mixed[1]) * inverse
    for p in range(PAIRS):
        out_ref[:, p * 128 : (p + 1) * 128] = out[p * span : (p + 1) * span].astype(BF16)
    product = do32 * out
    do_t = (do32 * inverse).T.astype(BF16)
    q_t = (q.astype(F32) * inverse).T.astype(BF16)
    dq = dk = dv = 0.0
    for h in range(2):
        head = slice(h * HEAD_DIM, (h + 1) * HEAD_DIM)
        delta = jnp.sum(jnp.where(low == (h == 0), product, 0.0), axis=1, keepdims=True)
        dprob = dot_nt(do, values[h])
        dscore = (expd[h].astype(F32) * (dprob - delta)).astype(BF16)
        dq = dq + dot(dscore, keys[h])
        dk = dk + dot(q_t[head], dscore)
        dv = dv + dot(do_t[head], expd[h])
    dq = dq * (inverse * SCALE)
    for p in range(PAIRS):
        dq_ref[:, p * 128 : (p + 1) * 128] = turn(dq[p * span : (p + 1) * span], tables, -1).astype(BF16)
    both = jnp.concatenate([dk, dv], axis=0).T.astype(BF16)
    for k in range(depth):
        even_out_ref[k] = both[2 * k * span : (2 * k + 1) * span]
        odd_out_ref[k] = both[(2 * k + 1) * span : (2 * k + 2) * span]


def loop_kernel(groups, span, block, count, place_ref, *refs):
    depth = count // 2
    pair_refs, refs = refs[:depth], refs[depth:]
    q_ref, do_ref, tables_ref, out_ref, dq_ref, even_out_ref, odd_out_ref = refs[:7]
    kv_scr, e_ref, kv_t_ref, max_ref, acc_ref, ext_ref = refs[7:]
    tables = [tables_ref[i] for i in range(3)]
    rows = groups * span
    per = block // span
    y, z = place_ref[2], place_ref[3]
    used = (2 * (z + 1) + per - 1) // per
    group, group_count = pl.program_id(1), pl.num_programs(1)
    low = lax.broadcasted_iota(jnp.int32, (1, 128), 1) < HEAD_DIM
    lanes = lax.broadcasted_iota(jnp.int32, (rows, 128), 1)

    def stacked(ref):
        return jnp.concatenate([ref[:, p * 128 : (p + 1) * 128] for p in range(groups)], axis=0)

    @pl.when(group == 0)
    def _():
        for i in range(count):
            kv_scr[i * span : (i + 1) * span] = pair_refs[i // 2][i % 2]

    q = stacked(q_ref)
    do = stacked(do_ref)

    def load(b):
        kv = kv_scr[pl.ds(pl.multiple_of(b * block, block), block)]
        swapped = pltpu.roll(kv.astype(F32), HEAD_DIM, 1).astype(BF16)
        return kv, swapped, jnp.zeros_like(kv)

    def absent(b):
        row = lax.broadcasted_iota(jnp.int32, (block, 128), 0) + b * block
        lane = lax.broadcasted_iota(jnp.int32, (block, 128), 1)
        mask = jnp.where(present(row // span, y, z), 0.0, MASKED)
        return jnp.where(lane < 2, -1.0, jnp.where(lane == 2, mask, 0.0)).astype(BF16)

    def key_tiles(b):
        kv, swapped, zero = load(b)
        ext = absent(b)
        return [
            jnp.concatenate([jnp.where(low, kv, zero), ext], axis=1),
            jnp.concatenate([jnp.where(low, zero, swapped), ext], axis=1),
        ]

    def value_tiles(b):
        kv, swapped, zero = load(b)
        ext = absent(b)
        return [
            jnp.concatenate([jnp.where(low, swapped, zero), ext], axis=1),
            jnp.concatenate([jnp.where(low, zero, kv), ext], axis=1),
        ]

    def seen():
        token = lax.broadcasted_iota(jnp.int32, (rows, block), 0) % span
        key = lax.broadcasted_iota(jnp.int32, (rows, block), 1)
        return (key <= token) | (key >= span)

    def extended(values):
        high = values.astype(BF16).astype(F32)
        rest = jnp.where(lanes == 1, values - high, jnp.where(lanes == 2, 1.0, 0.0))
        return jnp.where(lanes == 0, high, rest).astype(BF16)

    def over_blocks(step):
        step(0, True)

        def body(b, carry):
            step(b, False)
            return carry

        lax.fori_loop(1, used, body, 0)

    plain = jnp.concatenate([q, jnp.where(lanes == 2, 1.0, 0.0).astype(BF16)], axis=1)

    def maxima(b, diagonal):
        keys = key_tiles(b)
        for h in range(2):
            scores = dot_nt(plain, keys[h])
            if diagonal:
                scores = jnp.where(seen(), scores, MASKED)
            top = functools.reduce(jnp.maximum, [scores[:, i : i + 128] for i in range(0, block, 128)])
            max_ref[h] = top if diagonal else jnp.maximum(max_ref[h], top)

    over_blocks(maxima)
    for h in range(2):
        top = jnp.max(max_ref[h], axis=1, keepdims=True)
        ext_ref[h] = jnp.concatenate([q, extended(jnp.broadcast_to(top, (rows, 128)))], axis=1)

    def forward(b, diagonal):
        keys = key_tiles(b)
        kv, swapped, _ = load(b)
        one = jnp.ones_like(kv)
        values = (jnp.where(low, swapped, one), jnp.where(low, one, kv))
        for h in range(2):
            expd = jnp.exp(dot_nt(ext_ref[h], keys[h]))
            if diagonal:
                expd = jnp.where(seen(), expd, 0.0)
            expd = expd.astype(BF16)
            e_ref[b, h] = expd
            mixed = dot(expd, values[h])
            acc_ref[h] = mixed if diagonal else acc_ref[h] + mixed

    over_blocks(forward)
    first, second = acc_ref[0], acc_ref[1]
    total = jnp.where(low, pltpu.roll(first, HEAD_DIM, 1), pltpu.roll(second, HEAD_DIM, 1))
    inverse = 1.0 / total
    out = jnp.where(low, first, second) * inverse
    for p in range(groups):
        out_ref[:, p * 128 : (p + 1) * 128] = out[p * span : (p + 1) * span].astype(BF16)
    do32 = do.astype(F32)
    product = do32 * out
    high = product.astype(BF16)
    rest = (product - high.astype(F32)).astype(BF16)
    place = lax.broadcasted_iota(jnp.int32, (128, 128), 0)
    for h in range(2):
        ones = jnp.where((place < HEAD_DIM) == (h == 0), 1.0, 0.0).astype(BF16)
        delta = dot(high, ones) + dot(rest, ones)
        ext_ref[h] = jnp.concatenate([do, extended(delta)], axis=1)
    do_t = (do32 * inverse).T.astype(BF16)
    q_t = (q.astype(F32) * inverse).T.astype(BF16)

    def backward(b, start):
        values = value_tiles(b)
        kv, swapped, zero = load(b)
        keys = (jnp.where(low, kv, zero), jnp.where(low, zero, swapped))
        dq = dk = dv = 0.0
        for h in range(2):
            expd = e_ref[b, h]
            head = slice(h * HEAD_DIM, (h + 1) * HEAD_DIM)
            dscore = (expd.astype(F32) * dot_nt(ext_ref[h], values[h])).astype(BF16)
            dq = dq + dot(dscore, keys[h])
            dk = dk + dot(q_t[head], dscore)
            dv = dv + dot(do_t[head], expd)
        acc_ref[0] = dq if start else acc_ref[0] + dq
        both = jnp.concatenate([dk, dv], axis=0)
        kv_t_ref[b] = jnp.where(group == 0, both, kv_t_ref[b] + both)

    over_blocks(backward)
    dq = acc_ref[0] * (inverse * SCALE)
    for p in range(groups):
        dq_ref[:, p * 128 : (p + 1) * 128] = turn(dq[p * span : (p + 1) * span], tables, -1).astype(BF16)

    @pl.when(group == group_count - 1)
    def _():
        for b in range(count // per):
            used_block = jnp.where(b < used, kv_t_ref[b], 0.0).T.astype(BF16)
            for i in range(per):
                slot = b * per + i
                result = odd_out_ref if slot % 2 else even_out_ref
                result[slot // 2] = used_block[i * span : (i + 1) * span]


def attention(place, pairs, q, do, tables):
    depth = len(pairs)
    count = 2 * depth
    seqs, span, _ = q.shape
    single = count * span <= 1024
    groups = PAIRS if single else 2
    wide_spec = pl.BlockSpec((None, span, groups * 128), lambda s, i: (s, 0, i))
    pieces = pl.BlockSpec((depth, None, span, 128), lambda s, i: (0, s, 0, 0))
    two = pl.BlockSpec((2, None, span, 128), lambda s, i: (0, s, 0, 0))
    if single:
        kernel, scratch = functools.partial(whole_kernel, span, depth), []
    else:
        block = max(512, span)
        blocks = count * span // block
        rows = groups * span
        kernel = functools.partial(loop_kernel, groups, span, block, count)
        scratch = [
            pltpu.VMEM((count * span, 128), BF16),
            pltpu.VMEM((blocks, 2, rows, block), BF16),
            pltpu.VMEM((blocks, 128, block), F32),
            pltpu.VMEM((2, rows, 128), F32),
            pltpu.VMEM((2, rows, 128), F32),
            pltpu.VMEM((2, rows, 256), BF16),
        ]
    return pl.pallas_call(
        kernel,
        grid=(seqs, PAIRS // groups),
        in_specs=[SMEM] + [two] * depth + [wide_spec, wide_spec, pl.BlockSpec(tables.shape, lambda s, i: (0, 0, 0))],
        out_specs=[wide_spec] * 2 + [pieces] * 2,
        out_shape=[SHAPE((seqs, span, D), BF16), SHAPE((seqs, span, D), BF16)]
        + [SHAPE((depth, seqs, span, 128), BF16)] * 2,
        scratch_shapes=scratch,
        compiler_params=params(),
        cost_estimate=cost(10),
        name="attention",
    )(place, *pairs, q, do, tables)


def weights_kernel(place_ref, attn_ref, attn2_ref, g_ref, g2_ref, in_ref, in2_ref, q_ref, q2_ref, theirs_ref, mine_ref, small_ref, scr):
    half = D // 2
    y = place_ref[2]

    def products(left, right, line):
        at = pl.ds(pl.multiple_of(place_ref[0] * half, 128), half)
        small_ref[line : line + 1] = jnp.zeros_like(small_ref[line : line + 1])
        small_ref[line : line + 1, at] = jnp.sum(right.astype(F32), axis=0, keepdims=True)
        scr[...] = dot_tn(left, right).reshape(scr.shape)
        theirs_ref[0] = scr[:, pl.ds(1 - y, 1)].reshape(theirs_ref.shape[1:]).astype(BF16)
        mine_ref[0] = scr[:, pl.ds(y, 1)].reshape(mine_ref.shape[1:]).astype(BF16)

    both = lambda a, b: jnp.concatenate([a[...], b[...]], axis=0)

    @pl.when(pl.program_id(0) == 0)
    def _():
        products(both(attn_ref, attn2_ref), both(g_ref, g2_ref), 1)

    @pl.when(pl.program_id(0) == 1)
    def _():
        products(both(in_ref, in2_ref), both(q_ref, q2_ref), 0)


def weights(place, count, attn, attn2, g, g2, first_in, first_in2, grad, grad2):
    rows = attn.shape[0]
    depth, per, half = count // 2, D // count, D // 2
    whole = pl.BlockSpec((rows, D), lambda i, place: (0, 0), pipeline_mode=pl.Buffered(1))
    part = pl.BlockSpec((rows, half), lambda i, place: (0, place[0]), pipeline_mode=pl.Buffered(1))
    result = pl.BlockSpec((1, depth, per, half), lambda i, place: (i, 0, 0, 0))
    return pl.pallas_call(
        weights_kernel,
        grid_spec=pltpu.PrefetchScalarGridSpec(
            num_scalar_prefetch=1,
            grid=(2,),
            in_specs=[whole, whole, part, part, whole, whole, part, part],
            out_specs=[result, result, pl.BlockSpec((8, D), lambda i, place: (0, 0))],
            scratch_shapes=[pltpu.VMEM((depth, 2, per, half), F32)],
        ),
        out_shape=[SHAPE((2, depth, per, half), BF16), SHAPE((2, depth, per, half), BF16), SHAPE((8, D), F32)],
        compiler_params=params(),
        cost_estimate=cost(2.4),
        name="weights",
    )(place, attn, attn2, g, g2, first_in, first_in2, grad, grad2)


def mix_kernel(x_ref, mlp_ref, mlp2_ref, attn_ref, add_ref, wo_ref, output_ref):
    mlp = mlp_ref[...].astype(F32) + mlp2_ref[...].astype(F32)
    x = x_ref[...].astype(F32)
    output_ref[...] = (x + (mlp + dot(attn_ref[...], wo_ref[...])) + wide(add_ref)).astype(BF16)


def mix(x, mlp, mlp2, attn, add, wo):
    rows = x.shape[0]
    row = pl.BlockSpec((rows // 2, D), lambda i: (i, 0))
    return pl.pallas_call(
        mix_kernel,
        grid=(2,),
        in_specs=[row] * 4 + [pl.BlockSpec((D,), lambda i: (0,)), pl.BlockSpec((D, D), lambda i: (0, 0))],
        out_specs=row,
        out_shape=SHAPE((rows, D), BF16),
        compiler_params=params(),
        cost_estimate=cost(1.2),
        name="mix",
    )(x, mlp, mlp2, attn, add, wo)


def two_terms(values):
    high = values.astype(BF16)
    return high, (values - high.astype(F32)).astype(BF16)


def message_lines(ff):
    return -(-(ff // 128 + 6 * (D // 128) + 1) // 16) * 16


def finish_kernel(
    copies,
    count,
    lines,
    place_ref,
    *refs,
):
    kv_refs, refs = refs[:count], refs[count:]
    (
        extra_ref,
        x_ref,
        g_ref,
        q_ref,
        back_ref,
        back2_ref,
        gain_ref,
        bias_ref,
        gain2_ref,
        wqkv_ref,
        tables_ref,
        b1_ref,
        early_ref,
        tokens_ref,
        theirs_ref,
        mine_ref,
        vector_scr,
        weight_scr,
    ) = refs
    total = extra_ref[...].astype(F32)
    for ref in kv_refs:
        total += ref[...].astype(F32)
    tables = repeated(tables_ref, copies)
    grad = turn(total, key_tables(tables), -1).astype(BF16)
    x = x_ref[...].astype(F32)
    normed, inverse = normalize(x)
    gain = wide(gain_ref)
    first_in = normed * gain + wide(bias_ref)
    first_grad = dot_nt(jnp.concatenate([q_ref[...], grad], axis=1), wqkv_ref[...])
    second_grad = back_ref[...].astype(F32) + back2_ref[...].astype(F32)

    vector_scr[...] = jnp.zeros_like(vector_scr)
    b1 = b1_ref[...]
    b1_lines = b1.shape[1] // 128
    for i in range(b1_lines):
        vector_scr[pl.ds(place_ref[0] * b1_lines + i, 1)] = b1[:, i * 128 : (i + 1) * 128]
    at = 2 * b1_lines
    sums = [early_ref[0:1], early_ref[1:2]]
    for rows in (first_grad * normed, first_grad, second_grad * normed, second_grad):
        sums.append(jnp.sum(rows, axis=0, keepdims=True))
    sums.append(jnp.sum(grad.astype(F32), axis=0, keepdims=True))
    for row in sums:
        for i in range(row.shape[1] // 128):
            vector_scr[at : at + 1] = row[:, i * 128 : (i + 1) * 128]
            at += 1
    high, rest = two_terms(vector_scr[...])
    weight_scr[...] = dot(first_in.T.astype(BF16), grad).reshape(weight_scr.shape)
    y = place_ref[2]
    for message, at in ((theirs_ref, 1 - y), (mine_ref, y)):
        message[:lines] = high
        message[lines : 2 * lines] = rest
        message[2 * lines :] = weight_scr[:, pl.ds(at, 1)].reshape(-1, 128).astype(BF16)

    normed_grad = first_grad * gain + second_grad * wide(gain2_ref)
    mean = jnp.mean(normed_grad, axis=-1, keepdims=True)
    along_rows = jnp.mean(normed_grad * normed, axis=-1, keepdims=True)
    tokens_ref[...] = (g_ref[...].astype(F32) + inverse * (normed_grad - mean - normed * along_rows)).astype(BF16)


def finish(place, places, ff, kv_parts, extra, x, g, q_rows, back, back2, gain, bias, gain2, wqkv, tables, b1, early):
    rows = x.shape[0]
    lines = message_lines(ff)
    whole = lambda a: pl.BlockSpec(a.shape, lambda i: (0,) * a.ndim)
    arrays = (*kv_parts, extra, x, g, q_rows, back, back2, gain, bias, gain2, wqkv, tables, b1, early)
    return pl.pallas_call(
        functools.partial(finish_kernel, rows // tables.shape[1], len(kv_parts), lines),
        grid=(1,),
        in_specs=[SMEM] + [whole(a) for a in arrays],
        out_specs=[
            pl.BlockSpec((rows, D), lambda i: (0, 0)),
            pl.BlockSpec((2 * lines + D // 2, 128), lambda i: (0, 0)),
            pl.BlockSpec((2 * lines + D // 2, 128), lambda i: (0, 0)),
        ],
        out_shape=[SHAPE((rows, D), BF16)] + [SHAPE((2 * lines + D // 2, 128), BF16)] * 2,
        scratch_shapes=[pltpu.VMEM((lines, 128), F32), pltpu.VMEM((places // 2, 2, D // places, 128), F32)],
        compiler_params=params(),
        cost_estimate=cost(2.4),
        name="finish",
    )(place, *arrays)


def message_step(place, mine, come, lines, per, bit):
    count = (mine.shape[0] - 2 * lines) // per
    last = count == 1

    def kernel(place_ref, a_ref, b_ref, *refs):
        vector = tree_sum([ref[at : at + lines] for ref in (a_ref, b_ref) for at in (0, lines)])
        high, rest = two_terms(vector)
        weight = a_ref[2 * lines :].astype(F32) + b_ref[2 * lines :].astype(F32)
        own = (place_ref[3] >> bit) & 1
        if not last:
            refs[-1][...] = weight.reshape(count // 2, 2, per, 128)
        for result, at in zip(refs[: 1 if last else 2], (1 - own, own)):
            result[:lines] = high
            result[lines : 2 * lines] = rest
            rows = weight if last else refs[-1][:, pl.ds(at, 1)].reshape(-1, 128)
            result[2 * lines :] = rows.astype(BF16)

    results = 1 if last else 2
    scratch = [] if last else [pltpu.VMEM((count // 2, 2, per, 128), F32)]
    return pl.pallas_call(
        kernel,
        in_specs=[SMEM, VMEM, VMEM],
        out_specs=[VMEM] * results,
        out_shape=[SHAPE((2 * lines + count * per // results, 128), BF16)] * results,
        scratch_shapes=scratch,
        compiler_params=params(),
        cost_estimate=cost(0.6),
        name="message_step",
    )(place, mine, come)


def last_sums(messages, lines, widths):
    rows = messages[0].shape[0] - 2 * lines

    def kernel(*refs):
        sources, results = refs[: len(messages)], refs[len(messages) :]
        total = tree_sum([ref[...] for ref in sources])
        vector = total[:lines] + total[lines : 2 * lines]
        at = 0
        for result, width in zip(results[:-1], widths):
            for i in range(width // 128):
                result[i * 128 : (i + 1) * 128] = vector[at + i]
            at += width // 128
        results[-1][...] = total[2 * lines :]

    return pl.pallas_call(
        kernel,
        in_specs=[VMEM] * len(messages),
        out_specs=[VMEM] * (len(widths) + 1),
        out_shape=[SHAPE((width,), F32) for width in widths] + [SHAPE((rows, 128), F32)],
        compiler_params=params(),
        cost_estimate=cost(0.6),
        name="last_sums",
    )(*messages)


def local(
    tokens,
    ln1_gain,
    ln1_bias,
    qkv_weight,
    qkv_bias,
    out_weight,
    ln2_gain,
    ln2_bias,
    fc1_weight,
    fc1_bias,
    fc2_weight,
    out_bias,
    output_grad,
    key_value_grad,
):
    seqs, span, _ = tokens.shape
    rows = seqs * span
    ff = fc1_weight.shape[1]
    count = lax.axis_size("seq")
    batches = lax.axis_size("batch")
    depth = count // 2
    half_depth = depth // 2
    per1, per2 = D // count, ff // count
    own = lax.axis_index("seq").astype(jnp.int32)
    batch = lax.axis_index("batch").astype(jnp.int32)
    y, z = own & 1, own >> 1
    core, xs = batch & 1, batch >> 1
    place = jnp.stack([core, xs, y, z])
    x = tokens.reshape(rows, D)
    g = output_grad.reshape(rows, D)
    over_core = lambda v: flipped(v, "batch", 1)
    over_x = lambda v: flipped(v, "batch", 2)
    over_y = lambda v: flipped(v, "seq", 1)
    over_z = lambda v, bit: flipped(v, "seq", 2 << bit)
    z_bits = depth.bit_length() - 1
    flat = lambda v: v.reshape(rows, -1)

    def pair(mine, other, index, axis):
        first = jnp.where(index == 0, mine, other)
        second = jnp.where(index == 0, other, mine)
        return jnp.concatenate([first, second], axis=axis)

    def summed(*parts):
        return tree_sum(parts).astype(BF16)

    x_other, g_other = over_core(x), over_core(g)
    tables = rotary_tables(own * span, span)
    kv, first_in = project_keys(x, ln1_gain, ln1_bias, qkv_weight, qkv_bias, tables)
    kv3 = kv.reshape(seqs, span, 128)
    kv_y = over_y(kv3)
    first_other = over_core(first_in)
    q = project_queries(first_in, qkv_weight, qkv_bias, tables)
    (kv_y,) = after((kv_y,), q)
    two = jnp.stack([kv3, kv_y])
    pairs = [two] + [along(two, k) for k in range(1, depth)]

    x_fed, g_fed, first_other = after((x, g, first_other), two)
    (mlp, mlp_other, back, back_other, attn_grad, b1_grad, theirs1, mine1), (theirs2, mine2) = feed(
        place, count, *after((x_fed, x_other, g_fed, g_other), first_other), ln2_gain, ln2_bias, fc1_weight, fc1_bias.reshape(1, -1),
        fc2_weight, out_weight,
    )
    come1 = over_x(theirs1)
    come2 = over_z(theirs2, 0)
    mlp_come, back_come = over_core(mlp_other), over_core(back_other)

    q3, do3 = q.reshape(seqs, span, D), attn_grad.reshape(seqs, span, D)
    out, q_rows, even, odd = attention(place, pairs, q3, do3, tables)
    odd = over_y(odd)

    def halved(a, parts, height):
        return a.reshape(parts, 2, height, a.shape[-1])

    out, q_rows = flat(out), flat(q_rows)
    out_other, q_other = over_core(out), over_core(q_rows)
    mine1, come1, come2, mlp_come, back_come = after((mine1, come1, come2, mlp_come, back_come), out)
    view = lambda v: halved(v, depth // 2, per1)
    theirs1, mine1 = add_split(place, [(view(mine1), view(come1), 3)])
    come1 = over_z(theirs1, 0)

    out_other, q_other = after((out_other, q_other), theirs1)
    theirs3, mine3, early = weights(place, count, out, out_other, g, g_other, first_in, first_other, q_rows, q_other)
    come3 = over_y(theirs3)

    even, odd = after((even, odd), theirs3)
    kv_sums = [summed(even[k], odd[k]) for k in range(depth)]
    got = [along(kv_sums[k], -k) for k in range(1, depth)]

    mine2, come2 = after((mine2, come2), *kv_sums)
    height = per2 // 2
    view = lambda v: halved(v, half_depth, height)
    theirs2, mine2 = add_split(place, [(view(mine2), view(come2), 1)])
    come2 = over_x(theirs2)

    (x_mix,) = after((x,), theirs2)
    output = mix(x_mix, mlp, mlp_come, out, out_bias, out_weight)

    mine1, come1 = after((mine1, come1), output)
    view = lambda v: halved(v, depth // 2, per1 // 2)
    theirs1, mine1 = add_split(place, [(view(mine1), view(come1), 2)])
    come1 = over_y(theirs1)
    mine3, come3 = after((mine3, come3), theirs1)
    view3 = lambda v: halved(v, depth, per1)
    theirs3, mine3 = add_split(place, [(view3(mine3), view3(come3), 3)])
    come3 = over_z(theirs3, 0)

    got = after(got, theirs3)
    lines = message_lines(ff)
    tokens_grad, theirs4, mine4 = finish(
        place, count, ff, [flat(v) for v in (kv_sums[0], *got)], flat(key_value_grad), x, g, q_rows, back, back_come,
        ln1_gain, ln1_bias, ln2_gain, qkv_weight, tables, b1_grad, early,
    )
    come4 = over_y(theirs4)

    mine2, come2 = after((mine2, come2), tokens_grad)
    view = lambda v: halved(v, half_depth // 2, height)
    theirs2, mine2 = add_split(place, [(view(mine2), view(come2), 2)])
    come2 = over_y(theirs2)
    mine4, come4 = after((mine4, come4), theirs2)
    theirs4, mine4 = message_step(place, mine4, come4, lines, per1, 0)
    come4 = over_z(theirs4, 0)
    mine1, come1, mine3, come3 = after((mine1, come1, mine3, come3), theirs4)
    for bit in range(1, z_bits):
        parts = depth >> (bit + 1)
        view3 = lambda v: halved(v, 2 * parts, per1)
        view1 = lambda v: halved(v, parts, per1 // 2)
        theirs3, mine3, theirs1, mine1 = add_split(
            place, [(view3(mine3), view3(come3), 3 + bit), (view1(mine1), view1(come1), 3 + bit)]
        )
        come3, come1 = over_z(theirs3, bit), over_z(theirs1, bit)
    mine4, come4 = after((mine4, come4), theirs3)
    for bit in range(1, z_bits):
        theirs4, mine4 = message_step(place, mine4, come4, lines, per1, bit)
        come4 = over_z(theirs4, bit)
    mine2, come2 = after((mine2, come2), theirs4)
    for bit in range(1, z_bits - 1):
        view = lambda v: halved(v, half_depth >> (bit + 1), height)
        theirs2, mine2 = add_split(place, [(view(mine2), view(come2), 3 + bit)])
        come2 = over_z(theirs2, bit)
    sum2 = summed(mine2, come2).reshape(height, D)
    come2 = to_owner(sum2)

    mine3, come3 = after((mine3, come3), sum2)
    sum3 = summed(mine3, come3)
    other3 = over_x(sum3)
    mine4, come4 = after((mine4, come4), sum3)
    (message,) = message_step(place, mine4, come4, lines, per1, 0)
    got = [flipped(message, "batch", i) for i in range(1, batches)]
    mine1, come1 = after((mine1, come1), message)
    sum1 = summed(mine1, come1).reshape(per1 // 2, -1)
    other1 = over_x(sum1)
    sum2, come2 = after((sum2, come2), sum1)
    sum2 = summed(sum2, come2)
    other2 = over_x(sum2)

    sum3, other3 = after((sum3, other3), sum2)
    sum3 = summed(sum3, other3)
    other3 = over_core(sum3)
    sum1, other1 = after((sum1, other1), sum3)
    sum1 = pair(sum1, other1, xs, 0)
    other1 = over_core(sum1)
    got = after(got, sum1)
    widths = (ff,) + (D,) * 6 + (128,)
    b1_sum, q_sum, out_sum, gain1, bias1, gain2, bias2, kv_bias, kv_sum = last_sums([message, *got], lines, widths)

    owner = (z >> (z_bits - 1)) == core
    sum2, other2 = after((sum2, other2), kv_sum)
    sum2 = pair(sum2, other2, xs, 0)
    other2 = over_core(sum2)
    (other3,) = after((other3,), sum2)
    both3 = pair(sum3, other3, core, 2).astype(F32)
    (other1,) = after((other1,), both3)
    fc1_grad = pair(sum1, other1, core, 1).astype(F32)
    (other2,) = after((other2,), fc1_grad)
    fc2_grad = jnp.where(owner, sum2, other2).astype(F32)
    return (
        output.reshape(tokens.shape),
        kv3,
        tokens_grad.reshape(tokens.shape),
        gain1,
        bias1,
        jnp.concatenate([both3[1], kv_sum], axis=1),
        jnp.concatenate([q_sum, kv_bias]),
        both3[0],
        gain2,
        bias2,
        fc1_grad,
        b1_sum,
        fc2_grad,
        out_sum,
    )


def solution(mesh):
    part = P("batch", "seq", None)
    whole = P()
    split = P("seq", None)
    return jax.shard_map(
        local,
        mesh=mesh,
        in_specs=(part,) + (whole,) * 11 + (part, part),
        out_specs=(
            part, part, part, whole, whole, split, whole, split, whole, whole, split, whole, split, whole,
        ),
        check_vma=False,
    )
```

```python
import functools
import math

import jax
import jax.numpy as jnp
from jax import lax
from jax.experimental import pallas as pl
from jax.experimental.pallas import tpu as pltpu
from jax.sharding import PartitionSpec as P

D = 768
HEADS = 12
HEAD_DIM = 64
ROT = 16
PAIRS = HEADS // 2
SCALE = 1.0 / math.sqrt(HEAD_DIM)
NORM_EPS = 1e-05
MASKED = -1e30
F32 = jnp.float32
BF16 = jnp.bfloat16
VMEM_BYTES = 56 * 1024 * 1024


def dot(a, b):
    return lax.dot_general(a, b, (((1,), (0,)), ((), ())), preferred_element_type=F32)


def dot_nt(a, b):
    return lax.dot_general(a, b, (((1,), (1,)), ((), ())), preferred_element_type=F32)


def dot_tn(a, b):
    return lax.dot_general(a, b, (((0,), (0,)), ((), ())), preferred_element_type=F32)


def params():
    return pltpu.CompilerParams(vmem_limit_bytes=VMEM_BYTES)


def flipped(block, axis, bits):
    return lax.ppermute(block, axis, [(i, i ^ bits) for i in range(lax.axis_size(axis))])


def along(block, distance):
    size = lax.axis_size("seq")
    return lax.ppermute(block, "seq", [(i, (i + 2 * distance) % size) for i in range(size)])


def to_owner(block):
    size = lax.axis_size("seq")
    route = []
    for b in range(lax.axis_size("batch")):
        for i in range(size):
            j = i ^ (size // 2)
            if j // (size // 2) == b % 2:
                route.append((b * size + i, b * size + j))
    return lax.ppermute(block, ("batch", "seq"), route)


def after(values, *others):
    return lax.optimization_barrier((tuple(values), others))[0]


def tree_sum(parts):
    parts = [p.astype(F32) for p in parts]
    while len(parts) > 1:
        parts = [sum(parts[i : i + 2][1:], parts[i]) for i in range(0, len(parts), 2)]
    return parts[0]


def take(block, index, axis):
    return lax.dynamic_index_in_dim(block, index, axis, keepdims=False)


def normalize(rows):
    centre = jnp.mean(rows, axis=-1, keepdims=True)
    centred = rows - centre
    spread = jnp.mean(centred * centred, axis=-1, keepdims=True)
    inverse = lax.rsqrt(spread + NORM_EPS)
    return centred * inverse, inverse


def rotary_tables(first, count):
    lane = jnp.arange(128) % HEAD_DIM
    half = ROT // 2
    freqs = 10000.0 ** (-(lane % half).astype(F32) / half)
    places = (first + jnp.arange(count)).astype(F32) * 0.25
    angles = places[:, None] * freqs[None, :]
    cosine, sine = jnp.cos(angles), jnp.sin(angles)
    return jnp.stack(
        [
            jnp.where(lane < ROT, cosine, 1.0),
            jnp.where((lane >= half) & (lane < ROT), sine, 0.0),
            jnp.where(lane < half, -sine, 0.0),
        ]
    )


def turn(values, tables, sign):
    moved = pltpu.roll(values, ROT // 2, 1) * tables[1] + pltpu.roll(values, 128 - ROT // 2, 1) * tables[2]
    return values * tables[0] + (moved if sign > 0 else -moved)


def repeated(tables_ref, count):
    return [jnp.concatenate([tables_ref[i]] * count, axis=0) for i in range(3)]


def key_tables(tables):
    low = lax.broadcasted_iota(jnp.int32, (1, 128), 1) < HEAD_DIM
    return [jnp.where(low, tables[0], 1.0), jnp.where(low, tables[1], 0.0), jnp.where(low, tables[2], 0.0)]

VMEM = pl.BlockSpec(memory_space=pltpu.VMEM)
SMEM = pl.BlockSpec(memory_space=pltpu.SMEM)
SHAPE = jax.ShapeDtypeStruct


def cost(share):
    return pl.CostEstimate(flops=int(share * 3e9), bytes_accessed=0, transcendentals=0)


def wide(ref):
    return ref[...].reshape(1, -1)


def add_split(place, items, share=1.2):
    def kernel(place_ref, *refs):
        sources, results = refs[: 2 * len(items)], refs[2 * len(items) :]
        for n, (_, _, which) in enumerate(items):
            a, b = sources[2 * n], sources[2 * n + 1]
            own = place_ref[which] if which < 3 else lax.rem(lax.shift_right_logical(place_ref[3], which - 3), 2)
            for m in range(a.shape[0]):
                for result, at in ((results[2 * n], 1 - own), (results[2 * n + 1], own)):
                    result[m] = (a[m, at].astype(F32) + b[m, at].astype(F32)).astype(BF16)

    shapes = []
    for a, _, _ in items:
        shapes += [SHAPE((a.shape[0],) + a.shape[2:], BF16)] * 2
    arrays = [v for item in items for v in item[:2]]
    return pl.pallas_call(
        kernel,
        in_specs=[SMEM] + [VMEM] * len(arrays),
        out_specs=[VMEM] * len(shapes),
        out_shape=shapes,
        compiler_params=params(),
        cost_estimate=cost(share),
        name="add_split",
    )(place, *arrays)


def exchange_split(place, mine1, come1, mine2, come2):
    def kernel(place_ref, a1, b1, a2, b2, theirs, keep1, keep2):
        y = place_ref[2]
        row = 0
        for a, b, keep in ((a1, b1, keep1), (a2, b2, keep2)):
            m, _, r, c = a.shape
            part = a[:, pl.ds(1 - y, 1)].astype(F32) + b[:, pl.ds(1 - y, 1)].astype(F32)
            part = part.reshape(m * r, c).astype(BF16)
            for at in range(0, c, D // 2):
                theirs[row : row + m * r] = part[:, at : at + D // 2]
                row += m * r
            part = a[:, pl.ds(y, 1)].astype(F32) + b[:, pl.ds(y, 1)].astype(F32)
            keep[...] = part.reshape(m, r, c).astype(BF16)

    shapes = [(a.shape[0],) + a.shape[2:] for a in (mine1, mine2)]
    size = sum(math.prod(s) for s in shapes)
    return pl.pallas_call(
        kernel,
        in_specs=[SMEM] + [VMEM] * 4,
        out_specs=[VMEM] * 3,
        out_shape=[SHAPE((size // (D // 2), D // 2), BF16)] + [SHAPE(s, BF16) for s in shapes],
        compiler_params=params(),
        cost_estimate=cost(1.2),
        name="exchange_split",
    )(place, mine1, come1, mine2, come2)


def exchange_add(place, mine1, mine2, come, bit):
    def kernel(place_ref, a1, a2, b, theirs, keep, total):
        row = 0
        parts = []
        for a in (a1, a2):
            m, r, c = a.shape
            columns = []
            for _ in range(0, c, D // 2):
                columns.append(b[row : row + m * r])
                row += m * r
            parts.append(jnp.concatenate(columns, axis=1).astype(F32).reshape(m, r, c))
        own = (place_ref[3] >> bit) & 1
        total[...] = (a2[...].astype(F32) + parts[1]).astype(BF16)
        both = (a1[...].astype(F32) + parts[0]).astype(BF16)
        m, r, c = a1.shape
        both = both.reshape(m // 2, 2, r, c)
        lower, upper = both[:, 0], both[:, 1]
        theirs[...] = jnp.where(own == 0, upper, lower)
        keep[...] = jnp.where(own == 0, lower, upper)

    half = SHAPE((mine1.shape[0] // 2,) + mine1.shape[1:], BF16)
    return pl.pallas_call(
        kernel,
        in_specs=[SMEM] + [VMEM] * 3,
        out_specs=[VMEM] * 3,
        out_shape=[half, half, SHAPE(mine2.shape, BF16)],
        compiler_params=params(),
        cost_estimate=cost(0.01),
        name="exchange_add",
    )(place, mine1, mine2, come)


def add_cut(place, a, b):
    parts = a.shape[1]

    def kernel(place_ref, a_ref, b_ref, *results):
        for i in range(parts):
            at = place_ref[3] ^ i
            for k in range(a.shape[0]):
                results[i][k] = (a_ref[k, at].astype(F32) + b_ref[k, at].astype(F32)).astype(BF16)

    return pl.pallas_call(
        kernel,
        in_specs=[SMEM, VMEM, VMEM],
        out_specs=[VMEM] * parts,
        out_shape=[SHAPE((a.shape[0],) + a.shape[2:], BF16)] * parts,
        compiler_params=params(),
        cost_estimate=cost(1.2),
        name="add_cut",
    )(place, a, b)


def keys_kernel(copies, x_ref, gain_ref, bias_ref, weight_ref, add_ref, tables_ref, kv_ref, first_ref):
    normed, _ = normalize(x_ref[...].astype(F32))
    first_in = (normed * wide(gain_ref) + wide(bias_ref)).astype(BF16)
    first_ref[...] = first_in
    part = dot(first_in, weight_ref[...]) + wide(add_ref)[:, D:]
    kv_ref[...] = turn(part, key_tables(repeated(tables_ref, copies)), 1).astype(BF16)


def queries_kernel(copies, first_ref, weight_ref, add_ref, tables_ref, q_ref):
    first_in = first_ref[...]
    tables = repeated(tables_ref, copies)
    bias = wide(add_ref)
    for p in range(PAIRS):
        columns = slice(p * 128, (p + 1) * 128)
        part = dot(first_in, weight_ref[:, columns]) + bias[:, columns]
        q_ref[:, columns] = (turn(part, tables, 1) * SCALE).astype(BF16)


def project_keys(x, gain, bias, weight, add, tables):
    rows = x.shape[0]
    whole = lambda a: pl.BlockSpec(a.shape, lambda i: (0,) * a.ndim)
    return pl.pallas_call(
        functools.partial(keys_kernel, rows // tables.shape[1]),
        grid=(1,),
        in_specs=[
            whole(x),
            whole(gain),
            whole(bias),
            pl.BlockSpec((D, 128), lambda i: (0, D // 128)),
            whole(add),
            whole(tables),
        ],
        out_specs=[pl.BlockSpec((rows, 128), lambda i: (0, 0)), pl.BlockSpec((rows, D), lambda i: (0, 0))],
        out_shape=[SHAPE((rows, 128), BF16), SHAPE((rows, D), BF16)],
        compiler_params=params(),
        cost_estimate=cost(1),
        name="project_keys",
    )(x, gain, bias, weight, add, tables)


def project_queries(first_in, weight, add, tables):
    rows = first_in.shape[0]
    whole = lambda a: pl.BlockSpec(a.shape, lambda i: (0,) * a.ndim)
    return pl.pallas_call(
        functools.partial(queries_kernel, rows // tables.shape[1]),
        grid=(1,),
        in_specs=[
            whole(first_in),
            pl.BlockSpec((D, D), lambda i: (0, 0)),
            whole(add),
            whole(tables),
        ],
        out_specs=pl.BlockSpec((rows, D), lambda i: (0, 0)),
        out_shape=SHAPE((rows, D), BF16),
        compiler_params=params(),
        cost_estimate=cost(2),
        name="project_queries",
    )(first_in, weight, add, tables)


def gelu_parts(h):
    t = pl.reciprocal(1.0 + (0.3275911 / math.sqrt(2.0)) * jnp.abs(h))
    e = jnp.exp(-0.5 * h * h)
    poly = 0.5 * 1.061405429
    for coefficient in (-1.453152027, 1.421413741, -0.284496736, 0.254829592):
        poly = poly * t + 0.5 * coefficient
    tail = poly * t * e
    cdf = jnp.where(h >= 0.0, 1.0 - tail, tail)
    return h * cdf, cdf + h * e * (1.0 / math.sqrt(2.0 * math.pi))


def feed_kernel(
    place_ref,
    x_ref,
    xx_ref,
    g_ref,
    gg_ref,
    gain_ref,
    bias_ref,
    w1_ref,
    b1_ref,
    w2_ref,
    wo_ref,
    mlp_ref,
    back_ref,
    other_ref,
    attn_grad_ref,
    b1_grad_ref,
    theirs1_ref,
    mine1_ref,
    *refs,
):
    grad_refs, (in_scr, in_t_scr, g_scr, mlp_scr, back_scr) = refs[:-5], refs[-5:]
    step, steps = pl.program_id(0), pl.num_programs(0)
    rows = x_ref.shape[0]

    @pl.when(step == 0)
    def _():
        for i, (tokens, grads) in enumerate(((x_ref, g_ref), (xx_ref, gg_ref))):
            at = slice(i * rows, (i + 1) * rows)
            normed, _ = normalize(tokens[...].astype(F32))
            second_in = normed * wide(gain_ref) + wide(bias_ref)
            in_scr[at] = second_in.astype(BF16)
            in_t_scr[:, :, :, at] = second_in.T.astype(BF16).reshape(in_t_scr.shape[:3] + (rows,))
            g_scr[at] = grads[...]
        attn_grad_ref[...] = dot_nt(g_ref[...], wo_ref[...]).astype(BF16)

    g = g_scr[...]
    w1 = w1_ref[...]
    w2 = w2_ref[...]
    act, slope = gelu_parts(dot(in_scr[...], w1) + b1_ref[...])
    act = act.astype(BF16)
    pre = dot_nt(g, w2) * slope
    pre16 = pre.astype(BF16)
    b1_grad_ref[...] = jnp.sum(pre, axis=0, keepdims=True)
    mlp = dot(act, w2)
    grad = dot_tn(act, g).astype(BF16)
    if len(grad_refs) == 1:
        grad_refs[0][...] = grad
    for i in range(len(grad_refs) if len(grad_refs) > 1 else 0):

        @pl.when(step == i)
        def _(i=i):
            grad_refs[i][...] = grad

    back = dot_nt(pre16, w1)
    own = place_ref[1]
    for result, at in ((theirs1_ref, 1 - own), (mine1_ref, own)):
        left = in_t_scr[:, pl.ds(at, 1)].reshape(D // 2, 2 * rows)
        result[...] = dot(left, pre16).astype(BF16).reshape(result.shape)

    @pl.when(step == 0)
    def _():
        mlp_scr[...] = mlp
        back_scr[...] = back

    @pl.when((step > 0) & (step < steps - 1))
    def _():
        mlp_scr[...] += mlp
        back_scr[...] += back

    @pl.when(step == steps - 1)
    def _():
        for i, (scr, last, own_ref) in enumerate(((mlp_scr, mlp, mlp_ref), (back_scr, back, back_ref))):
            total = (scr[...] + last).astype(BF16)
            own_ref[...] = total[:rows]
            other_ref[i] = total[rows:]


CHUNK = 512


def feed(place, count, x, xx, g, gg, gain, bias, w1, b1, w2, wo):
    rows = x.shape[0]
    half = w1.shape[1] // 2
    depth = count // 2
    per = D // count // 2
    pieces = depth // 2
    aligned = pieces == 2 and half % 512 == 0
    chunk = half // pieces if aligned else CHUNK
    steps = half // chunk
    single = pl.Buffered(1)
    whole = lambda a: pl.BlockSpec(a.shape, lambda i, place: (0,) * a.ndim, pipeline_mode=single)
    fixed = lambda *shape: pl.BlockSpec(shape, lambda i, place: (0, 0))
    if aligned:
        piece = lambda i, place: (place[3] ^ (1 - i)) & 1
        grad_specs = [fixed(chunk, D)] * pieces
        grad_shapes = [SHAPE((chunk, D), BF16)] * pieces
    else:
        piece = lambda i, place: i
        grad_specs = [pl.BlockSpec((chunk, D), lambda i, place: (i, 0))]
        grad_shapes = [SHAPE((half, D), BF16)]
    at = lambda i, place: place[0] * steps + piece(i, place)
    cut = pl.BlockSpec((count, per, chunk), lambda i, place: (0, 0, piece(i, place)))
    spec = pltpu.PrefetchScalarGridSpec(
        num_scalar_prefetch=1,
        grid=(steps,),
        in_specs=[
            whole(x),
            whole(xx),
            whole(g),
            whole(gg),
            whole(gain),
            whole(bias),
            pl.BlockSpec((D, chunk), lambda i, place: (0, at(i, place))),
            pl.BlockSpec((1, chunk), lambda i, place: (0, at(i, place))),
            pl.BlockSpec((chunk, D), lambda i, place: (at(i, place), 0)),
            whole(wo),
        ],
        out_specs=[
            fixed(rows, D),
            fixed(rows, D),
            pl.BlockSpec((2, rows, D), lambda i, place: (0, 0, 0)),
            fixed(rows, D),
        ]
        + [pl.BlockSpec((1, chunk), lambda i, place: (0, piece(i, place))), cut, cut]
        + grad_specs,
        scratch_shapes=[
            pltpu.VMEM((2 * rows, D), BF16),
            pltpu.VMEM((count, 2, per, 2 * rows), BF16),
            pltpu.VMEM((2 * rows, D), BF16),
            pltpu.VMEM((2 * rows, D), F32),
            pltpu.VMEM((2 * rows, D), F32),
        ],
    )
    result = pl.pallas_call(
        feed_kernel,
        grid_spec=spec,
        out_shape=[SHAPE((rows, D), BF16), SHAPE((rows, D), BF16), SHAPE((2, rows, D), BF16), SHAPE((rows, D), BF16)]
        + [SHAPE((1, half), F32), SHAPE((count, per, half), BF16), SHAPE((count, per, half), BF16)]
        + grad_shapes,
        compiler_params=params(),
        cost_estimate=cost(12),
        name="feed_forward",
    )(place, x, xx, g, gg, gain, bias, w1, b1, w2, wo)
    grads = result[7:]
    if not aligned:
        cut = grads[0].reshape(pieces // 2, 2, -1, D)
        low = place[3] & 1
        grads = [take(cut, 1 - low, 1), take(cut, low, 1)]
    return result[:7], grads


def present(slot, y, z):
    back = slot // 2
    return (back <= z) & ((slot % 2 == 0) | (back >= 1) | (y == 1))


def whole_kernel(span, depth, place_ref, *refs):
    pair_refs, (q_ref, do_ref, tables_ref, rows_ref, even_out_ref, odd_out_ref) = refs[:depth], refs[depth:]
    out_ref, dq_ref = rows_ref.at[0], rows_ref.at[1]
    y, z = place_ref[2], place_ref[3]
    tables = [tables_ref[i] for i in range(3)]
    rows = PAIRS * span
    low = lax.broadcasted_iota(jnp.int32, (1, 128), 1) < HEAD_DIM

    def stacked(ref):
        return jnp.concatenate([ref[:, p * 128 : (p + 1) * 128] for p in range(PAIRS)], axis=0)

    blocks = [ref[i] for ref in pair_refs for i in range(2)]
    kv = jnp.concatenate(blocks, axis=0)
    swapped = pltpu.roll(kv.astype(F32), HEAD_DIM, 1).astype(BF16)
    zero, one = jnp.zeros_like(kv), jnp.ones_like(kv)
    keys = (jnp.where(low, kv, zero), jnp.where(low, zero, swapped))
    values = (jnp.where(low, swapped, zero), jnp.where(low, zero, kv))
    summing = (jnp.where(low, swapped, one), jnp.where(low, one, kv))
    slot = lax.broadcasted_iota(jnp.int32, (1, (2 * depth - 1) * span), 1) // span + 1
    absent = jnp.where(present(slot, y, z), 0.0, MASKED)
    token = lax.broadcasted_iota(jnp.int32, (rows, span), 0) % span
    seen = lax.broadcasted_iota(jnp.int32, (rows, span), 1) <= token
    q = stacked(q_ref)
    do = stacked(do_ref)
    do32 = do.astype(F32)

    expd, mixed = [], []
    for h in range(2):
        scores = dot_nt(q, keys[h])
        scores = jnp.concatenate([jnp.where(seen, scores[:, :span], MASKED), scores[:, span:] + absent], axis=1)
        top = jnp.max(scores, axis=1, keepdims=True)
        expd.append(jnp.exp(scores - top).astype(BF16))
        mixed.append(dot(expd[h], summing[h]))
    total = jnp.where(low, pltpu.roll(mixed[0], HEAD_DIM, 1), pltpu.roll(mixed[1], HEAD_DIM, 1))
    inverse = 1.0 / total
    out = jnp.where(low, mixed[0], mixed[1]) * inverse
    for p in range(PAIRS):
        out_ref[:, p * 128 : (p + 1) * 128] = out[p * span : (p + 1) * span].astype(BF16)
    product = do32 * out
    do_t = (do32 * inverse).T.astype(BF16)
    q_t = (q.astype(F32) * inverse).T.astype(BF16)
    dq = dk = dv = 0.0
    for h in range(2):
        head = slice(h * HEAD_DIM, (h + 1) * HEAD_DIM)
        delta = jnp.sum(jnp.where(low == (h == 0), product, 0.0), axis=1, keepdims=True)
        dprob = dot_nt(do, values[h])
        dscore = (expd[h].astype(F32) * (dprob - delta)).astype(BF16)
        dq = dq + dot(dscore, keys[h])
        dk = dk + dot(q_t[head], dscore)
        dv = dv + dot(do_t[head], expd[h])
    dq = dq * (inverse * SCALE)
    for p in range(PAIRS):
        dq_ref[:, p * 128 : (p + 1) * 128] = turn(dq[p * span : (p + 1) * span], tables, -1).astype(BF16)
    both = jnp.concatenate([dk, dv], axis=0).T.astype(BF16)
    for k in range(depth):
        even_out_ref[k] = both[2 * k * span : (2 * k + 1) * span]
        odd_out_ref[k] = both[(2 * k + 1) * span : (2 * k + 2) * span]


def loop_kernel(groups, span, block, count, place_ref, *refs):
    depth = count // 2
    pair_refs, refs = refs[:depth], refs[depth:]
    q_ref, do_ref, tables_ref, rows_ref, even_out_ref, odd_out_ref = refs[:6]
    out_ref, dq_ref = rows_ref.at[0], rows_ref.at[1]
    kv_scr, e_ref, kv_t_ref, max_ref, acc_ref, ext_ref = refs[6:]
    tables = [tables_ref[i] for i in range(3)]
    rows = groups * span
    per = block // span
    y, z = place_ref[2], place_ref[3]
    used = (2 * (z + 1) + per - 1) // per
    group, group_count = pl.program_id(1), pl.num_programs(1)
    low = lax.broadcasted_iota(jnp.int32, (1, 128), 1) < HEAD_DIM
    lanes = lax.broadcasted_iota(jnp.int32, (rows, 128), 1)

    def stacked(ref):
        return jnp.concatenate([ref[:, p * 128 : (p + 1) * 128] for p in range(groups)], axis=0)

    @pl.when(group == 0)
    def _():
        for i in range(count):
            kv_scr[i * span : (i + 1) * span] = pair_refs[i // 2][i % 2]

    q = stacked(q_ref)
    do = stacked(do_ref)

    def load(b):
        kv = kv_scr[pl.ds(pl.multiple_of(b * block, block), block)]
        swapped = pltpu.roll(kv.astype(F32), HEAD_DIM, 1).astype(BF16)
        return kv, swapped, jnp.zeros_like(kv)

    def absent(b):
        row = lax.broadcasted_iota(jnp.int32, (block, 128), 0) + b * block
        lane = lax.broadcasted_iota(jnp.int32, (block, 128), 1)
        mask = jnp.where(present(row // span, y, z), 0.0, MASKED)
        return jnp.where(lane < 2, -1.0, jnp.where(lane == 2, mask, 0.0)).astype(BF16)

    def key_tiles(b):
        kv, swapped, zero = load(b)
        ext = absent(b)
        return [
            jnp.concatenate([jnp.where(low, kv, zero), ext], axis=1),
            jnp.concatenate([jnp.where(low, zero, swapped), ext], axis=1),
        ]

    def value_tiles(b):
        kv, swapped, zero = load(b)
        ext = absent(b)
        return [
            jnp.concatenate([jnp.where(low, swapped, zero), ext], axis=1),
            jnp.concatenate([jnp.where(low, zero, kv), ext], axis=1),
        ]

    def seen():
        token = lax.broadcasted_iota(jnp.int32, (rows, block), 0) % span
        key = lax.broadcasted_iota(jnp.int32, (rows, block), 1)
        return (key <= token) | (key >= span)

    def extended(values):
        high = values.astype(BF16).astype(F32)
        rest = jnp.where(lanes == 1, values - high, jnp.where(lanes == 2, 1.0, 0.0))
        return jnp.where(lanes == 0, high, rest).astype(BF16)

    def over_blocks(step):
        step(0, True)

        def body(b, carry):
            step(b, False)
            return carry

        lax.fori_loop(1, used, body, 0)

    plain = jnp.concatenate([q, jnp.where(lanes == 2, 1.0, 0.0).astype(BF16)], axis=1)

    def maxima(b, diagonal):
        keys = key_tiles(b)
        for h in range(2):
            scores = dot_nt(plain, keys[h])
            if diagonal:
                scores = jnp.where(seen(), scores, MASKED)
            top = functools.reduce(jnp.maximum, [scores[:, i : i + 128] for i in range(0, block, 128)])
            max_ref[h] = top if diagonal else jnp.maximum(max_ref[h], top)

    over_blocks(maxima)
    for h in range(2):
        top = jnp.max(max_ref[h], axis=1, keepdims=True)
        ext_ref[h] = jnp.concatenate([q, extended(jnp.broadcast_to(top, (rows, 128)))], axis=1)

    def forward(b, diagonal):
        keys = key_tiles(b)
        kv, swapped, _ = load(b)
        one = jnp.ones_like(kv)
        values = (jnp.where(low, swapped, one), jnp.where(low, one, kv))
        for h in range(2):
            expd = jnp.exp(dot_nt(ext_ref[h], keys[h]))
            if diagonal:
                expd = jnp.where(seen(), expd, 0.0)
            expd = expd.astype(BF16)
            e_ref[b, h] = expd
            mixed = dot(expd, values[h])
            acc_ref[h] = mixed if diagonal else acc_ref[h] + mixed

    over_blocks(forward)
    first, second = acc_ref[0], acc_ref[1]
    total = jnp.where(low, pltpu.roll(first, HEAD_DIM, 1), pltpu.roll(second, HEAD_DIM, 1))
    inverse = 1.0 / total
    out = jnp.where(low, first, second) * inverse
    for p in range(groups):
        out_ref[:, p * 128 : (p + 1) * 128] = out[p * span : (p + 1) * span].astype(BF16)
    do32 = do.astype(F32)
    product = do32 * out
    high = product.astype(BF16)
    rest = (product - high.astype(F32)).astype(BF16)
    place = lax.broadcasted_iota(jnp.int32, (128, 128), 0)
    for h in range(2):
        ones = jnp.where((place < HEAD_DIM) == (h == 0), 1.0, 0.0).astype(BF16)
        delta = dot(high, ones) + dot(rest, ones)
        ext_ref[h] = jnp.concatenate([do, extended(delta)], axis=1)
    do_t = (do32 * inverse).T.astype(BF16)
    q_t = (q.astype(F32) * inverse).T.astype(BF16)

    def backward(b, start):
        values = value_tiles(b)
        kv, swapped, zero = load(b)
        keys = (jnp.where(low, kv, zero), jnp.where(low, zero, swapped))
        dq = dk = dv = 0.0
        for h in range(2):
            expd = e_ref[b, h]
            head = slice(h * HEAD_DIM, (h + 1) * HEAD_DIM)
            dscore = (expd.astype(F32) * dot_nt(ext_ref[h], values[h])).astype(BF16)
            dq = dq + dot(dscore, keys[h])
            dk = dk + dot(q_t[head], dscore)
            dv = dv + dot(do_t[head], expd)
        acc_ref[0] = dq if start else acc_ref[0] + dq
        both = jnp.concatenate([dk, dv], axis=0)
        kv_t_ref[b] = jnp.where(group == 0, both, kv_t_ref[b] + both)

    over_blocks(backward)
    dq = acc_ref[0] * (inverse * SCALE)
    for p in range(groups):
        dq_ref[:, p * 128 : (p + 1) * 128] = turn(dq[p * span : (p + 1) * span], tables, -1).astype(BF16)

    @pl.when(group == group_count - 1)
    def _():
        for b in range(count // per):
            used_block = jnp.where(b < used, kv_t_ref[b], 0.0).T.astype(BF16)
            for i in range(per):
                slot = b * per + i
                result = odd_out_ref if slot % 2 else even_out_ref
                result[slot // 2] = used_block[i * span : (i + 1) * span]


def attention(place, pairs, q, do, tables):
    depth = len(pairs)
    count = 2 * depth
    seqs, span, _ = q.shape
    single = count * span <= 1024
    groups = PAIRS if single else 2
    wide_spec = pl.BlockSpec((None, span, groups * 128), lambda s, i: (s, 0, i))
    pieces = pl.BlockSpec((depth, None, span, 128), lambda s, i: (0, s, 0, 0))
    two = pl.BlockSpec((2, None, span, 128), lambda s, i: (0, s, 0, 0))
    if single:
        kernel, scratch = functools.partial(whole_kernel, span, depth), []
    else:
        block = max(512, span)
        blocks = count * span // block
        rows = groups * span
        kernel = functools.partial(loop_kernel, groups, span, block, count)
        scratch = [
            pltpu.VMEM((count * span, 128), BF16),
            pltpu.VMEM((blocks, 2, rows, block), BF16),
            pltpu.VMEM((blocks, 128, block), F32),
            pltpu.VMEM((2, rows, 128), F32),
            pltpu.VMEM((2, rows, 128), F32),
            pltpu.VMEM((2, rows, 256), BF16),
        ]
    return pl.pallas_call(
        kernel,
        grid=(seqs, PAIRS // groups),
        in_specs=[SMEM] + [two] * depth + [wide_spec, wide_spec, pl.BlockSpec(tables.shape, lambda s, i: (0, 0, 0))],
        out_specs=[pl.BlockSpec((2, None, span, groups * 128), lambda s, i: (0, s, 0, i))] + [pieces] * 2,
        out_shape=[SHAPE((2, seqs, span, D), BF16)]
        + [SHAPE((depth, seqs, span, 128), BF16)] * 2,
        scratch_shapes=scratch,
        compiler_params=params(),
        cost_estimate=cost(10),
        name="attention",
    )(place, *pairs, q, do, tables)


def weights_kernel(place_ref, attn_ref, attn2_ref, g_ref, g2_ref, in_ref, in2_ref, q_ref, q2_ref, theirs_ref, mine_ref, small_ref, scr):
    half = D // 2
    y = place_ref[2]

    def products(left, right, line):
        at = pl.ds(pl.multiple_of(place_ref[0] * half, 128), half)
        small_ref[line : line + 1] = jnp.zeros_like(small_ref[line : line + 1])
        small_ref[line : line + 1, at] = jnp.sum(right.astype(F32), axis=0, keepdims=True)
        scr[...] = dot_tn(left, right).reshape(scr.shape)
        theirs_ref[0] = scr[:, pl.ds(1 - y, 1)].reshape(theirs_ref.shape[1:]).astype(BF16)
        mine_ref[0] = scr[:, pl.ds(y, 1)].reshape(mine_ref.shape[1:]).astype(BF16)

    both = lambda a, b: jnp.concatenate([a[...], b[...]], axis=0)

    @pl.when(pl.program_id(0) == 0)
    def _():
        products(both(attn_ref, attn2_ref), both(g_ref, g2_ref), 1)

    @pl.when(pl.program_id(0) == 1)
    def _():
        products(both(in_ref, in2_ref), both(q_ref, q2_ref), 0)


def weights(place, count, both, both2, g, g2, first_in, first_in2):
    rows = g.shape[0]
    depth, per, half = count // 2, D // count, D // 2
    whole = pl.BlockSpec((rows, D), lambda i, place: (0, 0), pipeline_mode=pl.Buffered(1))
    part = pl.BlockSpec((rows, half), lambda i, place: (0, place[0]), pipeline_mode=pl.Buffered(1))
    attn_part = pl.BlockSpec((None, rows, D), lambda i, place: (0, 0, 0), pipeline_mode=pl.Buffered(1))
    q_part = pl.BlockSpec((None, rows, half), lambda i, place: (1, 0, place[0]), pipeline_mode=pl.Buffered(1))
    result = pl.BlockSpec((1, depth, per, half), lambda i, place: (i, 0, 0, 0))
    return pl.pallas_call(
        weights_kernel,
        grid_spec=pltpu.PrefetchScalarGridSpec(
            num_scalar_prefetch=1,
            grid=(2,),
            in_specs=[attn_part, attn_part, part, part, whole, whole, q_part, q_part],
            out_specs=[result, result, pl.BlockSpec((8, D), lambda i, place: (0, 0))],
            scratch_shapes=[pltpu.VMEM((depth, 2, per, half), F32)],
        ),
        out_shape=[SHAPE((2, depth, per, half), BF16), SHAPE((2, depth, per, half), BF16), SHAPE((8, D), F32)],
        compiler_params=params(),
        cost_estimate=cost(2.4),
        name="weights",
    )(place, both, both2, g, g2, first_in, first_in2, both, both2)


def mix_kernel(x_ref, mlp_ref, mlp2_ref, attn_ref, add_ref, wo_ref, output_ref):
    mlp = mlp_ref[...].astype(F32) + mlp2_ref[...].astype(F32)
    x = x_ref[...].astype(F32)
    output_ref[...] = (x + (mlp + dot(attn_ref[...], wo_ref[...])) + wide(add_ref)).astype(BF16)


def mix(x, mlp, other, both, add, wo):
    rows = x.shape[0]
    row = pl.BlockSpec((rows // 2, D), lambda i: (i, 0))
    first = pl.BlockSpec((None, rows // 2, D), lambda i: (0, i, 0))
    return pl.pallas_call(
        mix_kernel,
        grid=(2,),
        in_specs=[row, row, first, first, pl.BlockSpec((D,), lambda i: (0,)), pl.BlockSpec((D, D), lambda i: (0, 0))],
        out_specs=row,
        out_shape=SHAPE((rows, D), BF16),
        compiler_params=params(),
        cost_estimate=cost(1.2),
        name="mix",
    )(x, mlp, other, both, add, wo)


def two_terms(values):
    high = values.astype(BF16)
    return high, (values - high.astype(F32)).astype(BF16)


def message_lines(ff):
    return -(-(ff // 128 + 6 * (D // 128) + 1) // 16) * 16


def finish_kernel(
    copies,
    count,
    lines,
    place_ref,
    *refs,
):
    kv_refs, refs = refs[:count], refs[count:]
    (
        extra_ref,
        x_ref,
        g_ref,
        q_ref,
        back_ref,
        back2_ref,
        gain_ref,
        bias_ref,
        gain2_ref,
        wqkv_ref,
        tables_ref,
        b1_ref,
        early_ref,
        tokens_ref,
        theirs_ref,
        mine_ref,
        vector_scr,
        weight_scr,
    ) = refs
    total = extra_ref[...].astype(F32)
    for ref in kv_refs:
        total += ref[...].astype(F32)
    tables = repeated(tables_ref, copies)
    grad = turn(total, key_tables(tables), -1).astype(BF16)
    x = x_ref[...].astype(F32)
    normed, inverse = normalize(x)
    gain = wide(gain_ref)
    first_in = normed * gain + wide(bias_ref)
    first_grad = dot_nt(jnp.concatenate([q_ref[...], grad], axis=1), wqkv_ref[...])
    second_grad = back_ref[...].astype(F32) + back2_ref[...].astype(F32)

    vector_scr[...] = jnp.zeros_like(vector_scr)
    b1 = b1_ref[...]
    b1_lines = b1.shape[1] // 128
    for i in range(b1_lines):
        vector_scr[pl.ds(place_ref[0] * b1_lines + i, 1)] = b1[:, i * 128 : (i + 1) * 128]
    at = 2 * b1_lines
    sums = [early_ref[0:1], jnp.sum(grad.astype(F32), axis=0, keepdims=True), early_ref[1:2]]
    for rows in (first_grad * normed, first_grad, second_grad * normed, second_grad):
        sums.append(jnp.sum(rows, axis=0, keepdims=True))
    for row in sums:
        for i in range(row.shape[1] // 128):
            vector_scr[at : at + 1] = row[:, i * 128 : (i + 1) * 128]
            at += 1
    high, rest = two_terms(vector_scr[...])
    weight_scr[...] = dot(first_in.T.astype(BF16), grad).reshape(weight_scr.shape)
    y = place_ref[2]
    for message, at in ((theirs_ref, 1 - y), (mine_ref, y)):
        message[:lines] = high
        message[lines : 2 * lines] = rest
        message[2 * lines :] = weight_scr[:, pl.ds(at, 1)].reshape(-1, 128).astype(BF16)

    normed_grad = first_grad * gain + second_grad * wide(gain2_ref)
    mean = jnp.mean(normed_grad, axis=-1, keepdims=True)
    along_rows = jnp.mean(normed_grad * normed, axis=-1, keepdims=True)
    tokens_ref[...] = (g_ref[...].astype(F32) + inverse * (normed_grad - mean - normed * along_rows)).astype(BF16)


def finish(place, places, ff, kv_parts, extra, x, g, both, back, other, gain, bias, gain2, wqkv, tables, b1, early):
    rows = x.shape[0]
    lines = message_lines(ff)
    whole = lambda a: pl.BlockSpec(a.shape, lambda i: (0,) * a.ndim)
    second = pl.BlockSpec((None, rows, D), lambda i: (1, 0, 0))
    before, between, behind = (*kv_parts, extra, x, g), (back,), (gain, bias, gain2, wqkv, tables, b1, early)
    return pl.pallas_call(
        functools.partial(finish_kernel, rows // tables.shape[1], len(kv_parts), lines),
        grid=(1,),
        in_specs=[SMEM]
        + [whole(a) for a in before]
        + [second]
        + [whole(a) for a in between]
        + [second]
        + [whole(a) for a in behind],
        out_specs=[
            pl.BlockSpec((rows, D), lambda i: (0, 0)),
            pl.BlockSpec((2 * lines + D // 2, 128), lambda i: (0, 0)),
            pl.BlockSpec((2 * lines + D // 2, 128), lambda i: (0, 0)),
        ],
        out_shape=[SHAPE((rows, D), BF16)] + [SHAPE((2 * lines + D // 2, 128), BF16)] * 2,
        scratch_shapes=[pltpu.VMEM((lines, 128), F32), pltpu.VMEM((places // 2, 2, D // places, 128), F32)],
        compiler_params=params(),
        cost_estimate=cost(2.4),
        name="finish",
    )(place, *before, both, *between, other, *behind)


def message_cut(place, mine, come, lines, per):
    count = (mine.shape[0] - 2 * lines) // per

    def kernel(place_ref, a_ref, b_ref, *refs):
        results, scr = refs[:-1], refs[-1]
        high, rest = two_terms(tree_sum([ref[at : at + lines] for ref in (a_ref, b_ref) for at in (0, lines)]))
        scr[...] = (a_ref[2 * lines :].astype(F32) + b_ref[2 * lines :].astype(F32)).reshape(scr.shape)
        for i, result in enumerate(results):
            result[:lines] = high
            result[lines : 2 * lines] = rest
            result[2 * lines :] = scr[place_ref[3] ^ i].astype(BF16)

    return pl.pallas_call(
        kernel,
        in_specs=[SMEM, VMEM, VMEM],
        out_specs=[VMEM] * count,
        out_shape=[SHAPE((2 * lines + per, 128), BF16)] * count,
        scratch_shapes=[pltpu.VMEM((count, per, 128), F32)],
        compiler_params=params(),
        cost_estimate=cost(0.6),
        name="message_cut",
    )(place, mine, come)


def message_sum(messages, lines):
    def kernel(*refs):
        result = refs[-1]
        total = tree_sum([ref[...] for ref in refs[:-1]])
        high, rest = two_terms(total[:lines] + total[lines : 2 * lines])
        result[:lines] = high
        result[lines : 2 * lines] = rest
        result[2 * lines :] = total[2 * lines :].astype(BF16)

    return pl.pallas_call(
        kernel,
        in_specs=[VMEM] * len(messages),
        out_specs=VMEM,
        out_shape=SHAPE(messages[0].shape, BF16),
        compiler_params=params(),
        cost_estimate=cost(0.6),
        name="message_sum",
    )(*messages)


def last_sums(messages, lines, widths):
    rows = messages[0].shape[0] - 2 * lines

    def kernel(*refs):
        sources, results = refs[: len(messages)], refs[len(messages) :]
        total = tree_sum([ref[...] for ref in sources])
        vector = total[:lines] + total[lines : 2 * lines]
        at = 0
        for result, width in zip(results[:-1], widths):
            for i in range(width // 128):
                result[i * 128 : (i + 1) * 128] = vector[at + i]
            at += width // 128
        results[-1][...] = total[2 * lines :]

    return pl.pallas_call(
        kernel,
        in_specs=[VMEM] * len(messages),
        out_specs=[VMEM] * (len(widths) + 1),
        out_shape=[SHAPE((width,), F32) for width in widths] + [SHAPE((rows, 128), F32)],
        compiler_params=params(),
        cost_estimate=cost(0.6),
        name="last_sums",
    )(*messages)


def local(
    tokens,
    ln1_gain,
    ln1_bias,
    qkv_weight,
    qkv_bias,
    out_weight,
    ln2_gain,
    ln2_bias,
    fc1_weight,
    fc1_bias,
    fc2_weight,
    out_bias,
    output_grad,
    key_value_grad,
):
    seqs, span, _ = tokens.shape
    rows = seqs * span
    ff = fc1_weight.shape[1]
    count = lax.axis_size("seq")
    batches = lax.axis_size("batch")
    depth = count // 2
    half_depth = depth // 2
    per1, per2 = D // count, ff // count
    own = lax.axis_index("seq").astype(jnp.int32)
    batch = lax.axis_index("batch").astype(jnp.int32)
    y, z = own & 1, own >> 1
    core, xs = batch & 1, batch >> 1
    place = jnp.stack([core, xs, y, z])
    x = tokens.reshape(rows, D)
    g = output_grad.reshape(rows, D)
    over_core = lambda v: flipped(v, "batch", 1)
    over_x = lambda v: flipped(v, "batch", 2)
    over_y = lambda v: flipped(v, "seq", 1)
    over_z = lambda v, bit: flipped(v, "seq", 2 << bit)
    z_bits = depth.bit_length() - 1
    flat = lambda v: v.reshape(rows, -1)

    def pair(mine, other, index, axis):
        first = jnp.where(index == 0, mine, other)
        second = jnp.where(index == 0, other, mine)
        return jnp.concatenate([first, second], axis=axis)

    def summed(*parts):
        return tree_sum(parts).astype(BF16)

    x_other, g_other = over_core(x), over_core(g)
    tables = rotary_tables(own * span, span)
    kv, first_in = project_keys(x, ln1_gain, ln1_bias, qkv_weight, qkv_bias, tables)
    kv3 = kv.reshape(seqs, span, 128)
    kv_y = over_y(kv3)
    first_other = over_core(first_in)
    q = project_queries(first_in, qkv_weight, qkv_bias, tables)
    (kv_y,) = after((kv_y,), q)
    two = jnp.stack([kv3, kv_y])
    pairs = [two] + [along(two, k) for k in range(1, depth)]

    x_fed, g_fed, first_other = after((x, g, first_other), two)
    (mlp, back, feed_other, attn_grad, b1_grad, theirs1, mine1), (theirs2, mine2) = feed(
        place, count, *after((x_fed, x_other, g_fed, g_other), first_other), ln2_gain, ln2_bias, fc1_weight, fc1_bias.reshape(1, -1),
        fc2_weight, out_weight,
    )
    come1 = over_x(theirs1)
    come2 = over_z(theirs2, 0)
    feed_come = over_core(feed_other)

    q3, do3 = q.reshape(seqs, span, D), attn_grad.reshape(seqs, span, D)
    both, even, odd = attention(place, pairs, q3, do3, tables)
    odd = over_y(odd)

    def halved(a, parts, height):
        return a.reshape(parts, 2, height, a.shape[-1])

    both = both.reshape(2, rows, D)
    both_other = over_core(both)
    mine1, come1, mine2, come2, feed_come = after((mine1, come1, mine2, come2, feed_come), both)
    height = per2 // 2
    view1 = lambda v: halved(v, depth // 2, per1)
    view2 = lambda v: halved(v, half_depth, height)
    theirs1, mine1, theirs2, mine2 = add_split(
        place, [(view1(mine1), view1(come1), 3), (view2(mine2), view2(come2), 1)], 6
    )
    come1, come2 = over_z(theirs1, 0), over_x(theirs2)

    (both_other,) = after((both_other,), theirs1)
    theirs3, mine3, early = weights(place, count, both, both_other, g, g_other, first_in, first_other)
    come3 = over_y(theirs3)

    even, odd = after((even, odd), theirs3)
    kv_sums = [summed(even[k], odd[k]) for k in range(depth)]
    (x_mix,) = after((x,), *kv_sums)
    output = mix(x_mix, mlp, feed_come, both, out_bias, out_weight)
    (kv_next,) = after((kv_sums[1],), output)
    got = [along(kv_next, -1)] + [along(kv_sums[k], -k) for k in range(2, depth)]

    mine1, come1, mine2, come2 = after((mine1, come1, mine2, come2), output)
    view1 = lambda v: halved(v, depth // 2, per1 // 2)
    view2 = lambda v: halved(v, half_depth // 2, height)
    theirs12, mine1, mine2 = exchange_split(place, view1(mine1), view1(come1), view2(mine2), view2(come2))
    come12 = over_y(theirs12)
    mine3, come3 = after((mine3, come3), theirs12)
    parts3 = add_cut(place, mine3, come3)
    come3 = [flipped(parts3[i], "seq", 2 * i) for i in range(1, depth)]

    got = after(got, parts3[0])
    lines = message_lines(ff)
    tokens_grad, theirs4, mine4 = finish(
        place, count, ff, [flat(v) for v in (kv_sums[0], *got)], flat(key_value_grad), x, g, both, back, feed_come,
        ln1_gain, ln1_bias, ln2_gain, qkv_weight, tables, b1_grad, early,
    )
    come4 = over_y(theirs4)

    mine1, mine2, come12 = after((mine1, mine2, come12), tokens_grad)
    theirs1, mine1, sum2 = exchange_add(place, mine1, mine2, come12, 1)
    come1 = over_z(theirs1, 1)
    for bit in range(2, z_bits):
        view1 = lambda v: halved(v, depth >> (bit + 1), per1 // 2)
        theirs1, mine1 = add_split(place, [(view1(mine1), view1(come1), 3 + bit)], 0.01)
        come1 = over_z(theirs1, bit)
    for bit in range(1, z_bits - 1):
        sum2 = halved(sum2, half_depth >> (bit + 1), height)
        own_bit = (z >> bit) & 1
        sum2 = summed(take(sum2, own_bit, 1), over_z(take(sum2, 1 - own_bit, 1), bit))
    sum2 = sum2.reshape(height, D)
    come2 = to_owner(sum2)

    come3 = after(come3, theirs1, sum2)
    sum3 = summed(parts3[0], *come3)
    other3 = over_x(sum3)
    mine4, come4 = after((mine4, come4), sum3)
    parts4 = message_cut(place, mine4, come4, lines, per1)
    come4 = [flipped(parts4[i], "seq", 2 * i) for i in range(1, depth)]
    mine1, come1 = after((mine1, come1), parts4[0])
    sum1 = summed(mine1, come1).reshape(per1 // 2, -1)
    other1 = over_x(sum1)
    sum3, other3 = after((sum3, other3), sum1)
    sum3 = summed(sum3, other3)
    other3 = over_core(sum3)
    sum2, come2 = after((sum2, come2), sum3)
    sum2 = summed(sum2, come2)
    other2 = over_x(sum2)
    come4 = after(come4, sum2)
    message = message_sum([parts4[0], *come4], lines)
    got = [flipped(message, "batch", i) for i in range(1, batches)]
    sum1, other1 = after((sum1, other1), message)

    sum1 = pair(sum1, other1, xs, 0)
    other1 = over_core(sum1)
    sum2, other2 = after((sum2, other2), sum1)
    sum2 = pair(sum2, other2, xs, 0)
    other2 = over_core(sum2)
    got = after(got, sum2)
    widths = (ff, D + 128) + (D,) * 5
    b1_sum, qkv_sum, out_sum, gain1, bias1, gain2, bias2, kv_sum = last_sums([message, *got], lines, widths)

    owner = (z >> (z_bits - 1)) == core
    (other3,) = after((other3,), kv_sum)
    both3 = pair(sum3, other3, core, 2).astype(F32)
    (other1,) = after((other1,), both3)
    fc1_grad = pair(sum1, other1, core, 1).astype(F32)
    (other2,) = after((other2,), fc1_grad)
    fc2_grad = jnp.where(owner, sum2, other2).astype(F32)
    return (
        output.reshape(tokens.shape),
        kv3,
        tokens_grad.reshape(tokens.shape),
        gain1,
        bias1,
        jnp.concatenate([both3[1], kv_sum], axis=1),
        qkv_sum,
        both3[0],
        gain2,
        bias2,
        fc1_grad,
        b1_sum,
        fc2_grad,
        out_sum,
    )


def solution(mesh):
    part = P("batch", "seq", None)
    whole = P()
    split = P("seq", None)
    return jax.shard_map(
        local,
        mesh=mesh,
        in_specs=(part,) + (whole,) * 11 + (part, part),
        out_specs=(
            part, part, part, whole, whole, split, whole, split, whole, whole, split, whole, split, whole,
        ),
        check_vma=False,
    )
```

```python
import functools
import math

import jax
import jax.numpy as jnp
from jax import lax
from jax.experimental import pallas as pl
from jax.experimental.pallas import tpu as pltpu
from jax.sharding import PartitionSpec as P

D = 768
HEADS = 12
HEAD_DIM = 64
ROT = 16
PAIRS = HEADS // 2
SCALE = 1.0 / math.sqrt(HEAD_DIM)
NORM_EPS = 1e-05
MASKED = -1e30
F32 = jnp.float32
BF16 = jnp.bfloat16
VMEM_BYTES = 56 * 1024 * 1024
FULL_BYTES = 63 * 1024 * 1024


def dot(a, b):
    return lax.dot_general(a, b, (((1,), (0,)), ((), ())), preferred_element_type=F32)


def dot_nt(a, b):
    return lax.dot_general(a, b, (((1,), (1,)), ((), ())), preferred_element_type=F32)


def dot_tn(a, b):
    return lax.dot_general(a, b, (((0,), (0,)), ((), ())), preferred_element_type=F32)


def params(limit=VMEM_BYTES):
    return pltpu.CompilerParams(vmem_limit_bytes=limit)


def flipped(block, axis, bits):
    return lax.ppermute(block, axis, [(i, i ^ bits) for i in range(lax.axis_size(axis))])


def along(block, distance):
    size = lax.axis_size("seq")
    return lax.ppermute(block, "seq", [(i, (i + 2 * distance) % size) for i in range(size)])


def owners(size):
    return [(b, i) for b in range(lax.axis_size("batch")) for i in range(size) if i // (size // 2) == b % 2]


def to_owner(block):
    size = lax.axis_size("seq")
    route = [(b * size + (i ^ (size // 2)), b * size + i) for b, i in owners(size)]
    return lax.ppermute(block, ("batch", "seq"), route)


def between_owners(block):
    size = lax.axis_size("seq")
    route = [(b * size + i, (b ^ 2) * size + i) for b, i in owners(size)]
    return lax.ppermute(block, ("batch", "seq"), route)


def after(values, *others):
    return lax.optimization_barrier((tuple(values), others))[0]


def tree_sum(parts):
    parts = [p.astype(F32) for p in parts]
    while len(parts) > 1:
        parts = [sum(parts[i : i + 2][1:], parts[i]) for i in range(0, len(parts), 2)]
    return parts[0]


def take(block, index, axis):
    return lax.dynamic_index_in_dim(block, index, axis, keepdims=False)


def normalize(rows):
    centre = jnp.mean(rows, axis=-1, keepdims=True)
    centred = rows - centre
    spread = jnp.mean(centred * centred, axis=-1, keepdims=True)
    inverse = lax.rsqrt(spread + NORM_EPS)
    return centred * inverse, inverse


def rotary_tables(first, count):
    kind = lax.broadcasted_iota(jnp.int32, (3, count, 128), 0)
    place = lax.broadcasted_iota(jnp.int32, (3, count, 128), 1)
    lane = lax.broadcasted_iota(jnp.int32, (3, count, 128), 2) % HEAD_DIM
    half = ROT // 2
    freqs = 10000.0 ** (-(lane % half).astype(F32) / half)
    angles = (first + place).astype(F32) * 0.25 * freqs
    cosine = jnp.where(lane < ROT, jnp.cos(angles), 1.0)
    sine = jnp.sin(angles)
    below = jnp.where((lane >= half) & (lane < ROT), sine, 0.0)
    above = jnp.where(lane < half, -sine, 0.0)
    return jnp.where(kind == 0, cosine, jnp.where(kind == 1, below, above))


def turn(values, tables, sign):
    moved = pltpu.roll(values, ROT // 2, 1) * tables[1] + pltpu.roll(values, 128 - ROT // 2, 1) * tables[2]
    return values * tables[0] + (moved if sign > 0 else -moved)


def repeated(tables_ref, count):
    return [jnp.concatenate([tables_ref[i]] * count, axis=0) for i in range(3)]


def key_tables(tables):
    low = lax.broadcasted_iota(jnp.int32, (1, 128), 1) < HEAD_DIM
    return [jnp.where(low, tables[0], 1.0), jnp.where(low, tables[1], 0.0), jnp.where(low, tables[2], 0.0)]

VMEM = pl.BlockSpec(memory_space=pltpu.VMEM)
SMEM = pl.BlockSpec(memory_space=pltpu.SMEM)
SHAPE = jax.ShapeDtypeStruct


def cost(share):
    return pl.CostEstimate(flops=int(share * 3e9), bytes_accessed=0, transcendentals=0)


def wide(ref):
    return ref[...].reshape(1, -1)


def add_split(place, items, share=1.2):
    def kernel(place_ref, *refs):
        sources, results = refs[: 2 * len(items)], refs[2 * len(items) :]
        for n, (_, _, which) in enumerate(items):
            a, b = sources[2 * n], sources[2 * n + 1]
            own = place_ref[which] if which < 3 else lax.rem(lax.shift_right_logical(place_ref[3], which - 3), 2)
            for m in range(a.shape[0]):
                for result, at in ((results[2 * n], 1 - own), (results[2 * n + 1], own)):
                    result[m] = (a[m, at].astype(F32) + b[m, at].astype(F32)).astype(BF16)

    shapes = []
    for a, _, _ in items:
        shapes += [SHAPE((a.shape[0],) + a.shape[2:], BF16)] * 2
    arrays = [v for item in items for v in item[:2]]
    return pl.pallas_call(
        kernel,
        in_specs=[SMEM] + [VMEM] * len(arrays),
        out_specs=[VMEM] * len(shapes),
        out_shape=shapes,
        compiler_params=params(),
        cost_estimate=cost(share),
        name="add_split",
    )(place, *arrays)


def exchange_split(place, mine1, come1, mine2, come2):
    def kernel(place_ref, a1, b1, a2, b2, theirs, keep1, keep2):
        y = place_ref[2]
        row = 0
        for a, b, keep in ((a1, b1, keep1), (a2, b2, keep2)):
            m, _, r, c = a.shape
            part = a[:, pl.ds(1 - y, 1)].astype(F32) + b[:, pl.ds(1 - y, 1)].astype(F32)
            part = part.reshape(m * r, c).astype(BF16)
            for at in range(0, c, D // 2):
                theirs[row : row + m * r] = part[:, at : at + D // 2]
                row += m * r
            part = a[:, pl.ds(y, 1)].astype(F32) + b[:, pl.ds(y, 1)].astype(F32)
            keep[...] = part.reshape(m, r, c).astype(BF16)

    shapes = [(a.shape[0],) + a.shape[2:] for a in (mine1, mine2)]
    size = sum(math.prod(s) for s in shapes)
    return pl.pallas_call(
        kernel,
        in_specs=[SMEM] + [VMEM] * 4,
        out_specs=[VMEM] * 3,
        out_shape=[SHAPE((size // (D // 2), D // 2), BF16)] + [SHAPE(s, BF16) for s in shapes],
        compiler_params=params(FULL_BYTES),
        cost_estimate=cost(1.2),
        name="exchange_split",
    )(place, mine1, come1, mine2, come2)


def exchange_add(place, mine1, mine2, come, bit):
    def kernel(place_ref, a1, a2, b, theirs, keep, total):
        row = 0
        parts = []
        for a in (a1, a2):
            m, r, c = a.shape
            columns = []
            for _ in range(0, c, D // 2):
                columns.append(b[row : row + m * r])
                row += m * r
            parts.append(jnp.concatenate(columns, axis=1).astype(F32).reshape(m, r, c))
        own = (place_ref[3] >> bit) & 1
        total[...] = (a2[...].astype(F32) + parts[1]).astype(BF16)
        both = (a1[...].astype(F32) + parts[0]).astype(BF16)
        m, r, c = a1.shape
        both = both.reshape(m // 2, 2, r, c)
        lower, upper = both[:, 0], both[:, 1]
        theirs[...] = jnp.where(own == 0, upper, lower)
        keep[...] = jnp.where(own == 0, lower, upper)

    half = SHAPE((mine1.shape[0] // 2,) + mine1.shape[1:], BF16)
    return pl.pallas_call(
        kernel,
        in_specs=[SMEM] + [VMEM] * 3,
        out_specs=[VMEM] * 3,
        out_shape=[half, half, SHAPE(mine2.shape, BF16)],
        compiler_params=params(),
        cost_estimate=cost(0.01),
        name="exchange_add",
    )(place, mine1, mine2, come)


def add_cut(place, a, b):
    parts = a.shape[1]

    def kernel(place_ref, a_ref, b_ref, *results):
        for i in range(parts):
            at = place_ref[3] ^ i
            for k in range(a.shape[0]):
                results[i][k] = (a_ref[k, at].astype(F32) + b_ref[k, at].astype(F32)).astype(BF16)

    return pl.pallas_call(
        kernel,
        in_specs=[SMEM, VMEM, VMEM],
        out_specs=[VMEM] * parts,
        out_shape=[SHAPE((a.shape[0],) + a.shape[2:], BF16)] * parts,
        compiler_params=params(FULL_BYTES),
        cost_estimate=cost(1.2),
        name="add_cut",
    )(place, a, b)


def keys_kernel(copies, x_ref, gain_ref, bias_ref, weight_ref, add_ref, tables_ref, kv_ref, first_ref):
    normed, _ = normalize(x_ref[...].astype(F32))
    first_in = (normed * wide(gain_ref) + wide(bias_ref)).astype(BF16)
    first_ref[...] = first_in
    part = dot(first_in, weight_ref[...]) + wide(add_ref)[:, D:]
    kv_ref[...] = turn(part, key_tables(repeated(tables_ref, copies)), 1).astype(BF16)


def queries_kernel(copies, first_ref, weight_ref, add_ref, tables_ref, q_ref):
    first_in = first_ref[...]
    tables = repeated(tables_ref, copies)
    bias = wide(add_ref)
    for p in range(PAIRS):
        columns = slice(p * 128, (p + 1) * 128)
        part = dot(first_in, weight_ref[:, columns]) + bias[:, columns]
        q_ref[:, columns] = (turn(part, tables, 1) * SCALE).astype(BF16)


def project_keys(x, gain, bias, weight, add, tables):
    rows = x.shape[0]
    whole = lambda a: pl.BlockSpec(a.shape, lambda i: (0,) * a.ndim)
    return pl.pallas_call(
        functools.partial(keys_kernel, rows // tables.shape[1]),
        grid=(1,),
        in_specs=[
            whole(x),
            whole(gain),
            whole(bias),
            pl.BlockSpec((D, 128), lambda i: (0, D // 128)),
            whole(add),
            whole(tables),
        ],
        out_specs=[pl.BlockSpec((rows, 128), lambda i: (0, 0)), pl.BlockSpec((rows, D), lambda i: (0, 0))],
        out_shape=[SHAPE((rows, 128), BF16), SHAPE((rows, D), BF16)],
        compiler_params=params(),
        cost_estimate=cost(1),
        name="project_keys",
    )(x, gain, bias, weight, add, tables)


def project_queries(first_in, weight, add, tables):
    rows = first_in.shape[0]
    whole = lambda a: pl.BlockSpec(a.shape, lambda i: (0,) * a.ndim)
    return pl.pallas_call(
        functools.partial(queries_kernel, rows // tables.shape[1]),
        grid=(1,),
        in_specs=[
            whole(first_in),
            pl.BlockSpec((D, D), lambda i: (0, 0)),
            whole(add),
            whole(tables),
        ],
        out_specs=pl.BlockSpec((rows, D), lambda i: (0, 0)),
        out_shape=SHAPE((rows, D), BF16),
        compiler_params=params(),
        cost_estimate=cost(2),
        name="project_queries",
    )(first_in, weight, add, tables)


def gelu_parts(h):
    t = pl.reciprocal(1.0 + (0.3275911 / math.sqrt(2.0)) * jnp.abs(h))
    e = jnp.exp(-0.5 * h * h)
    poly = 0.5 * 1.061405429
    for coefficient in (-1.453152027, 1.421413741, -0.284496736, 0.254829592):
        poly = poly * t + 0.5 * coefficient
    tail = poly * t * e
    cdf = jnp.where(h >= 0.0, 1.0 - tail, tail)
    return h * cdf, cdf + h * e * (1.0 / math.sqrt(2.0 * math.pi))


def feed_kernel(
    place_ref,
    x_ref,
    xx_ref,
    g_ref,
    gg_ref,
    gain_ref,
    bias_ref,
    w1_ref,
    b1_ref,
    w2_ref,
    wo_ref,
    mlp_ref,
    back_ref,
    other_ref,
    attn_grad_ref,
    b1_grad_ref,
    theirs1_ref,
    mine1_ref,
    *refs,
):
    grad_refs, (in_scr, in_t_scr, g_scr, mlp_scr, back_scr) = refs[:-5], refs[-5:]
    step, steps = pl.program_id(0), pl.num_programs(0)
    rows = x_ref.shape[0]

    @pl.when(step == 0)
    def _():
        for i, (tokens, grads) in enumerate(((x_ref, g_ref), (xx_ref, gg_ref))):
            at = slice(i * rows, (i + 1) * rows)
            normed, _ = normalize(tokens[...].astype(F32))
            second_in = normed * wide(gain_ref) + wide(bias_ref)
            in_scr[at] = second_in.astype(BF16)
            in_t_scr[:, :, :, at] = second_in.T.astype(BF16).reshape(in_t_scr.shape[:3] + (rows,))
            g_scr[at] = grads[...]
        attn_grad_ref[...] = dot_nt(g_ref[...], wo_ref[...]).astype(BF16)

    g = g_scr[...]
    w1 = w1_ref[...]
    w2 = w2_ref[...]
    act, slope = gelu_parts(dot(in_scr[...], w1) + b1_ref[...])
    act = act.astype(BF16)
    pre = dot_nt(g, w2) * slope
    pre16 = pre.astype(BF16)
    b1_grad_ref[...] = jnp.sum(pre, axis=0, keepdims=True)
    mlp = dot(act, w2)
    grad = dot_tn(act, g).astype(BF16)
    if len(grad_refs) == 1:
        grad_refs[0][...] = grad
    for i in range(len(grad_refs) if len(grad_refs) > 1 else 0):

        @pl.when(step == i)
        def _(i=i):
            grad_refs[i][...] = grad

    back = dot_nt(pre16, w1)
    own = place_ref[1]
    for result, at in ((theirs1_ref, 1 - own), (mine1_ref, own)):
        left = in_t_scr[:, pl.ds(at, 1)].reshape(D // 2, 2 * rows)
        result[...] = dot(left, pre16).astype(BF16).reshape(result.shape)

    @pl.when(step == 0)
    def _():
        mlp_scr[...] = mlp
        back_scr[...] = back

    @pl.when((step > 0) & (step < steps - 1))
    def _():
        mlp_scr[...] += mlp
        back_scr[...] += back

    @pl.when(step == steps - 1)
    def _():
        for i, (scr, last, own_ref) in enumerate(((mlp_scr, mlp, mlp_ref), (back_scr, back, back_ref))):
            total = (scr[...] + last).astype(BF16)
            own_ref[...] = total[:rows]
            other_ref[i] = total[rows:]


CHUNK = 512


def feed(place, count, x, xx, g, gg, gain, bias, w1, b1, w2, wo):
    rows = x.shape[0]
    half = w1.shape[1] // 2
    depth = count // 2
    per = D // count // 2
    pieces = depth // 2
    aligned = pieces == 2 and half % 512 == 0
    chunk = half // pieces if aligned else CHUNK
    steps = half // chunk
    single = pl.Buffered(1)
    whole = lambda a: pl.BlockSpec(a.shape, lambda i, place: (0,) * a.ndim, pipeline_mode=single)
    fixed = lambda *shape: pl.BlockSpec(shape, lambda i, place: (0, 0))
    if aligned:
        piece = lambda i, place: (place[3] ^ (1 - i)) & 1
        grad_specs = [fixed(chunk, D)] * pieces
        grad_shapes = [SHAPE((chunk, D), BF16)] * pieces
    else:
        piece = lambda i, place: i
        grad_specs = [pl.BlockSpec((chunk, D), lambda i, place: (i, 0))]
        grad_shapes = [SHAPE((half, D), BF16)]
    at = lambda i, place: place[0] * steps + piece(i, place)
    cut = pl.BlockSpec((count, per, chunk), lambda i, place: (0, 0, piece(i, place)))
    spec = pltpu.PrefetchScalarGridSpec(
        num_scalar_prefetch=1,
        grid=(steps,),
        in_specs=[
            whole(x),
            whole(xx),
            whole(g),
            whole(gg),
            whole(gain),
            whole(bias),
            pl.BlockSpec((D, chunk), lambda i, place: (0, at(i, place))),
            pl.BlockSpec((1, chunk), lambda i, place: (0, at(i, place))),
            pl.BlockSpec((chunk, D), lambda i, place: (at(i, place), 0)),
            whole(wo),
        ],
        out_specs=[
            fixed(rows, D),
            fixed(rows, D),
            pl.BlockSpec((2, rows, D), lambda i, place: (0, 0, 0)),
            fixed(rows, D),
        ]
        + [pl.BlockSpec((1, chunk), lambda i, place: (0, piece(i, place))), cut, cut]
        + grad_specs,
        scratch_shapes=[
            pltpu.VMEM((2 * rows, D), BF16),
            pltpu.VMEM((count, 2, per, 2 * rows), BF16),
            pltpu.VMEM((2 * rows, D), BF16),
            pltpu.VMEM((2 * rows, D), F32),
            pltpu.VMEM((2 * rows, D), F32),
        ],
    )
    result = pl.pallas_call(
        feed_kernel,
        grid_spec=spec,
        out_shape=[SHAPE((rows, D), BF16), SHAPE((rows, D), BF16), SHAPE((2, rows, D), BF16), SHAPE((rows, D), BF16)]
        + [SHAPE((1, half), F32), SHAPE((count, per, half), BF16), SHAPE((count, per, half), BF16)]
        + grad_shapes,
        compiler_params=params(FULL_BYTES),
        cost_estimate=cost(12),
        name="feed_forward",
    )(place, x, xx, g, gg, gain, bias, w1, b1, w2, wo)
    grads = result[7:]
    if not aligned:
        cut = grads[0].reshape(pieces // 2, 2, -1, D)
        low = place[3] & 1
        grads = [take(cut, 1 - low, 1), take(cut, low, 1)]
    return result[:7], grads


def present(slot, y, z):
    back = slot // 2
    return (back <= z) & ((slot % 2 == 0) | (back >= 1) | (y == 1))


def whole_kernel(span, depth, place_ref, *refs):
    pair_refs, (q_ref, do_ref, tables_ref, rows_ref, even_out_ref, odd_out_ref) = refs[:depth], refs[depth:]
    out_ref, dq_ref = rows_ref.at[0], rows_ref.at[1]
    y, z = place_ref[2], place_ref[3]
    tables = [tables_ref[i] for i in range(3)]
    rows = PAIRS * span
    low = lax.broadcasted_iota(jnp.int32, (1, 128), 1) < HEAD_DIM

    def stacked(ref):
        return jnp.concatenate([ref[:, p * 128 : (p + 1) * 128] for p in range(PAIRS)], axis=0)

    blocks = [ref[i] for ref in pair_refs for i in range(2)]
    kv = jnp.concatenate(blocks, axis=0)
    swapped = pltpu.roll(kv.astype(F32), HEAD_DIM, 1).astype(BF16)
    zero, one = jnp.zeros_like(kv), jnp.ones_like(kv)
    keys = (jnp.where(low, kv, zero), jnp.where(low, zero, swapped))
    values = (jnp.where(low, swapped, zero), jnp.where(low, zero, kv))
    summing = (jnp.where(low, swapped, one), jnp.where(low, one, kv))
    slot = lax.broadcasted_iota(jnp.int32, (1, (2 * depth - 1) * span), 1) // span + 1
    absent = jnp.where(present(slot, y, z), 0.0, MASKED)
    token = lax.broadcasted_iota(jnp.int32, (rows, span), 0) % span
    seen = lax.broadcasted_iota(jnp.int32, (rows, span), 1) <= token
    q = stacked(q_ref)
    do = stacked(do_ref)
    do32 = do.astype(F32)

    expd, mixed = [], []
    for h in range(2):
        scores = dot_nt(q, keys[h])
        scores = jnp.concatenate([jnp.where(seen, scores[:, :span], MASKED), scores[:, span:] + absent], axis=1)
        top = jnp.max(scores, axis=1, keepdims=True)
        expd.append(jnp.exp(scores - top).astype(BF16))
        mixed.append(dot(expd[h], summing[h]))
    total = jnp.where(low, pltpu.roll(mixed[0], HEAD_DIM, 1), pltpu.roll(mixed[1], HEAD_DIM, 1))
    inverse = 1.0 / total
    out = jnp.where(low, mixed[0], mixed[1]) * inverse
    for p in range(PAIRS):
        out_ref[:, p * 128 : (p + 1) * 128] = out[p * span : (p + 1) * span].astype(BF16)
    product = do32 * out
    do_t = (do32 * inverse).T.astype(BF16)
    q_t = (q.astype(F32) * inverse).T.astype(BF16)
    dq = dk = dv = 0.0
    for h in range(2):
        head = slice(h * HEAD_DIM, (h + 1) * HEAD_DIM)
        delta = jnp.sum(jnp.where(low == (h == 0), product, 0.0), axis=1, keepdims=True)
        dprob = dot_nt(do, values[h])
        dscore = (expd[h].astype(F32) * (dprob - delta)).astype(BF16)
        dq = dq + dot(dscore, keys[h])
        dk = dk + dot(q_t[head], dscore)
        dv = dv + dot(do_t[head], expd[h])
    dq = dq * (inverse * SCALE)
    for p in range(PAIRS):
        dq_ref[:, p * 128 : (p + 1) * 128] = turn(dq[p * span : (p + 1) * span], tables, -1).astype(BF16)
    both = jnp.concatenate([dk, dv], axis=0).T.astype(BF16)
    for k in range(depth):
        even_out_ref[k] = both[2 * k * span : (2 * k + 1) * span]
        odd_out_ref[k] = both[(2 * k + 1) * span : (2 * k + 2) * span]


def loop_kernel(groups, span, block, count, place_ref, *refs):
    depth = count // 2
    pair_refs, refs = refs[:depth], refs[depth:]
    q_ref, do_ref, tables_ref, rows_ref, even_out_ref, odd_out_ref = refs[:6]
    out_ref, dq_ref = rows_ref.at[0], rows_ref.at[1]
    kv_scr, e_ref, kv_t_ref, max_ref, acc_ref, ext_ref = refs[6:]
    tables = [tables_ref[i] for i in range(3)]
    rows = groups * span
    per = block // span
    y, z = place_ref[2], place_ref[3]
    used = (2 * (z + 1) + per - 1) // per
    group, group_count = pl.program_id(1), pl.num_programs(1)
    low = lax.broadcasted_iota(jnp.int32, (1, 128), 1) < HEAD_DIM
    lanes = lax.broadcasted_iota(jnp.int32, (rows, 128), 1)

    def stacked(ref):
        return jnp.concatenate([ref[:, p * 128 : (p + 1) * 128] for p in range(groups)], axis=0)

    @pl.when(group == 0)
    def _():
        for i in range(count):
            kv_scr[i * span : (i + 1) * span] = pair_refs[i // 2][i % 2]

    q = stacked(q_ref)
    do = stacked(do_ref)

    def load(b):
        kv = kv_scr[pl.ds(pl.multiple_of(b * block, block), block)]
        swapped = pltpu.roll(kv.astype(F32), HEAD_DIM, 1).astype(BF16)
        return kv, swapped, jnp.zeros_like(kv)

    def absent(b):
        row = lax.broadcasted_iota(jnp.int32, (block, 128), 0) + b * block
        lane = lax.broadcasted_iota(jnp.int32, (block, 128), 1)
        mask = jnp.where(present(row // span, y, z), 0.0, MASKED)
        return jnp.where(lane < 2, -1.0, jnp.where(lane == 2, mask, 0.0)).astype(BF16)

    def key_tiles(b):
        kv, swapped, zero = load(b)
        ext = absent(b)
        return [
            jnp.concatenate([jnp.where(low, kv, zero), ext], axis=1),
            jnp.concatenate([jnp.where(low, zero, swapped), ext], axis=1),
        ]

    def value_tiles(b):
        kv, swapped, zero = load(b)
        ext = absent(b)
        return [
            jnp.concatenate([jnp.where(low, swapped, zero), ext], axis=1),
            jnp.concatenate([jnp.where(low, zero, kv), ext], axis=1),
        ]

    def seen():
        token = lax.broadcasted_iota(jnp.int32, (rows, block), 0) % span
        key = lax.broadcasted_iota(jnp.int32, (rows, block), 1)
        return (key <= token) | (key >= span)

    def extended(values):
        high = values.astype(BF16).astype(F32)
        rest = jnp.where(lanes == 1, values - high, jnp.where(lanes == 2, 1.0, 0.0))
        return jnp.where(lanes == 0, high, rest).astype(BF16)

    def over_blocks(step):
        step(0, True)

        def body(b, carry):
            step(b, False)
            return carry

        lax.fori_loop(1, used, body, 0)

    plain = jnp.concatenate([q, jnp.where(lanes == 2, 1.0, 0.0).astype(BF16)], axis=1)

    def maxima(b, diagonal):
        keys = key_tiles(b)
        for h in range(2):
            scores = dot_nt(plain, keys[h])
            if diagonal:
                scores = jnp.where(seen(), scores, MASKED)
            top = functools.reduce(jnp.maximum, [scores[:, i : i + 128] for i in range(0, block, 128)])
            max_ref[h] = top if diagonal else jnp.maximum(max_ref[h], top)

    over_blocks(maxima)
    for h in range(2):
        top = jnp.max(max_ref[h], axis=1, keepdims=True)
        ext_ref[h] = jnp.concatenate([q, extended(jnp.broadcast_to(top, (rows, 128)))], axis=1)

    def forward(b, diagonal):
        keys = key_tiles(b)
        kv, swapped, _ = load(b)
        one = jnp.ones_like(kv)
        values = (jnp.where(low, swapped, one), jnp.where(low, one, kv))
        for h in range(2):
            expd = jnp.exp(dot_nt(ext_ref[h], keys[h]))
            if diagonal:
                expd = jnp.where(seen(), expd, 0.0)
            expd = expd.astype(BF16)
            e_ref[b, h] = expd
            mixed = dot(expd, values[h])
            acc_ref[h] = mixed if diagonal else acc_ref[h] + mixed

    over_blocks(forward)
    first, second = acc_ref[0], acc_ref[1]
    total = jnp.where(low, pltpu.roll(first, HEAD_DIM, 1), pltpu.roll(second, HEAD_DIM, 1))
    inverse = 1.0 / total
    out = jnp.where(low, first, second) * inverse
    for p in range(groups):
        out_ref[:, p * 128 : (p + 1) * 128] = out[p * span : (p + 1) * span].astype(BF16)
    do32 = do.astype(F32)
    product = do32 * out
    high = product.astype(BF16)
    rest = (product - high.astype(F32)).astype(BF16)
    place = lax.broadcasted_iota(jnp.int32, (128, 128), 0)
    for h in range(2):
        ones = jnp.where((place < HEAD_DIM) == (h == 0), 1.0, 0.0).astype(BF16)
        delta = dot(high, ones) + dot(rest, ones)
        ext_ref[h] = jnp.concatenate([do, extended(delta)], axis=1)
    do_t = (do32 * inverse).T.astype(BF16)
    q_t = (q.astype(F32) * inverse).T.astype(BF16)

    def backward(b, start):
        values = value_tiles(b)
        kv, swapped, zero = load(b)
        keys = (jnp.where(low, kv, zero), jnp.where(low, zero, swapped))
        dq = dk = dv = 0.0
        for h in range(2):
            expd = e_ref[b, h]
            head = slice(h * HEAD_DIM, (h + 1) * HEAD_DIM)
            dscore = (expd.astype(F32) * dot_nt(ext_ref[h], values[h])).astype(BF16)
            dq = dq + dot(dscore, keys[h])
            dk = dk + dot(q_t[head], dscore)
            dv = dv + dot(do_t[head], expd)
        acc_ref[0] = dq if start else acc_ref[0] + dq
        both = jnp.concatenate([dk, dv], axis=0)
        kv_t_ref[b] = jnp.where(group == 0, both, kv_t_ref[b] + both)

    over_blocks(backward)
    dq = acc_ref[0] * (inverse * SCALE)
    for p in range(groups):
        dq_ref[:, p * 128 : (p + 1) * 128] = turn(dq[p * span : (p + 1) * span], tables, -1).astype(BF16)

    @pl.when(group == group_count - 1)
    def _():
        for b in range(count // per):
            used_block = jnp.where(b < used, kv_t_ref[b], 0.0).T.astype(BF16)
            for i in range(per):
                slot = b * per + i
                result = odd_out_ref if slot % 2 else even_out_ref
                result[slot // 2] = used_block[i * span : (i + 1) * span]


def attention(place, pairs, q, do, tables):
    depth = len(pairs)
    count = 2 * depth
    seqs, span, _ = q.shape
    single = count * span <= 1024
    groups = PAIRS if single else 2
    wide_spec = pl.BlockSpec((None, span, groups * 128), lambda s, i: (s, 0, i))
    pieces = pl.BlockSpec((depth, None, span, 128), lambda s, i: (0, s, 0, 0))
    two = pl.BlockSpec((2, None, span, 128), lambda s, i: (0, s, 0, 0))
    if single:
        kernel, scratch = functools.partial(whole_kernel, span, depth), []
    else:
        block = max(512, span)
        blocks = count * span // block
        rows = groups * span
        kernel = functools.partial(loop_kernel, groups, span, block, count)
        scratch = [
            pltpu.VMEM((count * span, 128), BF16),
            pltpu.VMEM((blocks, 2, rows, block), BF16),
            pltpu.VMEM((blocks, 128, block), F32),
            pltpu.VMEM((2, rows, 128), F32),
            pltpu.VMEM((2, rows, 128), F32),
            pltpu.VMEM((2, rows, 256), BF16),
        ]
    return pl.pallas_call(
        kernel,
        grid=(seqs, PAIRS // groups),
        in_specs=[SMEM] + [two] * depth + [wide_spec, wide_spec, pl.BlockSpec(tables.shape, lambda s, i: (0, 0, 0))],
        out_specs=[pl.BlockSpec((2, None, span, groups * 128), lambda s, i: (0, s, 0, i))] + [pieces] * 2,
        out_shape=[SHAPE((2, seqs, span, D), BF16)]
        + [SHAPE((depth, seqs, span, 128), BF16)] * 2,
        scratch_shapes=scratch,
        compiler_params=params(FULL_BYTES),
        cost_estimate=cost(10),
        name="attention",
    )(place, *pairs, q, do, tables)


def weights_kernel(place_ref, attn_ref, attn2_ref, g_ref, g2_ref, in_ref, in2_ref, q_ref, q2_ref, theirs_ref, mine_ref, small_ref, scr):
    half = D // 2
    y = place_ref[2]

    def products(left, right, line):
        at = pl.ds(pl.multiple_of(place_ref[0] * half, 128), half)
        small_ref[line : line + 1] = jnp.zeros_like(small_ref[line : line + 1])
        small_ref[line : line + 1, at] = jnp.sum(right.astype(F32), axis=0, keepdims=True)
        scr[...] = dot_tn(left, right).reshape(scr.shape)
        theirs_ref[0] = scr[:, pl.ds(1 - y, 1)].reshape(theirs_ref.shape[1:]).astype(BF16)
        mine_ref[0] = scr[:, pl.ds(y, 1)].reshape(mine_ref.shape[1:]).astype(BF16)

    both = lambda a, b: jnp.concatenate([a[...], b[...]], axis=0)

    @pl.when(pl.program_id(0) == 0)
    def _():
        products(both(attn_ref, attn2_ref), both(g_ref, g2_ref), 1)

    @pl.when(pl.program_id(0) == 1)
    def _():
        products(both(in_ref, in2_ref), both(q_ref, q2_ref), 0)


def weights(place, count, both, both2, g, g2, first_in, first_in2):
    rows = g.shape[0]
    depth, per, half = count // 2, D // count, D // 2
    whole = pl.BlockSpec((rows, D), lambda i, place: (0, 0), pipeline_mode=pl.Buffered(1))
    part = pl.BlockSpec((rows, half), lambda i, place: (0, place[0]), pipeline_mode=pl.Buffered(1))
    attn_part = pl.BlockSpec((None, rows, D), lambda i, place: (0, 0, 0), pipeline_mode=pl.Buffered(1))
    q_part = pl.BlockSpec((None, rows, half), lambda i, place: (1, 0, place[0]), pipeline_mode=pl.Buffered(1))
    result = pl.BlockSpec((1, depth, per, half), lambda i, place: (i, 0, 0, 0))
    return pl.pallas_call(
        weights_kernel,
        grid_spec=pltpu.PrefetchScalarGridSpec(
            num_scalar_prefetch=1,
            grid=(2,),
            in_specs=[attn_part, attn_part, part, part, whole, whole, q_part, q_part],
            out_specs=[result, result, pl.BlockSpec((8, D), lambda i, place: (0, 0))],
            scratch_shapes=[pltpu.VMEM((depth, 2, per, half), F32)],
        ),
        out_shape=[SHAPE((2, depth, per, half), BF16), SHAPE((2, depth, per, half), BF16), SHAPE((8, D), F32)],
        compiler_params=params(),
        cost_estimate=cost(2.4),
        name="weights",
    )(place, both, both2, g, g2, first_in, first_in2, both, both2)


def mix_kernel(x_ref, mlp_ref, mlp2_ref, attn_ref, add_ref, wo_ref, output_ref):
    mlp = mlp_ref[...].astype(F32) + mlp2_ref[...].astype(F32)
    x = x_ref[...].astype(F32)
    output_ref[...] = (x + (mlp + dot(attn_ref[...], wo_ref[...])) + wide(add_ref)).astype(BF16)


def mix(x, mlp, other, both, add, wo):
    rows = x.shape[0]
    row = pl.BlockSpec((rows // 2, D), lambda i: (i, 0))
    first = pl.BlockSpec((None, rows // 2, D), lambda i: (0, i, 0))
    return pl.pallas_call(
        mix_kernel,
        grid=(2,),
        in_specs=[row, row, first, first, pl.BlockSpec((D,), lambda i: (0,)), pl.BlockSpec((D, D), lambda i: (0, 0))],
        out_specs=row,
        out_shape=SHAPE((rows, D), BF16),
        compiler_params=params(),
        cost_estimate=cost(1.2),
        name="mix",
    )(x, mlp, other, both, add, wo)


def two_terms(values):
    high = values.astype(BF16)
    return high, (values - high.astype(F32)).astype(BF16)


def message_lines(ff):
    return -(-(ff // 128 + 6 * (D // 128) + 1) // 16) * 16


def finish_kernel(
    copies,
    count,
    lines,
    place_ref,
    *refs,
):
    kv_refs, refs = refs[:count], refs[count:]
    (
        extra_ref,
        x_ref,
        g_ref,
        q_ref,
        back_ref,
        back2_ref,
        gain_ref,
        bias_ref,
        gain2_ref,
        wqkv_ref,
        tables_ref,
        b1_ref,
        early_ref,
        tokens_ref,
        theirs_ref,
        mine_ref,
        vector_scr,
        weight_scr,
    ) = refs
    total = extra_ref[...].astype(F32)
    for ref in kv_refs:
        total += ref[...].astype(F32)
    tables = repeated(tables_ref, copies)
    grad = turn(total, key_tables(tables), -1).astype(BF16)
    x = x_ref[...].astype(F32)
    normed, inverse = normalize(x)
    gain = wide(gain_ref)
    first_in = normed * gain + wide(bias_ref)
    first_grad = dot_nt(jnp.concatenate([q_ref[...], grad], axis=1), wqkv_ref[...])
    second_grad = back_ref[...].astype(F32) + back2_ref[...].astype(F32)

    vector_scr[...] = jnp.zeros_like(vector_scr)
    b1 = b1_ref[...]
    b1_lines = b1.shape[1] // 128
    for i in range(b1_lines):
        vector_scr[pl.ds(place_ref[0] * b1_lines + i, 1)] = b1[:, i * 128 : (i + 1) * 128]
    at = 2 * b1_lines
    sums = [early_ref[0:1], jnp.sum(grad.astype(F32), axis=0, keepdims=True), early_ref[1:2]]
    for rows in (first_grad * normed, first_grad, second_grad * normed, second_grad):
        sums.append(jnp.sum(rows, axis=0, keepdims=True))
    for row in sums:
        for i in range(row.shape[1] // 128):
            vector_scr[at : at + 1] = row[:, i * 128 : (i + 1) * 128]
            at += 1
    high, rest = two_terms(vector_scr[...])
    weight_scr[...] = dot(first_in.T.astype(BF16), grad).reshape(weight_scr.shape)
    y = place_ref[2]
    for message, at in ((theirs_ref, 1 - y), (mine_ref, y)):
        message[:lines] = high
        message[lines : 2 * lines] = rest
        message[2 * lines :] = weight_scr[:, pl.ds(at, 1)].reshape(-1, 128).astype(BF16)

    normed_grad = first_grad * gain + second_grad * wide(gain2_ref)
    mean = jnp.mean(normed_grad, axis=-1, keepdims=True)
    along_rows = jnp.mean(normed_grad * normed, axis=-1, keepdims=True)
    tokens_ref[...] = (g_ref[...].astype(F32) + inverse * (normed_grad - mean - normed * along_rows)).astype(BF16)


def finish(place, places, ff, kv_parts, extra, x, g, both, back, other, gain, bias, gain2, wqkv, tables, b1, early):
    rows = x.shape[0]
    lines = message_lines(ff)
    whole = lambda a: pl.BlockSpec(a.shape, lambda i: (0,) * a.ndim)
    second = pl.BlockSpec((None, rows, D), lambda i: (1, 0, 0))
    before, between, behind = (*kv_parts, extra, x, g), (back,), (gain, bias, gain2, wqkv, tables, b1, early)
    return pl.pallas_call(
        functools.partial(finish_kernel, rows // tables.shape[1], len(kv_parts), lines),
        grid=(1,),
        in_specs=[SMEM]
        + [whole(a) for a in before]
        + [second]
        + [whole(a) for a in between]
        + [second]
        + [whole(a) for a in behind],
        out_specs=[
            pl.BlockSpec((rows, D), lambda i: (0, 0)),
            pl.BlockSpec((2 * lines + D // 2, 128), lambda i: (0, 0)),
            pl.BlockSpec((2 * lines + D // 2, 128), lambda i: (0, 0)),
        ],
        out_shape=[SHAPE((rows, D), BF16)] + [SHAPE((2 * lines + D // 2, 128), BF16)] * 2,
        scratch_shapes=[pltpu.VMEM((lines, 128), F32), pltpu.VMEM((places // 2, 2, D // places, 128), F32)],
        compiler_params=params(),
        cost_estimate=cost(2.4),
        name="finish",
    )(place, *before, both, *between, other, *behind)


def message_cut(place, mine, come, lines, per):
    count = (mine.shape[0] - 2 * lines) // per

    def kernel(place_ref, a_ref, b_ref, *refs):
        results, scr = refs[:-1], refs[-1]
        high, rest = two_terms(tree_sum([ref[at : at + lines] for ref in (a_ref, b_ref) for at in (0, lines)]))
        scr[...] = (a_ref[2 * lines :].astype(F32) + b_ref[2 * lines :].astype(F32)).reshape(scr.shape)
        for i, result in enumerate(results):
            result[:lines] = high
            result[lines : 2 * lines] = rest
            result[2 * lines :] = scr[place_ref[3] ^ i].astype(BF16)

    return pl.pallas_call(
        kernel,
        in_specs=[SMEM, VMEM, VMEM],
        out_specs=[VMEM] * count,
        out_shape=[SHAPE((2 * lines + per, 128), BF16)] * count,
        scratch_shapes=[pltpu.VMEM((count, per, 128), F32)],
        compiler_params=params(),
        cost_estimate=cost(0.6),
        name="message_cut",
    )(place, mine, come)


def message_sum(messages, lines):
    def kernel(*refs):
        result = refs[-1]
        total = tree_sum([ref[...] for ref in refs[:-1]])
        high, rest = two_terms(total[:lines] + total[lines : 2 * lines])
        result[:lines] = high
        result[lines : 2 * lines] = rest
        result[2 * lines :] = total[2 * lines :].astype(BF16)

    return pl.pallas_call(
        kernel,
        in_specs=[VMEM] * len(messages),
        out_specs=VMEM,
        out_shape=SHAPE(messages[0].shape, BF16),
        compiler_params=params(),
        cost_estimate=cost(0.6),
        name="message_sum",
    )(*messages)


def last_sums(place, messages, lines, widths, top, mine2, other2, mine3, other3):
    count = len(messages)
    half = D // 2
    per = mine3.shape[1]

    def kernel(place_ref, *refs):
        sources, (a2, b2, a3, b3) = refs[:count], refs[count : count + 4]
        vectors, (second, out, qkv) = refs[count + 4 : -3], refs[-3:]
        core = place_ref[0]
        total = tree_sum([ref[...] for ref in sources])
        vector = total[:lines] + total[lines : 2 * lines]
        at = 0
        for result, width in zip(vectors, widths):
            for i in range(width // 128):
                result[i * 128 : (i + 1) * 128] = vector[at + i]
            at += width // 128
        owner = (place_ref[3] >> top) == core
        second[...] = jnp.where(owner, a2[...].astype(F32), b2[...].astype(F32))
        for i, result in ((0, out), (1, qkv)):
            own, other = a3[i].astype(F32), b3[i].astype(F32)
            result[:, :half] = jnp.where(core == 0, own, other)
            result[:, half:D] = jnp.where(core == 0, other, own)
        qkv[:, D:] = total[2 * lines :]

    return pl.pallas_call(
        kernel,
        in_specs=[SMEM] + [VMEM] * (count + 4),
        out_specs=[VMEM] * (len(widths) + 3),
        out_shape=[SHAPE((width,), F32) for width in widths]
        + [SHAPE(mine2.shape, F32), SHAPE((per, D), F32), SHAPE((per, D + 128), F32)],
        compiler_params=params(),
        cost_estimate=cost(0.6),
        name="last_sums",
    )(place, *messages, mine2, other2, mine3, other3)


def local(
    tokens,
    ln1_gain,
    ln1_bias,
    qkv_weight,
    qkv_bias,
    out_weight,
    ln2_gain,
    ln2_bias,
    fc1_weight,
    fc1_bias,
    fc2_weight,
    out_bias,
    output_grad,
    key_value_grad,
):
    seqs, span, _ = tokens.shape
    rows = seqs * span
    ff = fc1_weight.shape[1]
    count = lax.axis_size("seq")
    batches = lax.axis_size("batch")
    depth = count // 2
    half_depth = depth // 2
    per1, per2 = D // count, ff // count
    own = lax.axis_index("seq").astype(jnp.int32)
    batch = lax.axis_index("batch").astype(jnp.int32)
    y, z = own & 1, own >> 1
    core, xs = batch & 1, batch >> 1
    place = jnp.stack([core, xs, y, z])
    x = tokens.reshape(rows, D)
    g = output_grad.reshape(rows, D)
    over_core = lambda v: flipped(v, "batch", 1)
    over_x = lambda v: flipped(v, "batch", 2)
    over_y = lambda v: flipped(v, "seq", 1)
    over_z = lambda v, bit: flipped(v, "seq", 2 << bit)
    z_bits = depth.bit_length() - 1
    flat = lambda v: v.reshape(rows, -1)

    def pair(mine, other, index, axis):
        first = jnp.where(index == 0, mine, other)
        second = jnp.where(index == 0, other, mine)
        return jnp.concatenate([first, second], axis=axis)

    def summed(*parts):
        return tree_sum(parts).astype(BF16)

    x_other, g_other = over_core(x), over_core(g)
    tables = rotary_tables(own * span, span)
    kv, first_in = project_keys(x, ln1_gain, ln1_bias, qkv_weight, qkv_bias, tables)
    kv3 = kv.reshape(seqs, span, 128)
    kv_y = over_y(kv3)
    first_other = over_core(first_in)
    q = project_queries(first_in, qkv_weight, qkv_bias, tables)
    (kv_y,) = after((kv_y,), q)
    two = jnp.stack([kv3, kv_y])
    pairs = [two] + [along(two, k) for k in range(1, depth)]

    x_fed, g_fed, first_other = after((x, g, first_other), two)
    (mlp, back, feed_other, attn_grad, b1_grad, theirs1, mine1), (theirs2, mine2) = feed(
        place, count, *after((x_fed, x_other, g_fed, g_other), first_other), ln2_gain, ln2_bias, fc1_weight, fc1_bias.reshape(1, -1),
        fc2_weight, out_weight,
    )
    come1 = over_x(theirs1)
    come2 = over_z(theirs2, 0)
    feed_come = over_core(feed_other)

    q3, do3 = q.reshape(seqs, span, D), attn_grad.reshape(seqs, span, D)
    both, even, odd = attention(place, pairs, q3, do3, tables)
    odd = over_y(odd)

    def halved(a, parts, height):
        return a.reshape(parts, 2, height, a.shape[-1])

    both = both.reshape(2, rows, D)
    both_other = over_core(both)
    mine1, come1, mine2, come2, feed_come = after((mine1, come1, mine2, come2, feed_come), both)
    height = per2 // 2
    view1 = lambda v: halved(v, depth // 2, per1)
    view2 = lambda v: halved(v, half_depth, height)
    theirs1, mine1, theirs2, mine2 = add_split(
        place, [(view1(mine1), view1(come1), 3), (view2(mine2), view2(come2), 1)], 6
    )
    come1, come2 = over_z(theirs1, 0), over_x(theirs2)

    (both_other,) = after((both_other,), theirs1)
    theirs3, mine3, early = weights(place, count, both, both_other, g, g_other, first_in, first_other)
    come3 = over_y(theirs3)

    even, odd = after((even, odd), theirs3)
    kv_sums = [summed(even[k], odd[k]) for k in range(depth)]
    (x_mix,) = after((x,), *kv_sums)
    output = mix(x_mix, mlp, feed_come, both, out_bias, out_weight)
    (kv_next,) = after((kv_sums[1],), output)
    got = [along(kv_next, -1)] + [along(kv_sums[k], -k) for k in range(2, depth)]

    mine1, come1, mine2, come2 = after((mine1, come1, mine2, come2), output)
    view1 = lambda v: halved(v, depth // 2, per1 // 2)
    view2 = lambda v: halved(v, half_depth // 2, height)
    theirs12, mine1, mine2 = exchange_split(place, view1(mine1), view1(come1), view2(mine2), view2(come2))
    come12 = over_y(theirs12)
    mine3, come3 = after((mine3, come3), theirs12)
    parts3 = add_cut(place, mine3, come3)
    come3 = [flipped(parts3[i], "seq", 2 * i) for i in range(1, depth)]

    got = after(got, parts3[0])
    lines = message_lines(ff)
    tokens_grad, theirs4, mine4 = finish(
        place, count, ff, [flat(v) for v in (kv_sums[0], *got)], flat(key_value_grad), x, g, both, back, feed_come,
        ln1_gain, ln1_bias, ln2_gain, qkv_weight, tables, b1_grad, early,
    )
    come4 = over_y(theirs4)

    mine1, mine2, come12 = after((mine1, mine2, come12), tokens_grad)
    theirs1, mine1, sum2 = exchange_add(place, mine1, mine2, come12, 1)
    come1 = over_z(theirs1, 1)
    for bit in range(2, z_bits):
        view1 = lambda v: halved(v, depth >> (bit + 1), per1 // 2)
        theirs1, mine1 = add_split(place, [(view1(mine1), view1(come1), 3 + bit)], 0.01)
        come1 = over_z(theirs1, bit)
    for bit in range(1, z_bits - 1):
        sum2 = halved(sum2, half_depth >> (bit + 1), height)
        own_bit = (z >> bit) & 1
        sum2 = summed(take(sum2, own_bit, 1), over_z(take(sum2, 1 - own_bit, 1), bit))
    sum2 = sum2.reshape(height, D)
    come2 = to_owner(sum2)

    come3 = after(come3, theirs1, sum2)
    mine4, come4 = after((mine4, come4), *come3)
    parts4 = message_cut(place, mine4, come4, lines, per1)
    come4 = [flipped(parts4[i], "seq", 2 * i) for i in range(1, depth)]
    mine1, come1 = after((mine1, come1), parts4[0])
    sum1 = summed(mine1, come1).reshape(per1 // 2, -1)
    other1 = over_x(sum1)
    come3 = after(come3, sum1)
    sum3 = summed(parts3[0], *come3)
    other3 = over_x(sum3)
    sum2, come2 = after((sum2, come2), sum3)
    sum2 = summed(sum2, come2)
    other2 = between_owners(sum2)
    come4 = after(come4, sum2)
    message = message_sum([parts4[0], *come4], lines)
    got = [flipped(message, "batch", i) for i in range(1, batches)]

    sum1, other1 = after((sum1, other1), message)
    sum1 = pair(sum1, other1, xs, 0)
    other1 = over_core(sum1)
    sum3, other3 = after((sum3, other3), sum1)
    sum3 = summed(sum3, other3)
    other3 = over_core(sum3)
    sum2, other2 = after((sum2, other2), sum3)
    sum2 = pair(sum2, other2, xs, 0)
    other2 = over_core(sum2)

    (other1,) = after((other1,), sum2)
    fc1_grad = pair(sum1, other1, core, 1).astype(F32)
    got = after(got, fc1_grad)
    widths = (ff, D + 128) + (D,) * 5
    b1_sum, qkv_sum, out_sum, gain1, bias1, gain2, bias2, fc2_grad, out_grad, qkv_grad = last_sums(
        place, [message, *got], lines, widths, z_bits - 1, sum2, other2, sum3, other3
    )
    return (
        output.reshape(tokens.shape),
        kv3,
        tokens_grad.reshape(tokens.shape),
        gain1,
        bias1,
        qkv_grad,
        qkv_sum,
        out_grad,
        gain2,
        bias2,
        fc1_grad,
        b1_sum,
        fc2_grad,
        out_sum,
    )


def solution(mesh):
    part = P("batch", "seq", None)
    whole = P()
    split = P("seq", None)
    return jax.shard_map(
        local,
        mesh=mesh,
        in_specs=(part,) + (whole,) * 11 + (part, part),
        out_specs=(
            part, part, part, whole, whole, split, whole, split, whole, whole, split, whole, split, whole,
        ),
        check_vma=False,
    )
```

```python
import functools
import math

import jax
import jax.numpy as jnp
from jax import lax
from jax.experimental import pallas as pl
from jax.experimental.pallas import tpu as pltpu
from jax.sharding import PartitionSpec as P

D = 768
HEADS = 12
HEAD_DIM = 64
ROT = 16
PAIRS = HEADS // 2
SCALE = 1.0 / math.sqrt(HEAD_DIM)
NORM_EPS = 1e-05
MASKED = -1e30
F32 = jnp.float32
BF16 = jnp.bfloat16
VMEM_BYTES = 56 * 1024 * 1024
FULL_BYTES = 63 * 1024 * 1024


def dot(a, b):
    return lax.dot_general(a, b, (((1,), (0,)), ((), ())), preferred_element_type=F32)


def dot_nt(a, b):
    return lax.dot_general(a, b, (((1,), (1,)), ((), ())), preferred_element_type=F32)


def dot_tn(a, b):
    return lax.dot_general(a, b, (((0,), (0,)), ((), ())), preferred_element_type=F32)


def params(limit=VMEM_BYTES):
    return pltpu.CompilerParams(vmem_limit_bytes=limit)


def flipped(block, axis, bits):
    return lax.ppermute(block, axis, [(i, i ^ bits) for i in range(lax.axis_size(axis))])


def along(block, distance):
    size = lax.axis_size("seq")
    return lax.ppermute(block, "seq", [(i, (i + 2 * distance) % size) for i in range(size)])


def owners(size):
    return [(b, i) for b in range(lax.axis_size("batch")) for i in range(size) if i // (size // 2) == b % 2]


def to_owner(block):
    size = lax.axis_size("seq")
    route = [(b * size + (i ^ (size // 2)), b * size + i) for b, i in owners(size)]
    return lax.ppermute(block, ("batch", "seq"), route)


def between_owners(block):
    size = lax.axis_size("seq")
    route = [(b * size + i, (b ^ 2) * size + i) for b, i in owners(size)]
    return lax.ppermute(block, ("batch", "seq"), route)


def after(values, *others):
    return lax.optimization_barrier((tuple(values), others))[0]


def tree_sum(parts):
    parts = [p.astype(F32) for p in parts]
    while len(parts) > 1:
        parts = [sum(parts[i : i + 2][1:], parts[i]) for i in range(0, len(parts), 2)]
    return parts[0]


def take(block, index, axis):
    return lax.dynamic_index_in_dim(block, index, axis, keepdims=False)


def normalize(rows):
    centre = jnp.mean(rows, axis=-1, keepdims=True)
    centred = rows - centre
    spread = jnp.mean(centred * centred, axis=-1, keepdims=True)
    inverse = lax.rsqrt(spread + NORM_EPS)
    return centred * inverse, inverse


def rotary_tables(first, count):
    kind = lax.broadcasted_iota(jnp.int32, (3, count, 128), 0)
    place = lax.broadcasted_iota(jnp.int32, (3, count, 128), 1)
    lane = lax.broadcasted_iota(jnp.int32, (3, count, 128), 2) % HEAD_DIM
    half = ROT // 2
    freqs = 10000.0 ** (-(lane % half).astype(F32) / half)
    angles = (first + place).astype(F32) * 0.25 * freqs
    cosine = jnp.where(lane < ROT, jnp.cos(angles), 1.0)
    sine = jnp.sin(angles)
    below = jnp.where((lane >= half) & (lane < ROT), sine, 0.0)
    above = jnp.where(lane < half, -sine, 0.0)
    return jnp.where(kind == 0, cosine, jnp.where(kind == 1, below, above))


def turn(values, tables, sign):
    moved = pltpu.roll(values, ROT // 2, 1) * tables[1] + pltpu.roll(values, 128 - ROT // 2, 1) * tables[2]
    return values * tables[0] + (moved if sign > 0 else -moved)


def repeated(tables_ref, count):
    return [jnp.concatenate([tables_ref[i]] * count, axis=0) for i in range(3)]


def key_tables(tables):
    low = lax.broadcasted_iota(jnp.int32, (1, 128), 1) < HEAD_DIM
    return [jnp.where(low, tables[0], 1.0), jnp.where(low, tables[1], 0.0), jnp.where(low, tables[2], 0.0)]

VMEM = pl.BlockSpec(memory_space=pltpu.VMEM)
SMEM = pl.BlockSpec(memory_space=pltpu.SMEM)
SHAPE = jax.ShapeDtypeStruct


def cost(share):
    return pl.CostEstimate(flops=int(share * 3e9), bytes_accessed=0, transcendentals=0)


def wide(ref):
    return ref[...].reshape(1, -1)


def add_split(place, items, share=1.2):
    def kernel(place_ref, *refs):
        sources, results = refs[: 2 * len(items)], refs[2 * len(items) :]
        for n, (_, _, which) in enumerate(items):
            a, b = sources[2 * n], sources[2 * n + 1]
            own = place_ref[which] if which < 3 else lax.rem(lax.shift_right_logical(place_ref[3], which - 3), 2)
            for m in range(a.shape[0]):
                for result, at in ((results[2 * n], 1 - own), (results[2 * n + 1], own)):
                    result[m] = (a[m, at].astype(F32) + b[m, at].astype(F32)).astype(BF16)

    shapes = []
    for a, _, _ in items:
        shapes += [SHAPE((a.shape[0],) + a.shape[2:], BF16)] * 2
    arrays = [v for item in items for v in item[:2]]
    return pl.pallas_call(
        kernel,
        in_specs=[SMEM] + [VMEM] * len(arrays),
        out_specs=[VMEM] * len(shapes),
        out_shape=shapes,
        compiler_params=params(FULL_BYTES),
        cost_estimate=cost(share),
        name="add_split",
    )(place, *arrays)


def exchange_split(place, mine1, come1, mine2, come2):
    def kernel(place_ref, a1, b1, a2, b2, theirs, keep1, keep2):
        y = place_ref[2]
        row = 0
        for a, b, keep in ((a1, b1, keep1), (a2, b2, keep2)):
            m, _, r, c = a.shape
            part = a[:, pl.ds(1 - y, 1)].astype(F32) + b[:, pl.ds(1 - y, 1)].astype(F32)
            part = part.reshape(m * r, c).astype(BF16)
            for at in range(0, c, D // 2):
                theirs[row : row + m * r] = part[:, at : at + D // 2]
                row += m * r
            part = a[:, pl.ds(y, 1)].astype(F32) + b[:, pl.ds(y, 1)].astype(F32)
            keep[...] = part.reshape(m, r, c).astype(BF16)

    shapes = [(a.shape[0],) + a.shape[2:] for a in (mine1, mine2)]
    size = sum(math.prod(s) for s in shapes)
    return pl.pallas_call(
        kernel,
        in_specs=[SMEM] + [VMEM] * 4,
        out_specs=[VMEM] * 3,
        out_shape=[SHAPE((size // (D // 2), D // 2), BF16)] + [SHAPE(s, BF16) for s in shapes],
        compiler_params=params(FULL_BYTES),
        cost_estimate=cost(1.2),
        name="exchange_split",
    )(place, mine1, come1, mine2, come2)


def exchange_add(place, mine1, mine2, come, bit):
    def kernel(place_ref, a1, a2, b, theirs, keep, total):
        row = 0
        parts = []
        for a in (a1, a2):
            m, r, c = a.shape
            columns = []
            for _ in range(0, c, D // 2):
                columns.append(b[row : row + m * r])
                row += m * r
            parts.append(jnp.concatenate(columns, axis=1).astype(F32).reshape(m, r, c))
        own = (place_ref[3] >> bit) & 1
        total[...] = (a2[...].astype(F32) + parts[1]).astype(BF16)
        both = (a1[...].astype(F32) + parts[0]).astype(BF16)
        m, r, c = a1.shape
        both = both.reshape(m // 2, 2, r, c)
        lower, upper = both[:, 0], both[:, 1]
        theirs[...] = jnp.where(own == 0, upper, lower)
        keep[...] = jnp.where(own == 0, lower, upper)

    half = SHAPE((mine1.shape[0] // 2,) + mine1.shape[1:], BF16)
    return pl.pallas_call(
        kernel,
        in_specs=[SMEM] + [VMEM] * 3,
        out_specs=[VMEM] * 3,
        out_shape=[half, half, SHAPE(mine2.shape, BF16)],
        compiler_params=params(),
        cost_estimate=cost(0.01),
        name="exchange_add",
    )(place, mine1, mine2, come)


def add_cut(place, a, b):
    parts = a.shape[1]

    def kernel(place_ref, a_ref, b_ref, *results):
        for i in range(parts):
            at = place_ref[3] ^ i
            for k in range(a.shape[0]):
                results[i][k] = (a_ref[k, at].astype(F32) + b_ref[k, at].astype(F32)).astype(BF16)

    return pl.pallas_call(
        kernel,
        in_specs=[SMEM, VMEM, VMEM],
        out_specs=[VMEM] * parts,
        out_shape=[SHAPE((a.shape[0],) + a.shape[2:], BF16)] * parts,
        compiler_params=params(FULL_BYTES),
        cost_estimate=cost(1.2),
        name="add_cut",
    )(place, a, b)


def keys_kernel(copies, x_ref, gain_ref, bias_ref, weight_ref, add_ref, tables_ref, kv_ref, first_ref):
    normed, _ = normalize(x_ref[...].astype(F32))
    first_in = (normed * wide(gain_ref) + wide(bias_ref)).astype(BF16)
    first_ref[...] = first_in
    part = dot(first_in, weight_ref[...]) + wide(add_ref)[:, D:]
    kv_ref[...] = turn(part, key_tables(repeated(tables_ref, copies)), 1).astype(BF16)


def queries_kernel(copies, first_ref, weight_ref, add_ref, tables_ref, q_ref):
    first_in = first_ref[...]
    tables = repeated(tables_ref, copies)
    rows = dot(first_in, weight_ref[...]) + wide(add_ref)[:, :D]
    for p in range(PAIRS):
        columns = slice(p * 128, (p + 1) * 128)
        q_ref[:, columns] = (turn(rows[:, columns], tables, 1) * SCALE).astype(BF16)


def project_keys(x, gain, bias, weight, add, tables):
    rows = x.shape[0]
    whole = lambda a: pl.BlockSpec(a.shape, lambda i: (0,) * a.ndim)
    return pl.pallas_call(
        functools.partial(keys_kernel, rows // tables.shape[1]),
        grid=(1,),
        in_specs=[
            whole(x),
            whole(gain),
            whole(bias),
            pl.BlockSpec((D, 128), lambda i: (0, D // 128)),
            whole(add),
            whole(tables),
        ],
        out_specs=[pl.BlockSpec((rows, 128), lambda i: (0, 0)), pl.BlockSpec((rows, D), lambda i: (0, 0))],
        out_shape=[SHAPE((rows, 128), BF16), SHAPE((rows, D), BF16)],
        compiler_params=params(),
        cost_estimate=cost(1),
        name="project_keys",
    )(x, gain, bias, weight, add, tables)


def project_queries(first_in, weight, add, tables):
    rows = first_in.shape[0]
    whole = lambda a: pl.BlockSpec(a.shape, lambda i: (0,) * a.ndim)
    return pl.pallas_call(
        functools.partial(queries_kernel, rows // tables.shape[1]),
        grid=(1,),
        in_specs=[
            whole(first_in),
            pl.BlockSpec((D, D), lambda i: (0, 0)),
            whole(add),
            whole(tables),
        ],
        out_specs=pl.BlockSpec((rows, D), lambda i: (0, 0)),
        out_shape=SHAPE((rows, D), BF16),
        compiler_params=params(),
        cost_estimate=cost(2),
        name="project_queries",
    )(first_in, weight, add, tables)


def gelu_parts(h):
    t = pl.reciprocal(1.0 + (0.3275911 / math.sqrt(2.0)) * jnp.abs(h))
    e = jnp.exp(-0.5 * h * h)
    poly = 0.5 * 1.061405429
    for coefficient in (-1.453152027, 1.421413741, -0.284496736, 0.254829592):
        poly = poly * t + 0.5 * coefficient
    tail = poly * t * e
    cdf = jnp.where(h >= 0.0, 1.0 - tail, tail)
    return h * cdf, cdf + h * e * (1.0 / math.sqrt(2.0 * math.pi))


def feed_kernel(
    place_ref,
    x_ref,
    xx_ref,
    g_ref,
    gg_ref,
    gain_ref,
    bias_ref,
    w1_ref,
    b1_ref,
    w2_ref,
    wo_ref,
    mlp_ref,
    back_ref,
    other_ref,
    attn_grad_ref,
    b1_grad_ref,
    theirs1_ref,
    mine1_ref,
    *refs,
):
    grad_refs, (in_scr, in_t_scr, g_scr, mlp_scr, back_scr) = refs[:-5], refs[-5:]
    step, steps = pl.program_id(0), pl.num_programs(0)
    rows = x_ref.shape[0]

    @pl.when(step == 0)
    def _():
        for i, (tokens, grads) in enumerate(((x_ref, g_ref), (xx_ref, gg_ref))):
            at = slice(i * rows, (i + 1) * rows)
            normed, _ = normalize(tokens[...].astype(F32))
            second_in = normed * wide(gain_ref) + wide(bias_ref)
            in_scr[at] = second_in.astype(BF16)
            in_t_scr[:, :, :, at] = second_in.T.astype(BF16).reshape(in_t_scr.shape[:3] + (rows,))
            g_scr[at] = grads[...]
        attn_grad_ref[...] = dot_nt(g_ref[...], wo_ref[...]).astype(BF16)

    g = g_scr[...]
    w1 = w1_ref[...]
    w2 = w2_ref[...]
    act, slope = gelu_parts(dot(in_scr[...], w1) + b1_ref[...])
    act = act.astype(BF16)
    pre = dot_nt(g, w2) * slope
    pre16 = pre.astype(BF16)
    b1_grad_ref[...] = jnp.sum(pre, axis=0, keepdims=True)
    mlp = dot(act, w2)
    grad = dot_tn(act, g).astype(BF16)
    if len(grad_refs) == 1:
        grad_refs[0][...] = grad
    for i in range(len(grad_refs) if len(grad_refs) > 1 else 0):

        @pl.when(step == i)
        def _(i=i):
            grad_refs[i][...] = grad

    back = dot_nt(pre16, w1)
    own = place_ref[1]
    for result, at in ((theirs1_ref, 1 - own), (mine1_ref, own)):
        left = in_t_scr[:, pl.ds(at, 1)].reshape(D // 2, 2 * rows)
        result[...] = dot(left, pre16).astype(BF16).reshape(result.shape)

    @pl.when(step == 0)
    def _():
        mlp_scr[...] = mlp
        back_scr[...] = back

    @pl.when((step > 0) & (step < steps - 1))
    def _():
        mlp_scr[...] += mlp
        back_scr[...] += back

    @pl.when(step == steps - 1)
    def _():
        for i, (scr, last, own_ref) in enumerate(((mlp_scr, mlp, mlp_ref), (back_scr, back, back_ref))):
            total = (scr[...] + last).astype(BF16)
            own_ref[...] = total[:rows]
            other_ref[i] = total[rows:]


CHUNK = 512


def feed(place, count, x, xx, g, gg, gain, bias, w1, b1, w2, wo):
    rows = x.shape[0]
    half = w1.shape[1] // 2
    depth = count // 2
    per = D // count // 2
    pieces = depth // 2
    aligned = pieces == 2 and half % 512 == 0
    chunk = half // pieces if aligned else CHUNK
    steps = half // chunk
    single = pl.Buffered(1)
    whole = lambda a: pl.BlockSpec(a.shape, lambda i, place: (0,) * a.ndim, pipeline_mode=single)
    fixed = lambda *shape: pl.BlockSpec(shape, lambda i, place: (0, 0))
    if aligned:
        piece = lambda i, place: (place[3] ^ (1 - i)) & 1
        grad_specs = [fixed(chunk, D)] * pieces
        grad_shapes = [SHAPE((chunk, D), BF16)] * pieces
    else:
        piece = lambda i, place: i
        grad_specs = [pl.BlockSpec((chunk, D), lambda i, place: (i, 0))]
        grad_shapes = [SHAPE((half, D), BF16)]
    at = lambda i, place: place[0] * steps + piece(i, place)
    cut = pl.BlockSpec((count, per, chunk), lambda i, place: (0, 0, piece(i, place)))
    spec = pltpu.PrefetchScalarGridSpec(
        num_scalar_prefetch=1,
        grid=(steps,),
        in_specs=[
            whole(x),
            whole(xx),
            whole(g),
            whole(gg),
            whole(gain),
            whole(bias),
            pl.BlockSpec((D, chunk), lambda i, place: (0, at(i, place))),
            pl.BlockSpec((1, chunk), lambda i, place: (0, at(i, place))),
            pl.BlockSpec((chunk, D), lambda i, place: (at(i, place), 0)),
            whole(wo),
        ],
        out_specs=[
            fixed(rows, D),
            fixed(rows, D),
            pl.BlockSpec((2, rows, D), lambda i, place: (0, 0, 0)),
            fixed(rows, D),
        ]
        + [pl.BlockSpec((1, chunk), lambda i, place: (0, piece(i, place))), cut, cut]
        + grad_specs,
        scratch_shapes=[
            pltpu.VMEM((2 * rows, D), BF16),
            pltpu.VMEM((count, 2, per, 2 * rows), BF16),
            pltpu.VMEM((2 * rows, D), BF16),
            pltpu.VMEM((2 * rows, D), F32),
            pltpu.VMEM((2 * rows, D), F32),
        ],
    )
    result = pl.pallas_call(
        feed_kernel,
        grid_spec=spec,
        out_shape=[SHAPE((rows, D), BF16), SHAPE((rows, D), BF16), SHAPE((2, rows, D), BF16), SHAPE((rows, D), BF16)]
        + [SHAPE((1, half), F32), SHAPE((count, per, half), BF16), SHAPE((count, per, half), BF16)]
        + grad_shapes,
        compiler_params=params(FULL_BYTES),
        cost_estimate=cost(12),
        name="feed_forward",
    )(place, x, xx, g, gg, gain, bias, w1, b1, w2, wo)
    grads = result[7:]
    if not aligned:
        cut = grads[0].reshape(pieces // 2, 2, -1, D)
        low = place[3] & 1
        grads = [take(cut, 1 - low, 1), take(cut, low, 1)]
    return result[:7], grads


def present(slot, y, z):
    back = slot // 2
    return (back <= z) & ((slot % 2 == 0) | (back >= 1) | (y == 1))


def whole_kernel(span, depth, place_ref, *refs):
    pair_refs, (q_ref, do_ref, tables_ref, rows_ref, even_out_ref, odd_out_ref) = refs[:depth], refs[depth:]
    out_ref, dq_ref = rows_ref.at[0], rows_ref.at[1]
    y, z = place_ref[2], place_ref[3]
    tables = [tables_ref[i] for i in range(3)]
    rows = PAIRS * span
    low = lax.broadcasted_iota(jnp.int32, (1, 128), 1) < HEAD_DIM

    def stacked(ref):
        return jnp.concatenate([ref[:, p * 128 : (p + 1) * 128] for p in range(PAIRS)], axis=0)

    blocks = [ref[i] for ref in pair_refs for i in range(2)]
    kv = jnp.concatenate(blocks, axis=0)
    swapped = pltpu.roll(kv.astype(F32), HEAD_DIM, 1).astype(BF16)
    zero, one = jnp.zeros_like(kv), jnp.ones_like(kv)
    keys = (jnp.where(low, kv, zero), jnp.where(low, zero, swapped))
    values = (jnp.where(low, swapped, zero), jnp.where(low, zero, kv))
    summing = (jnp.where(low, swapped, one), jnp.where(low, one, kv))
    slot = lax.broadcasted_iota(jnp.int32, (1, (2 * depth - 1) * span), 1) // span + 1
    absent = jnp.where(present(slot, y, z), 0.0, MASKED)
    token = lax.broadcasted_iota(jnp.int32, (rows, span), 0) % span
    seen = lax.broadcasted_iota(jnp.int32, (rows, span), 1) <= token
    q = stacked(q_ref)
    do = stacked(do_ref)
    do32 = do.astype(F32)

    expd, mixed = [], []
    for h in range(2):
        scores = dot_nt(q, keys[h])
        scores = jnp.concatenate([jnp.where(seen, scores[:, :span], MASKED), scores[:, span:] + absent], axis=1)
        top = jnp.max(scores, axis=1, keepdims=True)
        expd.append(jnp.exp(scores - top).astype(BF16))
        mixed.append(dot(expd[h], summing[h]))
    total = jnp.where(low, pltpu.roll(mixed[0], HEAD_DIM, 1), pltpu.roll(mixed[1], HEAD_DIM, 1))
    inverse = 1.0 / total
    out = jnp.where(low, mixed[0], mixed[1]) * inverse
    for p in range(PAIRS):
        out_ref[:, p * 128 : (p + 1) * 128] = out[p * span : (p + 1) * span].astype(BF16)
    product = do32 * out
    do_t = (do32 * inverse).T.astype(BF16)
    q_t = (q.astype(F32) * inverse).T.astype(BF16)
    dq = dk = dv = 0.0
    for h in range(2):
        head = slice(h * HEAD_DIM, (h + 1) * HEAD_DIM)
        delta = jnp.sum(jnp.where(low == (h == 0), product, 0.0), axis=1, keepdims=True)
        dprob = dot_nt(do, values[h])
        dscore = (expd[h].astype(F32) * (dprob - delta)).astype(BF16)
        dq = dq + dot(dscore, keys[h])
        dk = dk + dot(q_t[head], dscore)
        dv = dv + dot(do_t[head], expd[h])
    dq = dq * (inverse * SCALE)
    for p in range(PAIRS):
        dq_ref[:, p * 128 : (p + 1) * 128] = turn(dq[p * span : (p + 1) * span], tables, -1).astype(BF16)
    both = jnp.concatenate([dk, dv], axis=0).T.astype(BF16)
    for k in range(depth):
        even_out_ref[k] = both[2 * k * span : (2 * k + 1) * span]
        odd_out_ref[k] = both[(2 * k + 1) * span : (2 * k + 2) * span]


def loop_kernel(groups, span, block, count, place_ref, *refs):
    depth = count // 2
    pair_refs, refs = refs[:depth], refs[depth:]
    q_ref, do_ref, tables_ref, rows_ref, even_out_ref, odd_out_ref = refs[:6]
    out_ref, dq_ref = rows_ref.at[0], rows_ref.at[1]
    kv_scr, e_ref, kv_t_ref, max_ref, acc_ref, ext_ref = refs[6:]
    tables = [tables_ref[i] for i in range(3)]
    rows = groups * span
    per = block // span
    y, z = place_ref[2], place_ref[3]
    used = (2 * (z + 1) + per - 1) // per
    group, group_count = pl.program_id(1), pl.num_programs(1)
    low = lax.broadcasted_iota(jnp.int32, (1, 128), 1) < HEAD_DIM
    lanes = lax.broadcasted_iota(jnp.int32, (rows, 128), 1)

    def stacked(ref):
        return jnp.concatenate([ref[:, p * 128 : (p + 1) * 128] for p in range(groups)], axis=0)

    @pl.when(group == 0)
    def _():
        for i in range(count):
            kv_scr[i * span : (i + 1) * span] = pair_refs[i // 2][i % 2]

    q = stacked(q_ref)
    do = stacked(do_ref)

    def load(b):
        kv = kv_scr[pl.ds(pl.multiple_of(b * block, block), block)]
        swapped = pltpu.roll(kv.astype(F32), HEAD_DIM, 1).astype(BF16)
        return kv, swapped, jnp.zeros_like(kv)

    def absent(b):
        row = lax.broadcasted_iota(jnp.int32, (block, 128), 0) + b * block
        lane = lax.broadcasted_iota(jnp.int32, (block, 128), 1)
        mask = jnp.where(present(row // span, y, z), 0.0, MASKED)
        return jnp.where(lane < 2, -1.0, jnp.where(lane == 2, mask, 0.0)).astype(BF16)

    def key_tiles(b):
        kv, swapped, zero = load(b)
        ext = absent(b)
        return [
            jnp.concatenate([jnp.where(low, kv, zero), ext], axis=1),
            jnp.concatenate([jnp.where(low, zero, swapped), ext], axis=1),
        ]

    def value_tiles(b):
        kv, swapped, zero = load(b)
        ext = absent(b)
        return [
            jnp.concatenate([jnp.where(low, swapped, zero), ext], axis=1),
            jnp.concatenate([jnp.where(low, zero, kv), ext], axis=1),
        ]

    def seen():
        token = lax.broadcasted_iota(jnp.int32, (rows, block), 0) % span
        key = lax.broadcasted_iota(jnp.int32, (rows, block), 1)
        return (key <= token) | (key >= span)

    def extended(values):
        high = values.astype(BF16).astype(F32)
        rest = jnp.where(lanes == 1, values - high, jnp.where(lanes == 2, 1.0, 0.0))
        return jnp.where(lanes == 0, high, rest).astype(BF16)

    def over_blocks(step):
        step(0, True)

        def body(b, carry):
            step(b, False)
            return carry

        lax.fori_loop(1, used, body, 0)

    plain = jnp.concatenate([q, jnp.where(lanes == 2, 1.0, 0.0).astype(BF16)], axis=1)

    def maxima(b, diagonal):
        keys = key_tiles(b)
        for h in range(2):
            scores = dot_nt(plain, keys[h])
            if diagonal:
                scores = jnp.where(seen(), scores, MASKED)
            top = functools.reduce(jnp.maximum, [scores[:, i : i + 128] for i in range(0, block, 128)])
            max_ref[h] = top if diagonal else jnp.maximum(max_ref[h], top)

    over_blocks(maxima)
    for h in range(2):
        top = jnp.max(max_ref[h], axis=1, keepdims=True)
        ext_ref[h] = jnp.concatenate([q, extended(jnp.broadcast_to(top, (rows, 128)))], axis=1)

    def forward(b, diagonal):
        keys = key_tiles(b)
        kv, swapped, _ = load(b)
        one = jnp.ones_like(kv)
        values = (jnp.where(low, swapped, one), jnp.where(low, one, kv))
        for h in range(2):
            expd = jnp.exp(dot_nt(ext_ref[h], keys[h]))
            if diagonal:
                expd = jnp.where(seen(), expd, 0.0)
            expd = expd.astype(BF16)
            e_ref[b, h] = expd
            mixed = dot(expd, values[h])
            acc_ref[h] = mixed if diagonal else acc_ref[h] + mixed

    over_blocks(forward)
    first, second = acc_ref[0], acc_ref[1]
    total = jnp.where(low, pltpu.roll(first, HEAD_DIM, 1), pltpu.roll(second, HEAD_DIM, 1))
    inverse = 1.0 / total
    out = jnp.where(low, first, second) * inverse
    for p in range(groups):
        out_ref[:, p * 128 : (p + 1) * 128] = out[p * span : (p + 1) * span].astype(BF16)
    do32 = do.astype(F32)
    product = do32 * out
    high = product.astype(BF16)
    rest = (product - high.astype(F32)).astype(BF16)
    place = lax.broadcasted_iota(jnp.int32, (128, 128), 0)
    for h in range(2):
        ones = jnp.where((place < HEAD_DIM) == (h == 0), 1.0, 0.0).astype(BF16)
        delta = dot(high, ones) + dot(rest, ones)
        ext_ref[h] = jnp.concatenate([do, extended(delta)], axis=1)
    do_t = (do32 * inverse).T.astype(BF16)
    q_t = (q.astype(F32) * inverse).T.astype(BF16)

    def backward(b, start):
        values = value_tiles(b)
        kv, swapped, zero = load(b)
        keys = (jnp.where(low, kv, zero), jnp.where(low, zero, swapped))
        dq = dk = dv = 0.0
        for h in range(2):
            expd = e_ref[b, h]
            head = slice(h * HEAD_DIM, (h + 1) * HEAD_DIM)
            dscore = (expd.astype(F32) * dot_nt(ext_ref[h], values[h])).astype(BF16)
            dq = dq + dot(dscore, keys[h])
            dk = dk + dot(q_t[head], dscore)
            dv = dv + dot(do_t[head], expd)
        acc_ref[0] = dq if start else acc_ref[0] + dq
        both = jnp.concatenate([dk, dv], axis=0)
        kv_t_ref[b] = jnp.where(group == 0, both, kv_t_ref[b] + both)

    over_blocks(backward)
    dq = acc_ref[0] * (inverse * SCALE)
    for p in range(groups):
        dq_ref[:, p * 128 : (p + 1) * 128] = turn(dq[p * span : (p + 1) * span], tables, -1).astype(BF16)

    @pl.when(group == group_count - 1)
    def _():
        for b in range(count // per):
            used_block = jnp.where(b < used, kv_t_ref[b], 0.0).T.astype(BF16)
            for i in range(per):
                slot = b * per + i
                result = odd_out_ref if slot % 2 else even_out_ref
                result[slot // 2] = used_block[i * span : (i + 1) * span]


def attention(place, pairs, q, do, tables):
    depth = len(pairs)
    count = 2 * depth
    seqs, span, _ = q.shape
    single = count * span <= 1024
    groups = PAIRS if single else 2
    wide_spec = pl.BlockSpec((None, span, groups * 128), lambda s, i: (s, 0, i))
    pieces = pl.BlockSpec((depth, None, span, 128), lambda s, i: (0, s, 0, 0))
    two = pl.BlockSpec((2, None, span, 128), lambda s, i: (0, s, 0, 0))
    if single:
        kernel, scratch = functools.partial(whole_kernel, span, depth), []
    else:
        block = max(512, span)
        blocks = count * span // block
        rows = groups * span
        kernel = functools.partial(loop_kernel, groups, span, block, count)
        scratch = [
            pltpu.VMEM((count * span, 128), BF16),
            pltpu.VMEM((blocks, 2, rows, block), BF16),
            pltpu.VMEM((blocks, 128, block), F32),
            pltpu.VMEM((2, rows, 128), F32),
            pltpu.VMEM((2, rows, 128), F32),
            pltpu.VMEM((2, rows, 256), BF16),
        ]
    return pl.pallas_call(
        kernel,
        grid=(seqs, PAIRS // groups),
        in_specs=[SMEM] + [two] * depth + [wide_spec, wide_spec, pl.BlockSpec(tables.shape, lambda s, i: (0, 0, 0))],
        out_specs=[pl.BlockSpec((2, None, span, groups * 128), lambda s, i: (0, s, 0, i))] + [pieces] * 2,
        out_shape=[SHAPE((2, seqs, span, D), BF16)]
        + [SHAPE((depth, seqs, span, 128), BF16)] * 2,
        scratch_shapes=scratch,
        compiler_params=params(FULL_BYTES),
        cost_estimate=cost(10),
        name="attention",
    )(place, *pairs, q, do, tables)


def weights_kernel(place_ref, attn_ref, attn2_ref, g_ref, g2_ref, in_ref, in2_ref, q_ref, q2_ref, theirs_ref, mine_ref, small_ref, scr):
    half = D // 2
    y = place_ref[2]

    def products(left, right, line):
        at = pl.ds(pl.multiple_of(place_ref[0] * half, 128), half)
        small_ref[line : line + 1] = jnp.zeros_like(small_ref[line : line + 1])
        small_ref[line : line + 1, at] = jnp.sum(right.astype(F32), axis=0, keepdims=True)
        scr[...] = dot_tn(left, right).reshape(scr.shape)
        theirs_ref[0] = scr[:, pl.ds(1 - y, 1)].reshape(theirs_ref.shape[1:]).astype(BF16)
        mine_ref[0] = scr[:, pl.ds(y, 1)].reshape(mine_ref.shape[1:]).astype(BF16)

    both = lambda a, b: jnp.concatenate([a[...], b[...]], axis=0)

    @pl.when(pl.program_id(0) == 0)
    def _():
        products(both(attn_ref, attn2_ref), both(g_ref, g2_ref), 1)

    @pl.when(pl.program_id(0) == 1)
    def _():
        products(both(in_ref, in2_ref), both(q_ref, q2_ref), 0)


def weights(place, count, both, both2, g, g2, first_in, first_in2):
    rows = g.shape[0]
    depth, per, half = count // 2, D // count, D // 2
    whole = pl.BlockSpec((rows, D), lambda i, place: (0, 0), pipeline_mode=pl.Buffered(1))
    part = pl.BlockSpec((rows, half), lambda i, place: (0, place[0]), pipeline_mode=pl.Buffered(1))
    attn_part = pl.BlockSpec((None, rows, D), lambda i, place: (0, 0, 0), pipeline_mode=pl.Buffered(1))
    q_part = pl.BlockSpec((None, rows, half), lambda i, place: (1, 0, place[0]), pipeline_mode=pl.Buffered(1))
    result = pl.BlockSpec((1, depth, per, half), lambda i, place: (i, 0, 0, 0))
    return pl.pallas_call(
        weights_kernel,
        grid_spec=pltpu.PrefetchScalarGridSpec(
            num_scalar_prefetch=1,
            grid=(2,),
            in_specs=[attn_part, attn_part, part, part, whole, whole, q_part, q_part],
            out_specs=[result, result, pl.BlockSpec((8, D), lambda i, place: (0, 0))],
            scratch_shapes=[pltpu.VMEM((depth, 2, per, half), F32)],
        ),
        out_shape=[SHAPE((2, depth, per, half), BF16), SHAPE((2, depth, per, half), BF16), SHAPE((8, D), F32)],
        compiler_params=params(FULL_BYTES),
        cost_estimate=cost(2.4),
        name="weights",
    )(place, both, both2, g, g2, first_in, first_in2, both, both2)


def mix_kernel(x_ref, mlp_ref, mlp2_ref, attn_ref, add_ref, wo_ref, output_ref):
    mlp = mlp_ref[...].astype(F32) + mlp2_ref[...].astype(F32)
    x = x_ref[...].astype(F32)
    output_ref[...] = (x + (mlp + dot(attn_ref[...], wo_ref[...])) + wide(add_ref)).astype(BF16)


def mix(x, mlp, other, both, add, wo):
    rows = x.shape[0]
    row = pl.BlockSpec((rows, D), lambda i: (i, 0))
    first = pl.BlockSpec((None, rows, D), lambda i: (0, i, 0))
    return pl.pallas_call(
        mix_kernel,
        grid=(1,),
        in_specs=[row, row, first, first, pl.BlockSpec((D,), lambda i: (0,)), pl.BlockSpec((D, D), lambda i: (0, 0))],
        out_specs=row,
        out_shape=SHAPE((rows, D), BF16),
        compiler_params=params(),
        cost_estimate=cost(1.2),
        name="mix",
    )(x, mlp, other, both, add, wo)


def two_terms(values):
    high = values.astype(BF16)
    return high, (values - high.astype(F32)).astype(BF16)


def message_lines(ff):
    return -(-(ff // 128 + 6 * (D // 128) + 1) // 16) * 16


def finish_kernel(
    copies,
    count,
    lines,
    place_ref,
    *refs,
):
    kv_refs, refs = refs[:count], refs[count:]
    (
        extra_ref,
        x_ref,
        g_ref,
        q_ref,
        back_ref,
        back2_ref,
        gain_ref,
        bias_ref,
        gain2_ref,
        wqkv_ref,
        tables_ref,
        b1_ref,
        early_ref,
        tokens_ref,
        theirs_ref,
        mine_ref,
        vector_scr,
        weight_scr,
    ) = refs
    total = extra_ref[...].astype(F32)
    for ref in kv_refs:
        total += ref[...].astype(F32)
    tables = repeated(tables_ref, copies)
    grad = turn(total, key_tables(tables), -1).astype(BF16)
    x = x_ref[...].astype(F32)
    normed, inverse = normalize(x)
    gain = wide(gain_ref)
    first_in = normed * gain + wide(bias_ref)
    first_grad = dot_nt(jnp.concatenate([q_ref[...], grad], axis=1), wqkv_ref[...])
    second_grad = back_ref[...].astype(F32) + back2_ref[...].astype(F32)

    vector_scr[...] = jnp.zeros_like(vector_scr)
    b1 = b1_ref[...]
    b1_lines = b1.shape[1] // 128
    for i in range(b1_lines):
        vector_scr[pl.ds(place_ref[0] * b1_lines + i, 1)] = b1[:, i * 128 : (i + 1) * 128]
    at = 2 * b1_lines
    sums = [early_ref[0:1], jnp.sum(grad.astype(F32), axis=0, keepdims=True), early_ref[1:2]]
    for rows in (first_grad * normed, first_grad, second_grad * normed, second_grad):
        sums.append(jnp.sum(rows, axis=0, keepdims=True))
    for row in sums:
        for i in range(row.shape[1] // 128):
            vector_scr[at : at + 1] = row[:, i * 128 : (i + 1) * 128]
            at += 1
    high, rest = two_terms(vector_scr[...])
    weight_scr[...] = dot(first_in.T.astype(BF16), grad).reshape(weight_scr.shape)
    y = place_ref[2]
    for message, at in ((theirs_ref, 1 - y), (mine_ref, y)):
        message[:lines] = high
        message[lines : 2 * lines] = rest
        message[2 * lines :] = weight_scr[:, pl.ds(at, 1)].reshape(-1, 128).astype(BF16)

    normed_grad = first_grad * gain + second_grad * wide(gain2_ref)
    mean = jnp.mean(normed_grad, axis=-1, keepdims=True)
    along_rows = jnp.mean(normed_grad * normed, axis=-1, keepdims=True)
    tokens_ref[...] = (g_ref[...].astype(F32) + inverse * (normed_grad - mean - normed * along_rows)).astype(BF16)


def finish(place, places, ff, kv_parts, extra, x, g, both, back, other, gain, bias, gain2, wqkv, tables, b1, early):
    rows = x.shape[0]
    lines = message_lines(ff)
    whole = lambda a: pl.BlockSpec(a.shape, lambda i: (0,) * a.ndim)
    second = pl.BlockSpec((None, rows, D), lambda i: (1, 0, 0))
    before, between, behind = (*kv_parts, extra, x, g), (back,), (gain, bias, gain2, wqkv, tables, b1, early)
    return pl.pallas_call(
        functools.partial(finish_kernel, rows // tables.shape[1], len(kv_parts), lines),
        grid=(1,),
        in_specs=[SMEM]
        + [whole(a) for a in before]
        + [second]
        + [whole(a) for a in between]
        + [second]
        + [whole(a) for a in behind],
        out_specs=[
            pl.BlockSpec((rows, D), lambda i: (0, 0)),
            pl.BlockSpec((2 * lines + D // 2, 128), lambda i: (0, 0)),
            pl.BlockSpec((2 * lines + D // 2, 128), lambda i: (0, 0)),
        ],
        out_shape=[SHAPE((rows, D), BF16)] + [SHAPE((2 * lines + D // 2, 128), BF16)] * 2,
        scratch_shapes=[pltpu.VMEM((lines, 128), F32), pltpu.VMEM((places // 2, 2, D // places, 128), F32)],
        compiler_params=params(),
        cost_estimate=cost(2.4),
        name="finish",
    )(place, *before, both, *between, other, *behind)


def message_cut(place, mine, come, lines, per):
    count = (mine.shape[0] - 2 * lines) // per

    def kernel(place_ref, a_ref, b_ref, *refs):
        results, scr = refs[:-1], refs[-1]
        high, rest = two_terms(tree_sum([ref[at : at + lines] for ref in (a_ref, b_ref) for at in (0, lines)]))
        scr[...] = (a_ref[2 * lines :].astype(F32) + b_ref[2 * lines :].astype(F32)).reshape(scr.shape)
        for i, result in enumerate(results):
            result[:lines] = high
            result[lines : 2 * lines] = rest
            result[2 * lines :] = scr[place_ref[3] ^ i].astype(BF16)

    return pl.pallas_call(
        kernel,
        in_specs=[SMEM, VMEM, VMEM],
        out_specs=[VMEM] * count,
        out_shape=[SHAPE((2 * lines + per, 128), BF16)] * count,
        scratch_shapes=[pltpu.VMEM((count, per, 128), F32)],
        compiler_params=params(),
        cost_estimate=cost(0.6),
        name="message_cut",
    )(place, mine, come)


def message_sum(messages, lines):
    def kernel(*refs):
        result = refs[-1]
        total = tree_sum([ref[...] for ref in refs[:-1]])
        high, rest = two_terms(total[:lines] + total[lines : 2 * lines])
        result[:lines] = high
        result[lines : 2 * lines] = rest
        result[2 * lines :] = total[2 * lines :].astype(BF16)

    return pl.pallas_call(
        kernel,
        in_specs=[VMEM] * len(messages),
        out_specs=VMEM,
        out_shape=SHAPE(messages[0].shape, BF16),
        compiler_params=params(),
        cost_estimate=cost(0.6),
        name="message_sum",
    )(*messages)


def last_sums(place, messages, lines, widths, top, mine2, other2, mine3, other3):
    count = len(messages)
    half = D // 2
    per = mine3.shape[1]

    def kernel(place_ref, *refs):
        sources, (a2, b2, a3, b3) = refs[:count], refs[count : count + 4]
        vectors, (second, out, qkv) = refs[count + 4 : -3], refs[-3:]
        core = place_ref[0]
        total = tree_sum([ref[...] for ref in sources])
        vector = total[:lines] + total[lines : 2 * lines]
        at = 0
        for result, width in zip(vectors, widths):
            for i in range(width // 128):
                result[i * 128 : (i + 1) * 128] = vector[at + i]
            at += width // 128
        owner = (place_ref[3] >> top) == core
        second[...] = jnp.where(owner, a2[...].astype(F32), b2[...].astype(F32))
        for i, result in ((0, out), (1, qkv)):
            own, other = a3[i].astype(F32), b3[i].astype(F32)
            result[:, :half] = jnp.where(core == 0, own, other)
            result[:, half:D] = jnp.where(core == 0, other, own)
        qkv[:, D:] = total[2 * lines :]

    return pl.pallas_call(
        kernel,
        in_specs=[SMEM] + [VMEM] * (count + 4),
        out_specs=[VMEM] * (len(widths) + 3),
        out_shape=[SHAPE((width,), F32) for width in widths]
        + [SHAPE(mine2.shape, F32), SHAPE((per, D), F32), SHAPE((per, D + 128), F32)],
        compiler_params=params(),
        cost_estimate=cost(0.6),
        name="last_sums",
    )(place, *messages, mine2, other2, mine3, other3)


def local(
    tokens,
    ln1_gain,
    ln1_bias,
    qkv_weight,
    qkv_bias,
    out_weight,
    ln2_gain,
    ln2_bias,
    fc1_weight,
    fc1_bias,
    fc2_weight,
    out_bias,
    output_grad,
    key_value_grad,
):
    seqs, span, _ = tokens.shape
    rows = seqs * span
    ff = fc1_weight.shape[1]
    count = lax.axis_size("seq")
    batches = lax.axis_size("batch")
    depth = count // 2
    half_depth = depth // 2
    per1, per2 = D // count, ff // count
    own = lax.axis_index("seq").astype(jnp.int32)
    batch = lax.axis_index("batch").astype(jnp.int32)
    y, z = own & 1, own >> 1
    core, xs = batch & 1, batch >> 1
    place = jnp.stack([core, xs, y, z])
    x = tokens.reshape(rows, D)
    g = output_grad.reshape(rows, D)
    over_core = lambda v: flipped(v, "batch", 1)
    over_x = lambda v: flipped(v, "batch", 2)
    over_y = lambda v: flipped(v, "seq", 1)
    over_z = lambda v, bit: flipped(v, "seq", 2 << bit)
    z_bits = depth.bit_length() - 1
    flat = lambda v: v.reshape(rows, -1)

    def pair(mine, other, index, axis):
        first = jnp.where(index == 0, mine, other)
        second = jnp.where(index == 0, other, mine)
        return jnp.concatenate([first, second], axis=axis)

    def summed(*parts):
        return tree_sum(parts).astype(BF16)

    x_other, g_other = over_core(x), over_core(g)
    tables = rotary_tables(own * span, span)
    kv, first_in = project_keys(x, ln1_gain, ln1_bias, qkv_weight, qkv_bias, tables)
    kv3 = kv.reshape(seqs, span, 128)
    kv_y = over_y(kv3)
    first_other = over_core(first_in)
    q = project_queries(first_in, qkv_weight, qkv_bias, tables)
    (kv_y,) = after((kv_y,), q)
    two = jnp.stack([kv3, kv_y])
    pairs = [two] + [along(two, k) for k in range(1, depth)]

    x_fed, g_fed, first_other = after((x, g, first_other), two)
    (mlp, back, feed_other, attn_grad, b1_grad, theirs1, mine1), (theirs2, mine2) = feed(
        place, count, *after((x_fed, x_other, g_fed, g_other), first_other), ln2_gain, ln2_bias, fc1_weight, fc1_bias.reshape(1, -1),
        fc2_weight, out_weight,
    )
    come1 = over_x(theirs1)
    come2 = over_z(theirs2, 0)
    feed_come = over_core(feed_other)

    q3, do3 = q.reshape(seqs, span, D), attn_grad.reshape(seqs, span, D)
    both, even, odd = attention(place, pairs, q3, do3, tables)
    odd = over_y(odd)

    def halved(a, parts, height):
        return a.reshape(parts, 2, height, a.shape[-1])

    both = both.reshape(2, rows, D)
    both_other = over_core(both)
    mine1, come1, mine2, come2, feed_come = after((mine1, come1, mine2, come2, feed_come), both)
    height = per2 // 2
    view1 = lambda v: halved(v, depth // 2, per1)
    view2 = lambda v: halved(v, half_depth, height)
    theirs1, mine1, theirs2, mine2 = add_split(
        place, [(view1(mine1), view1(come1), 3), (view2(mine2), view2(come2), 1)], 6
    )
    come1, come2 = over_z(theirs1, 0), over_x(theirs2)

    (both_other,) = after((both_other,), theirs1)
    theirs3, mine3, early = weights(place, count, both, both_other, g, g_other, first_in, first_other)
    come3 = over_y(theirs3)

    even, odd = after((even, odd), theirs3)
    kv_sums = [summed(even[k], odd[k]) for k in range(depth)]
    (x_mix,) = after((x,), *kv_sums)
    output = mix(x_mix, mlp, feed_come, both, out_bias, out_weight)
    (kv_next,) = after((kv_sums[1],), output)
    got = [along(kv_next, -1)] + [along(kv_sums[k], -k) for k in range(2, depth)]

    mine1, come1, mine2, come2 = after((mine1, come1, mine2, come2), output)
    view1 = lambda v: halved(v, depth // 2, per1 // 2)
    view2 = lambda v: halved(v, half_depth // 2, height)
    theirs12, mine1, mine2 = exchange_split(place, view1(mine1), view1(come1), view2(mine2), view2(come2))
    come12 = over_y(theirs12)
    mine3, come3 = after((mine3, come3), theirs12)
    parts3 = add_cut(place, mine3, come3)
    come3 = [flipped(parts3[i], "seq", 2 * i) for i in range(1, depth)]

    got = after(got, parts3[0])
    lines = message_lines(ff)
    tokens_grad, theirs4, mine4 = finish(
        place, count, ff, [flat(v) for v in (kv_sums[0], *got)], flat(key_value_grad), x, g, both, back, feed_come,
        ln1_gain, ln1_bias, ln2_gain, qkv_weight, tables, b1_grad, early,
    )
    come4 = over_y(theirs4)

    mine1, mine2, come12 = after((mine1, mine2, come12), tokens_grad)
    theirs1, mine1, sum2 = exchange_add(place, mine1, mine2, come12, 1)
    come1 = over_z(theirs1, 1)
    for bit in range(2, z_bits):
        view1 = lambda v: halved(v, depth >> (bit + 1), per1 // 2)
        theirs1, mine1 = add_split(place, [(view1(mine1), view1(come1), 3 + bit)], 0.01)
        come1 = over_z(theirs1, bit)
    for bit in range(1, z_bits - 1):
        sum2 = halved(sum2, half_depth >> (bit + 1), height)
        own_bit = (z >> bit) & 1
        sum2 = summed(take(sum2, own_bit, 1), over_z(take(sum2, 1 - own_bit, 1), bit))
    sum2 = sum2.reshape(height, D)
    come2 = to_owner(sum2)

    come3 = after(come3, theirs1, sum2)
    mine4, come4 = after((mine4, come4), *come3)
    parts4 = message_cut(place, mine4, come4, lines, per1)
    come4 = [flipped(parts4[i], "seq", 2 * i) for i in range(1, depth)]
    mine1, come1 = after((mine1, come1), parts4[0])
    sum1 = summed(mine1, come1).reshape(per1 // 2, -1)
    other1 = over_x(sum1)
    come3 = after(come3, sum1)
    sum3 = summed(parts3[0], *come3)
    other3 = over_x(sum3)
    sum2, come2 = after((sum2, come2), sum3)
    sum2 = summed(sum2, come2)
    other2 = between_owners(sum2)
    come4 = after(come4, sum2)
    message = message_sum([parts4[0], *come4], lines)
    got = [flipped(message, "batch", i) for i in range(1, batches)]

    sum1, other1 = after((sum1, other1), message)
    sum1 = pair(sum1, other1, xs, 0)
    other1 = over_core(sum1)
    sum3, other3 = after((sum3, other3), sum1)
    sum3 = summed(sum3, other3)
    other3 = over_core(sum3)
    sum2, other2 = after((sum2, other2), sum3)
    sum2 = pair(sum2, other2, xs, 0)
    other2 = over_core(sum2)

    (other1,) = after((other1,), sum2)
    fc1_grad = pair(sum1, other1, core, 1).astype(F32)
    got = after(got, fc1_grad)
    widths = (ff, D + 128) + (D,) * 5
    b1_sum, qkv_sum, out_sum, gain1, bias1, gain2, bias2, fc2_grad, out_grad, qkv_grad = last_sums(
        place, [message, *got], lines, widths, z_bits - 1, sum2, other2, sum3, other3
    )
    return (
        output.reshape(tokens.shape),
        kv3,
        tokens_grad.reshape(tokens.shape),
        gain1,
        bias1,
        qkv_grad,
        qkv_sum,
        out_grad,
        gain2,
        bias2,
        fc1_grad,
        b1_sum,
        fc2_grad,
        out_sum,
    )


def solution(mesh):
    part = P("batch", "seq", None)
    whole = P()
    split = P("seq", None)
    return jax.shard_map(
        local,
        mesh=mesh,
        in_specs=(part,) + (whole,) * 11 + (part, part),
        out_specs=(
            part, part, part, whole, whole, split, whole, split, whole, whole, split, whole, split, whole,
        ),
        check_vma=False,
    )
```

```python
import functools
import math

import jax
import jax.numpy as jnp
from jax import lax
from jax.experimental import pallas as pl
from jax.experimental.pallas import tpu as pltpu
from jax.sharding import PartitionSpec as P

D = 768
HEADS = 12
HEAD_DIM = 64
ROT = 16
PAIRS = HEADS // 2
SCALE = 1.0 / math.sqrt(HEAD_DIM)
NORM_EPS = 1e-05
MASKED = -1e30
F32 = jnp.float32
BF16 = jnp.bfloat16
VMEM_BYTES = 56 * 1024 * 1024
FULL_BYTES = 63 * 1024 * 1024


def dot(a, b):
    return lax.dot_general(a, b, (((1,), (0,)), ((), ())), preferred_element_type=F32)


def dot_nt(a, b):
    return lax.dot_general(a, b, (((1,), (1,)), ((), ())), preferred_element_type=F32)


def dot_tn(a, b):
    return lax.dot_general(a, b, (((0,), (0,)), ((), ())), preferred_element_type=F32)


def params(limit=VMEM_BYTES):
    return pltpu.CompilerParams(vmem_limit_bytes=limit)


def flipped(block, axis, bits):
    return lax.ppermute(block, axis, [(i, i ^ bits) for i in range(lax.axis_size(axis))])


def along(block, distance):
    size = lax.axis_size("seq")
    return lax.ppermute(block, "seq", [(i, (i + 2 * distance) % size) for i in range(size)])


def owners(size):
    return [(b, i) for b in range(lax.axis_size("batch")) for i in range(size) if i // (size // 2) == b % 2]


def to_owner(block):
    size = lax.axis_size("seq")
    route = [(b * size + (i ^ (size // 2)), b * size + i) for b, i in owners(size)]
    return lax.ppermute(block, ("batch", "seq"), route)


def between_owners(block):
    size = lax.axis_size("seq")
    route = [(b * size + i, (b ^ 2) * size + i) for b, i in owners(size)]
    return lax.ppermute(block, ("batch", "seq"), route)


def after(values, *others):
    return lax.optimization_barrier((tuple(values), others))[0]


def tree_sum(parts):
    parts = [p.astype(F32) for p in parts]
    while len(parts) > 1:
        parts = [sum(parts[i : i + 2][1:], parts[i]) for i in range(0, len(parts), 2)]
    return parts[0]


def take(block, index, axis):
    return lax.dynamic_index_in_dim(block, index, axis, keepdims=False)


def normalize(rows):
    centre = jnp.mean(rows, axis=-1, keepdims=True)
    centred = rows - centre
    spread = jnp.mean(centred * centred, axis=-1, keepdims=True)
    inverse = lax.rsqrt(spread + NORM_EPS)
    return centred * inverse, inverse


def rotary_tables(first, count):
    kind = lax.broadcasted_iota(jnp.int32, (3, count, 128), 0)
    place = lax.broadcasted_iota(jnp.int32, (3, count, 128), 1)
    lane = lax.broadcasted_iota(jnp.int32, (3, count, 128), 2) % HEAD_DIM
    half = ROT // 2
    freqs = 10000.0 ** (-(lane % half).astype(F32) / half)
    angles = (first + place).astype(F32) * 0.25 * freqs
    cosine = jnp.where(lane < ROT, jnp.cos(angles), 1.0)
    sine = jnp.sin(angles)
    below = jnp.where((lane >= half) & (lane < ROT), sine, 0.0)
    above = jnp.where(lane < half, -sine, 0.0)
    return jnp.where(kind == 0, cosine, jnp.where(kind == 1, below, above))


def turn(values, tables, sign):
    moved = pltpu.roll(values, ROT // 2, 1) * tables[1] + pltpu.roll(values, 128 - ROT // 2, 1) * tables[2]
    return values * tables[0] + (moved if sign > 0 else -moved)


def repeated(tables_ref, count):
    return [jnp.concatenate([tables_ref[i]] * count, axis=0) for i in range(3)]


def key_tables(tables):
    low = lax.broadcasted_iota(jnp.int32, (1, 128), 1) < HEAD_DIM
    return [jnp.where(low, tables[0], 1.0), jnp.where(low, tables[1], 0.0), jnp.where(low, tables[2], 0.0)]

VMEM = pl.BlockSpec(memory_space=pltpu.VMEM)
SMEM = pl.BlockSpec(memory_space=pltpu.SMEM)
SHAPE = jax.ShapeDtypeStruct


def cost(share):
    return pl.CostEstimate(flops=int(share * 3e9), bytes_accessed=0, transcendentals=0)


def wide(ref):
    return ref[...].reshape(1, -1)


def add_split(place, items, share=1.2):
    def kernel(place_ref, *refs):
        sources, results = refs[: 2 * len(items)], refs[2 * len(items) :]
        for n, (_, _, which) in enumerate(items):
            a, b = sources[2 * n], sources[2 * n + 1]
            own = place_ref[which] if which < 3 else lax.rem(lax.shift_right_logical(place_ref[3], which - 3), 2)
            for m in range(a.shape[0]):
                for result, at in ((results[2 * n], 1 - own), (results[2 * n + 1], own)):
                    result[m] = (a[m, at].astype(F32) + b[m, at].astype(F32)).astype(BF16)

    shapes = []
    for a, _, _ in items:
        shapes += [SHAPE((a.shape[0],) + a.shape[2:], BF16)] * 2
    arrays = [v for item in items for v in item[:2]]
    return pl.pallas_call(
        kernel,
        in_specs=[SMEM] + [VMEM] * len(arrays),
        out_specs=[VMEM] * len(shapes),
        out_shape=shapes,
        compiler_params=params(FULL_BYTES),
        cost_estimate=cost(share),
        name="add_split",
    )(place, *arrays)


def exchange_split(place, mine1, come1, mine2, come2):
    def kernel(place_ref, a1, b1, a2, b2, theirs, keep1, keep2):
        y = place_ref[2]
        row = 0
        for a, b, keep in ((a1, b1, keep1), (a2, b2, keep2)):
            m, _, r, c = a.shape
            part = a[:, pl.ds(1 - y, 1)].astype(F32) + b[:, pl.ds(1 - y, 1)].astype(F32)
            part = part.reshape(m * r, c).astype(BF16)
            for at in range(0, c, D // 2):
                theirs[row : row + m * r] = part[:, at : at + D // 2]
                row += m * r
            part = a[:, pl.ds(y, 1)].astype(F32) + b[:, pl.ds(y, 1)].astype(F32)
            keep[...] = part.reshape(m, r, c).astype(BF16)

    shapes = [(a.shape[0],) + a.shape[2:] for a in (mine1, mine2)]
    size = sum(math.prod(s) for s in shapes)
    return pl.pallas_call(
        kernel,
        in_specs=[SMEM] + [VMEM] * 4,
        out_specs=[VMEM] * 3,
        out_shape=[SHAPE((size // (D // 2), D // 2), BF16)] + [SHAPE(s, BF16) for s in shapes],
        compiler_params=params(FULL_BYTES),
        cost_estimate=cost(1.2),
        name="exchange_split",
    )(place, mine1, come1, mine2, come2)


def exchange_add(place, mine1, mine2, come, bit):
    def kernel(place_ref, a1, a2, b, theirs, keep, total):
        row = 0
        parts = []
        for a in (a1, a2):
            m, r, c = a.shape
            columns = []
            for _ in range(0, c, D // 2):
                columns.append(b[row : row + m * r])
                row += m * r
            parts.append(jnp.concatenate(columns, axis=1).astype(F32).reshape(m, r, c))
        own = (place_ref[3] >> bit) & 1
        total[...] = (a2[...].astype(F32) + parts[1]).astype(BF16)
        both = (a1[...].astype(F32) + parts[0]).astype(BF16)
        m, r, c = a1.shape
        both = both.reshape(m // 2, 2, r, c)
        lower, upper = both[:, 0], both[:, 1]
        theirs[...] = jnp.where(own == 0, upper, lower)
        keep[...] = jnp.where(own == 0, lower, upper)

    half = SHAPE((mine1.shape[0] // 2,) + mine1.shape[1:], BF16)
    return pl.pallas_call(
        kernel,
        in_specs=[SMEM] + [VMEM] * 3,
        out_specs=[VMEM] * 3,
        out_shape=[half, half, SHAPE(mine2.shape, BF16)],
        compiler_params=params(),
        cost_estimate=cost(0.01),
        name="exchange_add",
    )(place, mine1, mine2, come)


def add_cut(place, a, b):
    parts = a.shape[1]

    def kernel(place_ref, a_ref, b_ref, *results):
        for i in range(parts):
            at = place_ref[3] ^ i
            for k in range(a.shape[0]):
                results[i][k] = (a_ref[k, at].astype(F32) + b_ref[k, at].astype(F32)).astype(BF16)

    return pl.pallas_call(
        kernel,
        in_specs=[SMEM, VMEM, VMEM],
        out_specs=[VMEM] * parts,
        out_shape=[SHAPE((a.shape[0],) + a.shape[2:], BF16)] * parts,
        compiler_params=params(FULL_BYTES),
        cost_estimate=cost(1.2),
        name="add_cut",
    )(place, a, b)


def keys_kernel(copies, x_ref, gain_ref, bias_ref, weight_ref, add_ref, tables_ref, kv_ref, first_ref):
    normed, _ = normalize(x_ref[...].astype(F32))
    first_in = (normed * wide(gain_ref) + wide(bias_ref)).astype(BF16)
    first_ref[...] = first_in
    part = dot(first_in, weight_ref[...]) + wide(add_ref)[:, D:]
    kv_ref[...] = turn(part, key_tables(repeated(tables_ref, copies)), 1).astype(BF16)


def queries_kernel(copies, first_ref, weight_ref, add_ref, tables_ref, q_ref):
    first_in = first_ref[...]
    tables = repeated(tables_ref, copies)
    rows = dot(first_in, weight_ref[...]) + wide(add_ref)[:, :D]
    for p in range(PAIRS):
        columns = slice(p * 128, (p + 1) * 128)
        q_ref[:, columns] = (turn(rows[:, columns], tables, 1) * SCALE).astype(BF16)


def project_keys(x, gain, bias, weight, add, tables):
    rows = x.shape[0]
    whole = lambda a: pl.BlockSpec(a.shape, lambda i: (0,) * a.ndim)
    return pl.pallas_call(
        functools.partial(keys_kernel, rows // tables.shape[1]),
        grid=(1,),
        in_specs=[
            whole(x),
            whole(gain),
            whole(bias),
            pl.BlockSpec((D, 128), lambda i: (0, D // 128)),
            whole(add),
            whole(tables),
        ],
        out_specs=[pl.BlockSpec((rows, 128), lambda i: (0, 0)), pl.BlockSpec((rows, D), lambda i: (0, 0))],
        out_shape=[SHAPE((rows, 128), BF16), SHAPE((rows, D), BF16)],
        compiler_params=params(),
        cost_estimate=cost(1),
        name="project_keys",
    )(x, gain, bias, weight, add, tables)


def project_queries(first_in, weight, add, tables):
    rows = first_in.shape[0]
    whole = lambda a: pl.BlockSpec(a.shape, lambda i: (0,) * a.ndim)
    return pl.pallas_call(
        functools.partial(queries_kernel, rows // tables.shape[1]),
        grid=(1,),
        in_specs=[
            whole(first_in),
            pl.BlockSpec((D, D), lambda i: (0, 0)),
            whole(add),
            whole(tables),
        ],
        out_specs=pl.BlockSpec((rows, D), lambda i: (0, 0)),
        out_shape=SHAPE((rows, D), BF16),
        compiler_params=params(),
        cost_estimate=cost(2),
        name="project_queries",
    )(first_in, weight, add, tables)


def gelu_parts(h):
    t = pl.reciprocal(1.0 + (0.3275911 / math.sqrt(2.0)) * jnp.abs(h))
    e = jnp.exp(-0.5 * h * h)
    poly = 0.5 * 1.061405429
    for coefficient in (-1.453152027, 1.421413741, -0.284496736, 0.254829592):
        poly = poly * t + 0.5 * coefficient
    tail = poly * t * e
    cdf = jnp.where(h >= 0.0, 1.0 - tail, tail)
    return h * cdf, cdf + h * e * (1.0 / math.sqrt(2.0 * math.pi))


def feed_kernel(
    place_ref,
    x_ref,
    xx_ref,
    g_ref,
    gg_ref,
    gain_ref,
    bias_ref,
    w1_ref,
    b1_ref,
    w2_ref,
    wo_ref,
    mlp_ref,
    back_ref,
    other_ref,
    attn_grad_ref,
    b1_grad_ref,
    theirs1_ref,
    mine1_ref,
    *refs,
):
    grad_refs, (in_scr, in_t_scr, g_scr, mlp_scr, back_scr) = refs[:-5], refs[-5:]
    step, steps = pl.program_id(0), pl.num_programs(0)
    rows = x_ref.shape[0]

    @pl.when(step == 0)
    def _():
        for i, (tokens, grads) in enumerate(((x_ref, g_ref), (xx_ref, gg_ref))):
            at = slice(i * rows, (i + 1) * rows)
            normed, _ = normalize(tokens[...].astype(F32))
            second_in = normed * wide(gain_ref) + wide(bias_ref)
            in_scr[at] = second_in.astype(BF16)
            in_t_scr[:, :, :, at] = second_in.T.astype(BF16).reshape(in_t_scr.shape[:3] + (rows,))
            g_scr[at] = grads[...]
        attn_grad_ref[...] = dot_nt(g_ref[...], wo_ref[...]).astype(BF16)

    g = g_scr[...]
    w1 = w1_ref[...]
    w2 = w2_ref[...]
    act, slope = gelu_parts(dot(in_scr[...], w1) + b1_ref[...])
    act = act.astype(BF16)
    pre = dot_nt(g, w2) * slope
    pre16 = pre.astype(BF16)
    b1_grad_ref[...] = jnp.sum(pre, axis=0, keepdims=True)
    mlp = dot(act, w2)
    grad = dot_tn(act, g).astype(BF16)
    if len(grad_refs) == 1:
        grad_refs[0][...] = grad
    for i in range(len(grad_refs) if len(grad_refs) > 1 else 0):

        @pl.when(step == i)
        def _(i=i):
            grad_refs[i][...] = grad

    back = dot_nt(pre16, w1)
    own = place_ref[1]
    for result, at in ((theirs1_ref, 1 - own), (mine1_ref, own)):
        left = in_t_scr[:, pl.ds(at, 1)].reshape(D // 2, 2 * rows)
        result[...] = dot(left, pre16).astype(BF16).reshape(result.shape)

    @pl.when(step == 0)
    def _():
        mlp_scr[...] = mlp
        back_scr[...] = back

    @pl.when((step > 0) & (step < steps - 1))
    def _():
        mlp_scr[...] += mlp
        back_scr[...] += back

    @pl.when(step == steps - 1)
    def _():
        for i, (scr, last, own_ref) in enumerate(((mlp_scr, mlp, mlp_ref), (back_scr, back, back_ref))):
            total = (scr[...] + last).astype(BF16)
            own_ref[...] = total[:rows]
            other_ref[i] = total[rows:]


CHUNK = 512


def feed(place, count, x, xx, g, gg, gain, bias, w1, b1, w2, wo):
    rows = x.shape[0]
    half = w1.shape[1] // 2
    depth = count // 2
    per = D // count // 2
    pieces = depth // 2
    aligned = pieces == 2 and half % 512 == 0
    chunk = half // pieces if aligned else CHUNK
    steps = half // chunk
    single = pl.Buffered(1)
    whole = lambda a: pl.BlockSpec(a.shape, lambda i, place: (0,) * a.ndim, pipeline_mode=single)
    fixed = lambda *shape: pl.BlockSpec(shape, lambda i, place: (0, 0))
    if aligned:
        piece = lambda i, place: (place[3] ^ (1 - i)) & 1
        grad_specs = [fixed(chunk, D)] * pieces
        grad_shapes = [SHAPE((chunk, D), BF16)] * pieces
    else:
        piece = lambda i, place: i
        grad_specs = [pl.BlockSpec((chunk, D), lambda i, place: (i, 0))]
        grad_shapes = [SHAPE((half, D), BF16)]
    at = lambda i, place: place[0] * steps + piece(i, place)
    cut = pl.BlockSpec((count, per, chunk), lambda i, place: (0, 0, piece(i, place)))
    spec = pltpu.PrefetchScalarGridSpec(
        num_scalar_prefetch=1,
        grid=(steps,),
        in_specs=[
            whole(x),
            whole(xx),
            whole(g),
            whole(gg),
            whole(gain),
            whole(bias),
            pl.BlockSpec((D, chunk), lambda i, place: (0, at(i, place))),
            pl.BlockSpec((1, chunk), lambda i, place: (0, at(i, place))),
            pl.BlockSpec((chunk, D), lambda i, place: (at(i, place), 0)),
            whole(wo),
        ],
        out_specs=[
            fixed(rows, D),
            fixed(rows, D),
            pl.BlockSpec((2, rows, D), lambda i, place: (0, 0, 0)),
            fixed(rows, D),
        ]
        + [pl.BlockSpec((1, chunk), lambda i, place: (0, piece(i, place))), cut, cut]
        + grad_specs,
        scratch_shapes=[
            pltpu.VMEM((2 * rows, D), BF16),
            pltpu.VMEM((count, 2, per, 2 * rows), BF16),
            pltpu.VMEM((2 * rows, D), BF16),
            pltpu.VMEM((2 * rows, D), F32),
            pltpu.VMEM((2 * rows, D), F32),
        ],
    )
    result = pl.pallas_call(
        feed_kernel,
        grid_spec=spec,
        out_shape=[SHAPE((rows, D), BF16), SHAPE((rows, D), BF16), SHAPE((2, rows, D), BF16), SHAPE((rows, D), BF16)]
        + [SHAPE((1, half), F32), SHAPE((count, per, half), BF16), SHAPE((count, per, half), BF16)]
        + grad_shapes,
        compiler_params=params(FULL_BYTES),
        cost_estimate=cost(12),
        name="feed_forward",
    )(place, x, xx, g, gg, gain, bias, w1, b1, w2, wo)
    grads = result[7:]
    if not aligned:
        cut = grads[0].reshape(pieces // 2, 2, -1, D)
        low = place[3] & 1
        grads = [take(cut, 1 - low, 1), take(cut, low, 1)]
    return result[:7], grads


def present(slot, y, z):
    back = slot // 2
    return (back <= z) & ((slot % 2 == 0) | (back >= 1) | (y == 1))


def whole_kernel(span, depth, place_ref, *refs):
    pair_refs, (q_ref, do_ref, tables_ref, rows_ref, even_out_ref, odd_out_ref) = refs[:depth], refs[depth:]
    out_ref, dq_ref = rows_ref.at[0], rows_ref.at[1]
    y, z = place_ref[2], place_ref[3]
    tables = [tables_ref[i] for i in range(3)]
    rows = PAIRS * span
    low = lax.broadcasted_iota(jnp.int32, (1, 128), 1) < HEAD_DIM

    def stacked(ref):
        return jnp.concatenate([ref[:, p * 128 : (p + 1) * 128] for p in range(PAIRS)], axis=0)

    blocks = [ref[i] for ref in pair_refs for i in range(2)]
    kv = jnp.concatenate(blocks, axis=0)
    swapped = pltpu.roll(kv.astype(F32), HEAD_DIM, 1).astype(BF16)
    zero, one = jnp.zeros_like(kv), jnp.ones_like(kv)
    keys = (jnp.where(low, kv, zero), jnp.where(low, zero, swapped))
    values = (jnp.where(low, swapped, zero), jnp.where(low, zero, kv))
    summing = (jnp.where(low, swapped, one), jnp.where(low, one, kv))
    slot = lax.broadcasted_iota(jnp.int32, (1, (2 * depth - 1) * span), 1) // span + 1
    absent = jnp.where(present(slot, y, z), 0.0, MASKED)
    token = lax.broadcasted_iota(jnp.int32, (rows, span), 0) % span
    seen = lax.broadcasted_iota(jnp.int32, (rows, span), 1) <= token
    q = stacked(q_ref)
    do = stacked(do_ref)
    do32 = do.astype(F32)

    every = [dot_nt(q, keys[h]) for h in range(2)]
    expd, mixed = [], []
    for h in range(2):
        scores = every[h]
        scores = jnp.concatenate([jnp.where(seen, scores[:, :span], MASKED), scores[:, span:] + absent], axis=1)
        top = jnp.max(scores, axis=1, keepdims=True)
        expd.append(jnp.exp(scores - top).astype(BF16))
    for h in range(2):
        mixed.append(dot(expd[h], summing[h]))
    total = jnp.where(low, pltpu.roll(mixed[0], HEAD_DIM, 1), pltpu.roll(mixed[1], HEAD_DIM, 1))
    inverse = 1.0 / total
    out = jnp.where(low, mixed[0], mixed[1]) * inverse
    for p in range(PAIRS):
        out_ref[:, p * 128 : (p + 1) * 128] = out[p * span : (p + 1) * span].astype(BF16)
    dprobs = [dot_nt(do, values[h]) for h in range(2)]
    product = do32 * out
    do_t = (do32 * inverse).T.astype(BF16)
    q_t = (q.astype(F32) * inverse).T.astype(BF16)
    dq = dk = dv = 0.0
    for h in range(2):
        head = slice(h * HEAD_DIM, (h + 1) * HEAD_DIM)
        delta = jnp.sum(jnp.where(low == (h == 0), product, 0.0), axis=1, keepdims=True)
        dprob = dprobs[h]
        dscore = (expd[h].astype(F32) * (dprob - delta)).astype(BF16)
        dq = dq + dot(dscore, keys[h])
        dk = dk + dot(q_t[head], dscore)
        dv = dv + dot(do_t[head], expd[h])
    dq = dq * (inverse * SCALE)
    for p in range(PAIRS):
        dq_ref[:, p * 128 : (p + 1) * 128] = turn(dq[p * span : (p + 1) * span], tables, -1).astype(BF16)
    both = jnp.concatenate([dk, dv], axis=0).T.astype(BF16)
    for k in range(depth):
        even_out_ref[k] = both[2 * k * span : (2 * k + 1) * span]
        odd_out_ref[k] = both[(2 * k + 1) * span : (2 * k + 2) * span]


def loop_kernel(groups, span, block, count, place_ref, *refs):
    depth = count // 2
    pair_refs, refs = refs[:depth], refs[depth:]
    q_ref, do_ref, tables_ref, rows_ref, even_out_ref, odd_out_ref = refs[:6]
    out_ref, dq_ref = rows_ref.at[0], rows_ref.at[1]
    kv_scr, e_ref, kv_t_ref, max_ref, acc_ref, ext_ref = refs[6:]
    tables = [tables_ref[i] for i in range(3)]
    rows = groups * span
    per = block // span
    y, z = place_ref[2], place_ref[3]
    used = (2 * (z + 1) + per - 1) // per
    group, group_count = pl.program_id(1), pl.num_programs(1)
    low = lax.broadcasted_iota(jnp.int32, (1, 128), 1) < HEAD_DIM
    lanes = lax.broadcasted_iota(jnp.int32, (rows, 128), 1)

    def stacked(ref):
        return jnp.concatenate([ref[:, p * 128 : (p + 1) * 128] for p in range(groups)], axis=0)

    @pl.when(group == 0)
    def _():
        for i in range(count):
            kv_scr[i * span : (i + 1) * span] = pair_refs[i // 2][i % 2]

    q = stacked(q_ref)
    do = stacked(do_ref)

    def load(b):
        kv = kv_scr[pl.ds(pl.multiple_of(b * block, block), block)]
        swapped = pltpu.roll(kv.astype(F32), HEAD_DIM, 1).astype(BF16)
        return kv, swapped, jnp.zeros_like(kv)

    def absent(b):
        row = lax.broadcasted_iota(jnp.int32, (block, 128), 0) + b * block
        lane = lax.broadcasted_iota(jnp.int32, (block, 128), 1)
        mask = jnp.where(present(row // span, y, z), 0.0, MASKED)
        return jnp.where(lane < 2, -1.0, jnp.where(lane == 2, mask, 0.0)).astype(BF16)

    def key_tiles(b):
        kv, swapped, zero = load(b)
        ext = absent(b)
        return [
            jnp.concatenate([jnp.where(low, kv, zero), ext], axis=1),
            jnp.concatenate([jnp.where(low, zero, swapped), ext], axis=1),
        ]

    def value_tiles(b):
        kv, swapped, zero = load(b)
        ext = absent(b)
        return [
            jnp.concatenate([jnp.where(low, swapped, zero), ext], axis=1),
            jnp.concatenate([jnp.where(low, zero, kv), ext], axis=1),
        ]

    def seen():
        token = lax.broadcasted_iota(jnp.int32, (rows, block), 0) % span
        key = lax.broadcasted_iota(jnp.int32, (rows, block), 1)
        return (key <= token) | (key >= span)

    def extended(values):
        high = values.astype(BF16).astype(F32)
        rest = jnp.where(lanes == 1, values - high, jnp.where(lanes == 2, 1.0, 0.0))
        return jnp.where(lanes == 0, high, rest).astype(BF16)

    def over_blocks(step):
        step(0, True)

        def body(b, carry):
            step(b, False)
            return carry

        lax.fori_loop(1, used, body, 0)

    plain = jnp.concatenate([q, jnp.where(lanes == 2, 1.0, 0.0).astype(BF16)], axis=1)

    def maxima(b, diagonal):
        keys = key_tiles(b)
        for h in range(2):
            scores = dot_nt(plain, keys[h])
            if diagonal:
                scores = jnp.where(seen(), scores, MASKED)
            top = functools.reduce(jnp.maximum, [scores[:, i : i + 128] for i in range(0, block, 128)])
            max_ref[h] = top if diagonal else jnp.maximum(max_ref[h], top)

    over_blocks(maxima)
    for h in range(2):
        top = jnp.max(max_ref[h], axis=1, keepdims=True)
        ext_ref[h] = jnp.concatenate([q, extended(jnp.broadcast_to(top, (rows, 128)))], axis=1)

    def forward(b, diagonal):
        keys = key_tiles(b)
        kv, swapped, _ = load(b)
        one = jnp.ones_like(kv)
        values = (jnp.where(low, swapped, one), jnp.where(low, one, kv))
        for h in range(2):
            expd = jnp.exp(dot_nt(ext_ref[h], keys[h]))
            if diagonal:
                expd = jnp.where(seen(), expd, 0.0)
            expd = expd.astype(BF16)
            e_ref[b, h] = expd
            mixed = dot(expd, values[h])
            acc_ref[h] = mixed if diagonal else acc_ref[h] + mixed

    over_blocks(forward)
    first, second = acc_ref[0], acc_ref[1]
    total = jnp.where(low, pltpu.roll(first, HEAD_DIM, 1), pltpu.roll(second, HEAD_DIM, 1))
    inverse = 1.0 / total
    out = jnp.where(low, first, second) * inverse
    for p in range(groups):
        out_ref[:, p * 128 : (p + 1) * 128] = out[p * span : (p + 1) * span].astype(BF16)
    do32 = do.astype(F32)
    product = do32 * out
    high = product.astype(BF16)
    rest = (product - high.astype(F32)).astype(BF16)
    place = lax.broadcasted_iota(jnp.int32, (128, 128), 0)
    for h in range(2):
        ones = jnp.where((place < HEAD_DIM) == (h == 0), 1.0, 0.0).astype(BF16)
        delta = dot(high, ones) + dot(rest, ones)
        ext_ref[h] = jnp.concatenate([do, extended(delta)], axis=1)
    do_t = (do32 * inverse).T.astype(BF16)
    q_t = (q.astype(F32) * inverse).T.astype(BF16)

    def backward(b, start):
        values = value_tiles(b)
        kv, swapped, zero = load(b)
        keys = (jnp.where(low, kv, zero), jnp.where(low, zero, swapped))
        dq = dk = dv = 0.0
        for h in range(2):
            expd = e_ref[b, h]
            head = slice(h * HEAD_DIM, (h + 1) * HEAD_DIM)
            dscore = (expd.astype(F32) * dot_nt(ext_ref[h], values[h])).astype(BF16)
            dq = dq + dot(dscore, keys[h])
            dk = dk + dot(q_t[head], dscore)
            dv = dv + dot(do_t[head], expd)
        acc_ref[0] = dq if start else acc_ref[0] + dq
        both = jnp.concatenate([dk, dv], axis=0)
        kv_t_ref[b] = jnp.where(group == 0, both, kv_t_ref[b] + both)

    over_blocks(backward)
    dq = acc_ref[0] * (inverse * SCALE)
    for p in range(groups):
        dq_ref[:, p * 128 : (p + 1) * 128] = turn(dq[p * span : (p + 1) * span], tables, -1).astype(BF16)

    @pl.when(group == group_count - 1)
    def _():
        for b in range(count // per):
            used_block = jnp.where(b < used, kv_t_ref[b], 0.0).T.astype(BF16)
            for i in range(per):
                slot = b * per + i
                result = odd_out_ref if slot % 2 else even_out_ref
                result[slot // 2] = used_block[i * span : (i + 1) * span]


def attention(place, pairs, q, do, tables):
    depth = len(pairs)
    count = 2 * depth
    seqs, span, _ = q.shape
    single = count * span <= 1024
    groups = PAIRS if single else 2
    wide_spec = pl.BlockSpec((None, span, groups * 128), lambda s, i: (s, 0, i))
    pieces = pl.BlockSpec((depth, None, span, 128), lambda s, i: (0, s, 0, 0))
    two = pl.BlockSpec((2, None, span, 128), lambda s, i: (0, s, 0, 0))
    if single:
        kernel, scratch = functools.partial(whole_kernel, span, depth), []
    else:
        block = max(512, span)
        blocks = count * span // block
        rows = groups * span
        kernel = functools.partial(loop_kernel, groups, span, block, count)
        scratch = [
            pltpu.VMEM((count * span, 128), BF16),
            pltpu.VMEM((blocks, 2, rows, block), BF16),
            pltpu.VMEM((blocks, 128, block), F32),
            pltpu.VMEM((2, rows, 128), F32),
            pltpu.VMEM((2, rows, 128), F32),
            pltpu.VMEM((2, rows, 256), BF16),
        ]
    return pl.pallas_call(
        kernel,
        grid=(seqs, PAIRS // groups),
        in_specs=[SMEM] + [two] * depth + [wide_spec, wide_spec, pl.BlockSpec(tables.shape, lambda s, i: (0, 0, 0))],
        out_specs=[pl.BlockSpec((2, None, span, groups * 128), lambda s, i: (0, s, 0, i))] + [pieces] * 2,
        out_shape=[SHAPE((2, seqs, span, D), BF16)]
        + [SHAPE((depth, seqs, span, 128), BF16)] * 2,
        scratch_shapes=scratch,
        compiler_params=params(FULL_BYTES),
        cost_estimate=cost(10),
        name="attention",
    )(place, *pairs, q, do, tables)


def weights_kernel(place_ref, attn_ref, attn2_ref, g_ref, g2_ref, in_ref, in2_ref, q_ref, q2_ref, theirs_ref, mine_ref, small_ref, scr):
    half = D // 2
    y = place_ref[2]

    def products(left, right, line):
        at = pl.ds(pl.multiple_of(place_ref[0] * half, 128), half)
        small_ref[line : line + 1] = jnp.zeros_like(small_ref[line : line + 1])
        small_ref[line : line + 1, at] = jnp.sum(right.astype(F32), axis=0, keepdims=True)
        scr[...] = dot_tn(left, right).reshape(scr.shape)
        theirs_ref[0] = scr[:, pl.ds(1 - y, 1)].reshape(theirs_ref.shape[1:]).astype(BF16)
        mine_ref[0] = scr[:, pl.ds(y, 1)].reshape(mine_ref.shape[1:]).astype(BF16)

    both = lambda a, b: jnp.concatenate([a[...], b[...]], axis=0)

    @pl.when(pl.program_id(0) == 0)
    def _():
        products(both(attn_ref, attn2_ref), both(g_ref, g2_ref), 1)

    @pl.when(pl.program_id(0) == 1)
    def _():
        products(both(in_ref, in2_ref), both(q_ref, q2_ref), 0)


def weights(place, count, both, both2, g, g2, first_in, first_in2):
    rows = g.shape[0]
    depth, per, half = count // 2, D // count, D // 2
    whole = pl.BlockSpec((rows, D), lambda i, place: (0, 0), pipeline_mode=pl.Buffered(1))
    part = pl.BlockSpec((rows, half), lambda i, place: (0, place[0]), pipeline_mode=pl.Buffered(1))
    attn_part = pl.BlockSpec((None, rows, D), lambda i, place: (0, 0, 0), pipeline_mode=pl.Buffered(1))
    q_part = pl.BlockSpec((None, rows, half), lambda i, place: (1, 0, place[0]), pipeline_mode=pl.Buffered(1))
    result = pl.BlockSpec((1, depth, per, half), lambda i, place: (i, 0, 0, 0))
    return pl.pallas_call(
        weights_kernel,
        grid_spec=pltpu.PrefetchScalarGridSpec(
            num_scalar_prefetch=1,
            grid=(2,),
            in_specs=[attn_part, attn_part, part, part, whole, whole, q_part, q_part],
            out_specs=[result, result, pl.BlockSpec((8, D), lambda i, place: (0, 0))],
            scratch_shapes=[pltpu.VMEM((depth, 2, per, half), F32)],
        ),
        out_shape=[SHAPE((2, depth, per, half), BF16), SHAPE((2, depth, per, half), BF16), SHAPE((8, D), F32)],
        compiler_params=params(FULL_BYTES),
        cost_estimate=cost(2.4),
        name="weights",
    )(place, both, both2, g, g2, first_in, first_in2, both, both2)


def mix_kernel(x_ref, mlp_ref, mlp2_ref, attn_ref, add_ref, wo_ref, output_ref):
    mlp = mlp_ref[...].astype(F32) + mlp2_ref[...].astype(F32)
    x = x_ref[...].astype(F32)
    output_ref[...] = (x + (mlp + dot(attn_ref[...], wo_ref[...])) + wide(add_ref)).astype(BF16)


def mix(x, mlp, other, both, add, wo):
    rows = x.shape[0]
    row = pl.BlockSpec((rows, D), lambda i: (i, 0))
    first = pl.BlockSpec((None, rows, D), lambda i: (0, i, 0))
    return pl.pallas_call(
        mix_kernel,
        grid=(1,),
        in_specs=[row, row, first, first, pl.BlockSpec((D,), lambda i: (0,)), pl.BlockSpec((D, D), lambda i: (0, 0))],
        out_specs=row,
        out_shape=SHAPE((rows, D), BF16),
        compiler_params=params(),
        cost_estimate=cost(1.2),
        name="mix",
    )(x, mlp, other, both, add, wo)


def two_terms(values):
    high = values.astype(BF16)
    return high, (values - high.astype(F32)).astype(BF16)


def message_lines(ff):
    return -(-(ff // 128 + 6 * (D // 128) + 1) // 16) * 16


def finish_kernel(
    copies,
    count,
    lines,
    place_ref,
    *refs,
):
    kv_refs, refs = refs[:count], refs[count:]
    (
        extra_ref,
        x_ref,
        g_ref,
        q_ref,
        back_ref,
        back2_ref,
        gain_ref,
        bias_ref,
        gain2_ref,
        wqkv_ref,
        tables_ref,
        b1_ref,
        early_ref,
        tokens_ref,
        theirs_ref,
        mine_ref,
        vector_scr,
        weight_scr,
    ) = refs
    total = extra_ref[...].astype(F32)
    for ref in kv_refs:
        total += ref[...].astype(F32)
    tables = repeated(tables_ref, copies)
    grad = turn(total, key_tables(tables), -1).astype(BF16)
    x = x_ref[...].astype(F32)
    normed, inverse = normalize(x)
    gain = wide(gain_ref)
    first_in = normed * gain + wide(bias_ref)
    first_grad = dot_nt(jnp.concatenate([q_ref[...], grad], axis=1), wqkv_ref[...])
    second_grad = back_ref[...].astype(F32) + back2_ref[...].astype(F32)

    vector_scr[...] = jnp.zeros_like(vector_scr)
    b1 = b1_ref[...]
    b1_lines = b1.shape[1] // 128
    for i in range(b1_lines):
        vector_scr[pl.ds(place_ref[0] * b1_lines + i, 1)] = b1[:, i * 128 : (i + 1) * 128]
    at = 2 * b1_lines
    sums = [early_ref[0:1], jnp.sum(grad.astype(F32), axis=0, keepdims=True), early_ref[1:2]]
    for rows in (first_grad * normed, first_grad, second_grad * normed, second_grad):
        sums.append(jnp.sum(rows, axis=0, keepdims=True))
    for row in sums:
        for i in range(row.shape[1] // 128):
            vector_scr[at : at + 1] = row[:, i * 128 : (i + 1) * 128]
            at += 1
    high, rest = two_terms(vector_scr[...])
    weight_scr[...] = dot(first_in.T.astype(BF16), grad).reshape(weight_scr.shape)
    y = place_ref[2]
    for message, at in ((theirs_ref, 1 - y), (mine_ref, y)):
        message[:lines] = high
        message[lines : 2 * lines] = rest
        message[2 * lines :] = weight_scr[:, pl.ds(at, 1)].reshape(-1, 128).astype(BF16)

    normed_grad = first_grad * gain + second_grad * wide(gain2_ref)
    mean = jnp.mean(normed_grad, axis=-1, keepdims=True)
    along_rows = jnp.mean(normed_grad * normed, axis=-1, keepdims=True)
    tokens_ref[...] = (g_ref[...].astype(F32) + inverse * (normed_grad - mean - normed * along_rows)).astype(BF16)


def finish(place, places, ff, kv_parts, extra, x, g, both, back, other, gain, bias, gain2, wqkv, tables, b1, early):
    rows = x.shape[0]
    lines = message_lines(ff)
    whole = lambda a: pl.BlockSpec(a.shape, lambda i: (0,) * a.ndim)
    second = pl.BlockSpec((None, rows, D), lambda i: (1, 0, 0))
    before, between, behind = (*kv_parts, extra, x, g), (back,), (gain, bias, gain2, wqkv, tables, b1, early)
    return pl.pallas_call(
        functools.partial(finish_kernel, rows // tables.shape[1], len(kv_parts), lines),
        grid=(1,),
        in_specs=[SMEM]
        + [whole(a) for a in before]
        + [second]
        + [whole(a) for a in between]
        + [second]
        + [whole(a) for a in behind],
        out_specs=[
            pl.BlockSpec((rows, D), lambda i: (0, 0)),
            pl.BlockSpec((2 * lines + D // 2, 128), lambda i: (0, 0)),
            pl.BlockSpec((2 * lines + D // 2, 128), lambda i: (0, 0)),
        ],
        out_shape=[SHAPE((rows, D), BF16)] + [SHAPE((2 * lines + D // 2, 128), BF16)] * 2,
        scratch_shapes=[pltpu.VMEM((lines, 128), F32), pltpu.VMEM((places // 2, 2, D // places, 128), F32)],
        compiler_params=params(),
        cost_estimate=cost(2.4),
        name="finish",
    )(place, *before, both, *between, other, *behind)


def message_cut(place, mine, come, lines, per):
    count = (mine.shape[0] - 2 * lines) // per

    def kernel(place_ref, a_ref, b_ref, *refs):
        results, scr = refs[:-1], refs[-1]
        high, rest = two_terms(tree_sum([ref[at : at + lines] for ref in (a_ref, b_ref) for at in (0, lines)]))
        scr[...] = (a_ref[2 * lines :].astype(F32) + b_ref[2 * lines :].astype(F32)).reshape(scr.shape)
        for i, result in enumerate(results):
            result[:lines] = high
            result[lines : 2 * lines] = rest
            result[2 * lines :] = scr[place_ref[3] ^ i].astype(BF16)

    return pl.pallas_call(
        kernel,
        in_specs=[SMEM, VMEM, VMEM],
        out_specs=[VMEM] * count,
        out_shape=[SHAPE((2 * lines + per, 128), BF16)] * count,
        scratch_shapes=[pltpu.VMEM((count, per, 128), F32)],
        compiler_params=params(),
        cost_estimate=cost(0.6),
        name="message_cut",
    )(place, mine, come)


def message_sum(messages, lines):
    def kernel(*refs):
        result = refs[-1]
        total = tree_sum([ref[...] for ref in refs[:-1]])
        high, rest = two_terms(total[:lines] + total[lines : 2 * lines])
        result[:lines] = high
        result[lines : 2 * lines] = rest
        result[2 * lines :] = total[2 * lines :].astype(BF16)

    return pl.pallas_call(
        kernel,
        in_specs=[VMEM] * len(messages),
        out_specs=VMEM,
        out_shape=SHAPE(messages[0].shape, BF16),
        compiler_params=params(),
        cost_estimate=cost(0.6),
        name="message_sum",
    )(*messages)


def last_sums(place, messages, lines, widths, top, mine2, other2, mine3, other3):
    count = len(messages)
    half = D // 2
    per = mine3.shape[1]

    def kernel(place_ref, *refs):
        sources, (a2, b2, a3, b3) = refs[:count], refs[count : count + 4]
        vectors, (second, out, qkv) = refs[count + 4 : -3], refs[-3:]
        core = place_ref[0]
        total = tree_sum([ref[...] for ref in sources])
        vector = total[:lines] + total[lines : 2 * lines]
        at = 0
        for result, width in zip(vectors, widths):
            for i in range(width // 128):
                result[i * 128 : (i + 1) * 128] = vector[at + i]
            at += width // 128
        owner = (place_ref[3] >> top) == core
        second[...] = jnp.where(owner, a2[...].astype(F32), b2[...].astype(F32))
        for i, result in ((0, out), (1, qkv)):
            own, other = a3[i].astype(F32), b3[i].astype(F32)
            result[:, :half] = jnp.where(core == 0, own, other)
            result[:, half:D] = jnp.where(core == 0, other, own)
        qkv[:, D:] = total[2 * lines :]

    return pl.pallas_call(
        kernel,
        in_specs=[SMEM] + [VMEM] * (count + 4),
        out_specs=[VMEM] * (len(widths) + 3),
        out_shape=[SHAPE((width,), F32) for width in widths]
        + [SHAPE(mine2.shape, F32), SHAPE((per, D), F32), SHAPE((per, D + 128), F32)],
        compiler_params=params(),
        cost_estimate=cost(0.6),
        name="last_sums",
    )(place, *messages, mine2, other2, mine3, other3)


def local(
    tokens,
    ln1_gain,
    ln1_bias,
    qkv_weight,
    qkv_bias,
    out_weight,
    ln2_gain,
    ln2_bias,
    fc1_weight,
    fc1_bias,
    fc2_weight,
    out_bias,
    output_grad,
    key_value_grad,
):
    seqs, span, _ = tokens.shape
    rows = seqs * span
    ff = fc1_weight.shape[1]
    count = lax.axis_size("seq")
    batches = lax.axis_size("batch")
    depth = count // 2
    half_depth = depth // 2
    per1, per2 = D // count, ff // count
    own = lax.axis_index("seq").astype(jnp.int32)
    batch = lax.axis_index("batch").astype(jnp.int32)
    y, z = own & 1, own >> 1
    core, xs = batch & 1, batch >> 1
    place = jnp.stack([core, xs, y, z])
    x = tokens.reshape(rows, D)
    g = output_grad.reshape(rows, D)
    over_core = lambda v: flipped(v, "batch", 1)
    over_x = lambda v: flipped(v, "batch", 2)
    over_y = lambda v: flipped(v, "seq", 1)
    over_z = lambda v, bit: flipped(v, "seq", 2 << bit)
    z_bits = depth.bit_length() - 1
    flat = lambda v: v.reshape(rows, -1)

    def pair(mine, other, index, axis):
        first = jnp.where(index == 0, mine, other)
        second = jnp.where(index == 0, other, mine)
        return jnp.concatenate([first, second], axis=axis)

    def summed(*parts):
        return tree_sum(parts).astype(BF16)

    x_other, g_other = over_core(x), over_core(g)
    tables = rotary_tables(own * span, span)
    kv, first_in = project_keys(x, ln1_gain, ln1_bias, qkv_weight, qkv_bias, tables)
    kv3 = kv.reshape(seqs, span, 128)
    kv_y = over_y(kv3)
    first_other = over_core(first_in)
    q = project_queries(first_in, qkv_weight, qkv_bias, tables)
    (kv_y,) = after((kv_y,), q)
    two = jnp.stack([kv3, kv_y])
    pairs = [two] + [along(two, k) for k in range(1, depth)]

    x_fed, g_fed, first_other = after((x, g, first_other), two)
    (mlp, back, feed_other, attn_grad, b1_grad, theirs1, mine1), (theirs2, mine2) = feed(
        place, count, *after((x_fed, x_other, g_fed, g_other), first_other), ln2_gain, ln2_bias, fc1_weight, fc1_bias.reshape(1, -1),
        fc2_weight, out_weight,
    )
    come1 = over_x(theirs1)
    come2 = over_z(theirs2, 0)
    feed_come = over_core(feed_other)

    q3, do3 = q.reshape(seqs, span, D), attn_grad.reshape(seqs, span, D)
    both, even, odd = attention(place, pairs, q3, do3, tables)
    odd = over_y(odd)

    def halved(a, parts, height):
        return a.reshape(parts, 2, height, a.shape[-1])

    both = both.reshape(2, rows, D)
    both_other = over_core(both)
    mine1, come1, mine2, come2, feed_come = after((mine1, come1, mine2, come2, feed_come), both)
    height = per2 // 2
    view1 = lambda v: halved(v, depth // 2, per1)
    view2 = lambda v: halved(v, half_depth, height)
    theirs1, mine1, theirs2, mine2 = add_split(
        place, [(view1(mine1), view1(come1), 3), (view2(mine2), view2(come2), 1)], 6
    )
    come1, come2 = over_z(theirs1, 0), over_x(theirs2)

    (both_other,) = after((both_other,), theirs1)
    theirs3, mine3, early = weights(place, count, both, both_other, g, g_other, first_in, first_other)
    come3 = over_y(theirs3)

    even, odd = after((even, odd), theirs3)
    kv_sums = [summed(even[k], odd[k]) for k in range(depth)]
    (x_mix,) = after((x,), *kv_sums)
    output = mix(x_mix, mlp, feed_come, both, out_bias, out_weight)
    (kv_next,) = after((kv_sums[1],), output)
    got = [along(kv_next, -1)] + [along(kv_sums[k], -k) for k in range(2, depth)]

    mine1, come1, mine2, come2 = after((mine1, come1, mine2, come2), output)
    view1 = lambda v: halved(v, depth // 2, per1 // 2)
    view2 = lambda v: halved(v, half_depth // 2, height)
    theirs12, mine1, mine2 = exchange_split(place, view1(mine1), view1(come1), view2(mine2), view2(come2))
    come12 = over_y(theirs12)
    mine3, come3 = after((mine3, come3), theirs12)
    parts3 = add_cut(place, mine3, come3)
    come3 = [flipped(parts3[i], "seq", 2 * i) for i in range(1, depth)]

    got = after(got, parts3[0])
    lines = message_lines(ff)
    tokens_grad, theirs4, mine4 = finish(
        place, count, ff, [flat(v) for v in (kv_sums[0], *got)], flat(key_value_grad), x, g, both, back, feed_come,
        ln1_gain, ln1_bias, ln2_gain, qkv_weight, tables, b1_grad, early,
    )
    come4 = over_y(theirs4)

    mine1, mine2, come12 = after((mine1, mine2, come12), tokens_grad)
    theirs1, mine1, sum2 = exchange_add(place, mine1, mine2, come12, 1)
    come1 = over_z(theirs1, 1)
    for bit in range(2, z_bits):
        view1 = lambda v: halved(v, depth >> (bit + 1), per1 // 2)
        theirs1, mine1 = add_split(place, [(view1(mine1), view1(come1), 3 + bit)], 0.01)
        come1 = over_z(theirs1, bit)
    for bit in range(1, z_bits - 1):
        sum2 = halved(sum2, half_depth >> (bit + 1), height)
        own_bit = (z >> bit) & 1
        sum2 = summed(take(sum2, own_bit, 1), over_z(take(sum2, 1 - own_bit, 1), bit))
    sum2 = sum2.reshape(height, D)
    come2 = to_owner(sum2)

    come3 = after(come3, theirs1, sum2)
    mine4, come4 = after((mine4, come4), *come3)
    parts4 = message_cut(place, mine4, come4, lines, per1)
    come4 = [flipped(parts4[i], "seq", 2 * i) for i in range(1, depth)]
    mine1, come1 = after((mine1, come1), parts4[0])
    sum1 = summed(mine1, come1).reshape(per1 // 2, -1)
    other1 = over_x(sum1)
    come3 = after(come3, sum1)
    sum3 = summed(parts3[0], *come3)
    other3 = over_x(sum3)
    sum2, come2 = after((sum2, come2), sum3)
    sum2 = summed(sum2, come2)
    other2 = between_owners(sum2)
    come4 = after(come4, sum2)
    message = message_sum([parts4[0], *come4], lines)
    got = [flipped(message, "batch", i) for i in range(1, batches)]

    sum1, other1 = after((sum1, other1), message)
    sum1 = pair(sum1, other1, xs, 0)
    other1 = over_core(sum1)
    sum3, other3 = after((sum3, other3), sum1)
    sum3 = summed(sum3, other3)
    other3 = over_core(sum3)
    sum2, other2 = after((sum2, other2), sum3)
    sum2 = pair(sum2, other2, xs, 0)
    other2 = over_core(sum2)

    (other1,) = after((other1,), sum2)
    fc1_grad = pair(sum1, other1, core, 1).astype(F32)
    got = after(got, fc1_grad)
    widths = (ff, D + 128) + (D,) * 5
    b1_sum, qkv_sum, out_sum, gain1, bias1, gain2, bias2, fc2_grad, out_grad, qkv_grad = last_sums(
        place, [message, *got], lines, widths, z_bits - 1, sum2, other2, sum3, other3
    )
    return (
        output.reshape(tokens.shape),
        kv3,
        tokens_grad.reshape(tokens.shape),
        gain1,
        bias1,
        qkv_grad,
        qkv_sum,
        out_grad,
        gain2,
        bias2,
        fc1_grad,
        b1_sum,
        fc2_grad,
        out_sum,
    )


def solution(mesh):
    part = P("batch", "seq", None)
    whole = P()
    split = P("seq", None)
    return jax.shard_map(
        local,
        mesh=mesh,
        in_specs=(part,) + (whole,) * 11 + (part, part),
        out_specs=(
            part, part, part, whole, whole, split, whole, split, whole, whole, split, whole, split, whole,
        ),
        check_vma=False,
    )
```
